32 devices in a mesh: obs: 4 (over x, core), pix: 2 (over y), chan: 4 (over z).
Axes of the slice: x: 2, y: 2, z: 4, core: 2. Of those that a mesh axis runs over, the one named last changes fastest.
Arguments:
- spectra: bfloat16 [16384, 4608], P(('obs', 'pix'), 'chan'), may hold values from -6 to 6
- enc_weight: bfloat16 [4608, 256], P('chan'), may hold values from -0.09375 to 0.09375
- pix_tile: int32 [16384, 1], P(('obs', 'pix')), may hold values from 0 to 1; in each aligned block of 512 rows (0 to 511, 512 to 1023, ...) at most 512 rows name the same one
- pix_local: int32 [16384], P(('obs', 'pix')), may hold values from 0 to 4095
- foot_weight: float32 [16384], P(('obs', 'pix')), may hold values from 0.001 to 0.01
- cotangent: bfloat16 [8192, 256], P('pix'), may hold values from -6 to 6
- adjoint: int32 [8, 8192], P(None, 'pix'), may hold values from 0 to 8191, as said below
- mixing: float32 [8, 256], replicated, may hold values from -2 to 2
Outputs:
- grad_enc: float32 [4608, 256], P('chan')
The draws below stay inside these ranges and needn't reach their ends.
Inputs may be any that keep to these rules, and one draw needn't show every extreme that they name: `pix_tile`: in each aligned block of 512 rows no tile is named by more than 512 rows, a bound that some block reaches. `adjoint`: every entry is a pixel at most 128 away in index from its column's pixel; in every column the first entry is exactly 128 away.
All inputs are finite; a program needn't handle non-finite values.
Results may differ from the reference program's by a relative error of at most 0.006.
Values may be sent and summed in bfloat16 or wider, within the bound.
No kernel may reach another device: no remote copies, remote signals or barrier semaphores. Data moves between devices by JAX's collectives and lax.ppermute only.
A program may use at most 128 MiB of HBM per device.

```python
import math
import jax
import jax.numpy as jnp
import numpy as np
from jax import lax

CHANNELS = 4608
EMBED = 256
NEIGH = 8
HALO = 128
PT = 4096
QROWS = 512
CAP = 512
NTILES = 2
NPIX = 8192
FOOTPRINTS = 16384
N_CHAN = 4


def draw_adjoint(key, part):
    key_offset, key_sign = jax.random.split(jax.random.fold_in(key, 17))
    position = jnp.arange(NPIX, dtype=jnp.int32)
    offsets = jax.random.randint(key_offset, (NEIGH, NPIX), -HALO, HALO + 1).astype(jnp.int32)
    signs = (jax.random.randint(key_sign, (NPIX,), 0, 2) * 2 - 1).astype(jnp.int32)
    offsets = offsets.at[0].set(signs * HALO)
    candidate = position[None, :] + offsets
    inside = (candidate >= 0) & (candidate < NPIX)
    return jnp.where(inside, candidate, position[None, :] - offsets).astype(jnp.int32)


def touch_ends(array, rng, low, top_value):
    place = [jax.random.randint(jax.random.fold_in(rng, axis), (), 0, length) for axis, length in enumerate(array.shape)]
    widest = array.shape.index(max(array.shape))
    next_to = place[:widest] + [(place[widest] + 1) % array.shape[widest]] + place[widest + 1:]
    return array.at[tuple(place)].set(low).at[tuple(next_to)].set(top_value)


def level_of(own_key, shape, cuts, least, high):
    def one(dim, parts):
        draws = jax.random.uniform(jax.random.fold_in(jax.random.fold_in(own_key, 6), dim), (parts,), jnp.float32, least / len(cuts), high / len(cuts))
        return jnp.repeat(jnp.exp(draws), shape[dim] // parts).reshape((-1,) + (1,) * (len(shape) - dim - 1))

    gain = one(*cuts[0])
    for cut in cuts[1:]:
        gain = gain * one(*cut)
    return gain


def deal_out(own_key, own, number, rows, amount, top, most, lean):
    sequence = jax.random.permutation(own_key, amount)
    heavy_load, ordinary = load_shares(amount, rows * top, most, lean, True), load_shares(amount, rows * top, most, lean, False)
    places = jnp.arange(amount)

    def named(tallies, rotation):
        used = int((tallies > 0).sum())
        fixed = max(1, used // 4)
        moved = fixed + (places - fixed + rotation * (used - fixed)) % max(1, amount - fixed)
        return jnp.zeros((amount,), jnp.int32).at[sequence[jnp.where(places < fixed, places, moved)]].set(jnp.asarray(tallies, jnp.int32))

    tallies = jnp.where(number % 4 == 0, named(heavy_load, number // 4), named(ordinary, number - number // 4 - 1))
    mixed = jax.random.permutation(jax.random.fold_in(own, 3), amount)
    giver, receiver = mixed[0:amount // 2 * 2:2], mixed[1:amount // 2 * 2:2]
    slack = jnp.minimum(tallies[giver] - 1, most - tallies[receiver]) // 2
    slack = jnp.where((giver == sequence[0]) | (receiver == sequence[0]) | (tallies[receiver] == 0), 0, jnp.maximum(slack, 0))
    moved = jax.random.randint(jax.random.fold_in(own, 4), (amount // 2,), 0, 1 << 20) % (slack + 1)
    tallies = tallies.at[giver].add(-moved).at[receiver].add(moved)
    labels = jnp.searchsorted(jnp.cumsum(tallies), jnp.arange(rows * top), side="right").astype(jnp.int32)
    listing = labels.reshape(top, rows).T
    listing = listing[jax.random.permutation(jax.random.fold_in(own, 1), rows)]
    rotation = jax.random.randint(jax.random.fold_in(own, 2), (rows, 1), 0, top)
    return jnp.take_along_axis(listing, (jnp.arange(top)[None, :] + rotation) % top, axis=1)


def load_shares(number_of, total, bound, lean, full):
    loads = [(1 << 20) // math.isqrt(grade ** lean) + 1 for grade in range(1, number_of + 1)]
    largest = bound if full else min(bound, max(-(-total // number_of), total * loads[0] // sum(loads)))
    least = 1 if total - largest >= number_of - 1 else 0
    holding, surplus = [largest] + [least] * (number_of - 1), total - largest - least * (number_of - 1)
    while surplus > 0:
        free = [i for i in range(1, number_of) if holding[i] < largest] or [i for i in range(1, number_of) if holding[i] < bound]
        mass, budget = sum([loads[i] for i in free]), surplus
        for i in free:
            more = min(bound - holding[i], max(1, budget * loads[i] // mass), surplus)
            holding[i] = holding[i] + more
            surplus = surplus - more
    return np.array(holding)


def bell_draw(key, shape, width, bound, pieces=(), kind=jnp.bfloat16):
    values = width * jax.random.normal(key, shape, jnp.float32)
    if pieces:
        values = values * level_of(key, shape, pieces, -0.22, 0.18)
    return jnp.clip(values, -bound, bound).astype(kind)


def setup_inputs(seed: int = 0) -> dict:
    key_of = jax.random.split(jax.random.key(seed), 9)
    spectra = bell_draw(key_of[0], (FOOTPRINTS, CHANNELS), 1.0, 6.0, ((0, 8), (1, 4)))
    enc_weight = bell_draw(key_of[1], (CHANNELS, EMBED), CHANNELS ** -0.5, 0.09375, ((0, 4),))
    pix_tile_keys = jax.random.split(jax.random.fold_in(key_of[2], 1), FOOTPRINTS // QROWS)
    pix_tile_turns = jax.random.permutation(jax.random.fold_in(key_of[2], 3), FOOTPRINTS // QROWS)
    pix_tile = jax.vmap(lambda own, number: deal_out(jax.random.fold_in(key_of[2], 2), own, number, QROWS, NTILES, 1, CAP, 2))(pix_tile_keys, pix_tile_turns).reshape((FOOTPRINTS, 1))
    pix_local = touch_ends(jax.random.randint(key_of[3], (FOOTPRINTS,), 0, PT), jax.random.fold_in(key_of[3], 1), 0, PT - 1).astype(jnp.int32)
    foot_weight = jnp.clip(jnp.exp(math.log(0.01) - 2.30258502 * jax.random.uniform(key_of[4], (FOOTPRINTS,), jnp.float32) ** level_of(key_of[4], (FOOTPRINTS,), ((0, 8),), -0.2, 0.2)), 0.001, 0.01)
    cotangent = bell_draw(key_of[5], (NPIX, EMBED), 1.0, 6.0, ((0, 2),))
    adjoint = draw_adjoint(jax.random.fold_in(key_of[8], 71), 0)
    mixing = bell_draw(key_of[7], (NEIGH, EMBED), 0.35, 2.0, (), jnp.float32)
    return dict(spectra=spectra, enc_weight=enc_weight, pix_tile=pix_tile, pix_local=pix_local, foot_weight=foot_weight, cotangent=cotangent, adjoint=adjoint, mixing=mixing)


def reference(spectra, enc_weight, pix_tile, pix_local, foot_weight, cotangent, adjoint, mixing):
    group_width = CHANNELS // N_CHAN
    pre = jnp.zeros((spectra.shape[0], enc_weight.shape[1]), jnp.float32)
    for group in range(N_CHAN):
        lower = group * group_width
        partial_value = jnp.dot(spectra[:, lower:lower + group_width], enc_weight[lower:lower + group_width], preferred_element_type=jnp.float32)
        rounded = lax.optimization_barrier(partial_value.astype(jnp.bfloat16))
        pre = pre + rounded.astype(jnp.float32)
    sigma = jax.nn.sigmoid(pre)
    deriv = sigma * (1.0 + pre * (1.0 - sigma))
    summed = cotangent.astype(jnp.float32)
    for neighbor in range(NEIGH):
        summed = summed + jnp.take(cotangent, adjoint[neighbor], axis=0).astype(jnp.float32) * mixing[neighbor]
    pixel_grad = summed.astype(jnp.bfloat16)
    pixel_index = (pix_tile[:, 0] * PT + pix_local).astype(jnp.int32)
    fetched = jnp.take(pixel_grad, pixel_index, axis=0).astype(jnp.float32)
    grad_pre = (foot_weight[:, None] * deriv * fetched).astype(jnp.bfloat16)
    return lax.dot_general(spectra, grad_pre, (((0,), (0,)), ((), ())), preferred_element_type=jnp.float32)
```

```python
import jax
import jax.numpy as jnp
from jax import lax
from jax.sharding import PartitionSpec as P

NEIGH = 8
HALO = 128


def extended(value, sides, width):
    for axis, dim in sides:
        size, length = (lax.axis_size(axis), value.shape[dim])
        up = [(i, (i + 1) % size) for i in range(size - 1)]
        down = [(j, i) for i, j in up]
        last = lax.slice_in_dim(value, length - width, length, axis=dim)
        first = lax.slice_in_dim(value, 0, width, axis=dim)
        before = lax.ppermute(last, axis, up)
        after = lax.ppermute(first, axis, down)
        value = jnp.concatenate([before, value, after], axis=dim)
    return value


def fetch_rows(pixel_grad, tile_ids, local_ids, capacity):
    tile_count = lax.axis_size("pix")
    feature_count = pixel_grad.shape[1]
    onehot = (tile_ids[:, None] == jnp.arange(tile_count, dtype=jnp.int32)[None, :]).astype(
        jnp.int32
    )
    place_rank = jnp.sum((jnp.cumsum(onehot, axis=0) - 1) * onehot, axis=1)
    slot_index = tile_ids * capacity + place_rank
    outgoing = jnp.full((tile_count * capacity,), -1, jnp.int32).at[slot_index].set(local_ids)
    outgoing = outgoing.reshape(tile_count, capacity)
    requested = lax.all_to_all(outgoing, "pix", split_axis=0, concat_axis=0, tiled=True)
    usable = requested >= 0
    fetched = jnp.take(pixel_grad, jnp.where(usable, requested, 0), axis=0)
    fetched = jnp.where(usable[..., None], fetched, jnp.zeros_like(fetched))
    answers = lax.all_to_all(fetched, "pix", split_axis=0, concat_axis=0, tiled=True)
    return jnp.take(answers.reshape(tile_count * capacity, feature_count), slot_index, axis=0)


def pre_gradient(pre, fetched, weights):
    sigma = jax.nn.sigmoid(pre)
    deriv = sigma * (1.0 + pre * (1.0 - sigma))
    return (weights[:, None] * deriv * fetched.astype(jnp.float32)).astype(jnp.bfloat16)


def swap(value, axis, bit):
    size = lax.axis_size(axis)
    return lax.ppermute(value, axis, [(i, i ^ bit) for i in range(size)])


def halves(value, which, dim=0):
    length = value.shape[dim] // 2
    own = lax.dynamic_slice_in_dim(value, which * length, length, dim)
    other = lax.dynamic_slice_in_dim(value, (1 - which) * length, length, dim)
    return own, other


def joined(own, other, which):
    first = jnp.where(which == 0, own, other)
    second = jnp.where(which == 0, other, own)
    return jnp.concatenate([first, second], axis=0)


def bits_of(axis):
    size = lax.axis_size(axis)
    index = lax.axis_index(axis)
    return [(1 << n, (index >> n) & 1) for n in range(size.bit_length() - 1)]


def sum_and_split(parts, axis):
    total = parts.astype(jnp.float32)
    for bit, which in bits_of(axis):
        keep, send = halves(total, which)
        total = keep + swap(send.astype(jnp.bfloat16), axis, bit).astype(jnp.float32)
    return total


def gather_back(rows, axis):
    for bit, which in reversed(bits_of(axis)):
        rows = joined(rows, swap(rows, axis, bit), which)
    return rows


def split_start(rows, axis):
    start = 0
    for _, which in bits_of(axis):
        rows = rows // 2
        start = start + which * rows
    return start


def add_swapped(value, axis, bit):
    value = lax.reduce_precision(value, 8, 7)
    return value + swap(value.astype(jnp.bfloat16), axis, bit).astype(jnp.float32)


def sum_over_panels(value):
    core = lax.axis_index("obs") & 1
    keep, send = halves(value, core)
    keep = keep + swap(send.astype(jnp.bfloat16), "obs", 1).astype(jnp.float32)
    upper, lower = jnp.split(keep, 2, axis=0)
    upper, lower = add_swapped(upper, "obs", 2), add_swapped(lower, "pix", 1)
    upper, lower = add_swapped(upper, "pix", 1), add_swapped(lower, "obs", 2)
    own = jnp.concatenate([upper, lower], axis=0)
    return joined(own, swap(own, "obs", 1), core)


def shards(spectra, enc_weight, pix_tile, pix_local, foot_weight, cotangent, adjoint, mixing):
    tile_count = lax.axis_size("pix")
    groups = lax.axis_size("chan")
    tile_rows = cotangent.shape[0]
    feature_count = cotangent.shape[1]
    padded = extended(cotangent, (("pix", 0),), HALO)
    block_count = tile_rows // HALO
    stacked = padded.reshape(block_count + 2, HALO, feature_count)
    windows = jnp.concatenate(
        (stacked[:block_count], stacked[1 : block_count + 1], stacked[2 : block_count + 2]), axis=1
    )
    anchor = lax.axis_index("pix") * tile_rows - HALO
    block_start = (jnp.arange(block_count, dtype=jnp.int32) * HALO)[:, None]
    columns = jnp.arange(3 * HALO, dtype=jnp.int32)[None, None, :]
    summed = cotangent.astype(jnp.float32)
    for neighbor in range(NEIGH):
        within = (adjoint[neighbor] - anchor).reshape(block_count, HALO) - block_start
        selector = (within[:, :, None] == columns).astype(jnp.bfloat16)
        picked = jnp.einsum("bij,bje->bie", selector, windows, preferred_element_type=jnp.float32)
        summed = summed + picked.reshape(tile_rows, feature_count) * mixing[neighbor]
    pixel_grad = summed.astype(jnp.bfloat16)
    all_rows = spectra.shape[0]
    quarter = all_rows // groups
    capacity_part = 2 * quarter // tile_count
    pre = sum_and_split(
        jnp.dot(spectra, enc_weight, preferred_element_type=jnp.float32).astype(jnp.bfloat16),
        "chan",
    )
    first_row = split_start(all_rows, "chan")
    tile_ids = lax.dynamic_slice_in_dim(pix_tile[:, 0], first_row, quarter, 0)
    local_ids = lax.dynamic_slice_in_dim(pix_local, first_row, quarter, 0)
    weights = lax.dynamic_slice_in_dim(foot_weight, first_row, quarter, 0)
    fetched = fetch_rows(pixel_grad, tile_ids, local_ids, capacity_part)
    grad_part = pre_gradient(pre, fetched, weights)
    local_grad = lax.dot_general(
        spectra,
        gather_back(grad_part, "chan"),
        (((0,), (0,)), ((), ())),
        preferred_element_type=jnp.float32,
    )
    if lax.axis_size("obs") == 4 and lax.axis_size("pix") == 2:
        return sum_over_panels(local_grad)
    return lax.psum(local_grad, ("obs", "pix"))


def solution(mesh):
    return jax.shard_map(
        shards,
        mesh=mesh,
        in_specs=(
            P(("obs", "pix"), "chan"),
            P("chan", None),
            P(("obs", "pix"), None),
            P(("obs", "pix")),
            P(("obs", "pix")),
            P("pix", None),
            P(None, "pix"),
            P(),
        ),
        out_specs=P("chan", None),
        check_vma=False,
    )
```

```python
import jax
import jax.numpy as jnp
from jax import lax
from jax.experimental import pallas as pl
from jax.experimental.pallas import tpu as pltpu
from jax.sharding import PartitionSpec as P

NEIGH = 8
HALO = 128
BLOCK = 256
VMEM = 40 * 1024 * 1024


def extended(value, axis, width):
    size, length = lax.axis_size(axis), value.shape[0]
    last = lax.slice_in_dim(value, length - width, length, axis=0)
    first = lax.slice_in_dim(value, 0, width, axis=0)
    if size == 2:
        index = lax.axis_index(axis)
        other = lax.ppermute(jnp.where(index == 0, last, first), axis, [(0, 1), (1, 0)])
        return jnp.concatenate([other, value, other], axis=0)
    up = [(i, (i + 1) % size) for i in range(size - 1)]
    down = [(j, i) for i, j in up]
    before = lax.ppermute(last, axis, up)
    after = lax.ppermute(first, axis, down)
    return jnp.concatenate([before, value, after], axis=0)


def requests(tile_ids, local_ids, capacity):
    tile_count = lax.axis_size("pix")
    onehot = (tile_ids[:, None] == jnp.arange(tile_count, dtype=jnp.int32)[None, :]).astype(
        jnp.int32
    )
    place_rank = jnp.sum((jnp.cumsum(onehot, axis=0) - 1) * onehot, axis=1)
    slot_index = tile_ids * capacity + place_rank
    outgoing = jnp.full((tile_count * capacity,), 0, jnp.int32).at[slot_index].set(local_ids)
    outgoing = outgoing.reshape(tile_count, capacity)
    requested = lax.all_to_all(outgoing, "pix", split_axis=0, concat_axis=0, tiled=True)
    return slot_index, requested.reshape(-1)


def swap(value, axis, bit):
    size = lax.axis_size(axis)
    return lax.ppermute(value, axis, [(i, i ^ bit) for i in range(size)])


def halves(value, which, dim=0):
    length = value.shape[dim] // 2
    own = lax.dynamic_slice_in_dim(value, which * length, length, dim)
    other = lax.dynamic_slice_in_dim(value, (1 - which) * length, length, dim)
    return own, other


def joined(own, other, which):
    first = jnp.where(which == 0, own, other)
    second = jnp.where(which == 0, other, own)
    return jnp.concatenate([first, second], axis=0)


def gather_line(rows, axis):
    size, index = lax.axis_size(axis), lax.axis_index(axis)
    right = left = rows
    blocks = [jnp.zeros_like(rows) if size > 1 else rows] * size
    blocks = [jnp.where(index == place, rows, jnp.zeros_like(rows)) for place in range(size)]
    for step in range(size - 1):
        right = lax.ppermute(right, axis, [(i, i + 1) for i in range(step, size - 1)])
        left = lax.ppermute(left, axis, [(i + 1, i) for i in range(size - 1 - step)])
        for place in range(size):
            blocks[place] = jnp.where(index == place + 1 + step, right, blocks[place])
            blocks[place] = jnp.where(index == place - 1 - step, left, blocks[place])
    return jnp.stack(blocks)


def add_swapped(value, axis, bit):
    value = lax.reduce_precision(value, 8, 7)
    return value + swap(value.astype(jnp.bfloat16), axis, bit).astype(jnp.float32)


def sum_over_panels(value):
    core = lax.axis_index("obs") & 1
    keep, send = halves(value, core)
    keep = keep + swap(send.astype(jnp.bfloat16), "obs", 1).astype(jnp.float32)
    upper, lower = jnp.split(keep, 2, axis=0)
    upper, lower = add_swapped(upper, "obs", 2), add_swapped(lower, "pix", 1)
    upper, lower = add_swapped(upper, "pix", 1), add_swapped(lower, "obs", 2)
    own = jnp.concatenate([upper, lower], axis=0)
    return joined(own, swap(own, "obs", 1), core)


def project_kernel(start, spectra, weight, out):
    out[...] = jnp.dot(
        spectra[...], weight[...], preferred_element_type=jnp.float32
    ).astype(out.dtype)


def project(spectra, weight, first_block, rows, block):
    depth, width = weight.shape
    return pl.pallas_call(
        project_kernel,
        out_shape=jax.ShapeDtypeStruct((rows, width), jnp.bfloat16),
        grid_spec=pltpu.PrefetchScalarGridSpec(
            num_scalar_prefetch=1,
            grid=(rows // block,),
            in_specs=[
                pl.BlockSpec((block, depth), lambda i, start: (start[0] + i, 0)),
                pl.BlockSpec((depth, width), lambda i, start: (0, 0)),
            ],
            out_specs=pl.BlockSpec((block, width), lambda i, start: (i, 0)),
        ),
        compiler_params=pltpu.CompilerParams(vmem_limit_bytes=VMEM),
        cost_estimate=pl.CostEstimate(
            flops=2 * rows * depth * width,
            bytes_accessed=2 * (rows * depth + depth * width + rows * width),
            transcendentals=0,
        ),
        name="project",
    )(first_block.reshape(1).astype(jnp.int32), spectra, weight)


def pixel_kernel(anchor, wanted, adjoint, padded, mixing, out, grads, picked):
    step = pl.program_id(0)
    first = pl.multiple_of(step * BLOCK, BLOCK)
    within = (adjoint[...] - (anchor[0] + first)).T
    window = padded[pl.ds(first, BLOCK + 2 * HALO), :]
    total = padded[pl.ds(first + HALO, BLOCK), :].astype(jnp.float32)
    columns = lax.broadcasted_iota(jnp.int32, (BLOCK, BLOCK + 2 * HALO), 1)
    for neighbor in range(NEIGH):
        selector = (within[:, neighbor : neighbor + 1] == columns).astype(jnp.bfloat16)
        rows = jnp.dot(selector, window, preferred_element_type=jnp.float32)
        total = total + rows * mixing[neighbor : neighbor + 1, :]
    grads[pl.ds(first, BLOCK), :] = total.astype(jnp.bfloat16).astype(jnp.float32)

    @pl.when(step == pl.num_programs(0) - 1)
    def _():
        group = 16

        def body(turn, carry):
            base = pl.multiple_of(turn * group, group)
            for n in range(group):
                picked[n : n + 1, :] = grads[pl.ds(wanted[base + n], 1), :]
            out[pl.ds(base, group), :] = picked[...].astype(jnp.bfloat16)
            return carry

        lax.fori_loop(0, out.shape[0] // group, body, 0)


def pixel_rows(padded, adjoint, mixing, anchor, wanted):
    tile_rows = adjoint.shape[1]
    width = padded.shape[1]
    count = wanted.shape[0]
    return pl.pallas_call(
        pixel_kernel,
        out_shape=jax.ShapeDtypeStruct((count, width), jnp.bfloat16),
        grid=(tile_rows // BLOCK,),
        in_specs=[
            pl.BlockSpec(memory_space=pltpu.SMEM),
            pl.BlockSpec(memory_space=pltpu.SMEM),
            pl.BlockSpec((NEIGH, BLOCK), lambda i: (0, i)),
            pl.BlockSpec(padded.shape, lambda i: (0, 0)),
            pl.BlockSpec(mixing.shape, lambda i: (0, 0)),
        ],
        out_specs=pl.BlockSpec((count, width), lambda i: (0, 0)),
        scratch_shapes=[
            pltpu.VMEM((tile_rows, width), jnp.float32),
            pltpu.VMEM((16, width), jnp.float32),
        ],
        compiler_params=pltpu.CompilerParams(vmem_limit_bytes=VMEM),
        cost_estimate=pl.CostEstimate(
            flops=2 * NEIGH * tile_rows * (BLOCK + 2 * HALO) * width,
            bytes_accessed=4 * tile_rows * width,
            transcendentals=0,
        ),
        name="pixel_rows",
    )(anchor.reshape(1).astype(jnp.int32), wanted, adjoint, padded, mixing)


def pre_gradient(pre, fetched, weights):
    sigma = jax.nn.sigmoid(pre)
    deriv = sigma * (1.0 + pre * (1.0 - sigma))
    return (weights[:, None] * deriv * fetched.astype(jnp.float32)).astype(jnp.bfloat16)


def shards(spectra, enc_weight, pix_tile, pix_local, foot_weight, cotangent, adjoint, mixing):
    tile_count = lax.axis_size("pix")
    groups = lax.axis_size("chan")
    tile_rows = cotangent.shape[0]
    all_rows = spectra.shape[0]
    quarter = all_rows // groups
    half = all_rows // 2
    tile = lax.axis_index("pix")
    chan = lax.axis_index("chan")
    low, high = chan & 1, chan >> 1
    first_row = low * half + high * quarter

    send = project(spectra, enc_weight, (1 - low) * 2, half, quarter)
    received = swap(send, "chan", 1)

    padded = extended(cotangent, "pix", HALO)
    anchor = tile * tile_rows - HALO
    tile_ids = lax.dynamic_slice_in_dim(pix_tile[:, 0], first_row, quarter, 0)
    local_ids = lax.dynamic_slice_in_dim(pix_local, first_row, quarter, 0)
    weights = lax.dynamic_slice_in_dim(foot_weight, first_row, quarter, 0)
    capacity = 2 * quarter // tile_count
    if capacity >= quarter and tile_count == 2:
        wanted = jnp.concatenate([local_ids, swap(local_ids, "pix", 1)])
        rows = pixel_rows(padded, adjoint, mixing, anchor, wanted)
        answers = swap(rows[quarter:], "pix", 1)
        fetched = jnp.where((tile_ids == tile)[:, None], rows[:quarter], answers)
    else:
        slot_index, wanted = requests(tile_ids, local_ids, capacity)
        rows = pixel_rows(padded, adjoint, mixing, anchor, wanted)
        answers = lax.all_to_all(
            rows.reshape(tile_count, capacity, -1), "pix", split_axis=0, concat_axis=0, tiled=True
        )
        fetched = jnp.take(answers.reshape(tile_count * capacity, -1), slot_index, axis=0)

    keep = project(spectra, enc_weight, low * 2, half, quarter)
    total = keep.astype(jnp.float32) + received.astype(jnp.float32)
    keep, send = halves(total, high)
    pre = keep + swap(send.astype(jnp.bfloat16), "chan", 2).astype(jnp.float32)

    grad_part = pre_gradient(pre, fetched, weights)
    blocks = gather_line(grad_part, "chan")
    places = [(c & 1) * 2 + (c >> 1) for c in range(groups)]
    order = [places.index(q) for q in range(groups)]
    grads = jnp.concatenate([blocks[c] for c in order], axis=0)
    local_grad = lax.dot_general(
        spectra, grads, (((0,), (0,)), ((), ())), preferred_element_type=jnp.float32
    )
    if lax.axis_size("obs") == 4 and tile_count == 2:
        return sum_over_panels(local_grad)
    return lax.psum(local_grad, ("obs", "pix"))


def solution(mesh):
    return jax.shard_map(
        shards,
        mesh=mesh,
        in_specs=(
            P(("obs", "pix"), "chan"),
            P("chan", None),
            P(("obs", "pix"), None),
            P(("obs", "pix")),
            P(("obs", "pix")),
            P("pix", None),
            P(None, "pix"),
            P(),
        ),
        out_specs=P("chan", None),
        check_vma=False,
    )
```

```python
import jax
import jax.numpy as jnp
from jax import lax
from jax.experimental import pallas as pl
from jax.experimental.pallas import tpu as pltpu
from jax.sharding import PartitionSpec as P

NEIGH = 8
HALO = 128
BLOCK = 256
VMEM = 56 * 1024 * 1024


def edges(value, axis, width):
    size, length = lax.axis_size(axis), value.shape[0]
    last = lax.slice_in_dim(value, length - width, length, axis=0)
    first = lax.slice_in_dim(value, 0, width, axis=0)
    if size == 2:
        index = lax.axis_index(axis)
        other = lax.ppermute(jnp.where(index == 0, last, first), axis, [(0, 1), (1, 0)])
        return other, other
    up = [(i, i + 1) for i in range(size - 1)]
    return lax.ppermute(last, axis, up), lax.ppermute(first, axis, [(j, i) for i, j in up])


def requests(tile_ids, local_ids, capacity):
    tile_count = lax.axis_size("pix")
    onehot = (tile_ids[:, None] == jnp.arange(tile_count, dtype=jnp.int32)[None, :]).astype(
        jnp.int32
    )
    place_rank = jnp.sum((jnp.cumsum(onehot, axis=0) - 1) * onehot, axis=1)
    slot_index = tile_ids * capacity + place_rank
    outgoing = jnp.full((tile_count * capacity,), 0, jnp.int32).at[slot_index].set(local_ids)
    outgoing = outgoing.reshape(tile_count, capacity)
    requested = lax.all_to_all(outgoing, "pix", split_axis=0, concat_axis=0, tiled=True)
    return slot_index, requested.reshape(-1)


def swap(value, axis, bit):
    size = 1
    for name in (axis,) if isinstance(axis, str) else axis:
        size *= lax.axis_size(name)
    return lax.ppermute(value, axis, [(i, i ^ bit) for i in range(size)])


def project_kernel(quarters, spectra, weight, first, second):
    result = jnp.dot(
        spectra[...], weight[...], preferred_element_type=jnp.float32
    ).astype(first.dtype)

    @pl.when(pl.program_id(0) == 0)
    def _():
        first[...] = result

    @pl.when(pl.program_id(0) == 1)
    def _():
        second[...] = result


def project(spectra, weight, quarters):
    depth, width = weight.shape
    rows = spectra.shape[0] // 4
    part = jax.ShapeDtypeStruct((rows, width), jnp.bfloat16)
    return pl.pallas_call(
        project_kernel,
        out_shape=(part, part),
        grid_spec=pltpu.PrefetchScalarGridSpec(
            num_scalar_prefetch=1,
            grid=(2,),
            in_specs=[
                pl.BlockSpec((rows, depth), lambda i, quarters: (quarters[i], 0)),
                pl.BlockSpec((depth, width), lambda i, quarters: (0, 0)),
            ],
            out_specs=(
                pl.BlockSpec((rows, width), lambda i, quarters: (0, 0)),
                pl.BlockSpec((rows, width), lambda i, quarters: (0, 0)),
            ),
        ),
        compiler_params=pltpu.CompilerParams(vmem_limit_bytes=VMEM),
        cost_estimate=pl.CostEstimate(
            flops=4 * rows * depth * width,
            bytes_accessed=4 * rows * depth + 2 * depth * width + 4 * rows * width,
            transcendentals=0,
        ),
        name="project",
    )(quarters, spectra, weight)


def backproject_kernel(quarters, spectra, first, second, *rest):
    step = pl.program_id(0)
    before, total = rest if len(rest) == 2 else (None, rest[0])

    def product(rows):
        return lax.dot_general(
            spectra[...], rows[...], (((0,), (0,)), ((), ())), preferred_element_type=jnp.float32
        )

    @pl.when(step == 0)
    def _():
        total[...] = product(first) if before is None else before[...] + product(first)

    @pl.when(step == 1)
    def _():
        total[...] += product(second)


def backproject(spectra, quarters, first, second, before=None):
    depth = spectra.shape[1]
    rows, width = first.shape
    whole = [pl.BlockSpec(x.shape, lambda i, quarters: (0, 0)) for x in (first, second)]
    operands = (first, second)
    if before is not None:
        whole.append(pl.BlockSpec(before.shape, lambda i, quarters: (0, 0)))
        operands += (before,)
    return pl.pallas_call(
        backproject_kernel,
        out_shape=jax.ShapeDtypeStruct((depth, width), jnp.float32),
        grid_spec=pltpu.PrefetchScalarGridSpec(
            num_scalar_prefetch=1,
            grid=(2,),
            in_specs=[
                pl.BlockSpec((rows, depth), lambda i, quarters: (quarters[i], 0)),
                *whole,
            ],
            out_specs=pl.BlockSpec((depth, width), lambda i, quarters: (0, 0)),
        ),
        compiler_params=pltpu.CompilerParams(vmem_limit_bytes=VMEM),
        cost_estimate=pl.CostEstimate(
            flops=4 * rows * depth * width,
            bytes_accessed=4 * rows * depth + 8 * depth * width,
            transcendentals=0,
        ),
        name="backproject",
    )(quarters, spectra, *operands)


def column(row):
    return jnp.broadcast_to(row, (8, row.shape[1])).T[:, :1]


def pixel_kernel(anchor, wanted, adjoint, cotangent, above, below, mixing, out,
                 window, selector, grads):
    step = pl.program_id(0)
    last = pl.num_programs(0) - 1
    first = pl.multiple_of(step * BLOCK, BLOCK)
    wide = BLOCK + 2 * HALO

    window[HALO : HALO + BLOCK, :] = cotangent[pl.ds(first, BLOCK), :]

    @pl.when(step == 0)
    def _():
        window[:HALO, :] = above[...]

    @pl.when(step > 0)
    def _():
        window[:HALO, :] = cotangent[pl.ds(pl.multiple_of(first - HALO, HALO), HALO), :]

    @pl.when(step == last)
    def _():
        window[HALO + BLOCK :, :] = below[...]

    @pl.when(step < last)
    def _():
        window[HALO + BLOCK :, :] = cotangent[pl.ds(pl.multiple_of(first + BLOCK, HALO), HALO), :]

    within = (adjoint[...] - (anchor[0] + first + wide // 2)).T.astype(jnp.float32)
    columns = lax.broadcasted_iota(jnp.int32, (BLOCK, wide), 1) - wide // 2
    columns = columns.astype(jnp.float32).astype(jnp.bfloat16)
    for neighbor in range(1, NEIGH):
        place = within[:, neighbor : neighbor + 1].astype(jnp.bfloat16)
        selector[(neighbor - 1) * BLOCK : neighbor * BLOCK, :] = jnp.where(
            place == columns, jnp.bfloat16(1), jnp.bfloat16(0)
        )
    rows = jnp.dot(selector[...], window[...], preferred_element_type=jnp.float32)
    total = window[HALO : HALO + BLOCK, :].astype(jnp.float32)
    place = lax.broadcasted_iota(jnp.int32, (BLOCK, 1), 0).astype(jnp.float32) - wide // 2
    ahead = jnp.where(
        within[:, :1] == place,
        window[:BLOCK, :].astype(jnp.float32),
        window[2 * HALO :, :].astype(jnp.float32),
    )
    total = total + ahead * mixing[0:1, :]
    for neighbor in range(1, NEIGH):
        part = rows[(neighbor - 1) * BLOCK : neighbor * BLOCK, :]
        total = total + part * mixing[neighbor : neighbor + 1, :]
    grads[pl.ds(first, BLOCK), :] = total.astype(jnp.bfloat16)

    @pl.when(step == last)
    def _():
        group = wanted.shape[1]
        lanes = lax.broadcasted_iota(jnp.int32, (group, BLOCK), 1)
        lanes = lanes.astype(jnp.float32).astype(jnp.bfloat16)
        tile_rows = grads.shape[0]
        for turn in range(wanted.shape[0]):
            names = column(wanted[turn : turn + 1, :])
            found = jnp.zeros((group, grads.shape[1]), jnp.float32)
            picks = []
            for block in range(tile_rows // BLOCK):
                near = names - block * BLOCK
                near = jnp.where((near >= 0) & (near < BLOCK), near, -1)
                near = near.astype(jnp.float32).astype(jnp.bfloat16)
                picks.append(jnp.where(near == lanes, jnp.bfloat16(1), jnp.bfloat16(0)))
            found = jnp.dot(
                jnp.concatenate(picks, axis=1), grads[...], preferred_element_type=jnp.float32
            )
            out[turn * group : (turn + 1) * group, :] = found.astype(jnp.bfloat16)


def pixel_rows(cotangent, above, below, adjoint, mixing, anchor, wanted):
    tile_rows, width = cotangent.shape
    count = wanted.shape[0]
    group = 256
    wide = BLOCK + 2 * HALO
    return pl.pallas_call(
        pixel_kernel,
        out_shape=jax.ShapeDtypeStruct((count, width), jnp.bfloat16),
        grid=(tile_rows // BLOCK,),
        in_specs=[
            pl.BlockSpec(memory_space=pltpu.SMEM),
            pl.BlockSpec((count // group, group), lambda i: (0, 0)),
            pl.BlockSpec((NEIGH, BLOCK), lambda i: (0, i)),
            pl.BlockSpec(cotangent.shape, lambda i: (0, 0)),
            pl.BlockSpec(above.shape, lambda i: (0, 0)),
            pl.BlockSpec(below.shape, lambda i: (0, 0)),
            pl.BlockSpec(mixing.shape, lambda i: (0, 0)),
        ],
        out_specs=pl.BlockSpec((count, width), lambda i: (0, 0)),
        scratch_shapes=[
            pltpu.VMEM((wide, width), jnp.bfloat16),
            pltpu.VMEM(((NEIGH - 1) * BLOCK, wide), jnp.bfloat16),
            pltpu.VMEM((tile_rows, width), jnp.bfloat16),
        ],
        compiler_params=pltpu.CompilerParams(vmem_limit_bytes=VMEM),
        cost_estimate=pl.CostEstimate(
            flops=2 * NEIGH * tile_rows * wide * width,
            bytes_accessed=4 * tile_rows * width,
            transcendentals=0,
        ),
        name="pixel_rows",
    )(anchor.reshape(1), wanted.reshape(-1, group), adjoint, cotangent, above, below, mixing)


def gradient_kernel(own, near, far, tiles, tile, weights, mine, answers, out):
    pre = own[...].astype(jnp.float32) + near[...].astype(jnp.float32)
    pre = pre + far[...].astype(jnp.float32)
    sigma = jax.nn.sigmoid(pre)
    deriv = sigma * (1.0 + pre * (1.0 - sigma))
    fetched = jnp.where(
        tiles[...] == tile[0], mine[...].astype(jnp.float32), answers[...].astype(jnp.float32)
    )
    out[...] = (weights[...] * deriv * fetched).astype(out.dtype)


def pre_gradient(own, near, far, tiles, tile, weights, mine, answers):
    spec = pl.BlockSpec(memory_space=pltpu.VMEM)
    return pl.pallas_call(
        gradient_kernel,
        out_shape=jax.ShapeDtypeStruct(own.shape, jnp.bfloat16),
        in_specs=[spec] * 4 + [pl.BlockSpec(memory_space=pltpu.SMEM)] + [spec] * 3,
        out_specs=spec,
        compiler_params=pltpu.CompilerParams(vmem_limit_bytes=VMEM),
        name="pre_gradient",
    )(own, near, far, tiles, tile.reshape(1), weights, mine, answers)


def deal_kernel(place, keep, received, own, first, second, third):
    rows = own.shape[0]
    for out, bits in ((own, 0), (first, 1), (second, 2), (third, 3)):
        here = pl.ds(pl.multiple_of((place[0] ^ bits) * rows, rows), rows)
        value = keep[here, :] + received[here, :].astype(jnp.float32)
        out[...] = value.astype(out.dtype)


def deal(place, keep, received):
    rows, width = keep.shape[0] // 4, keep.shape[1]
    spec = pl.BlockSpec(memory_space=pltpu.VMEM)
    piece = jax.ShapeDtypeStruct((rows, width), jnp.bfloat16)
    return pl.pallas_call(
        deal_kernel,
        out_shape=(jax.ShapeDtypeStruct((rows, width), jnp.float32), piece, piece, piece),
        in_specs=[pl.BlockSpec(memory_space=pltpu.SMEM), spec, spec],
        out_specs=(spec,) * 4,
        compiler_params=pltpu.CompilerParams(vmem_limit_bytes=VMEM),
        name="deal",
    )(place.reshape(1), keep, received)


def collect_kernel(where, own, received, out):
    half, rows = own.shape[0], own.shape[0] // 4
    for pieces, core in ((own, where[0]), (received, 1 - where[0])):
        for bits in range(4):
            start = pl.multiple_of(core * half + (where[1] ^ bits) * rows, rows)
            out[pl.ds(start, rows), :] = pieces[bits * rows : (bits + 1) * rows, :].astype(
                jnp.float32
            )


def collect(core, place, own, received):
    spec = pl.BlockSpec(memory_space=pltpu.VMEM)
    return pl.pallas_call(
        collect_kernel,
        out_shape=jax.ShapeDtypeStruct((2 * own.shape[0], own.shape[1]), jnp.float32),
        in_specs=[pl.BlockSpec(memory_space=pltpu.SMEM), spec, spec],
        out_specs=spec,
        compiler_params=pltpu.CompilerParams(vmem_limit_bytes=VMEM),
        name="collect",
    )(jnp.stack([core, place]), own, received)


def sum_over_panels(value):
    both = ("obs", "pix")
    core = lax.axis_index("obs") & 1
    place = (lax.axis_index("obs") >> 1) + 2 * lax.axis_index("pix")
    half = value.shape[0] // 2
    keep = lax.dynamic_slice_in_dim(value, core * half, half, 0)
    send = lax.dynamic_slice_in_dim(value, (1 - core) * half, half, 0)
    received = swap(send.astype(jnp.bfloat16), "obs", 1)
    total, *pieces = deal(place, keep, received)
    for piece, bits in zip(pieces, (4, 1, 5)):
        total = total + swap(piece, both, bits).astype(jnp.float32)
    total = total.astype(jnp.bfloat16)
    own = jnp.concatenate([total] + [swap(total, both, bits) for bits in (4, 1, 5)], axis=0)
    return collect(core, place, own, swap(own, "obs", 1))


def shards(spectra, enc_weight, pix_tile, pix_local, foot_weight, cotangent, adjoint, mixing):
    tile_count = lax.axis_size("pix")
    tile_rows = cotangent.shape[0]
    quarter = spectra.shape[0] // lax.axis_size("chan")
    tile = lax.axis_index("pix")
    chan = lax.axis_index("chan")
    first_row = chan * quarter
    inner = (chan == 1) | (chan == 2)
    ahead, behind = [(0, 1), (3, 2)], [(1, 0), (2, 3)]
    middle = [(1, 2), (2, 1)]

    part2, part3 = project(spectra, enc_weight, jnp.stack([chan ^ 2, chan ^ 3]))
    outer2 = lax.ppermute(part2, "chan", ahead)
    inner2 = lax.ppermute(part2, "chan", middle)
    outer3 = lax.ppermute(part3, "chan", [(0, 2), (3, 1)])
    part0, part1 = project(spectra, enc_weight, jnp.stack([chan, chan ^ 1]))
    wide = jnp.float32
    sum1 = part1.astype(wide) + inner2.astype(wide) + outer3.astype(wide)
    sum3 = part3.astype(wide) + outer2.astype(wide)
    near = swap(sum1.astype(jnp.bfloat16), "chan", 1)
    far = lax.ppermute(sum3.astype(jnp.bfloat16), "chan", middle)

    above, below = edges(cotangent, "pix", HALO)
    anchor = tile * tile_rows - HALO
    tile_ids = lax.dynamic_slice_in_dim(pix_tile, first_row, quarter, 0)
    local_ids = lax.dynamic_slice_in_dim(pix_local, first_row, quarter, 0)
    weights = lax.dynamic_slice_in_dim(foot_weight, first_row, quarter, 0)[:, None]
    capacity = 2 * quarter // tile_count
    if capacity >= quarter and tile_count == 2:
        wanted = jnp.concatenate([local_ids, swap(local_ids, "pix", 1)])
        rows = pixel_rows(cotangent, above, below, adjoint, mixing, anchor, wanted)
        mine, answers = rows[:quarter], swap(rows[quarter:], "pix", 1)
    else:
        slot_index, wanted = requests(tile_ids[:, 0], local_ids, capacity)
        rows = pixel_rows(cotangent, above, below, adjoint, mixing, anchor, wanted)
        answers = lax.all_to_all(
            rows.reshape(tile_count, capacity, -1), "pix", split_axis=0, concat_axis=0, tiled=True
        )
        answers = jnp.take(answers.reshape(tile_count * capacity, -1), slot_index, axis=0)
        mine = answers
    grads = pre_gradient(part0, near, far, tile_ids, tile, weights, mine, answers)

    beside = swap(grads, "chan", 1)
    across = lax.ppermute(grads, "chan", middle)
    passed = lax.ppermute(across, "chan", behind)
    crossed = lax.ppermute(beside, "chan", middle)
    skipped = lax.ppermute(beside, "chan", [(2, 0), (1, 3)])
    local_grad = backproject(spectra, jnp.stack([chan, chan ^ 1]), grads, beside)
    local_grad = backproject(
        spectra,
        jnp.stack([chan ^ 2, chan ^ 3]),
        jnp.where(inner, crossed, passed),
        jnp.where(inner, across, skipped),
        local_grad,
    )
    if lax.axis_size("obs") == 4 and tile_count == 2:
        return sum_over_panels(local_grad)
    return lax.psum(local_grad, ("obs", "pix"))


def solution(mesh):
    return jax.shard_map(
        shards,
        mesh=mesh,
        in_specs=(
            P(("obs", "pix"), "chan"),
            P("chan", None),
            P(("obs", "pix"), None),
            P(("obs", "pix")),
            P(("obs", "pix")),
            P("pix", None),
            P(None, "pix"),
            P(),
        ),
        out_specs=P("chan", None),
        check_vma=False,
    )
```

```python
import functools

import jax
import jax.numpy as jnp
from jax import lax
from jax.experimental import pallas as pl
from jax.experimental.pallas import tpu as pltpu
from jax.sharding import PartitionSpec as P

NEIGH = 8
HALO = 128
MIB = 1024 * 1024


def edges(value, axis, width):
    size, length = lax.axis_size(axis), value.shape[0]
    last = lax.slice_in_dim(value, length - width, length, axis=0)
    first = lax.slice_in_dim(value, 0, width, axis=0)
    if size == 2:
        index = lax.axis_index(axis)
        other = lax.ppermute(jnp.where(index == 0, last, first), axis, [(0, 1), (1, 0)])
        return other, other
    up = [(i, i + 1) for i in range(size - 1)]
    return lax.ppermute(last, axis, up), lax.ppermute(first, axis, [(j, i) for i, j in up])


def requests(tile_ids, local_ids, capacity):
    tile_count = lax.axis_size("pix")
    onehot = (tile_ids[:, None] == jnp.arange(tile_count, dtype=jnp.int32)[None, :]).astype(
        jnp.int32
    )
    place_rank = jnp.sum((jnp.cumsum(onehot, axis=0) - 1) * onehot, axis=1)
    slot_index = tile_ids * capacity + place_rank
    outgoing = jnp.full((tile_count * capacity,), 0, jnp.int32).at[slot_index].set(local_ids)
    outgoing = outgoing.reshape(tile_count, capacity)
    requested = lax.all_to_all(outgoing, "pix", split_axis=0, concat_axis=0, tiled=True)
    return slot_index, requested.reshape(-1)


def swap(value, axis, bit):
    size = 1
    for name in (axis,) if isinstance(axis, str) else axis:
        size *= lax.axis_size(name)
    return lax.ppermute(value, axis, [(i, i ^ bit) for i in range(size)])


def memory(mib):
    return pltpu.CompilerParams(vmem_limit_bytes=mib * MIB)


def project_kernel(chan, spectra, weight, *parts):
    step = pl.program_id(0)
    result = jnp.dot(
        spectra[...], weight[...], preferred_element_type=jnp.float32
    ).astype(jnp.bfloat16)
    rows = result.shape[0]
    turns = parts[0].shape[0] // rows
    for index, part in enumerate(parts):
        for turn in range(turns):

            @pl.when(step == index * turns + turn)
            def _(part=part, turn=turn):
                part[turn * rows : (turn + 1) * rows, :] = result


def project(spectra, weight, chan):
    depth, width = weight.shape
    quarter = spectra.shape[0] // 4
    turns = 2
    part = jax.ShapeDtypeStruct((quarter, width), jnp.bfloat16)
    return pl.pallas_call(
        project_kernel,
        out_shape=(part,) * 4,
        grid_spec=pltpu.PrefetchScalarGridSpec(
            num_scalar_prefetch=1,
            grid=(4 * turns,),
            in_specs=[
                pl.BlockSpec(
                    (quarter // turns, depth),
                    lambda i, chan: ((chan[0] ^ (3 - i // turns)) * turns + i % turns, 0),
                ),
                pl.BlockSpec((depth, width), lambda i, chan: (0, 0)),
            ],
            out_specs=(pl.BlockSpec((quarter, width), lambda i, chan: (0, 0)),) * 4,
        ),
        compiler_params=memory(60),
        cost_estimate=pl.CostEstimate(
            flops=8 * quarter * depth * width,
            bytes_accessed=8 * quarter * depth + 2 * depth * width + 8 * quarter * width,
            transcendentals=0,
        ),
        name="project",
    )(chan.reshape(1), spectra, weight)


def turn_kernel(chan, spectra, out):
    out[...] = spectra[...].T


def turned(spectra, chan):
    rows, depth = spectra.shape[0] // 4, spectra.shape[1]
    return pl.pallas_call(
        turn_kernel,
        out_shape=jax.ShapeDtypeStruct((depth, 2 * rows), jnp.bfloat16),
        grid_spec=pltpu.PrefetchScalarGridSpec(
            num_scalar_prefetch=1,
            grid=(2,),
            in_specs=[pl.BlockSpec((rows, depth), lambda i, chan: (chan[0] ^ (2 + i), 0))],
            out_specs=pl.BlockSpec((depth, rows), lambda i, chan: (0, i)),
        ),
        compiler_params=memory(16),
        name="turned",
    )(chan.reshape(1), spectra)


def early_kernel(chan, spectra, first, second, total):
    step = pl.program_id(0)

    def product(rows):
        return lax.dot_general(
            spectra[...], rows[...], (((0,), (0,)), ((), ())), preferred_element_type=jnp.float32
        )

    @pl.when(step == 0)
    def _():
        total[...] = product(first)

    @pl.when(step == 1)
    def _():
        total[...] += product(second)


def early_product(spectra, chan, first, second):
    depth = spectra.shape[1]
    rows, width = first.shape
    whole = pl.BlockSpec((rows, width), lambda i, chan: (0, 0))
    return pl.pallas_call(
        early_kernel,
        out_shape=jax.ShapeDtypeStruct((depth, width), jnp.float32),
        grid_spec=pltpu.PrefetchScalarGridSpec(
            num_scalar_prefetch=1,
            grid=(2,),
            in_specs=[pl.BlockSpec((rows, depth), lambda i, chan: (chan[0] ^ i, 0)), whole, whole],
            out_specs=pl.BlockSpec((depth, width), lambda i, chan: (0, 0)),
        ),
        compiler_params=memory(16),
        cost_estimate=pl.CostEstimate(
            flops=4 * rows * depth * width,
            bytes_accessed=4 * rows * depth + 4 * depth * width,
            transcendentals=0,
        ),
        name="early_product",
    )(chan.reshape(1), spectra, first, second)


def late_kernel(where, flipped, before, crossed, passed, across, skipped, keep, send):
    chan, core = where[0], where[1]
    inner = (chan == 1) | (chan == 2)
    second = jnp.where(inner, crossed[...], passed[...])
    third = jnp.where(inner, across[...], skipped[...])
    rows = jnp.concatenate([second, third], axis=0)
    half = keep.shape[0]
    for out, which in ((send, 1 - core), (keep, core)):
        here = pl.ds(pl.multiple_of(which * half, half), half)
        product = jnp.dot(flipped[here, :], rows, preferred_element_type=jnp.float32)
        out[...] = (before[here, :] + product).astype(out.dtype)


def late_product(chan, core, flipped, before, crossed, passed, across, skipped):
    half, width = before.shape[0] // 2, before.shape[1]
    spec = pl.BlockSpec(memory_space=pltpu.VMEM)
    return pl.pallas_call(
        late_kernel,
        out_shape=(
            jax.ShapeDtypeStruct((half, width), jnp.float32),
            jax.ShapeDtypeStruct((half, width), jnp.bfloat16),
        ),
        in_specs=[pl.BlockSpec(memory_space=pltpu.SMEM)] + [spec] * 6,
        out_specs=(spec, spec),
        compiler_params=memory(16),
        name="late_product",
    )(jnp.stack([chan, core]), flipped, before, crossed, passed, across, skipped)


def pixel_kernel(count, start, places, *refs):
    *lists, cotangent, above, below, mixing, out, table, scale, sums = refs
    tile_rows, half = cotangent.shape[0], table.shape[1]

    def fill(first, values):
        values = values.astype(jnp.float32)
        for side in range(2):
            table[pl.ds(2 * first + side, values.shape[0], stride=2), :] = values[
                :, side * half : (side + 1) * half
            ]

    fill(0, above[...])
    fill(HALO + tile_rows, below[...])
    chunk = 256
    for first in range(0, tile_rows, chunk):
        fill(HALO + first, cotangent[first : first + chunk, :])
    for side in range(2):
        scale[pl.ds(side, NEIGH, stride=2), :] = mixing[:, side * half : (side + 1) * half]
    scales = [scale[2 * k : 2 * k + 2, :] for k in range(NEIGH)]

    group = 8
    for index, wanted in enumerate(lists):

        def body(turn, carry, index=index, wanted=wanted):
            base = turn * group
            for n in range(group):
                pixel = wanted[start[0] + base + n]
                total = table[pl.ds(2 * (pixel + HALO), 2), :]
                for k in range(NEIGH):
                    total = total + table[pl.ds(places[k, pixel], 2), :] * scales[k]
                sums[pl.ds(2 * (index * count + base + n), 2), :] = total
            return carry

        lax.fori_loop(0, count // group, body, 0)
    rows = out.shape[0]
    for side in range(2):
        out[:, side * half : (side + 1) * half] = sums[pl.ds(side, rows, stride=2), :].astype(
            out.dtype
        )


def pixel_rows(cotangent, above, below, adjoint, mixing, anchor, lists, start, count):
    tile_rows, width = cotangent.shape
    rows = count * len(lists)
    smem = pl.BlockSpec(memory_space=pltpu.SMEM)
    vmem = pl.BlockSpec(memory_space=pltpu.VMEM)
    return pl.pallas_call(
        functools.partial(pixel_kernel, count),
        out_shape=jax.ShapeDtypeStruct((rows, width), jnp.bfloat16),
        in_specs=[smem] * (2 + len(lists)) + [vmem] * 4,
        out_specs=vmem,
        scratch_shapes=[
            pltpu.VMEM((2 * (tile_rows + 2 * HALO), width // 2), jnp.float32),
            pltpu.VMEM((2 * NEIGH, width // 2), jnp.float32),
            pltpu.VMEM((2 * rows, width // 2), jnp.float32),
        ],
        compiler_params=memory(24),
        cost_estimate=pl.CostEstimate(
            flops=2 * NEIGH * tile_rows * 256 * width,
            bytes_accessed=4 * tile_rows * width,
            transcendentals=0,
        ),
        name="pixel_rows",
    )(start.reshape(1), (adjoint - anchor) * 2, *lists, cotangent, above, below, mixing)


def gradient_kernel(own, near, far, tiles, tile, weights, mine, answers, out):
    pre = own[...].astype(jnp.float32) + near[...].astype(jnp.float32)
    pre = pre + far[...].astype(jnp.float32)
    sigma = jax.nn.sigmoid(pre)
    deriv = sigma * (1.0 + pre * (1.0 - sigma))
    fetched = jnp.where(
        tiles[...] == tile[0], mine[...].astype(jnp.float32), answers[...].astype(jnp.float32)
    )
    out[...] = (weights[...] * deriv * fetched).astype(out.dtype)


def pre_gradient(own, near, far, tiles, tile, weights, mine, answers):
    spec = pl.BlockSpec(memory_space=pltpu.VMEM)
    return pl.pallas_call(
        gradient_kernel,
        out_shape=jax.ShapeDtypeStruct(own.shape, jnp.bfloat16),
        in_specs=[spec] * 4 + [pl.BlockSpec(memory_space=pltpu.SMEM)] + [spec] * 3,
        out_specs=spec,
        compiler_params=memory(16),
        name="pre_gradient",
    )(own, near, far, tiles, tile.reshape(1), weights, mine, answers)


def collect_kernel(core, own, received, out):
    half = own.shape[0]
    for piece, which in ((own, core[0]), (received, 1 - core[0])):
        out[pl.ds(pl.multiple_of(which * half, half), half), :] = piece[...].astype(jnp.float32)


def collect(core, own, received):
    spec = pl.BlockSpec(memory_space=pltpu.VMEM)
    return pl.pallas_call(
        collect_kernel,
        out_shape=jax.ShapeDtypeStruct((2 * own.shape[0], own.shape[1]), jnp.float32),
        in_specs=[pl.BlockSpec(memory_space=pltpu.SMEM), spec, spec],
        out_specs=spec,
        compiler_params=memory(16),
        name="collect",
    )(core.reshape(1), own, received)


def sum_over_panels(core, keep, send):
    both = ("obs", "pix")
    wide = jnp.float32
    value = keep + swap(send, "obs", 1).astype(wide)
    for order in ((4, 1), (1, 4)):
        value = lax.reduce_precision(value, 8, 7)
        other = lax.ppermute(
            value.astype(jnp.bfloat16), both, [(i, i ^ order[(i >> 1) & 1]) for i in range(8)]
        )
        value = value + other.astype(wide)
    value = lax.reduce_precision(value, 8, 7).astype(jnp.bfloat16)
    return collect(core, value, swap(value, "obs", 1))


def shards(spectra, enc_weight, pix_tile, pix_local, foot_weight, cotangent, adjoint, mixing):
    tile_count = lax.axis_size("pix")
    tile_rows = cotangent.shape[0]
    quarter = spectra.shape[0] // lax.axis_size("chan")
    tile = lax.axis_index("pix")
    chan = lax.axis_index("chan")
    first_row = chan * quarter
    middle = [(1, 2), (2, 1)]

    part3, part2, part1, part0 = project(spectra, enc_weight, chan)
    outer2 = lax.ppermute(part2, "chan", [(0, 1), (3, 2)])
    inner2 = lax.ppermute(part2, "chan", middle)
    outer3 = lax.ppermute(part3, "chan", [(0, 2), (3, 1)])
    wide = jnp.float32
    sum1 = part1.astype(wide) + inner2.astype(wide) + outer3.astype(wide)
    sum3 = part3.astype(wide) + outer2.astype(wide)
    near = swap(sum1.astype(jnp.bfloat16), "chan", 1)
    far = lax.ppermute(sum3.astype(jnp.bfloat16), "chan", middle)

    above, below = edges(cotangent, "pix", HALO)
    anchor = tile * tile_rows - HALO
    tile_ids = lax.dynamic_slice_in_dim(pix_tile, first_row, quarter, 0)
    weights = lax.dynamic_slice_in_dim(foot_weight, first_row, quarter, 0)[:, None]
    capacity = 2 * quarter // tile_count
    if capacity >= quarter and tile_count == 2:
        lists = (pix_local, swap(pix_local, "pix", 1))
        rows = pixel_rows(
            cotangent, above, below, adjoint, mixing, anchor, lists, first_row, quarter
        )
        mine, answers = rows[:quarter], swap(rows[quarter:], "pix", 1)
    else:
        local_ids = lax.dynamic_slice_in_dim(pix_local, first_row, quarter, 0)
        slot_index, wanted = requests(tile_ids[:, 0], local_ids, capacity)
        rows = pixel_rows(
            cotangent, above, below, adjoint, mixing, anchor, (wanted,), 0 * chan, wanted.shape[0]
        )
        answers = lax.all_to_all(
            rows.reshape(tile_count, capacity, -1), "pix", split_axis=0, concat_axis=0, tiled=True
        )
        answers = jnp.take(answers.reshape(tile_count * capacity, -1), slot_index, axis=0)
        mine = answers
    grads = pre_gradient(part0, near, far, tile_ids, tile, weights, mine, answers)

    beside = swap(grads, "chan", 1)
    across = lax.ppermute(grads, "chan", middle)
    passed = lax.ppermute(across, "chan", [(1, 0), (2, 3)])
    crossed = lax.ppermute(beside, "chan", middle)
    skipped = lax.ppermute(beside, "chan", [(2, 0), (1, 3)])
    flipped = turned(spectra, chan)
    core = lax.axis_index("obs") & 1
    early = early_product(spectra, chan, grads, beside)
    keep, send = late_product(chan, core, flipped, early, crossed, passed, across, skipped)
    if lax.axis_size("obs") == 4 and tile_count == 2:
        return sum_over_panels(core, keep, send)
    return lax.psum(collect(core, keep, send), ("obs", "pix"))


def solution(mesh):
    return jax.shard_map(
        shards,
        mesh=mesh,
        in_specs=(
            P(("obs", "pix"), "chan"),
            P("chan", None),
            P(("obs", "pix"), None),
            P(("obs", "pix")),
            P(("obs", "pix")),
            P("pix", None),
            P(None, "pix"),
            P(),
        ),
        out_specs=P("chan", None),
        check_vma=False,
    )
```

```python
import functools

import jax
import jax.numpy as jnp
from jax import lax
from jax.experimental import pallas as pl
from jax.experimental.pallas import tpu as pltpu
from jax.sharding import PartitionSpec as P

NEIGH = 8
HALO = 128
MIB = 1024 * 1024


def edges(value, axis, width):
    size, length = lax.axis_size(axis), value.shape[0]
    last = lax.slice_in_dim(value, length - width, length, axis=0)
    first = lax.slice_in_dim(value, 0, width, axis=0)
    if size == 2:
        index = lax.axis_index(axis)
        other = lax.ppermute(jnp.where(index == 0, last, first), axis, [(0, 1), (1, 0)])
        return other, other
    up = [(i, i + 1) for i in range(size - 1)]
    return lax.ppermute(last, axis, up), lax.ppermute(first, axis, [(j, i) for i, j in up])


def requests(tile_ids, local_ids, capacity):
    tile_count = lax.axis_size("pix")
    onehot = (tile_ids[:, None] == jnp.arange(tile_count, dtype=jnp.int32)[None, :]).astype(
        jnp.int32
    )
    place_rank = jnp.sum((jnp.cumsum(onehot, axis=0) - 1) * onehot, axis=1)
    slot_index = tile_ids * capacity + place_rank
    outgoing = jnp.full((tile_count * capacity,), 0, jnp.int32).at[slot_index].set(local_ids)
    outgoing = outgoing.reshape(tile_count, capacity)
    requested = lax.all_to_all(outgoing, "pix", split_axis=0, concat_axis=0, tiled=True)
    return slot_index, requested.reshape(-1)


def swap(value, axis, bit):
    size = 1
    for name in (axis,) if isinstance(axis, str) else axis:
        size *= lax.axis_size(name)
    return lax.ppermute(value, axis, [(i, i ^ bit) for i in range(size)])


def memory(mib):
    return pltpu.CompilerParams(vmem_limit_bytes=mib * MIB)


def project_kernel(chan, spectra, weight, part3, part2, part1, part0, held, near, sems):
    parts = (part3, part2, part1, part0)
    quarter = part0.shape[0]
    chunk = quarter // 2
    copies = [pltpu.make_async_copy(weight, near, sems.at[8])]
    places = []
    for turn in range(8):
        first = (chan[0] ^ (3 - turn // 2)) * quarter + (turn % 2) * chunk
        places.append(pl.ds(pl.multiple_of(first, chunk), chunk))
        copies.append(
            pltpu.make_async_copy(spectra.at[places[-1]], held.at[places[-1]], sems.at[turn])
        )
    for copy in copies:
        copy.start()
    copies[0].wait()
    for turn in range(8):
        copies[turn + 1].wait()
        result = jnp.dot(held[places[turn], :], near[...], preferred_element_type=jnp.float32)
        first = (turn % 2) * chunk
        parts[turn // 2][first : first + chunk, :] = result.astype(jnp.bfloat16)


def project(spectra, weight, chan):
    depth, width = weight.shape
    quarter = spectra.shape[0] // 4
    part = jax.ShapeDtypeStruct((quarter, width), jnp.bfloat16)
    vmem = pl.BlockSpec(memory_space=pltpu.VMEM)
    hbm = pl.BlockSpec(memory_space=pltpu.HBM)
    return pl.pallas_call(
        project_kernel,
        out_shape=(part,) * 4,
        in_specs=[pl.BlockSpec(memory_space=pltpu.SMEM), hbm, hbm],
        out_specs=(vmem,) * 4,
        scratch_shapes=[
            pltpu.VMEM(spectra.shape, jnp.bfloat16),
            pltpu.VMEM((depth, width), jnp.bfloat16),
            pltpu.SemaphoreType.DMA((9,)),
        ],
        compiler_params=memory(52),
        cost_estimate=pl.CostEstimate(
            flops=8 * quarter * depth * width,
            bytes_accessed=8 * quarter * depth + 2 * depth * width + 8 * quarter * width,
            transcendentals=0,
        ),
        name="project",
    )(chan.reshape(1), spectra, weight)


def turn_kernel(chan, spectra, *outs):
    rows = spectra.shape[0] // 4
    for turn in range(4):
        first = pl.multiple_of((chan[0] ^ turn) * rows, rows)
        side = turn % 2
        outs[turn // 2][:, side * rows : (side + 1) * rows] = spectra[pl.ds(first, rows), :].T


def turned(spectra, chan):
    rows, depth = spectra.shape[0] // 4, spectra.shape[1]
    vmem = pl.BlockSpec(memory_space=pltpu.VMEM)
    return pl.pallas_call(
        turn_kernel,
        out_shape=(jax.ShapeDtypeStruct((depth, 2 * rows), jnp.bfloat16),) * 2,
        in_specs=[pl.BlockSpec(memory_space=pltpu.SMEM), vmem],
        out_specs=(vmem,) * 2,
        compiler_params=memory(16),
        name="turned",
    )(chan.reshape(1), spectra)


def early_kernel(flipped, first, second, total):
    rows = jnp.concatenate([first[...], second[...]], axis=0)
    total[...] = jnp.dot(flipped[...], rows, preferred_element_type=jnp.float32)


def early_product(flipped, first, second):
    depth, width = flipped.shape[0], first.shape[1]
    vmem = pl.BlockSpec(memory_space=pltpu.VMEM)
    return pl.pallas_call(
        early_kernel,
        out_shape=jax.ShapeDtypeStruct((depth, width), jnp.float32),
        in_specs=[vmem] * 3,
        out_specs=vmem,
        compiler_params=memory(16),
        cost_estimate=pl.CostEstimate(
            flops=2 * flipped.shape[0] * flipped.shape[1] * width,
            bytes_accessed=2 * flipped.shape[0] * flipped.shape[1] + 4 * depth * width,
            transcendentals=0,
        ),
        name="early_product",
    )(flipped, first, second)


def late_kernel(where, flipped, before, crossed, passed, across, skipped, keep, send):
    chan, core = where[0], where[1]
    inner = (chan == 1) | (chan == 2)
    second = jnp.where(inner, crossed[...], passed[...])
    third = jnp.where(inner, across[...], skipped[...])
    rows = jnp.concatenate([second, third], axis=0)
    half = keep.shape[0]
    for out, which in ((send, 1 - core), (keep, core)):
        here = pl.ds(pl.multiple_of(which * half, half), half)
        product = jnp.dot(flipped[here, :], rows, preferred_element_type=jnp.float32)
        out[...] = (before[here, :] + product).astype(out.dtype)


def late_product(chan, core, flipped, before, crossed, passed, across, skipped):
    half, width = before.shape[0] // 2, before.shape[1]
    spec = pl.BlockSpec(memory_space=pltpu.VMEM)
    return pl.pallas_call(
        late_kernel,
        out_shape=(
            jax.ShapeDtypeStruct((half, width), jnp.float32),
            jax.ShapeDtypeStruct((half, width), jnp.bfloat16),
        ),
        in_specs=[pl.BlockSpec(memory_space=pltpu.SMEM)] + [spec] * 6,
        out_specs=(spec, spec),
        compiler_params=memory(16),
        name="late_product",
    )(jnp.stack([chan, core]), flipped, before, crossed, passed, across, skipped)


def pixel_kernel(count, start, places, *refs):
    *lists, cotangent, above, below, mixing, out, table, scale, sums, near, sem = refs
    tile_rows, half = cotangent.shape[0], table.shape[1]
    copy = pltpu.make_async_copy(places, near, sem)
    copy.start()

    def fill(first, values):
        values = values.astype(jnp.float32)
        for side in range(2):
            table[pl.ds(2 * first + side, values.shape[0], stride=2), :] = values[
                :, side * half : (side + 1) * half
            ]

    fill(0, above[...])
    fill(HALO + tile_rows, below[...])
    chunk = 256
    for first in range(0, tile_rows, chunk):
        fill(HALO + first, cotangent[first : first + chunk, :])
    for side in range(2):
        scale[pl.ds(side, NEIGH, stride=2), :] = mixing[:, side * half : (side + 1) * half]
    scales = [scale[2 * k : 2 * k + 2, :] for k in range(NEIGH)]
    copy.wait()

    group = 16
    for index, wanted in enumerate(lists):

        def body(turn, carry, index=index, wanted=wanted):
            base = turn * group
            for n in range(group):
                pixel = wanted[start[0] + base + n]
                terms = [table[pl.ds(2 * (pixel + HALO), 2), :]]
                for k in range(NEIGH):
                    terms.append(table[pl.ds(near[k, pixel], 2), :] * scales[k])
                while len(terms) > 1:
                    pairs = [x + y for x, y in zip(terms[::2], terms[1::2])]
                    terms = pairs + terms[len(terms) // 2 * 2 :]
                sums[pl.ds(2 * (index * count + base + n), 2), :] = terms[0]
            return carry

        lax.fori_loop(0, count // group, body, 0)
    rows = out.shape[0]
    for side in range(2):
        out[:, side * half : (side + 1) * half] = sums[pl.ds(side, rows, stride=2), :].astype(
            out.dtype
        )


def pixel_rows(cotangent, above, below, adjoint, mixing, anchor, lists, start, count):
    tile_rows, width = cotangent.shape
    rows = count * len(lists)
    smem = pl.BlockSpec(memory_space=pltpu.SMEM)
    vmem = pl.BlockSpec(memory_space=pltpu.VMEM)
    return pl.pallas_call(
        functools.partial(pixel_kernel, count),
        out_shape=jax.ShapeDtypeStruct((rows, width), jnp.bfloat16),
        in_specs=[smem, pl.BlockSpec(memory_space=pl.ANY)] + [smem] * len(lists) + [vmem] * 4,
        out_specs=vmem,
        scratch_shapes=[
            pltpu.VMEM((2 * (tile_rows + 2 * HALO), width // 2), jnp.float32),
            pltpu.VMEM((2 * NEIGH, width // 2), jnp.float32),
            pltpu.VMEM((2 * rows, width // 2), jnp.float32),
            pltpu.SMEM(adjoint.shape, jnp.int32),
            pltpu.SemaphoreType.DMA,
        ],
        compiler_params=memory(24),
        cost_estimate=pl.CostEstimate(
            flops=2 * NEIGH * tile_rows * 256 * width,
            bytes_accessed=4 * tile_rows * width,
            transcendentals=0,
        ),
        name="pixel_rows",
    )(start.reshape(1), (adjoint - anchor) * 2, *lists, cotangent, above, below, mixing)


def gradient_kernel(own, near, far, tiles, tile, weights, mine, answers, out):
    pre = own[...].astype(jnp.float32) + near[...].astype(jnp.float32)
    pre = pre + far[...].astype(jnp.float32)
    sigma = jax.nn.sigmoid(pre)
    deriv = sigma * (1.0 + pre * (1.0 - sigma))
    fetched = jnp.where(
        tiles[...] == tile[0], mine[...].astype(jnp.float32), answers[...].astype(jnp.float32)
    )
    out[...] = (weights[...] * deriv * fetched).astype(out.dtype)


def pre_gradient(own, near, far, tiles, tile, weights, mine, answers):
    spec = pl.BlockSpec(memory_space=pltpu.VMEM)
    return pl.pallas_call(
        gradient_kernel,
        out_shape=jax.ShapeDtypeStruct(own.shape, jnp.bfloat16),
        in_specs=[spec] * 4 + [pl.BlockSpec(memory_space=pltpu.SMEM)] + [spec] * 3,
        out_specs=spec,
        compiler_params=memory(16),
        name="pre_gradient",
    )(own, near, far, tiles, tile.reshape(1), weights, mine, answers)


def collect_kernel(core, own, received, out):
    half = own.shape[0]
    for piece, which in ((own, core[0]), (received, 1 - core[0])):
        out[pl.ds(pl.multiple_of(which * half, half), half), :] = piece[...].astype(jnp.float32)


def collect(core, own, received):
    spec = pl.BlockSpec(memory_space=pltpu.VMEM)
    return pl.pallas_call(
        collect_kernel,
        out_shape=jax.ShapeDtypeStruct((2 * own.shape[0], own.shape[1]), jnp.float32),
        in_specs=[pl.BlockSpec(memory_space=pltpu.SMEM), spec, spec],
        out_specs=spec,
        compiler_params=memory(16),
        name="collect",
    )(core.reshape(1), own, received)


def sum_over_panels(core, keep, send):
    both = ("obs", "pix")
    wide = jnp.float32
    value = keep + swap(send, "obs", 1).astype(wide)
    for order in ((4, 1), (1, 4)):
        value = lax.reduce_precision(value, 8, 7)
        other = lax.ppermute(
            value.astype(jnp.bfloat16), both, [(i, i ^ order[(i >> 1) & 1]) for i in range(8)]
        )
        value = value + other.astype(wide)
    value = lax.reduce_precision(value, 8, 7).astype(jnp.bfloat16)
    return collect(core, value, swap(value, "obs", 1))


def shards(spectra, enc_weight, pix_tile, pix_local, foot_weight, cotangent, adjoint, mixing):
    tile_count = lax.axis_size("pix")
    tile_rows = cotangent.shape[0]
    quarter = spectra.shape[0] // lax.axis_size("chan")
    tile = lax.axis_index("pix")
    chan = lax.axis_index("chan")
    first_row = chan * quarter
    middle = [(1, 2), (2, 1)]

    part3, part2, part1, part0 = project(spectra, enc_weight, chan)
    outer2 = lax.ppermute(part2, "chan", [(0, 1), (3, 2)])
    inner2 = lax.ppermute(part2, "chan", middle)
    outer3 = lax.ppermute(part3, "chan", [(0, 2), (3, 1)])
    wide = jnp.float32
    sum1 = part1.astype(wide) + inner2.astype(wide) + outer3.astype(wide)
    sum3 = part3.astype(wide) + outer2.astype(wide)
    near = swap(sum1.astype(jnp.bfloat16), "chan", 1)
    far = lax.ppermute(sum3.astype(jnp.bfloat16), "chan", middle)

    above, below = edges(cotangent, "pix", HALO)
    anchor = tile * tile_rows - HALO
    tile_ids = lax.dynamic_slice_in_dim(pix_tile, first_row, quarter, 0)
    weights = lax.dynamic_slice_in_dim(foot_weight, first_row, quarter, 0)[:, None]
    capacity = 2 * quarter // tile_count
    if capacity >= quarter and tile_count == 2:
        lists = (pix_local, swap(pix_local, "pix", 1))
        rows = pixel_rows(
            cotangent, above, below, adjoint, mixing, anchor, lists, first_row, quarter
        )
        mine, answers = rows[:quarter], swap(rows[quarter:], "pix", 1)
    else:
        local_ids = lax.dynamic_slice_in_dim(pix_local, first_row, quarter, 0)
        slot_index, wanted = requests(tile_ids[:, 0], local_ids, capacity)
        rows = pixel_rows(
            cotangent, above, below, adjoint, mixing, anchor, (wanted,), 0 * chan, wanted.shape[0]
        )
        answers = lax.all_to_all(
            rows.reshape(tile_count, capacity, -1), "pix", split_axis=0, concat_axis=0, tiled=True
        )
        answers = jnp.take(answers.reshape(tile_count * capacity, -1), slot_index, axis=0)
        mine = answers
    part0, flipped = lax.optimization_barrier((part0, turned(spectra, chan)))
    grads = pre_gradient(part0, near, far, tile_ids, tile, weights, mine, answers)

    beside = swap(grads, "chan", 1)
    across = lax.ppermute(grads, "chan", middle)
    passed = lax.ppermute(across, "chan", [(1, 0), (2, 3)])
    crossed = lax.ppermute(beside, "chan", middle)
    skipped = lax.ppermute(beside, "chan", [(2, 0), (1, 3)])
    core = lax.axis_index("obs") & 1
    early = early_product(flipped[0], grads, beside)
    keep, send = late_product(chan, core, flipped[1], early, crossed, passed, across, skipped)
    if lax.axis_size("obs") == 4 and tile_count == 2:
        return sum_over_panels(core, keep, send)
    return lax.psum(collect(core, keep, send), ("obs", "pix"))


def solution(mesh):
    return jax.shard_map(
        shards,
        mesh=mesh,
        in_specs=(
            P(("obs", "pix"), "chan"),
            P("chan", None),
            P(("obs", "pix"), None),
            P(("obs", "pix")),
            P(("obs", "pix")),
            P("pix", None),
            P(None, "pix"),
            P(),
        ),
        out_specs=P("chan", None),
        check_vma=False,
    )
```

```python
import functools

import jax
import jax.numpy as jnp
from jax import lax
from jax.experimental import pallas as pl
from jax.experimental.pallas import tpu as pltpu
from jax.sharding import PartitionSpec as P

NEIGH = 8
HALO = 128
MIB = 1024 * 1024


def edges(value, axis, width):
    size, length = lax.axis_size(axis), value.shape[0]
    last = lax.slice_in_dim(value, length - width, length, axis=0)
    first = lax.slice_in_dim(value, 0, width, axis=0)
    if size == 2:
        index = lax.axis_index(axis)
        other = lax.ppermute(jnp.where(index == 0, last, first), axis, [(0, 1), (1, 0)])
        return other, other
    up = [(i, i + 1) for i in range(size - 1)]
    return lax.ppermute(last, axis, up), lax.ppermute(first, axis, [(j, i) for i, j in up])


def requests(tile_ids, local_ids, capacity):
    tile_count = lax.axis_size("pix")
    onehot = (tile_ids[:, None] == jnp.arange(tile_count, dtype=jnp.int32)[None, :]).astype(
        jnp.int32
    )
    place_rank = jnp.sum((jnp.cumsum(onehot, axis=0) - 1) * onehot, axis=1)
    slot_index = tile_ids * capacity + place_rank
    outgoing = jnp.full((tile_count * capacity,), 0, jnp.int32).at[slot_index].set(local_ids)
    outgoing = outgoing.reshape(tile_count, capacity)
    requested = lax.all_to_all(outgoing, "pix", split_axis=0, concat_axis=0, tiled=True)
    return slot_index, requested.reshape(-1)


def swap(value, axis, bit):
    size = 1
    for name in (axis,) if isinstance(axis, str) else axis:
        size *= lax.axis_size(name)
    return lax.ppermute(value, axis, [(i, i ^ bit) for i in range(size)])


def memory(mib):
    return pltpu.CompilerParams(vmem_limit_bytes=mib * MIB)


def project_kernel(quarters, spectra, weight, out):
    rows = out.shape[0] // 2
    for turn in range(2):
        first = pl.multiple_of(quarters[turn] * rows, rows)
        result = jnp.dot(
            spectra[pl.ds(first, rows), :], weight[...], preferred_element_type=jnp.float32
        )
        out[turn * rows : (turn + 1) * rows, :] = result.astype(out.dtype)


def project(spectra, weight, chan, bits):
    depth, width = weight.shape
    rows = spectra.shape[0] // 2
    vmem = pl.BlockSpec(memory_space=pltpu.VMEM)

    def kernel(chan, spectra, weight, out):
        project_kernel((chan[0] ^ bits, chan[0] ^ 2 ^ bits), spectra, weight, out)

    return pl.pallas_call(
        kernel,
        out_shape=jax.ShapeDtypeStruct((rows, width), jnp.bfloat16),
        in_specs=[pl.BlockSpec(memory_space=pltpu.SMEM), vmem, vmem],
        out_specs=vmem,
        compiler_params=memory(16),
        cost_estimate=pl.CostEstimate(
            flops=2 * rows * depth * width,
            bytes_accessed=2 * rows * depth + 2 * depth * width + 2 * rows * width,
            transcendentals=0,
        ),
        name="project",
    )(chan.reshape(1), spectra, weight)


def turn_kernel(chan, spectra, *outs):
    rows = spectra.shape[0] // 4
    for turn in range(4):
        first = pl.multiple_of((chan[0] ^ turn) * rows, rows)
        side = turn % 2
        outs[turn // 2][:, side * rows : (side + 1) * rows] = spectra[pl.ds(first, rows), :].T


def turned(spectra, chan):
    rows, depth = spectra.shape[0] // 4, spectra.shape[1]
    vmem = pl.BlockSpec(memory_space=pltpu.VMEM)
    return pl.pallas_call(
        turn_kernel,
        out_shape=(jax.ShapeDtypeStruct((depth, 2 * rows), jnp.bfloat16),) * 2,
        in_specs=[pl.BlockSpec(memory_space=pltpu.SMEM), vmem],
        out_specs=(vmem,) * 2,
        compiler_params=memory(16),
        name="turned",
    )(chan.reshape(1), spectra)


def early_kernel(flipped, first, second, total):
    rows = jnp.concatenate([first[...], second[...]], axis=0)
    total[...] = jnp.dot(flipped[...], rows, preferred_element_type=jnp.float32)


def early_product(flipped, first, second):
    depth, width = flipped.shape[0], first.shape[1]
    vmem = pl.BlockSpec(memory_space=pltpu.VMEM)
    return pl.pallas_call(
        early_kernel,
        out_shape=jax.ShapeDtypeStruct((depth, width), jnp.float32),
        in_specs=[vmem] * 3,
        out_specs=vmem,
        compiler_params=memory(16),
        cost_estimate=pl.CostEstimate(
            flops=2 * flipped.shape[0] * flipped.shape[1] * width,
            bytes_accessed=2 * flipped.shape[0] * flipped.shape[1] + 4 * depth * width,
            transcendentals=0,
        ),
        name="early_product",
    )(flipped, first, second)


def late_kernel(other, where, flipped, before, crossed, passed, across, skipped, *outs):
    chan, core = where[0], where[1]
    inner = (chan == 1) | (chan == 2)
    second = jnp.where(inner, crossed[...], passed[...])
    third = jnp.where(inner, across[...], skipped[...])
    rows = jnp.concatenate([second, third], axis=0)
    size = outs[0].shape[0]
    for index, out in enumerate(outs):
        first = (core ^ other) * size * len(outs) + index * size
        here = pl.ds(pl.multiple_of(first, size), size)
        product = jnp.dot(flipped[here, :], rows, preferred_element_type=jnp.float32)
        out[...] = (before[here, :] + product).astype(out.dtype)


def late_product(other, where, flipped, before, crossed, passed, across, skipped):
    size, width = before.shape[0] // 4, before.shape[1]
    spec = pl.BlockSpec(memory_space=pltpu.VMEM)
    part = jax.ShapeDtypeStruct((size, width), jnp.bfloat16 if other else jnp.float32)
    return pl.pallas_call(
        functools.partial(late_kernel, other),
        out_shape=(part, part),
        in_specs=[pl.BlockSpec(memory_space=pltpu.SMEM)] + [spec] * 6,
        out_specs=(spec, spec),
        compiler_params=memory(16),
        cost_estimate=pl.CostEstimate(
            flops=4 * size * flipped.shape[1] * width,
            bytes_accessed=4 * size * flipped.shape[1] + 16 * size * width,
            transcendentals=0,
        ),
        name="late_product",
    )(where, flipped, before, crossed, passed, across, skipped)


def pixel_kernel(count, start, places, *refs):
    *lists, cotangent, above, below, mixing, out = refs[:-6]
    left, right, left_sums, right_sums, near, sem = refs[-6:]
    sides = ((left, left_sums), (right, right_sums))
    tile_rows, half = cotangent.shape[0], left.shape[1]
    copy = pltpu.make_async_copy(places, near, sem)
    copy.start()

    def fill(first, values):
        values = values.astype(jnp.float32)
        for side, (table, _) in enumerate(sides):
            table[first : first + values.shape[0], :] = values[:, side * half : (side + 1) * half]

    fill(0, above[...])
    fill(HALO + tile_rows, below[...])
    chunk = 256
    for first in range(0, tile_rows, chunk):
        fill(HALO + first, cotangent[first : first + chunk, :])
    scales = [
        [mixing[k : k + 1, side * half : (side + 1) * half] for k in range(NEIGH)]
        for side in range(2)
    ]
    copy.wait()

    group = 16
    for index, wanted in enumerate(lists):

        def body(turn, carry, index=index, wanted=wanted):
            base = turn * group
            for n in range(group):
                pixel = wanted[start[0] + base + n]
                spots = [near[k, pixel] for k in range(NEIGH)]
                for (table, sums), scale in zip(sides, scales):
                    terms = [table[pl.ds(pixel + HALO, 1), :]]
                    terms += [table[pl.ds(s, 1), :] * x for s, x in zip(spots, scale)]
                    while len(terms) > 1:
                        pairs = [x + y for x, y in zip(terms[::2], terms[1::2])]
                        terms = pairs + terms[len(terms) // 2 * 2 :]
                    sums[pl.ds(index * count + base + n, 1), :] = terms[0]
            return carry

        lax.fori_loop(0, count // group, body, 0)
    for side, (_, sums) in enumerate(sides):
        out[:, side * half : (side + 1) * half] = sums[...].astype(out.dtype)


def pixel_rows(cotangent, above, below, adjoint, mixing, anchor, lists, start, count):
    tile_rows, width = cotangent.shape
    rows = count * len(lists)
    smem = pl.BlockSpec(memory_space=pltpu.SMEM)
    vmem = pl.BlockSpec(memory_space=pltpu.VMEM)
    return pl.pallas_call(
        functools.partial(pixel_kernel, count),
        out_shape=jax.ShapeDtypeStruct((rows, width), jnp.bfloat16),
        in_specs=[smem, pl.BlockSpec(memory_space=pl.ANY)] + [smem] * len(lists) + [vmem] * 4,
        out_specs=vmem,
        scratch_shapes=[
            pltpu.VMEM((tile_rows + 2 * HALO, width // 2), jnp.float32),
            pltpu.VMEM((tile_rows + 2 * HALO, width // 2), jnp.float32),
            pltpu.VMEM((rows, width // 2), jnp.float32),
            pltpu.VMEM((rows, width // 2), jnp.float32),
            pltpu.SMEM(adjoint.shape, jnp.int32),
            pltpu.SemaphoreType.DMA,
        ],
        compiler_params=memory(16),
        cost_estimate=pl.CostEstimate(
            flops=6 * NEIGH * tile_rows * 256 * width,
            bytes_accessed=4 * tile_rows * width,
            transcendentals=0,
        ),
        name="pixel_rows",
    )(start.reshape(1), adjoint - anchor, *lists, cotangent, above, below, mixing)


def gradient_kernel(keep, near, far, tiles, tile, weights, mine, answers, out):
    rows = out.shape[0]
    pre = keep[:rows, :].astype(jnp.float32) + near[:rows, :].astype(jnp.float32)
    pre = pre + far[...].astype(jnp.float32)
    sigma = jax.nn.sigmoid(pre)
    deriv = sigma * (1.0 + pre * (1.0 - sigma))
    fetched = jnp.where(
        tiles[...] == tile[0], mine[:rows, :].astype(jnp.float32), answers[...].astype(jnp.float32)
    )
    out[...] = (weights[...] * deriv * fetched).astype(out.dtype)


def pre_gradient(keep, near, far, tiles, tile, weights, mine, answers):
    spec = pl.BlockSpec(memory_space=pltpu.VMEM)
    return pl.pallas_call(
        gradient_kernel,
        out_shape=jax.ShapeDtypeStruct(far.shape, jnp.bfloat16),
        in_specs=[spec] * 4 + [pl.BlockSpec(memory_space=pltpu.SMEM)] + [spec] * 3,
        out_specs=spec,
        compiler_params=memory(16),
        name="pre_gradient",
    )(keep, near, far, tiles, tile.reshape(1), weights, mine, answers)


def collect_kernel(core, *refs):
    *pieces, out = refs
    half, rows = out.shape[0] // 2, pieces[0].shape[0]
    count = len(pieces) // 2
    for index, piece in enumerate(pieces):
        which = core[0] if index < count else 1 - core[0]
        first = which * half + (index % count) * rows
        out[pl.ds(pl.multiple_of(first, rows), rows), :] = piece[...].astype(jnp.float32)


def collect(core, own, received):
    spec = pl.BlockSpec(memory_space=pltpu.VMEM)
    pieces = [*own, *received]
    rows, width = sum(piece.shape[0] for piece in pieces), own[0].shape[1]
    return pl.pallas_call(
        collect_kernel,
        out_shape=jax.ShapeDtypeStruct((rows, width), jnp.float32),
        in_specs=[pl.BlockSpec(memory_space=pltpu.SMEM)] + [spec] * len(pieces),
        out_specs=spec,
        compiler_params=memory(16),
        name="collect",
    )(core.reshape(1), *pieces)


def add_kernel(first, second, out):
    out[...] = (first[...].astype(jnp.float32) + second[...].astype(jnp.float32)).astype(out.dtype)


def added(first, second):
    spec = pl.BlockSpec(memory_space=pltpu.VMEM)
    return pl.pallas_call(
        add_kernel,
        out_shape=jax.ShapeDtypeStruct(first.shape, jnp.bfloat16),
        in_specs=[spec, spec],
        out_specs=spec,
        compiler_params=memory(16),
        name="added",
    )(first, second)


def sum_over_panels(core, parts, received):
    both = ("obs", "pix")
    parts = [added(part, other) for part, other in zip(parts, received)]
    for order in ((4, 1), (1, 4)):
        perm = [(i, i ^ order[(i >> 1) & 1]) for i in range(8)]
        parts = [added(part, lax.ppermute(part, both, perm)) for part in parts]
    return collect(core, parts, [swap(part, "obs", 1) for part in parts])


def shards(spectra, enc_weight, pix_tile, pix_local, foot_weight, cotangent, adjoint, mixing):
    tile_count = lax.axis_size("pix")
    tile_rows = cotangent.shape[0]
    quarter = spectra.shape[0] // lax.axis_size("chan")
    tile = lax.axis_index("pix")
    chan = lax.axis_index("chan")
    first_row = chan * quarter
    middle = [(1, 2), (2, 1)]

    send = project(spectra, enc_weight, chan, 1)
    near = swap(send, "chan", 1)
    keep = project(spectra, enc_weight, chan, 0)
    above, below = edges(cotangent, "pix", HALO)
    anchor = tile * tile_rows - HALO
    tile_ids = lax.dynamic_slice_in_dim(pix_tile, first_row, quarter, 0)
    weights = lax.dynamic_slice_in_dim(foot_weight, first_row, quarter, 0)[:, None]
    capacity = 2 * quarter // tile_count
    if capacity >= quarter and tile_count == 2:
        lists = (pix_local, swap(pix_local, "pix", 1))
        rows = pixel_rows(
            cotangent, above, below, adjoint, mixing, anchor, lists, first_row, quarter
        )
        answers = swap(rows[quarter:], "pix", 1)
    else:
        local_ids = lax.dynamic_slice_in_dim(pix_local, first_row, quarter, 0)
        slot_index, wanted = requests(tile_ids[:, 0], local_ids, capacity)
        rows = pixel_rows(
            cotangent, above, below, adjoint, mixing, anchor, (wanted,), 0 * chan, wanted.shape[0]
        )
        answers = lax.all_to_all(
            rows.reshape(tile_count, capacity, -1), "pix", split_axis=0, concat_axis=0, tiled=True
        )
        answers = jnp.take(answers.reshape(tile_count * capacity, -1), slot_index, axis=0)
        rows = answers
    near, rows = lax.optimization_barrier((near, rows))
    passed_on = keep[quarter:].astype(jnp.float32) + near[quarter:].astype(jnp.float32)
    far = swap(passed_on.astype(jnp.bfloat16), "chan", 2)
    far, flipped = lax.optimization_barrier((far, turned(spectra, chan)))
    grads = pre_gradient(keep, near, far, tile_ids, tile, weights, rows, answers)

    beside = swap(grads, "chan", 1)
    across = lax.ppermute(grads, "chan", middle)
    passed = lax.ppermute(across, "chan", [(1, 0), (2, 3)])
    crossed = lax.ppermute(beside, "chan", middle)
    skipped = lax.ppermute(beside, "chan", [(2, 0), (1, 3)])
    core = lax.axis_index("obs") & 1
    early = early_product(flipped[0], grads, beside)
    rest = (jnp.stack([chan, core]), flipped[1], early, crossed, passed, across, skipped)
    send = late_product(1, *rest)
    if lax.axis_size("obs") == 4 and tile_count == 2:
        received = [swap(part, "obs", 1) for part in send]
        return sum_over_panels(core, late_product(0, *rest), received)
    return lax.psum(collect(core, late_product(0, *rest), send), ("obs", "pix"))


def solution(mesh):
    return jax.shard_map(
        shards,
        mesh=mesh,
        in_specs=(
            P(("obs", "pix"), "chan"),
            P("chan", None),
            P(("obs", "pix"), None),
            P(("obs", "pix")),
            P(("obs", "pix")),
            P("pix", None),
            P(None, "pix"),
            P(),
        ),
        out_specs=P("chan", None),
        check_vma=False,
    )
```

```python
import functools

import jax
import jax.numpy as jnp
from jax import lax
from jax.experimental import pallas as pl
from jax.experimental.pallas import tpu as pltpu
from jax.sharding import PartitionSpec as P

NEIGH = 8
HALO = 128
MIB = 1024 * 1024
LARGE = 48


def edges(value, axis, width):
    size, length = lax.axis_size(axis), value.shape[0]
    last = lax.slice_in_dim(value, length - width, length, axis=0)
    first = lax.slice_in_dim(value, 0, width, axis=0)
    if size == 2:
        index = lax.axis_index(axis)
        other = lax.ppermute(jnp.where(index == 0, last, first), axis, [(0, 1), (1, 0)])
        return other, other
    up = [(i, i + 1) for i in range(size - 1)]
    return lax.ppermute(last, axis, up), lax.ppermute(first, axis, [(j, i) for i, j in up])


def requests(tile_ids, local_ids, capacity):
    tile_count = lax.axis_size("pix")
    onehot = (tile_ids[:, None] == jnp.arange(tile_count, dtype=jnp.int32)[None, :]).astype(
        jnp.int32
    )
    place_rank = jnp.sum((jnp.cumsum(onehot, axis=0) - 1) * onehot, axis=1)
    slot_index = tile_ids * capacity + place_rank
    outgoing = jnp.full((tile_count * capacity,), 0, jnp.int32).at[slot_index].set(local_ids)
    outgoing = outgoing.reshape(tile_count, capacity)
    requested = lax.all_to_all(outgoing, "pix", split_axis=0, concat_axis=0, tiled=True)
    return slot_index, requested.reshape(-1)


def swap(value, axis, bit):
    size = 1
    for name in (axis,) if isinstance(axis, str) else axis:
        size *= lax.axis_size(name)
    return lax.ppermute(value, axis, [(i, i ^ bit) for i in range(size)])


def memory(mib):
    return pltpu.CompilerParams(vmem_limit_bytes=mib * MIB)


def project_kernel(bits, chan, spectra, weight, out, held, near, sems):
    chunk = out.shape[0] // 4
    copies = [pltpu.make_async_copy(weight, near, sems.at[4])]
    for turn in range(4):
        first = ((chan[0] ^ bits ^ (turn // 2 * 2)) * 2 + turn % 2) * chunk
        copies.append(
            pltpu.make_async_copy(
                spectra.at[pl.ds(pl.multiple_of(first, chunk), chunk)],
                held.at[pl.ds(turn * chunk, chunk)],
                sems.at[turn],
            )
        )
    for copy in copies:
        copy.start()
    copies[0].wait()
    for turn in range(4):
        copies[turn + 1].wait()
        rows = pl.ds(turn * chunk, chunk)
        result = jnp.dot(held[rows, :], near[...], preferred_element_type=jnp.float32)
        out[rows, :] = result.astype(out.dtype)


def project(spectra, weight, chan, bits):
    depth, width = weight.shape
    rows = spectra.shape[0] // 2
    hbm = pl.BlockSpec(memory_space=pltpu.HBM)
    return pl.pallas_call(
        functools.partial(project_kernel, bits),
        out_shape=jax.ShapeDtypeStruct((rows, width), jnp.bfloat16),
        in_specs=[pl.BlockSpec(memory_space=pltpu.SMEM), hbm, hbm],
        out_specs=pl.BlockSpec(memory_space=pltpu.VMEM),
        scratch_shapes=[
            pltpu.VMEM((rows, depth), jnp.bfloat16),
            pltpu.VMEM((depth, width), jnp.bfloat16),
            pltpu.SemaphoreType.DMA((5,)),
        ],
        compiler_params=memory(LARGE),
        cost_estimate=pl.CostEstimate(
            flops=2 * rows * depth * width,
            bytes_accessed=2 * rows * depth + 2 * depth * width + 2 * rows * width,
            transcendentals=0,
        ),
        name="project",
    )(chan.reshape(1), spectra, weight)


def turned_product(left, right):
    return lax.dot_general(
        left, right, (((0,), (0,)), ((), ())), preferred_element_type=jnp.float32
    )


def early_kernel(chan, spectra, first, second, total, late, held, sems):
    rows = first.shape[0]
    copies = []
    for turn in range(4):
        start = pl.multiple_of((chan[0] ^ turn) * rows, rows)
        target = (held, late)[turn // 2].at[pl.ds(turn % 2 * rows, rows)]
        copies.append(pltpu.make_async_copy(spectra.at[pl.ds(start, rows)], target, sems.at[turn]))
    for copy in copies:
        copy.start()
    copies[0].wait()
    product = turned_product(held[:rows, :], first[...])
    copies[1].wait()
    total[...] = product + turned_product(held[rows:, :], second[...])
    copies[2].wait()
    copies[3].wait()


def early_product(spectra, chan, first, second):
    depth = spectra.shape[1]
    rows, width = first.shape
    vmem = pl.BlockSpec(memory_space=pltpu.VMEM)
    return pl.pallas_call(
        early_kernel,
        out_shape=(
            jax.ShapeDtypeStruct((depth, width), jnp.float32),
            jax.ShapeDtypeStruct((2 * rows, depth), jnp.bfloat16),
        ),
        in_specs=[
            pl.BlockSpec(memory_space=pltpu.SMEM),
            pl.BlockSpec(memory_space=pltpu.HBM),
            vmem,
            vmem,
        ],
        out_specs=(vmem, vmem),
        scratch_shapes=[
            pltpu.VMEM((2 * rows, depth), jnp.bfloat16),
            pltpu.SemaphoreType.DMA((4,)),
        ],
        compiler_params=memory(LARGE),
        cost_estimate=pl.CostEstimate(
            flops=4 * rows * depth * width,
            bytes_accessed=8 * rows * depth + 4 * depth * width,
            transcendentals=0,
        ),
        name="early_product",
    )(chan.reshape(1), spectra, first, second)


def late_kernel(where, held, before, crossed, passed, across, skipped, *outs):
    *outs, total = outs
    chan, core = where[0], where[1]
    inner = (chan == 1) | (chan == 2)
    second = jnp.where(inner, crossed[...], passed[...])
    third = jnp.where(inner, across[...], skipped[...])
    rows = jnp.concatenate([second, third], axis=0)
    total[...] = before[...] + turned_product(held[...], rows)
    size = outs[0].shape[0]
    for index, out in enumerate(outs):
        first = (core ^ (1 - index // 2)) * 2 * size + index % 2 * size
        here = pl.ds(pl.multiple_of(first, size), size)
        out[...] = total[here, :].astype(out.dtype)


def late_product(where, held, before, crossed, passed, across, skipped):
    size, width = before.shape[0] // 4, before.shape[1]
    spec = pl.BlockSpec(memory_space=pltpu.VMEM)
    send = jax.ShapeDtypeStruct((size, width), jnp.bfloat16)
    keep = jax.ShapeDtypeStruct((size, width), jnp.float32)
    outs = pl.pallas_call(
        late_kernel,
        out_shape=(send, send, keep, keep),
        in_specs=[pl.BlockSpec(memory_space=pltpu.SMEM)] + [spec] * 6,
        out_specs=(spec,) * 4,
        scratch_shapes=[pltpu.VMEM(before.shape, jnp.float32)],
        compiler_params=memory(16),
        cost_estimate=pl.CostEstimate(
            flops=2 * held.shape[0] * held.shape[1] * width,
            bytes_accessed=2 * held.shape[0] * held.shape[1] + 16 * size * width,
            transcendentals=0,
        ),
        name="late_product",
    )(where, held, before, crossed, passed, across, skipped)
    return outs[:2], outs[2:]


def pixel_kernel(count, start, places, *refs):
    lists = refs[: len(refs) // 2 - 5]
    cotangent, above, below, mixing = refs[len(lists) : len(lists) + 4]
    outs = refs[len(lists) + 4 : 2 * len(lists) + 4]
    table, scale, sums, held, near, sems = refs[2 * len(lists) + 4 :]
    tile_rows, half = held.shape[0], table.shape[1]
    chunk = tile_rows // 4
    copies = [
        pltpu.make_async_copy(
            cotangent.at[pl.ds(n * chunk, chunk)], held.at[pl.ds(n * chunk, chunk)], sems.at[n]
        )
        for n in range(4)
    ]
    copies.append(pltpu.make_async_copy(places, near, sems.at[4]))
    for copy in copies:
        copy.start()

    def fill(first, values):
        values = values.astype(jnp.float32)
        for side in range(2):
            table[pl.ds(2 * first + side, values.shape[0], stride=2), :] = values[
                :, side * half : (side + 1) * half
            ]

    for side in range(2):
        scale[pl.ds(side, NEIGH, stride=2), :] = mixing[:, side * half : (side + 1) * half]
    scales = [scale[2 * k : 2 * k + 2, :] for k in range(NEIGH)]
    fill(0, above[...])
    fill(HALO + tile_rows, below[...])
    for n in range(4):
        copies[n].wait()
        for first in range(n * chunk, (n + 1) * chunk, 256):
            fill(HALO + first, held[first : first + 256, :])
    copies[4].wait()

    group = 16
    for index, wanted in enumerate(lists):

        def body(turn, carry, index=index, wanted=wanted):
            base = turn * group
            totals = []
            for n in range(group):
                pixel = wanted[start[0] + base + n]
                terms = [table[pl.ds(2 * (pixel + HALO), 2), :]]
                for k in range(NEIGH):
                    terms.append(table[pl.ds(near[k, pixel], 2), :] * scales[k])
                while len(terms) > 1:
                    pairs = [x + y for x, y in zip(terms[::2], terms[1::2])]
                    terms = pairs + terms[len(terms) // 2 * 2 :]
                totals += terms
            for n, total in enumerate(totals):
                sums[pl.ds(2 * (index * count + base + n), 2), :] = total
            return carry

        lax.fori_loop(0, count // group, body, 0)
    for index, out in enumerate(outs):
        for side in range(2):
            out[:, side * half : (side + 1) * half] = sums[
                pl.ds(2 * index * count + side, count, stride=2), :
            ].astype(out.dtype)


def pixel_rows(cotangent, above, below, adjoint, mixing, anchor, lists, start, count):
    tile_rows, width = cotangent.shape
    smem = pl.BlockSpec(memory_space=pltpu.SMEM)
    vmem = pl.BlockSpec(memory_space=pltpu.VMEM)
    return pl.pallas_call(
        functools.partial(pixel_kernel, count),
        out_shape=(jax.ShapeDtypeStruct((count, width), jnp.bfloat16),) * len(lists),
        in_specs=[
            smem,
            pl.BlockSpec(memory_space=pl.ANY),
            *[smem] * len(lists),
            pl.BlockSpec(memory_space=pltpu.HBM),
            *[vmem] * 3,
        ],
        out_specs=(vmem,) * len(lists),
        scratch_shapes=[
            pltpu.VMEM((2 * (tile_rows + 2 * HALO), width // 2), jnp.float32),
            pltpu.VMEM((2 * NEIGH, width // 2), jnp.float32),
            pltpu.VMEM((2 * count * len(lists), width // 2), jnp.float32),
            pltpu.VMEM(cotangent.shape, cotangent.dtype),
            pltpu.SMEM(adjoint.shape, jnp.int32),
            pltpu.SemaphoreType.DMA((5,)),
        ],
        compiler_params=memory(LARGE),
        cost_estimate=pl.CostEstimate(
            flops=6 * NEIGH * tile_rows * 256 * width,
            bytes_accessed=4 * tile_rows * width,
            transcendentals=0,
        ),
        name="pixel_rows",
    )(start.reshape(1), (adjoint - anchor) * 2, *lists, cotangent, above, below, mixing)


def gradient_kernel(where, keep, near, far, tiles, weights, mine, answers, out):
    tile, chan = where[0], where[1]
    rows = out.shape[0]
    size = tiles.shape[1]
    count = rows // size
    group = 8 // count
    wide = jnp.float32
    first = pl.multiple_of(chan // group * 8, 8)

    def columns(values):
        turned = values[pl.ds(first, 8), :].T
        places = [turned[:, n * count : (n + 1) * count] for n in range(group)]
        picked = places[0]
        for n in range(1, group):
            picked = jnp.where(chan % group == n, places[n], picked)
        return picked

    own = columns(tiles).astype(wide)
    factors = columns(weights)
    for n in range(count):
        here = slice(n * size, (n + 1) * size)
        pre = keep[here, :].astype(wide) + near[here, :].astype(wide) + far[here, :].astype(wide)
        sigma = jax.nn.sigmoid(pre)
        deriv = sigma * (1.0 + pre * (1.0 - sigma))
        fetched = jnp.where(
            own[:, n : n + 1] == tile.astype(wide),
            mine[here, :].astype(wide),
            answers[here, :].astype(wide),
        )
        out[here, :] = (factors[:, n : n + 1] * deriv * fetched).astype(out.dtype)


def pre_gradient(tile, chan, keep, near, far, tiles, weights, mine, answers):
    spec = pl.BlockSpec(memory_space=pltpu.VMEM)
    tiles, weights = tiles.reshape(-1, 128), weights.reshape(-1, 128)
    return pl.pallas_call(
        gradient_kernel,
        out_shape=jax.ShapeDtypeStruct(far.shape, jnp.bfloat16),
        in_specs=[pl.BlockSpec(memory_space=pltpu.SMEM)] + [spec] * 7,
        out_specs=spec,
        compiler_params=memory(16),
        name="pre_gradient",
    )(jnp.stack([tile, chan]), keep, near, far, tiles, weights, mine, answers)


def collect_kernel(core, *refs):
    *pieces, out = refs
    half, rows = out.shape[0] // 2, pieces[0].shape[0]
    count = len(pieces) // 2
    for index, piece in enumerate(pieces):
        which = core[0] if index < count else 1 - core[0]
        first = which * half + (index % count) * rows
        out[pl.ds(pl.multiple_of(first, rows), rows), :] = piece[...].astype(jnp.float32)


def collect(core, own, received):
    spec = pl.BlockSpec(memory_space=pltpu.VMEM)
    pieces = [*own, *received]
    rows, width = sum(piece.shape[0] for piece in pieces), own[0].shape[1]
    return pl.pallas_call(
        collect_kernel,
        out_shape=jax.ShapeDtypeStruct((rows, width), jnp.float32),
        in_specs=[pl.BlockSpec(memory_space=pltpu.SMEM)] + [spec] * len(pieces),
        out_specs=spec,
        compiler_params=memory(16),
        name="collect",
    )(core.reshape(1), *pieces)


def add_kernel(first, second, out):
    out[...] = (first[...].astype(jnp.float32) + second[...].astype(jnp.float32)).astype(out.dtype)


def added(first, second):
    spec = pl.BlockSpec(memory_space=pltpu.VMEM)
    return pl.pallas_call(
        add_kernel,
        out_shape=jax.ShapeDtypeStruct(first.shape, jnp.bfloat16),
        in_specs=[spec, spec],
        out_specs=spec,
        compiler_params=memory(16),
        name="added",
    )(first, second)


def sum_over_panels(core, parts, received):
    both = ("obs", "pix")
    parts = [added(part, other) for part, other in zip(parts, received)]
    for order in ((4, 1), (1, 4)):
        perm = [(i, i ^ order[(i >> 1) & 1]) for i in range(8)]
        parts = [added(part, lax.ppermute(part, both, perm)) for part in parts]
    return collect(core, parts, [swap(part, "obs", 1) for part in parts])


def shards(spectra, enc_weight, pix_tile, pix_local, foot_weight, cotangent, adjoint, mixing):
    tile_count = lax.axis_size("pix")
    tile_rows = cotangent.shape[0]
    quarter = spectra.shape[0] // lax.axis_size("chan")
    tile = lax.axis_index("pix")
    chan = lax.axis_index("chan")
    first_row = chan * quarter
    middle = [(1, 2), (2, 1)]

    send = project(spectra, enc_weight, chan, 1)
    near = swap(send, "chan", 1)
    keep = project(spectra, enc_weight, chan, 0)
    above, below = edges(cotangent, "pix", HALO)
    anchor = tile * tile_rows - HALO
    capacity = 2 * quarter // tile_count
    if capacity >= quarter and tile_count == 2:
        lists = (pix_local, swap(pix_local, "pix", 1))
        mine, theirs = pixel_rows(
            cotangent, above, below, adjoint, mixing, anchor, lists, first_row, quarter
        )
        answers = swap(theirs, "pix", 1)
    else:
        tile_ids = lax.dynamic_slice_in_dim(pix_tile[:, 0], first_row, quarter, 0)
        local_ids = lax.dynamic_slice_in_dim(pix_local, first_row, quarter, 0)
        slot_index, wanted = requests(tile_ids, local_ids, capacity)
        (rows,) = pixel_rows(
            cotangent, above, below, adjoint, mixing, anchor, (wanted,), 0 * chan, wanted.shape[0]
        )
        answers = lax.all_to_all(
            rows.reshape(tile_count, capacity, -1), "pix", split_axis=0, concat_axis=0, tiled=True
        )
        mine = answers = jnp.take(answers.reshape(tile_count * capacity, -1), slot_index, axis=0)
    near, mine = lax.optimization_barrier((near, mine))
    passed_on = keep[quarter:].astype(jnp.float32) + near[quarter:].astype(jnp.float32)
    far = swap(passed_on.astype(jnp.bfloat16), "chan", 2)
    grads = pre_gradient(tile, chan, keep, near, far, pix_tile, foot_weight, mine, answers)

    beside = swap(grads, "chan", 1)
    across = lax.ppermute(grads, "chan", middle)
    passed = lax.ppermute(across, "chan", [(1, 0), (2, 3)])
    crossed = lax.ppermute(beside, "chan", middle)
    skipped = lax.ppermute(beside, "chan", [(2, 0), (1, 3)])
    core = lax.axis_index("obs") & 1
    early, held = early_product(spectra, chan, grads, beside)
    where = jnp.stack([chan, core])
    send, keep = late_product(where, held, early, crossed, passed, across, skipped)
    if lax.axis_size("obs") == 4 and tile_count == 2:
        return sum_over_panels(core, keep, [swap(part, "obs", 1) for part in send])
    return lax.psum(collect(core, keep, send), ("obs", "pix"))


def solution(mesh):
    return jax.shard_map(
        shards,
        mesh=mesh,
        in_specs=(
            P(("obs", "pix"), "chan"),
            P("chan", None),
            P(("obs", "pix"), None),
            P(("obs", "pix")),
            P(("obs", "pix")),
            P("pix", None),
            P(None, "pix"),
            P(),
        ),
        out_specs=P("chan", None),
        check_vma=False,
    )
```

```python
import functools

import jax
import jax.numpy as jnp
from jax import lax
from jax.experimental import pallas as pl
from jax.experimental.pallas import tpu as pltpu
from jax.sharding import PartitionSpec as P

NEIGH = 8
HALO = 128
MIB = 1024 * 1024
LARGE = 52


def edges(value, axis, width):
    size, length = lax.axis_size(axis), value.shape[0]
    last = lax.slice_in_dim(value, length - width, length, axis=0)
    first = lax.slice_in_dim(value, 0, width, axis=0)
    if size == 2:
        index = lax.axis_index(axis)
        other = lax.ppermute(jnp.where(index == 0, last, first), axis, [(0, 1), (1, 0)])
        return other, other
    up = [(i, i + 1) for i in range(size - 1)]
    return lax.ppermute(last, axis, up), lax.ppermute(first, axis, [(j, i) for i, j in up])


def requests(tile_ids, local_ids, capacity):
    tile_count = lax.axis_size("pix")
    onehot = (tile_ids[:, None] == jnp.arange(tile_count, dtype=jnp.int32)[None, :]).astype(
        jnp.int32
    )
    place_rank = jnp.sum((jnp.cumsum(onehot, axis=0) - 1) * onehot, axis=1)
    slot_index = tile_ids * capacity + place_rank
    outgoing = jnp.full((tile_count * capacity,), 0, jnp.int32).at[slot_index].set(local_ids)
    outgoing = outgoing.reshape(tile_count, capacity)
    requested = lax.all_to_all(outgoing, "pix", split_axis=0, concat_axis=0, tiled=True)
    return slot_index, requested.reshape(-1)


def swap(value, axis, bit):
    size = 1
    for name in (axis,) if isinstance(axis, str) else axis:
        size *= lax.axis_size(name)
    return lax.ppermute(value, axis, [(i, i ^ bit) for i in range(size)])


def memory(mib):
    return pltpu.CompilerParams(vmem_limit_bytes=mib * MIB)


def quarter_copies(spectra, weight, held, near, sems, chan, bits):
    chunk = held.shape[0] // 4
    copies = [pltpu.make_async_copy(weight, near, sems.at[4])]
    for turn in range(4):
        first = ((chan ^ bits ^ (turn // 2 * 2)) * 2 + turn % 2) * chunk
        copies.append(
            pltpu.make_async_copy(
                spectra.at[pl.ds(pl.multiple_of(first, chunk), chunk)],
                held.at[pl.ds(turn * chunk, chunk)],
                sems.at[turn],
            )
        )
    return copies


def project_rows(copies, held, near, out):
    chunk = held.shape[0] // 4
    copies[0].wait()
    for turn in range(4):
        copies[turn + 1].wait()
        rows = pl.ds(turn * chunk, chunk)
        result = jnp.dot(held[rows, :], near[...], preferred_element_type=jnp.float32)
        out[rows, :] = result.astype(out.dtype)


def project_kernel(chan, spectra, weight, out, held, near, sems):
    copies = quarter_copies(spectra, weight, held, near, sems, chan[0], 1)
    for copy in copies:
        copy.start()
    project_rows(copies, held, near, out)


def project(spectra, weight, chan):
    depth, width = weight.shape
    rows = spectra.shape[0] // 2
    hbm = pl.BlockSpec(memory_space=pltpu.HBM)
    return pl.pallas_call(
        project_kernel,
        out_shape=jax.ShapeDtypeStruct((rows, width), jnp.bfloat16),
        in_specs=[pl.BlockSpec(memory_space=pltpu.SMEM), hbm, hbm],
        out_specs=pl.BlockSpec(memory_space=pltpu.VMEM),
        scratch_shapes=[
            pltpu.VMEM((rows, depth), jnp.bfloat16),
            pltpu.VMEM((depth, width), jnp.bfloat16),
            pltpu.SemaphoreType.DMA((5,)),
        ],
        compiler_params=memory(LARGE),
        cost_estimate=pl.CostEstimate(
            flops=2 * rows * depth * width,
            bytes_accessed=2 * rows * depth + 2 * depth * width + 2 * rows * width,
            transcendentals=0,
        ),
        name="project",
    )(chan.reshape(1), spectra, weight)


def turned_product(left, right):
    return lax.dot_general(
        left, right, (((0,), (0,)), ((), ())), preferred_element_type=jnp.float32
    )


def early_kernel(chan, spectra, first, second, total, late, held, sems):
    rows = first.shape[0]
    copies = []
    for turn in range(4):
        start = pl.multiple_of((chan[0] ^ turn) * rows, rows)
        target = (held, late)[turn // 2].at[pl.ds(turn % 2 * rows, rows)]
        copies.append(pltpu.make_async_copy(spectra.at[pl.ds(start, rows)], target, sems.at[turn]))
    for copy in copies:
        copy.start()
    copies[0].wait()
    product = turned_product(held[:rows, :], first[...])
    copies[1].wait()
    total[...] = product + turned_product(held[rows:, :], second[...])
    copies[2].wait()
    copies[3].wait()


def early_product(spectra, chan, first, second):
    depth = spectra.shape[1]
    rows, width = first.shape
    vmem = pl.BlockSpec(memory_space=pltpu.VMEM)
    return pl.pallas_call(
        early_kernel,
        out_shape=(
            jax.ShapeDtypeStruct((depth, width), jnp.float32),
            jax.ShapeDtypeStruct((2 * rows, depth), jnp.bfloat16),
        ),
        in_specs=[
            pl.BlockSpec(memory_space=pltpu.SMEM),
            pl.BlockSpec(memory_space=pltpu.HBM),
            vmem,
            vmem,
        ],
        out_specs=(vmem, vmem),
        scratch_shapes=[
            pltpu.VMEM((2 * rows, depth), jnp.bfloat16),
            pltpu.SemaphoreType.DMA((4,)),
        ],
        compiler_params=memory(48),
        cost_estimate=pl.CostEstimate(
            flops=4 * rows * depth * width,
            bytes_accessed=8 * rows * depth + 4 * depth * width,
            transcendentals=0,
        ),
        name="early_product",
    )(chan.reshape(1), spectra, first, second)


def late_kernel(where, held, before, crossed, passed, across, skipped, *outs):
    *outs, total = outs
    chan, core = where[0], where[1]
    inner = (chan == 1) | (chan == 2)
    second = jnp.where(inner, crossed[...], passed[...])
    third = jnp.where(inner, across[...], skipped[...])
    rows = jnp.concatenate([second, third], axis=0)
    total[...] = before[...] + turned_product(held[...], rows)
    size = outs[0].shape[0]
    for index, out in enumerate(outs):
        first = (core ^ (1 - index // 2)) * 2 * size + index % 2 * size
        here = pl.ds(pl.multiple_of(first, size), size)
        out[...] = total[here, :].astype(out.dtype)


def late_product(where, held, before, crossed, passed, across, skipped):
    size, width = before.shape[0] // 4, before.shape[1]
    spec = pl.BlockSpec(memory_space=pltpu.VMEM)
    send = jax.ShapeDtypeStruct((size, width), jnp.bfloat16)
    keep = jax.ShapeDtypeStruct((size, width), jnp.float32)
    outs = pl.pallas_call(
        late_kernel,
        out_shape=(send, send, keep, keep),
        in_specs=[pl.BlockSpec(memory_space=pltpu.SMEM)] + [spec] * 6,
        out_specs=(spec,) * 4,
        scratch_shapes=[pltpu.VMEM(before.shape, jnp.float32)],
        compiler_params=memory(16),
        cost_estimate=pl.CostEstimate(
            flops=2 * held.shape[0] * held.shape[1] * width,
            bytes_accessed=2 * held.shape[0] * held.shape[1] + 16 * size * width,
            transcendentals=0,
        ),
        name="late_product",
    )(where, held, before, crossed, passed, across, skipped)
    return outs[:2], outs[2:]


def pixel_kernel(count, where, places, *refs):
    lists = refs[: (len(refs) - 16) // 3]
    names = refs[-len(lists) :]
    refs = refs[len(lists) : -len(lists)]
    cotangent, above, below, mixing, spectra, weight, keep = refs[:7]
    outs = refs[7 : 7 + len(lists)]
    table, scale, sums, held, near, block, factor, sems, more = refs[7 + len(lists) :]
    start, chan = where[0], where[1]
    tile_rows, half = held.shape[0], table.shape[1]
    chunk = tile_rows // 4
    copies = [pltpu.make_async_copy(places, near, sems.at[4])]
    copies += [
        pltpu.make_async_copy(wanted, name, sems.at[5 + n])
        for n, (wanted, name) in enumerate(zip(lists, names))
    ]
    parts = quarter_copies(spectra, weight, block, factor, more, chan, 0)
    rows = [
        pltpu.make_async_copy(
            cotangent.at[pl.ds(n * chunk, chunk)], held.at[pl.ds(n * chunk, chunk)], sems.at[n]
        )
        for n in range(4)
    ]
    for copy in copies + parts + rows:
        copy.start()
    project_rows(parts, block, factor, keep)

    def fill(first, values):
        values = values.astype(jnp.float32)
        for side in range(2):
            table[pl.ds(2 * first + side, values.shape[0], stride=2), :] = values[
                :, side * half : (side + 1) * half
            ]

    for side in range(2):
        scale[pl.ds(side, NEIGH, stride=2), :] = mixing[:, side * half : (side + 1) * half]
    scales = [scale[2 * k : 2 * k + 2, :] for k in range(NEIGH)]
    fill(0, above[...])
    fill(HALO + tile_rows, below[...])
    for n in range(4):
        rows[n].wait()
        for first in range(n * chunk, (n + 1) * chunk, 256):
            fill(HALO + first, held[first : first + 256, :])
    for copy in copies:
        copy.wait()

    group = 16
    for index, wanted in enumerate(names):

        def body(turn, carry, index=index, wanted=wanted):
            base = turn * group
            totals = []
            for n in range(group):
                pixel = wanted[start + base + n]
                terms = [table[pl.ds(2 * (pixel + HALO), 2), :]]
                for k in range(NEIGH // 2):
                    pair = near[k * tile_rows + pixel]
                    for place, scale in ((pair & 0xFFFF, k), (pair >> 16, k + NEIGH // 2)):
                        terms.append(table[pl.ds(place, 2), :] * scales[scale])
                while len(terms) > 1:
                    pairs = [x + y for x, y in zip(terms[::2], terms[1::2])]
                    terms = pairs + terms[len(terms) // 2 * 2 :]
                totals += terms
            for n, total in enumerate(totals):
                sums[pl.ds(2 * (index * count + base + n), 2), :] = total
            return carry

        lax.fori_loop(0, count // group, body, 0)
    for index, out in enumerate(outs):
        for side in range(2):
            out[:, side * half : (side + 1) * half] = sums[
                pl.ds(2 * index * count + side, count, stride=2), :
            ].astype(out.dtype)


def pixel_rows(
    cotangent, above, below, adjoint, mixing, anchor, lists, start, count, spectra, weight, chan
):
    tile_rows, width = cotangent.shape
    depth, rows = spectra.shape[1], spectra.shape[0] // 2
    places = (adjoint - anchor) * 2
    places = (places[: NEIGH // 2] | (places[NEIGH // 2 :] << 16)).reshape(-1)
    anywhere = pl.BlockSpec(memory_space=pl.ANY)
    hbm = pl.BlockSpec(memory_space=pltpu.HBM)
    vmem = pl.BlockSpec(memory_space=pltpu.VMEM)
    return pl.pallas_call(
        functools.partial(pixel_kernel, count),
        out_shape=(
            jax.ShapeDtypeStruct((rows, width), jnp.bfloat16),
            *[jax.ShapeDtypeStruct((count, width), jnp.bfloat16)] * len(lists),
        ),
        in_specs=[
            pl.BlockSpec(memory_space=pltpu.SMEM),
            anywhere,
            *[anywhere] * len(lists),
            hbm,
            *[vmem] * 3,
            hbm,
            hbm,
        ],
        out_specs=(vmem,) * (1 + len(lists)),
        scratch_shapes=[
            pltpu.VMEM((2 * (tile_rows + 2 * HALO), width // 2), jnp.float32),
            pltpu.VMEM((2 * NEIGH, width // 2), jnp.float32),
            pltpu.VMEM((2 * count * len(lists), width // 2), jnp.float32),
            pltpu.VMEM(cotangent.shape, cotangent.dtype),
            pltpu.SMEM(places.shape, jnp.int32),
            pltpu.VMEM((rows, depth), jnp.bfloat16),
            pltpu.VMEM((depth, width), jnp.bfloat16),
            pltpu.SemaphoreType.DMA((5 + len(lists),)),
            pltpu.SemaphoreType.DMA((5,)),
            *[pltpu.SMEM(names.shape, jnp.int32) for names in lists],
        ],
        compiler_params=memory(LARGE),
        cost_estimate=pl.CostEstimate(
            flops=6 * NEIGH * tile_rows * 256 * width,
            bytes_accessed=4 * tile_rows * width,
            transcendentals=0,
        ),
        name="pixel_rows",
    )(
        jnp.stack([start, chan]), places, *lists, cotangent, above, below, mixing, spectra, weight
    )


def gradient_kernel(where, keep, near, far, tiles, weights, mine, answers, out):
    tile, chan = where[0], where[1]
    rows = out.shape[0]
    size = tiles.shape[1]
    count = rows // size
    group = 8 // count
    wide = jnp.float32
    first = pl.multiple_of(chan // group * 8, 8)

    def columns(values):
        turned = values[pl.ds(first, 8), :].T
        places = [turned[:, n * count : (n + 1) * count] for n in range(group)]
        picked = places[0]
        for n in range(1, group):
            picked = jnp.where(chan % group == n, places[n], picked)
        return picked

    own = columns(tiles).astype(wide)
    factors = columns(weights)
    for n in range(count):
        here = slice(n * size, (n + 1) * size)
        pre = keep[here, :].astype(wide) + near[here, :].astype(wide) + far[here, :].astype(wide)
        sigma = jax.nn.sigmoid(pre)
        deriv = sigma * (1.0 + pre * (1.0 - sigma))
        fetched = jnp.where(
            own[:, n : n + 1] == tile.astype(wide),
            mine[here, :].astype(wide),
            answers[here, :].astype(wide),
        )
        out[here, :] = (factors[:, n : n + 1] * deriv * fetched).astype(out.dtype)


def pre_gradient(tile, chan, keep, near, far, tiles, weights, mine, answers):
    spec = pl.BlockSpec(memory_space=pltpu.VMEM)
    tiles, weights = tiles.reshape(-1, 128), weights.reshape(-1, 128)
    return pl.pallas_call(
        gradient_kernel,
        out_shape=jax.ShapeDtypeStruct(far.shape, jnp.bfloat16),
        in_specs=[pl.BlockSpec(memory_space=pltpu.SMEM)] + [spec] * 7,
        out_specs=spec,
        compiler_params=memory(16),
        name="pre_gradient",
    )(jnp.stack([tile, chan]), keep, near, far, tiles, weights, mine, answers)


def collect_kernel(core, *refs):
    *pieces, out = refs
    half, rows = out.shape[0] // 2, pieces[0].shape[0]
    count = len(pieces) // 2
    for index, piece in enumerate(pieces):
        which = core[0] if index < count else 1 - core[0]
        first = which * half + (index % count) * rows
        out[pl.ds(pl.multiple_of(first, rows), rows), :] = piece[...].astype(jnp.float32)


def collect(core, own, received):
    spec = pl.BlockSpec(memory_space=pltpu.VMEM)
    pieces = [*own, *received]
    rows, width = sum(piece.shape[0] for piece in pieces), own[0].shape[1]
    return pl.pallas_call(
        collect_kernel,
        out_shape=jax.ShapeDtypeStruct((rows, width), jnp.float32),
        in_specs=[pl.BlockSpec(memory_space=pltpu.SMEM)] + [spec] * len(pieces),
        out_specs=spec,
        compiler_params=memory(16),
        name="collect",
    )(core.reshape(1), *pieces)


def add_kernel(first, second, out):
    out[...] = (first[...].astype(jnp.float32) + second[...].astype(jnp.float32)).astype(out.dtype)


def added(first, second):
    spec = pl.BlockSpec(memory_space=pltpu.VMEM)
    return pl.pallas_call(
        add_kernel,
        out_shape=jax.ShapeDtypeStruct(first.shape, jnp.bfloat16),
        in_specs=[spec, spec],
        out_specs=spec,
        compiler_params=memory(16),
        name="added",
    )(first, second)


def sum_over_panels(core, parts, received):
    both = ("obs", "pix")
    parts = [added(part, other) for part, other in zip(parts, received)]
    for order in ((4, 1), (1, 4)):
        perm = [(i, i ^ order[(i >> 1) & 1]) for i in range(8)]
        parts = [added(part, lax.ppermute(part, both, perm)) for part in parts]
    return collect(core, parts, [swap(part, "obs", 1) for part in parts])


def shards(spectra, enc_weight, pix_tile, pix_local, foot_weight, cotangent, adjoint, mixing):
    tile_count = lax.axis_size("pix")
    tile_rows = cotangent.shape[0]
    quarter = spectra.shape[0] // lax.axis_size("chan")
    tile = lax.axis_index("pix")
    chan = lax.axis_index("chan")
    first_row = chan * quarter
    middle = [(1, 2), (2, 1)]

    send = project(spectra, enc_weight, chan)
    send, pix_local, edge_rows = lax.optimization_barrier((send, pix_local, cotangent))
    near = swap(send, "chan", 1)

    above, below = edges(edge_rows, "pix", HALO)
    anchor = tile * tile_rows - HALO
    capacity = 2 * quarter // tile_count
    pixels = (cotangent, above, below, adjoint, mixing, anchor)
    rest = (spectra, enc_weight, chan)
    if capacity >= quarter and tile_count == 2:
        lists = (pix_local, swap(pix_local, "pix", 1))
        keep, mine, theirs = pixel_rows(*pixels, lists, first_row, quarter, *rest)
        answers = swap(theirs, "pix", 1)
    else:
        tile_ids = lax.dynamic_slice_in_dim(pix_tile[:, 0], first_row, quarter, 0)
        local_ids = lax.dynamic_slice_in_dim(pix_local, first_row, quarter, 0)
        slot_index, wanted = requests(tile_ids, local_ids, capacity)
        keep, rows = pixel_rows(*pixels, (wanted,), 0 * chan, wanted.shape[0], *rest)
        answers = lax.all_to_all(
            rows.reshape(tile_count, capacity, -1), "pix", split_axis=0, concat_axis=0, tiled=True
        )
        mine = answers = jnp.take(answers.reshape(tile_count * capacity, -1), slot_index, axis=0)
    near, mine = lax.optimization_barrier((near, mine))
    passed_on = keep[quarter:].astype(jnp.float32) + near[quarter:].astype(jnp.float32)
    far = swap(passed_on.astype(jnp.bfloat16), "chan", 2)
    grads = pre_gradient(tile, chan, keep, near, far, pix_tile, foot_weight, mine, answers)

    beside = swap(grads, "chan", 1)
    across = lax.ppermute(grads, "chan", middle)
    passed = lax.ppermute(across, "chan", [(1, 0), (2, 3)])
    crossed = lax.ppermute(beside, "chan", middle)
    skipped = lax.ppermute(beside, "chan", [(2, 0), (1, 3)])
    core = lax.axis_index("obs") & 1
    early, held = early_product(spectra, chan, grads, beside)
    where = jnp.stack([chan, core])
    send, keep = late_product(where, held, early, crossed, passed, across, skipped)
    if lax.axis_size("obs") == 4 and tile_count == 2:
        return sum_over_panels(core, keep, [swap(part, "obs", 1) for part in send])
    return lax.psum(collect(core, keep, send), ("obs", "pix"))


def solution(mesh):
    return jax.shard_map(
        shards,
        mesh=mesh,
        in_specs=(
            P(("obs", "pix"), "chan"),
            P("chan", None),
            P(("obs", "pix"), None),
            P(("obs", "pix")),
            P(("obs", "pix")),
            P("pix", None),
            P(None, "pix"),
            P(),
        ),
        out_specs=P("chan", None),
        check_vma=False,
    )
```

```python
import functools

import jax
import jax.numpy as jnp
from jax import lax
from jax.experimental import pallas as pl
from jax.experimental.pallas import tpu as pltpu
from jax.sharding import PartitionSpec as P

NEIGH = 8
HALO = 128
MIB = 1024 * 1024
LARGE = 52
PIECES = 8


def edges(value, axis, width):
    size, length = lax.axis_size(axis), value.shape[0]
    last = lax.slice_in_dim(value, length - width, length, axis=0)
    first = lax.slice_in_dim(value, 0, width, axis=0)
    if size == 2:
        index = lax.axis_index(axis)
        other = lax.ppermute(jnp.where(index == 0, last, first), axis, [(0, 1), (1, 0)])
        return other, other
    up = [(i, i + 1) for i in range(size - 1)]
    return lax.ppermute(last, axis, up), lax.ppermute(first, axis, [(j, i) for i, j in up])


def requests(tile_ids, local_ids, capacity):
    tile_count = lax.axis_size("pix")
    onehot = (tile_ids[:, None] == jnp.arange(tile_count, dtype=jnp.int32)[None, :]).astype(
        jnp.int32
    )
    place_rank = jnp.sum((jnp.cumsum(onehot, axis=0) - 1) * onehot, axis=1)
    slot_index = tile_ids * capacity + place_rank
    outgoing = jnp.full((tile_count * capacity,), 0, jnp.int32).at[slot_index].set(local_ids)
    outgoing = outgoing.reshape(tile_count, capacity)
    requested = lax.all_to_all(outgoing, "pix", split_axis=0, concat_axis=0, tiled=True)
    return slot_index, requested.reshape(-1)


def swap(value, axis, bit):
    size = 1
    for name in (axis,) if isinstance(axis, str) else axis:
        size *= lax.axis_size(name)
    return lax.ppermute(value, axis, [(i, i ^ bit) for i in range(size)])


def memory(mib):
    return pltpu.CompilerParams(vmem_limit_bytes=mib * MIB)


def quarter_copies(spectra, weight, held, near, sems, chan, bits):
    chunk = held.shape[0] // len(bits) // 2
    copies = [pltpu.make_async_copy(weight, near, sems.at[2 * len(bits)])]
    for turn in range(2 * len(bits)):
        first = ((chan ^ bits[turn // 2]) * 2 + turn % 2) * chunk
        copies.append(
            pltpu.make_async_copy(
                spectra.at[pl.ds(pl.multiple_of(first, chunk), chunk)],
                held.at[pl.ds(turn * chunk, chunk)],
                sems.at[turn],
            )
        )
    return copies


def project_rows(copies, held, near, outs):
    chunk = outs[0].shape[0] // 2
    copies[0].wait()
    for turn in range(2 * len(outs)):
        copies[turn + 1].wait()
        rows = held[turn * chunk : (turn + 1) * chunk, :]
        result = jnp.dot(rows, near[...], preferred_element_type=jnp.float32)
        first = turn % 2 * chunk
        outs[turn // 2][first : first + chunk, :] = result.astype(outs[0].dtype)


def project_kernel(chan, spectra, weight, out, held, near, sems):
    copies = quarter_copies(spectra, weight, held, near, sems, chan[0], (3,))
    for copy in copies:
        copy.start()
    project_rows(copies, held, near, (out,))


def project(spectra, weight, chan):
    depth, width = weight.shape
    rows = spectra.shape[0] // 4
    hbm = pl.BlockSpec(memory_space=pltpu.HBM)
    return pl.pallas_call(
        project_kernel,
        out_shape=jax.ShapeDtypeStruct((rows, width), jnp.bfloat16),
        in_specs=[pl.BlockSpec(memory_space=pltpu.SMEM), hbm, hbm],
        out_specs=pl.BlockSpec(memory_space=pltpu.VMEM),
        scratch_shapes=[
            pltpu.VMEM((rows, depth), jnp.bfloat16),
            pltpu.VMEM((depth, width), jnp.bfloat16),
            pltpu.SemaphoreType.DMA((3,)),
        ],
        compiler_params=memory(LARGE),
        cost_estimate=pl.CostEstimate(
            flops=2 * rows * depth * width,
            bytes_accessed=2 * rows * depth + 2 * depth * width + 2 * rows * width,
            transcendentals=0,
        ),
        name="project",
    )(chan.reshape(1), spectra, weight)


def turned_product(left, right):
    return lax.dot_general(
        left, right, (((0,), (0,)), ((), ())), preferred_element_type=jnp.float32
    )


def early_kernel(chan, spectra, first, second, total, late, held, sems):
    rows = first.shape[0]
    copies = []
    for turn in range(4):
        start = pl.multiple_of((chan[0] ^ turn) * rows, rows)
        target = (held, late)[turn // 2].at[pl.ds(turn % 2 * rows, rows)]
        copies.append(pltpu.make_async_copy(spectra.at[pl.ds(start, rows)], target, sems.at[turn]))
    for copy in copies:
        copy.start()
    copies[0].wait()
    product = turned_product(held[:rows, :], first[...])
    copies[1].wait()
    total[...] = product + turned_product(held[rows:, :], second[...])
    copies[2].wait()
    copies[3].wait()


def early_product(spectra, chan, first, second):
    depth = spectra.shape[1]
    rows, width = first.shape
    vmem = pl.BlockSpec(memory_space=pltpu.VMEM)
    return pl.pallas_call(
        early_kernel,
        out_shape=(
            jax.ShapeDtypeStruct((depth, width), jnp.float32),
            jax.ShapeDtypeStruct((2 * rows, depth), jnp.bfloat16),
        ),
        in_specs=[
            pl.BlockSpec(memory_space=pltpu.SMEM),
            pl.BlockSpec(memory_space=pltpu.HBM),
            vmem,
            vmem,
        ],
        out_specs=(vmem, vmem),
        scratch_shapes=[
            pltpu.VMEM((2 * rows, depth), jnp.bfloat16),
            pltpu.SemaphoreType.DMA((4,)),
        ],
        compiler_params=memory(48),
        cost_estimate=pl.CostEstimate(
            flops=4 * rows * depth * width,
            bytes_accessed=8 * rows * depth + 4 * depth * width,
            transcendentals=0,
        ),
        name="early_product",
    )(chan.reshape(1), spectra, first, second)


def late_kernel(where, held, before, crossed, passed, across, skipped, *outs):
    *outs, total = outs
    chan, core = where[0], where[1]
    inner = (chan == 1) | (chan == 2)
    second = jnp.where(inner, crossed[...], passed[...])
    third = jnp.where(inner, across[...], skipped[...])
    rows = jnp.concatenate([second, third], axis=0)
    total[...] = before[...] + turned_product(held[...], rows)
    size = outs[0].shape[0]
    for index, out in enumerate(outs):
        first = (core ^ (1 - index // 2)) * 2 * size + index % 2 * size
        here = pl.ds(pl.multiple_of(first, size), size)
        out[...] = total[here, :].astype(out.dtype)


def late_product(where, held, before, crossed, passed, across, skipped):
    size, width = before.shape[0] // 4, before.shape[1]
    spec = pl.BlockSpec(memory_space=pltpu.VMEM)
    send = jax.ShapeDtypeStruct((size, width), jnp.bfloat16)
    keep = jax.ShapeDtypeStruct((size, width), jnp.float32)
    outs = pl.pallas_call(
        late_kernel,
        out_shape=(send, send, keep, keep),
        in_specs=[pl.BlockSpec(memory_space=pltpu.SMEM)] + [spec] * 6,
        out_specs=(spec,) * 4,
        scratch_shapes=[pltpu.VMEM(before.shape, jnp.float32)],
        compiler_params=memory(16),
        cost_estimate=pl.CostEstimate(
            flops=2 * held.shape[0] * held.shape[1] * width,
            bytes_accessed=2 * held.shape[0] * held.shape[1] + 16 * size * width,
            transcendentals=0,
        ),
        name="late_product",
    )(where, held, before, crossed, passed, across, skipped)
    return outs[:2], outs[2:]


def pixel_kernel(count, where, places, *refs):
    lists = refs[: (len(refs) - 18) // 3]
    names = refs[-len(lists) :]
    refs = refs[len(lists) : -len(lists)]
    cotangent, above, below, mixing, spectra, weight = refs[:6]
    quarters, outs = refs[6:9], refs[9 : 9 + len(lists)]
    table, scale, sums, held, near, block, factor, sems, more = refs[9 + len(lists) :]
    start, chan = where[0], where[1]
    tile_rows, half = held.shape[0], table.shape[1]
    chunk = tile_rows // 4
    piece = near.shape[0] // PIECES
    copies = [
        pltpu.make_async_copy(
            places.at[pl.ds(n * piece, piece)], near.at[pl.ds(n * piece, piece)], sems.at[4 + n]
        )
        for n in range(PIECES)
    ]
    copies += [
        pltpu.make_async_copy(wanted, name, sems.at[4 + PIECES + n])
        for n, (wanted, name) in enumerate(zip(lists, names))
    ]
    parts = quarter_copies(spectra, weight, block, factor, more, chan, (2, 1, 0))
    rows = [
        pltpu.make_async_copy(
            cotangent.at[pl.ds(n * chunk, chunk)], held.at[pl.ds(n * chunk, chunk)], sems.at[n]
        )
        for n in range(4)
    ]
    for copy in copies + parts + rows:
        copy.start()
    project_rows(parts, block, factor, quarters)

    def fill(first, values):
        values = values.astype(jnp.float32)
        for side in range(2):
            table[pl.ds(2 * first + side, values.shape[0], stride=2), :] = values[
                :, side * half : (side + 1) * half
            ]

    for side in range(2):
        scale[pl.ds(side, NEIGH, stride=2), :] = mixing[:, side * half : (side + 1) * half]
    scales = [scale[2 * k : 2 * k + 2, :] for k in range(NEIGH)]
    fill(0, above[...])
    fill(HALO + tile_rows, below[...])
    for n in range(4):
        rows[n].wait()
        for first in range(n * chunk, (n + 1) * chunk, 256):
            fill(HALO + first, held[first : first + 256, :])
    for copy in copies:
        copy.wait()

    group = 16
    for index, wanted in enumerate(names):

        def body(turn, carry, index=index, wanted=wanted):
            base = turn * group
            totals = []
            for n in range(group):
                pixel = wanted[start + base + n]
                terms = [table[pl.ds(2 * (pixel + HALO), 2), :]]
                for k in range(NEIGH // 2):
                    pair = near[k * tile_rows + pixel]
                    for place, scale in ((pair & 0xFFFF, k), (pair >> 16, k + NEIGH // 2)):
                        terms.append(table[pl.ds(place, 2), :] * scales[scale])
                while len(terms) > 1:
                    pairs = [x + y for x, y in zip(terms[::2], terms[1::2])]
                    terms = pairs + terms[len(terms) // 2 * 2 :]
                totals += terms
            for n, total in enumerate(totals):
                sums[pl.ds(2 * (index * count + base + n), 2), :] = total
            return carry

        lax.fori_loop(0, count // group, body, 0)
    for index, out in enumerate(outs):
        for side in range(2):
            out[:, side * half : (side + 1) * half] = sums[
                pl.ds(2 * index * count + side, count, stride=2), :
            ].astype(out.dtype)


def pixel_rows(
    cotangent, above, below, places, mixing, lists, start, count, spectra, weight, chan
):
    tile_rows, width = cotangent.shape
    depth, rows = spectra.shape[1], spectra.shape[0] // 4
    anywhere = pl.BlockSpec(memory_space=pl.ANY)
    hbm = pl.BlockSpec(memory_space=pltpu.HBM)
    vmem = pl.BlockSpec(memory_space=pltpu.VMEM)
    return pl.pallas_call(
        functools.partial(pixel_kernel, count),
        out_shape=(
            *[jax.ShapeDtypeStruct((rows, width), jnp.bfloat16)] * 3,
            *[jax.ShapeDtypeStruct((count, width), jnp.bfloat16)] * len(lists),
        ),
        in_specs=[
            pl.BlockSpec(memory_space=pltpu.SMEM),
            anywhere,
            *[anywhere] * len(lists),
            hbm,
            *[vmem] * 3,
            hbm,
            hbm,
        ],
        out_specs=(vmem,) * (3 + len(lists)),
        scratch_shapes=[
            pltpu.VMEM((2 * (tile_rows + 2 * HALO), width // 2), jnp.float32),
            pltpu.VMEM((2 * NEIGH, width // 2), jnp.float32),
            pltpu.VMEM((2 * count * len(lists), width // 2), jnp.float32),
            pltpu.VMEM(cotangent.shape, cotangent.dtype),
            pltpu.SMEM(places.shape, jnp.int32),
            pltpu.VMEM((3 * rows, depth), jnp.bfloat16),
            pltpu.VMEM((depth, width), jnp.bfloat16),
            pltpu.SemaphoreType.DMA((4 + PIECES + len(lists),)),
            pltpu.SemaphoreType.DMA((7,)),
            *[pltpu.SMEM(names.shape, jnp.int32) for names in lists],
        ],
        compiler_params=memory(LARGE),
        cost_estimate=pl.CostEstimate(
            flops=6 * NEIGH * tile_rows * 256 * width,
            bytes_accessed=4 * tile_rows * width,
            transcendentals=0,
        ),
        name="pixel_rows",
    )(
        jnp.stack([start, chan]), places, *lists, cotangent, above, below, mixing, spectra, weight
    )


def gradient_kernel(where, keep, near, far, tiles, weights, mine, answers, out):
    tile, chan = where[0], where[1]
    rows = out.shape[0]
    size = tiles.shape[1]
    count = rows // size
    group = 8 // count
    wide = jnp.float32
    first = pl.multiple_of(chan // group * 8, 8)

    def columns(values):
        turned = values[pl.ds(first, 8), :].T
        places = [turned[:, n * count : (n + 1) * count] for n in range(group)]
        picked = places[0]
        for n in range(1, group):
            picked = jnp.where(chan % group == n, places[n], picked)
        return picked

    own = columns(tiles).astype(wide)
    factors = columns(weights)
    for n in range(count):
        here = slice(n * size, (n + 1) * size)
        pre = keep[here, :].astype(wide) + near[here, :].astype(wide) + far[here, :].astype(wide)
        sigma = jax.nn.sigmoid(pre)
        deriv = sigma * (1.0 + pre * (1.0 - sigma))
        fetched = jnp.where(
            own[:, n : n + 1] == tile.astype(wide),
            mine[here, :].astype(wide),
            answers[here, :].astype(wide),
        )
        out[here, :] = (factors[:, n : n + 1] * deriv * fetched).astype(out.dtype)


def pre_gradient(tile, chan, keep, near, far, tiles, weights, mine, answers):
    spec = pl.BlockSpec(memory_space=pltpu.VMEM)
    tiles, weights = tiles.reshape(-1, 128), weights.reshape(-1, 128)
    return pl.pallas_call(
        gradient_kernel,
        out_shape=jax.ShapeDtypeStruct(far.shape, jnp.bfloat16),
        in_specs=[pl.BlockSpec(memory_space=pltpu.SMEM)] + [spec] * 7,
        out_specs=spec,
        compiler_params=memory(16),
        name="pre_gradient",
    )(jnp.stack([tile, chan]), keep, near, far, tiles, weights, mine, answers)


def collect_kernel(core, *refs):
    *pieces, out = refs
    half, rows = out.shape[0] // 2, pieces[0].shape[0]
    count = len(pieces) // 2
    for index, piece in enumerate(pieces):
        which = core[0] if index < count else 1 - core[0]
        first = which * half + (index % count) * rows
        out[pl.ds(pl.multiple_of(first, rows), rows), :] = piece[...].astype(jnp.float32)


def collect(core, own, received):
    spec = pl.BlockSpec(memory_space=pltpu.VMEM)
    pieces = [*own, *received]
    rows, width = sum(piece.shape[0] for piece in pieces), own[0].shape[1]
    return pl.pallas_call(
        collect_kernel,
        out_shape=jax.ShapeDtypeStruct((rows, width), jnp.float32),
        in_specs=[pl.BlockSpec(memory_space=pltpu.SMEM)] + [spec] * len(pieces),
        out_specs=spec,
        compiler_params=memory(16),
        name="collect",
    )(core.reshape(1), *pieces)


def add_kernel(first, second, out):
    out[...] = (first[...].astype(jnp.float32) + second[...].astype(jnp.float32)).astype(out.dtype)


def added(first, second):
    spec = pl.BlockSpec(memory_space=pltpu.VMEM)
    return pl.pallas_call(
        add_kernel,
        out_shape=jax.ShapeDtypeStruct(first.shape, jnp.bfloat16),
        in_specs=[spec, spec],
        out_specs=spec,
        compiler_params=memory(16),
        name="added",
    )(first, second)


def sum_over_panels(core, parts, received):
    both = ("obs", "pix")
    parts = [added(part, other) for part, other in zip(parts, received)]
    for order in ((4, 1), (1, 4)):
        perm = [(i, i ^ order[(i >> 1) & 1]) for i in range(8)]
        parts = [added(part, lax.ppermute(part, both, perm)) for part in parts]
    return collect(core, parts, [swap(part, "obs", 1) for part in parts])


def shards(spectra, enc_weight, pix_tile, pix_local, foot_weight, cotangent, adjoint, mixing):
    tile_count = lax.axis_size("pix")
    tile_rows = cotangent.shape[0]
    quarter = spectra.shape[0] // lax.axis_size("chan")
    tile = lax.axis_index("pix")
    chan = lax.axis_index("chan")
    first_row = chan * quarter
    middle = [(1, 2), (2, 1)]

    near_first = swap(project(spectra, enc_weight, chan), "chan", 1)
    places = (adjoint - (tile * tile_rows - HALO)) * 2
    places = (places[: NEIGH // 2] | (places[NEIGH // 2 :] << 16)).reshape(-1)

    above, below = edges(cotangent, "pix", HALO)
    capacity = 2 * quarter // tile_count
    pixels = (cotangent, above, below, places, mixing)
    rest = (spectra, enc_weight, chan)
    if capacity >= quarter and tile_count == 2:
        lists = (pix_local, swap(pix_local, "pix", 1))
        shared, send, keep, mine, rows = pixel_rows(*pixels, lists, first_row, quarter, *rest)
    else:
        tile_ids = lax.dynamic_slice_in_dim(pix_tile[:, 0], first_row, quarter, 0)
        local_ids = lax.dynamic_slice_in_dim(pix_local, first_row, quarter, 0)
        slot_index, wanted = requests(tile_ids, local_ids, capacity)
        shared, send, keep, rows = pixel_rows(*pixels, (wanted,), 0 * chan, wanted.shape[0], *rest)
    near_first, rows = lax.optimization_barrier((near_first, rows))
    passed_on = (shared.astype(jnp.float32) + near_first.astype(jnp.float32)).astype(jnp.bfloat16)
    passed_on, rows, send = lax.optimization_barrier((passed_on, rows, send))
    far = swap(passed_on, "chan", 2)
    near = swap(send, "chan", 1)
    if capacity >= quarter and tile_count == 2:
        answers = swap(rows, "pix", 1)
    else:
        answers = lax.all_to_all(
            rows.reshape(tile_count, capacity, -1), "pix", split_axis=0, concat_axis=0, tiled=True
        )
        mine = answers = jnp.take(answers.reshape(tile_count * capacity, -1), slot_index, axis=0)
    grads = pre_gradient(tile, chan, keep, near, far, pix_tile, foot_weight, mine, answers)

    beside = swap(grads, "chan", 1)
    across = lax.ppermute(grads, "chan", middle)
    passed = lax.ppermute(across, "chan", [(1, 0), (2, 3)])
    crossed = lax.ppermute(beside, "chan", middle)
    skipped = lax.ppermute(beside, "chan", [(2, 0), (1, 3)])
    core = lax.axis_index("obs") & 1
    early, held = early_product(spectra, chan, grads, beside)
    where = jnp.stack([chan, core])
    send, keep = late_product(where, held, early, crossed, passed, across, skipped)
    if lax.axis_size("obs") == 4 and tile_count == 2:
        return sum_over_panels(core, keep, [swap(part, "obs", 1) for part in send])
    return lax.psum(collect(core, keep, send), ("obs", "pix"))


def solution(mesh):
    return jax.shard_map(
        shards,
        mesh=mesh,
        in_specs=(
            P(("obs", "pix"), "chan"),
            P("chan", None),
            P(("obs", "pix"), None),
            P(("obs", "pix")),
            P(("obs", "pix")),
            P("pix", None),
            P(None, "pix"),
            P(),
        ),
        out_specs=P("chan", None),
        check_vma=False,
    )
```

```python
import functools

import jax
import jax.numpy as jnp
from jax import lax
from jax.experimental import pallas as pl
from jax.experimental.pallas import tpu as pltpu
from jax.sharding import PartitionSpec as P

NEIGH = 8
HALO = 128
MIB = 1024 * 1024
LARGE = 52


def edges(value, axis, width):
    size, length = lax.axis_size(axis), value.shape[0]
    last = lax.slice_in_dim(value, length - width, length, axis=0)
    first = lax.slice_in_dim(value, 0, width, axis=0)
    if size == 2:
        index = lax.axis_index(axis)
        other = lax.ppermute(jnp.where(index == 0, last, first), axis, [(0, 1), (1, 0)])
        return other, other
    up = [(i, i + 1) for i in range(size - 1)]
    return lax.ppermute(last, axis, up), lax.ppermute(first, axis, [(j, i) for i, j in up])


def requests(tile_ids, local_ids, capacity):
    tile_count = lax.axis_size("pix")
    onehot = (tile_ids[:, None] == jnp.arange(tile_count, dtype=jnp.int32)[None, :]).astype(
        jnp.int32
    )
    place_rank = jnp.sum((jnp.cumsum(onehot, axis=0) - 1) * onehot, axis=1)
    slot_index = tile_ids * capacity + place_rank
    outgoing = jnp.full((tile_count * capacity,), 0, jnp.int32).at[slot_index].set(local_ids)
    outgoing = outgoing.reshape(tile_count, capacity)
    requested = lax.all_to_all(outgoing, "pix", split_axis=0, concat_axis=0, tiled=True)
    return slot_index, requested.reshape(-1)


def swap(value, axis, bit):
    size = 1
    for name in (axis,) if isinstance(axis, str) else axis:
        size *= lax.axis_size(name)
    return lax.ppermute(value, axis, [(i, i ^ bit) for i in range(size)])


def memory(mib):
    return pltpu.CompilerParams(vmem_limit_bytes=mib * MIB)


def quarter_copies(spectra, weight, held, near, sems, chan, bits):
    chunk = held.shape[0] // len(bits) // 2
    copies = [pltpu.make_async_copy(weight, near, sems.at[2 * len(bits)])]
    for turn in range(2 * len(bits)):
        first = ((chan ^ bits[turn // 2]) * 2 + turn % 2) * chunk
        copies.append(
            pltpu.make_async_copy(
                spectra.at[pl.ds(pl.multiple_of(first, chunk), chunk)],
                held.at[pl.ds(turn * chunk, chunk)],
                sems.at[turn],
            )
        )
    return copies


def project_rows(copies, held, near, outs):
    chunk = outs[0].shape[0] // 2
    copies[0].wait()
    for turn in range(2 * len(outs)):
        copies[turn + 1].wait()
        rows = held[turn * chunk : (turn + 1) * chunk, :]
        result = jnp.dot(rows, near[...], preferred_element_type=jnp.float32)
        first = turn % 2 * chunk
        outs[turn // 2][first : first + chunk, :] = result.astype(outs[0].dtype)


def project_kernel(bits, chan, spectra, weight, *refs):
    *outs, held, near, sems = refs
    copies = quarter_copies(spectra, weight, held, near, sems, chan[0], bits)
    for copy in copies:
        copy.start()
    project_rows(copies, held, near, outs)


def project(spectra, weight, chan, bits):
    depth, width = weight.shape
    rows = spectra.shape[0] // 4
    hbm = pl.BlockSpec(memory_space=pltpu.HBM)
    return pl.pallas_call(
        functools.partial(project_kernel, bits),
        out_shape=(jax.ShapeDtypeStruct((rows, width), jnp.bfloat16),) * len(bits),
        in_specs=[pl.BlockSpec(memory_space=pltpu.SMEM), hbm, hbm],
        out_specs=(pl.BlockSpec(memory_space=pltpu.VMEM),) * len(bits),
        scratch_shapes=[
            pltpu.VMEM((len(bits) * rows, depth), jnp.bfloat16),
            pltpu.VMEM((depth, width), jnp.bfloat16),
            pltpu.SemaphoreType.DMA((2 * len(bits) + 1,)),
        ],
        compiler_params=memory(LARGE),
        cost_estimate=pl.CostEstimate(
            flops=2 * len(bits) * rows * depth * width,
            bytes_accessed=2 * len(bits) * rows * (depth + width) + 2 * depth * width,
            transcendentals=0,
        ),
        name="project",
    )(chan.reshape(1), spectra, weight)


def turned_product(left, right):
    return lax.dot_general(
        left, right, (((0,), (0,)), ((), ())), preferred_element_type=jnp.float32
    )


def early_kernel(chan, spectra, first, second, total, late, held, sems):
    rows = first.shape[0]
    copies = []
    for turn in range(4):
        start = pl.multiple_of((chan[0] ^ turn) * rows, rows)
        target = (held, late)[turn // 2].at[pl.ds(turn % 2 * rows, rows)]
        copies.append(pltpu.make_async_copy(spectra.at[pl.ds(start, rows)], target, sems.at[turn]))
    for copy in copies:
        copy.start()
    copies[0].wait()
    product = turned_product(held[:rows, :], first[...])
    copies[1].wait()
    total[...] = product + turned_product(held[rows:, :], second[...])
    copies[2].wait()
    copies[3].wait()


def early_product(spectra, chan, first, second):
    depth = spectra.shape[1]
    rows, width = first.shape
    vmem = pl.BlockSpec(memory_space=pltpu.VMEM)
    return pl.pallas_call(
        early_kernel,
        out_shape=(
            jax.ShapeDtypeStruct((depth, width), jnp.float32),
            jax.ShapeDtypeStruct((2 * rows, depth), jnp.bfloat16),
        ),
        in_specs=[
            pl.BlockSpec(memory_space=pltpu.SMEM),
            pl.BlockSpec(memory_space=pltpu.HBM),
            vmem,
            vmem,
        ],
        out_specs=(vmem, vmem),
        scratch_shapes=[
            pltpu.VMEM((2 * rows, depth), jnp.bfloat16),
            pltpu.SemaphoreType.DMA((4,)),
        ],
        compiler_params=memory(48),
        cost_estimate=pl.CostEstimate(
            flops=4 * rows * depth * width,
            bytes_accessed=8 * rows * depth + 4 * depth * width,
            transcendentals=0,
        ),
        name="early_product",
    )(chan.reshape(1), spectra, first, second)


def late_kernel(where, held, before, crossed, passed, across, skipped, *outs):
    *outs, total = outs
    chan, core = where[0], where[1]
    inner = (chan == 1) | (chan == 2)
    second = jnp.where(inner, crossed[...], passed[...])
    third = jnp.where(inner, across[...], skipped[...])
    rows = jnp.concatenate([second, third], axis=0)
    total[...] = before[...] + turned_product(held[...], rows)
    size = outs[0].shape[0]
    for index, out in enumerate(outs):
        first = (core ^ (1 - index // 2)) * 2 * size + index % 2 * size
        here = pl.ds(pl.multiple_of(first, size), size)
        out[...] = total[here, :].astype(out.dtype)


def late_product(where, held, before, crossed, passed, across, skipped):
    size, width = before.shape[0] // 4, before.shape[1]
    spec = pl.BlockSpec(memory_space=pltpu.VMEM)
    send = jax.ShapeDtypeStruct((size, width), jnp.bfloat16)
    keep = jax.ShapeDtypeStruct((size, width), jnp.float32)
    outs = pl.pallas_call(
        late_kernel,
        out_shape=(send, send, keep, keep),
        in_specs=[pl.BlockSpec(memory_space=pltpu.SMEM)] + [spec] * 6,
        out_specs=(spec,) * 4,
        scratch_shapes=[pltpu.VMEM(before.shape, jnp.float32)],
        compiler_params=memory(16),
        cost_estimate=pl.CostEstimate(
            flops=2 * held.shape[0] * held.shape[1] * width,
            bytes_accessed=2 * held.shape[0] * held.shape[1] + 16 * size * width,
            transcendentals=0,
        ),
        name="late_product",
    )(where, held, before, crossed, passed, across, skipped)
    return outs[:2], outs[2:]


def pixel_kernel(count, bits, where, places, wanted, cotangent, above, below, mixing, spectra,
                 weight, out, *refs):
    quarters, refs = refs[: len(bits)], refs[len(bits) :]
    table, scale, sums, held, near, names, block, factor, sems, more = refs
    start, chan = where[0], where[1]
    tile_rows, half = held.shape[0], table.shape[1]
    listed = names.shape[0]
    first_name = pl.multiple_of(start // listed * listed, listed)
    copies = [
        pltpu.make_async_copy(places, near, sems.at[4]),
        pltpu.make_async_copy(wanted.at[pl.ds(first_name, listed)], names, sems.at[5]),
    ]
    chunk = tile_rows // 4
    rows = [
        pltpu.make_async_copy(
            cotangent.at[pl.ds(n * chunk, chunk)], held.at[pl.ds(n * chunk, chunk)], sems.at[n]
        )
        for n in range(4)
    ]
    parts = quarter_copies(spectra, weight, block, factor, more, chan, bits) if bits else []
    for copy in copies + rows + parts:
        copy.start()

    def fill(first, values):
        values = values.astype(jnp.float32)
        for side in range(2):
            table[pl.ds(2 * first + side, values.shape[0], stride=2), :] = values[
                :, side * half : (side + 1) * half
            ]

    for side in range(2):
        scale[pl.ds(side, NEIGH, stride=2), :] = mixing[:, side * half : (side + 1) * half]
    scales = [scale[2 * k : 2 * k + 2, :] for k in range(NEIGH)]
    fill(0, above[...])
    fill(HALO + tile_rows, below[...])
    for n in range(4):
        rows[n].wait()
        for first in range(n * chunk, (n + 1) * chunk, 256):
            fill(HALO + first, held[first : first + 256, :])
    if bits:
        project_rows(parts, block, factor, quarters)
    for copy in copies:
        copy.wait()

    group = 32
    offset = start - first_name

    def body(turn, carry):
        base = turn * group
        totals = []
        for n in range(group):
            pixel = names[offset + base + n]
            terms = [table[pl.ds(2 * (pixel + HALO), 2), :]]
            for k in range(NEIGH // 2):
                pair = near[k * tile_rows + pixel]
                for place, scale in ((pair & 0xFFFF, k), (pair >> 16, k + NEIGH // 2)):
                    terms.append(table[pl.ds(place, 2), :] * scales[scale])
            while len(terms) > 1:
                pairs = [x + y for x, y in zip(terms[::2], terms[1::2])]
                terms = pairs + terms[len(terms) // 2 * 2 :]
            totals += terms
        for n, total in enumerate(totals):
            sums[pl.ds(2 * (base + n), 2), :] = total
        return carry

    lax.fori_loop(0, count // group, body, 0)
    for side in range(2):
        out[:, side * half : (side + 1) * half] = sums[pl.ds(side, count, stride=2), :].astype(
            out.dtype
        )


def pixel_rows(
    cotangent, above, below, places, mixing, wanted, start, count, spectra, weight, chan, bits
):
    tile_rows, width = cotangent.shape
    depth, rows = spectra.shape[1], spectra.shape[0] // 4
    listed = min(wanted.shape[0], 1024)
    anywhere = pl.BlockSpec(memory_space=pl.ANY)
    hbm = pl.BlockSpec(memory_space=pltpu.HBM)
    vmem = pl.BlockSpec(memory_space=pltpu.VMEM)
    return pl.pallas_call(
        functools.partial(pixel_kernel, count, bits),
        out_shape=(
            jax.ShapeDtypeStruct((count, width), jnp.bfloat16),
            *[jax.ShapeDtypeStruct((rows, width), jnp.bfloat16)] * len(bits),
        ),
        in_specs=[
            pl.BlockSpec(memory_space=pltpu.SMEM),
            anywhere,
            anywhere,
            hbm,
            *[vmem] * 3,
            hbm,
            hbm,
        ],
        out_specs=(vmem,) * (1 + len(bits)),
        scratch_shapes=[
            pltpu.VMEM((2 * (tile_rows + 2 * HALO), width // 2), jnp.float32),
            pltpu.VMEM((2 * NEIGH, width // 2), jnp.float32),
            pltpu.VMEM((2 * count, width // 2), jnp.float32),
            pltpu.VMEM(cotangent.shape, cotangent.dtype),
            pltpu.SMEM(places.shape, jnp.int32),
            pltpu.SMEM((listed,), jnp.int32),
            pltpu.VMEM((max(len(bits), 1) * rows, depth), jnp.bfloat16),
            pltpu.VMEM((depth, width), jnp.bfloat16),
            pltpu.SemaphoreType.DMA((6,)),
            pltpu.SemaphoreType.DMA((2 * len(bits) + 1,)),
        ],
        compiler_params=memory(LARGE),
        cost_estimate=pl.CostEstimate(
            flops=8 * NEIGH * count * 2048 * width,
            bytes_accessed=4 * tile_rows * width,
            transcendentals=0,
        ),
        name="pixel_rows",
    )(
        jnp.stack([start, chan]), places, wanted, cotangent, above, below, mixing, spectra, weight
    )


def gradient_kernel(where, keep, near, far, tiles, weights, mine, answers, out):
    tile, chan = where[0], where[1]
    rows = out.shape[0]
    size = tiles.shape[1]
    count = rows // size
    group = 8 // count
    wide = jnp.float32
    first = pl.multiple_of(chan // group * 8, 8)

    def columns(values):
        turned = values[pl.ds(first, 8), :].T
        places = [turned[:, n * count : (n + 1) * count] for n in range(group)]
        picked = places[0]
        for n in range(1, group):
            picked = jnp.where(chan % group == n, places[n], picked)
        return picked

    own = columns(tiles).astype(wide)
    factors = columns(weights)
    for n in range(count):
        here = slice(n * size, (n + 1) * size)
        pre = keep[here, :].astype(wide) + near[here, :].astype(wide) + far[here, :].astype(wide)
        sigma = jax.nn.sigmoid(pre)
        deriv = sigma * (1.0 + pre * (1.0 - sigma))
        fetched = jnp.where(
            own[:, n : n + 1] == tile.astype(wide),
            mine[here, :].astype(wide),
            answers[here, :].astype(wide),
        )
        out[here, :] = (factors[:, n : n + 1] * deriv * fetched).astype(out.dtype)


def pre_gradient(tile, chan, keep, near, far, tiles, weights, mine, answers):
    spec = pl.BlockSpec(memory_space=pltpu.VMEM)
    tiles, weights = tiles.reshape(-1, 128), weights.reshape(-1, 128)
    return pl.pallas_call(
        gradient_kernel,
        out_shape=jax.ShapeDtypeStruct(far.shape, jnp.bfloat16),
        in_specs=[pl.BlockSpec(memory_space=pltpu.SMEM)] + [spec] * 7,
        out_specs=spec,
        compiler_params=memory(16),
        name="pre_gradient",
    )(jnp.stack([tile, chan]), keep, near, far, tiles, weights, mine, answers)


def collect_kernel(core, *refs):
    *pieces, out = refs
    half, rows = out.shape[0] // 2, pieces[0].shape[0]
    count = len(pieces) // 2
    for index, piece in enumerate(pieces):
        which = core[0] if index < count else 1 - core[0]
        first = which * half + (index % count) * rows
        out[pl.ds(pl.multiple_of(first, rows), rows), :] = piece[...].astype(jnp.float32)


def collect(core, own, received):
    spec = pl.BlockSpec(memory_space=pltpu.VMEM)
    pieces = [*own, *received]
    rows, width = sum(piece.shape[0] for piece in pieces), own[0].shape[1]
    return pl.pallas_call(
        collect_kernel,
        out_shape=jax.ShapeDtypeStruct((rows, width), jnp.float32),
        in_specs=[pl.BlockSpec(memory_space=pltpu.SMEM)] + [spec] * len(pieces),
        out_specs=spec,
        compiler_params=memory(16),
        name="collect",
    )(core.reshape(1), *pieces)


def add_kernel(first, second, out):
    out[...] = (first[...].astype(jnp.float32) + second[...].astype(jnp.float32)).astype(out.dtype)


def added(first, second):
    spec = pl.BlockSpec(memory_space=pltpu.VMEM)
    return pl.pallas_call(
        add_kernel,
        out_shape=jax.ShapeDtypeStruct(first.shape, jnp.bfloat16),
        in_specs=[spec, spec],
        out_specs=spec,
        compiler_params=memory(16),
        name="added",
    )(first, second)


def sum_over_panels(core, parts, received):
    both = ("obs", "pix")
    parts = [added(part, other) for part, other in zip(parts, received)]
    for order in ((4, 1), (1, 4)):
        perm = [(i, i ^ order[(i >> 1) & 1]) for i in range(8)]
        parts = [added(part, lax.ppermute(part, both, perm)) for part in parts]
    return collect(core, parts, [swap(part, "obs", 1) for part in parts])


def shards(spectra, enc_weight, pix_tile, pix_local, foot_weight, cotangent, adjoint, mixing):
    tile_count = lax.axis_size("pix")
    tile_rows = cotangent.shape[0]
    quarter = spectra.shape[0] // lax.axis_size("chan")
    tile = lax.axis_index("pix")
    chan = lax.axis_index("chan")
    first_row = chan * quarter
    middle = [(1, 2), (2, 1)]

    near_first = swap(project(spectra, enc_weight, chan, (3,))[0], "chan", 1)
    places = (adjoint - (tile * tile_rows - HALO)) * 2
    places = (places[: NEIGH // 2] | (places[NEIGH // 2 :] << 16)).reshape(-1)

    above, below = edges(cotangent, "pix", HALO)
    capacity = 2 * quarter // tile_count
    pixels = (cotangent, above, below, places, mixing)
    rest = (spectra, enc_weight)
    paired = capacity >= quarter and tile_count == 2
    if paired:
        wanted, start, count = swap(pix_local, "pix", 1), first_row, quarter
    else:
        tile_ids = lax.dynamic_slice_in_dim(pix_tile[:, 0], first_row, quarter, 0)
        local_ids = lax.dynamic_slice_in_dim(pix_local, first_row, quarter, 0)
        slot_index, wanted = requests(tile_ids, local_ids, capacity)
        start, count = 0 * chan, wanted.shape[0]
    rows, shared = pixel_rows(*pixels, wanted, start, count, *rest, chan, (2,))
    near_first, rows = lax.optimization_barrier((near_first, rows))
    passed_on = (shared.astype(jnp.float32) + near_first.astype(jnp.float32)).astype(jnp.bfloat16)
    passed_on, rows, later = lax.optimization_barrier((passed_on, rows, chan))
    far = swap(passed_on, "chan", 2)
    send, keep = project(*rest, later, (1, 0))
    send, keep, later = lax.optimization_barrier((send, keep, later))
    near = swap(send, "chan", 1)
    if paired:
        answers = swap(rows, "pix", 1)
        (mine,) = pixel_rows(*pixels, pix_local, later * quarter, count, *rest, later, ())
    else:
        answers = lax.all_to_all(
            rows.reshape(tile_count, capacity, -1), "pix", split_axis=0, concat_axis=0, tiled=True
        )
        mine = answers = jnp.take(answers.reshape(tile_count * capacity, -1), slot_index, axis=0)
    grads = pre_gradient(tile, chan, keep, near, far, pix_tile, foot_weight, mine, answers)

    beside = swap(grads, "chan", 1)
    across = lax.ppermute(grads, "chan", middle)
    passed = lax.ppermute(across, "chan", [(1, 0), (2, 3)])
    crossed = lax.ppermute(beside, "chan", middle)
    skipped = lax.ppermute(beside, "chan", [(2, 0), (1, 3)])
    core = lax.axis_index("obs") & 1
    early, held = early_product(spectra, chan, grads, beside)
    where = jnp.stack([chan, core])
    send, keep = late_product(where, held, early, crossed, passed, across, skipped)
    if lax.axis_size("obs") == 4 and tile_count == 2:
        return sum_over_panels(core, keep, [swap(part, "obs", 1) for part in send])
    return lax.psum(collect(core, keep, send), ("obs", "pix"))


def solution(mesh):
    return jax.shard_map(
        shards,
        mesh=mesh,
        in_specs=(
            P(("obs", "pix"), "chan"),
            P("chan", None),
            P(("obs", "pix"), None),
            P(("obs", "pix")),
            P(("obs", "pix")),
            P("pix", None),
            P(None, "pix"),
            P(),
        ),
        out_specs=P("chan", None),
        check_vma=False,
    )
```

```python
import functools

import jax
import jax.numpy as jnp
from jax import lax
from jax.experimental import pallas as pl
from jax.experimental.pallas import tpu as pltpu
from jax.sharding import PartitionSpec as P

NEIGH = 8
HALO = 128
MIB = 1024 * 1024
LARGE = 52


def edges(value, axis, width):
    size, length = lax.axis_size(axis), value.shape[0]
    last = lax.slice_in_dim(value, length - width, length, axis=0)
    first = lax.slice_in_dim(value, 0, width, axis=0)
    if size == 2:
        index = lax.axis_index(axis)
        other = lax.ppermute(jnp.where(index == 0, last, first), axis, [(0, 1), (1, 0)])
        return other, other
    up = [(i, i + 1) for i in range(size - 1)]
    return lax.ppermute(last, axis, up), lax.ppermute(first, axis, [(j, i) for i, j in up])


def requests(tile_ids, local_ids, capacity):
    tile_count = lax.axis_size("pix")
    onehot = (tile_ids[:, None] == jnp.arange(tile_count, dtype=jnp.int32)[None, :]).astype(
        jnp.int32
    )
    place_rank = jnp.sum((jnp.cumsum(onehot, axis=0) - 1) * onehot, axis=1)
    slot_index = tile_ids * capacity + place_rank
    outgoing = jnp.full((tile_count * capacity,), 0, jnp.int32).at[slot_index].set(local_ids)
    outgoing = outgoing.reshape(tile_count, capacity)
    requested = lax.all_to_all(outgoing, "pix", split_axis=0, concat_axis=0, tiled=True)
    return slot_index, requested.reshape(-1)


def swap(value, axis, bit):
    size = 1
    for name in (axis,) if isinstance(axis, str) else axis:
        size *= lax.axis_size(name)
    return lax.ppermute(value, axis, [(i, i ^ bit) for i in range(size)])


def memory(mib):
    return pltpu.CompilerParams(vmem_limit_bytes=mib * MIB)


def quarter_copies(spectra, weight, held, near, sems, chan, bits):
    chunk = held.shape[0] // len(bits) // 2
    copies = [pltpu.make_async_copy(weight, near, sems.at[2 * len(bits)])]
    for turn in range(2 * len(bits)):
        first = ((chan ^ bits[turn // 2]) * 2 + turn % 2) * chunk
        copies.append(
            pltpu.make_async_copy(
                spectra.at[pl.ds(pl.multiple_of(first, chunk), chunk)],
                held.at[pl.ds(turn * chunk, chunk)],
                sems.at[turn],
            )
        )
    return copies


def project_rows(copies, held, near, outs):
    chunk = outs[0].shape[0] // 2
    copies[0].wait()
    for turn in range(2 * len(outs)):
        copies[turn + 1].wait()
        rows = held[turn * chunk : (turn + 1) * chunk, :]
        result = jnp.dot(rows, near[...], preferred_element_type=jnp.float32)
        first = turn % 2 * chunk
        outs[turn // 2][first : first + chunk, :] = result.astype(outs[0].dtype)


def project_kernel(bits, chan, spectra, weight, *refs):
    *outs, held, near, sems = refs
    copies = quarter_copies(spectra, weight, held, near, sems, chan[0], bits)
    for copy in copies:
        copy.start()
    project_rows(copies, held, near, outs)


def project(spectra, weight, chan, bits):
    depth, width = weight.shape
    rows = spectra.shape[0] // 4
    hbm = pl.BlockSpec(memory_space=pltpu.HBM)
    return pl.pallas_call(
        functools.partial(project_kernel, bits),
        out_shape=(jax.ShapeDtypeStruct((rows, width), jnp.bfloat16),) * len(bits),
        in_specs=[pl.BlockSpec(memory_space=pltpu.SMEM), hbm, hbm],
        out_specs=(pl.BlockSpec(memory_space=pltpu.VMEM),) * len(bits),
        scratch_shapes=[
            pltpu.VMEM((len(bits) * rows, depth), jnp.bfloat16),
            pltpu.VMEM((depth, width), jnp.bfloat16),
            pltpu.SemaphoreType.DMA((2 * len(bits) + 1,)),
        ],
        compiler_params=memory(LARGE),
        cost_estimate=pl.CostEstimate(
            flops=2 * len(bits) * rows * depth * width,
            bytes_accessed=2 * len(bits) * rows * (depth + width) + 2 * depth * width,
            transcendentals=0,
        ),
        name="project",
    )(chan.reshape(1), spectra, weight)


def turned_product(left, right):
    return lax.dot_general(
        left, right, (((0,), (0,)), ((), ())), preferred_element_type=jnp.float32
    )


def early_kernel(chan, spectra, first, second, third, total, late, held, sems):
    rows = first.shape[0]
    copies = []
    for turn, bits in enumerate((0, 1, 3, 2)):
        start = pl.multiple_of((chan[0] ^ bits) * rows, rows)
        target = held.at[pl.ds(turn * rows, rows)] if turn < 3 else late
        copies.append(pltpu.make_async_copy(spectra.at[pl.ds(start, rows)], target, sems.at[turn]))
    for copy in copies:
        copy.start()
    copies[0].wait()
    product = turned_product(held[:rows, :], first[...])
    copies[1].wait()
    product += turned_product(held[rows : 2 * rows, :], second[...])
    copies[2].wait()
    total[...] = product + turned_product(held[2 * rows :, :], third[...])
    copies[3].wait()


def early_product(spectra, chan, first, second, third):
    depth = spectra.shape[1]
    rows, width = first.shape
    vmem = pl.BlockSpec(memory_space=pltpu.VMEM)
    return pl.pallas_call(
        early_kernel,
        out_shape=(
            jax.ShapeDtypeStruct((depth, width), jnp.float32),
            jax.ShapeDtypeStruct((rows, depth), jnp.bfloat16),
        ),
        in_specs=[
            pl.BlockSpec(memory_space=pltpu.SMEM),
            pl.BlockSpec(memory_space=pltpu.HBM),
            *[vmem] * 3,
        ],
        out_specs=(vmem, vmem),
        scratch_shapes=[
            pltpu.VMEM((3 * rows, depth), jnp.bfloat16),
            pltpu.SemaphoreType.DMA((4,)),
        ],
        compiler_params=memory(48),
        cost_estimate=pl.CostEstimate(
            flops=6 * rows * depth * width,
            bytes_accessed=8 * rows * depth + 4 * depth * width,
            transcendentals=0,
        ),
        name="early_product",
    )(chan.reshape(1), spectra, first, second, third)


def late_kernel(core, held, before, rows, *outs):
    *outs, total = outs
    total[...] = before[...] + turned_product(held[...], rows[...])
    size = outs[0].shape[0]
    for index, out in enumerate(outs):
        first = (core[0] ^ (1 - index // 2)) * 2 * size + index % 2 * size
        here = pl.ds(pl.multiple_of(first, size), size)
        out[...] = total[here, :].astype(out.dtype)


def late_product(core, held, before, rows):
    size, width = before.shape[0] // 4, before.shape[1]
    spec = pl.BlockSpec(memory_space=pltpu.VMEM)
    send = jax.ShapeDtypeStruct((size, width), jnp.bfloat16)
    keep = jax.ShapeDtypeStruct((size, width), jnp.float32)
    outs = pl.pallas_call(
        late_kernel,
        out_shape=(send, send, keep, keep),
        in_specs=[pl.BlockSpec(memory_space=pltpu.SMEM)] + [spec] * 3,
        out_specs=(spec,) * 4,
        scratch_shapes=[pltpu.VMEM(before.shape, jnp.float32)],
        compiler_params=memory(16),
        cost_estimate=pl.CostEstimate(
            flops=2 * held.shape[0] * held.shape[1] * width,
            bytes_accessed=2 * held.shape[0] * held.shape[1] + 16 * size * width,
            transcendentals=0,
        ),
        name="late_product",
    )(core.reshape(1), held, before, rows)
    return outs[:2], outs[2:]


def pixel_kernel(count, bits, where, places, wanted, cotangent, above, below, mixing, spectra,
                 weight, out, *refs):
    quarters, refs = refs[: len(bits)], refs[len(bits) :]
    table, scale, sums, held, near, names, block, factor, sems, more = refs
    start, chan = where[0], where[1]
    tile_rows, half = held.shape[0], table.shape[1]
    listed = names.shape[0]
    first_name = pl.multiple_of(start // listed * listed, listed)
    copies = [
        pltpu.make_async_copy(places, near, sems.at[4]),
        pltpu.make_async_copy(wanted.at[pl.ds(first_name, listed)], names, sems.at[5]),
    ]
    chunk = tile_rows // 4
    rows = [
        pltpu.make_async_copy(
            cotangent.at[pl.ds(n * chunk, chunk)], held.at[pl.ds(n * chunk, chunk)], sems.at[n]
        )
        for n in range(4)
    ]
    parts = quarter_copies(spectra, weight, block, factor, more, chan, bits) if bits else []
    for copy in copies + rows + parts:
        copy.start()

    def fill(first, values):
        values = values.astype(jnp.float32)
        for side in range(2):
            table[pl.ds(2 * first + side, values.shape[0], stride=2), :] = values[
                :, side * half : (side + 1) * half
            ]

    for side in range(2):
        scale[pl.ds(side, NEIGH, stride=2), :] = mixing[:, side * half : (side + 1) * half]
    scales = [scale[2 * k : 2 * k + 2, :] for k in range(NEIGH)]
    fill(0, above[...])
    fill(HALO + tile_rows, below[...])
    for n in range(4):
        rows[n].wait()
        for first in range(n * chunk, (n + 1) * chunk, 256):
            fill(HALO + first, held[first : first + 256, :])
    if bits:
        project_rows(parts, block, factor, quarters)
    for copy in copies:
        copy.wait()

    group = 32
    offset = start - first_name

    def body(turn, carry):
        base = turn * group
        totals = []
        for n in range(group):
            pixel = names[offset + base + n]
            terms = [table[pl.ds(2 * (pixel + HALO), 2), :]]
            for k in range(NEIGH // 2):
                pair = near[k * tile_rows + pixel]
                for place, scale in ((pair & 0xFFFF, k), (pair >> 16, k + NEIGH // 2)):
                    terms.append(table[pl.ds(place, 2), :] * scales[scale])
            while len(terms) > 1:
                pairs = [x + y for x, y in zip(terms[::2], terms[1::2])]
                terms = pairs + terms[len(terms) // 2 * 2 :]
            totals += terms
        for n, total in enumerate(totals):
            sums[pl.ds(2 * (base + n), 2), :] = total
        return carry

    lax.fori_loop(0, count // group, body, 0)
    for side in range(2):
        out[:, side * half : (side + 1) * half] = sums[pl.ds(side, count, stride=2), :].astype(
            out.dtype
        )


def pixel_rows(
    cotangent, above, below, places, mixing, wanted, start, count, spectra, weight, chan, bits
):
    tile_rows, width = cotangent.shape
    depth, rows = spectra.shape[1], spectra.shape[0] // 4
    listed = min(wanted.shape[0], 1024)
    anywhere = pl.BlockSpec(memory_space=pl.ANY)
    hbm = pl.BlockSpec(memory_space=pltpu.HBM)
    vmem = pl.BlockSpec(memory_space=pltpu.VMEM)
    return pl.pallas_call(
        functools.partial(pixel_kernel, count, bits),
        out_shape=(
            jax.ShapeDtypeStruct((count, width), jnp.bfloat16),
            *[jax.ShapeDtypeStruct((rows, width), jnp.bfloat16)] * len(bits),
        ),
        in_specs=[
            pl.BlockSpec(memory_space=pltpu.SMEM),
            anywhere,
            anywhere,
            hbm,
            *[vmem] * 3,
            hbm,
            hbm,
        ],
        out_specs=(vmem,) * (1 + len(bits)),
        scratch_shapes=[
            pltpu.VMEM((2 * (tile_rows + 2 * HALO), width // 2), jnp.float32),
            pltpu.VMEM((2 * NEIGH, width // 2), jnp.float32),
            pltpu.VMEM((2 * count, width // 2), jnp.float32),
            pltpu.VMEM(cotangent.shape, cotangent.dtype),
            pltpu.SMEM(places.shape, jnp.int32),
            pltpu.SMEM((listed,), jnp.int32),
            pltpu.VMEM((max(len(bits), 1) * rows, depth), jnp.bfloat16),
            pltpu.VMEM((depth, width), jnp.bfloat16),
            pltpu.SemaphoreType.DMA((6,)),
            pltpu.SemaphoreType.DMA((2 * len(bits) + 1,)),
        ],
        compiler_params=memory(LARGE),
        cost_estimate=pl.CostEstimate(
            flops=8 * NEIGH * count * 2048 * width,
            bytes_accessed=4 * tile_rows * width,
            transcendentals=0,
        ),
        name="pixel_rows",
    )(
        jnp.stack([start, chan]), places, wanted, cotangent, above, below, mixing, spectra, weight
    )


def gradient_kernel(where, keep, near, far, tiles, weights, mine, answers, out):
    tile, chan = where[0], where[1]
    rows = out.shape[0]
    size = tiles.shape[1]
    count = rows // size
    group = 8 // count
    wide = jnp.float32
    first = pl.multiple_of(chan // group * 8, 8)

    def columns(values):
        turned = values[pl.ds(first, 8), :].T
        places = [turned[:, n * count : (n + 1) * count] for n in range(group)]
        picked = places[0]
        for n in range(1, group):
            picked = jnp.where(chan % group == n, places[n], picked)
        return picked

    own = columns(tiles).astype(wide)
    factors = columns(weights)
    for n in range(count):
        here = slice(n * size, (n + 1) * size)
        pre = keep[here, :].astype(wide) + near[here, :].astype(wide) + far[here, :].astype(wide)
        sigma = jax.nn.sigmoid(pre)
        deriv = sigma * (1.0 + pre * (1.0 - sigma))
        fetched = jnp.where(
            own[:, n : n + 1] == tile.astype(wide),
            mine[here, :].astype(wide),
            answers[here, :].astype(wide),
        )
        out[here, :] = (factors[:, n : n + 1] * deriv * fetched).astype(out.dtype)


def pre_gradient(tile, chan, keep, near, far, tiles, weights, mine, answers):
    spec = pl.BlockSpec(memory_space=pltpu.VMEM)
    tiles, weights = tiles.reshape(-1, 128), weights.reshape(-1, 128)
    return pl.pallas_call(
        gradient_kernel,
        out_shape=jax.ShapeDtypeStruct(far.shape, jnp.bfloat16),
        in_specs=[pl.BlockSpec(memory_space=pltpu.SMEM)] + [spec] * 7,
        out_specs=spec,
        compiler_params=memory(16),
        name="pre_gradient",
    )(jnp.stack([tile, chan]), keep, near, far, tiles, weights, mine, answers)


def collect_kernel(core, *refs):
    *pieces, out = refs
    half, rows = out.shape[0] // 2, pieces[0].shape[0]
    count = len(pieces) // 2
    for index, piece in enumerate(pieces):
        which = core[0] if index < count else 1 - core[0]
        first = which * half + (index % count) * rows
        out[pl.ds(pl.multiple_of(first, rows), rows), :] = piece[...].astype(jnp.float32)


def collect(core, own, received):
    spec = pl.BlockSpec(memory_space=pltpu.VMEM)
    pieces = [*own, *received]
    rows, width = sum(piece.shape[0] for piece in pieces), own[0].shape[1]
    return pl.pallas_call(
        collect_kernel,
        out_shape=jax.ShapeDtypeStruct((rows, width), jnp.float32),
        in_specs=[pl.BlockSpec(memory_space=pltpu.SMEM)] + [spec] * len(pieces),
        out_specs=spec,
        compiler_params=memory(16),
        name="collect",
    )(core.reshape(1), *pieces)


def add_kernel(first, second, out):
    out[...] = (first[...].astype(jnp.float32) + second[...].astype(jnp.float32)).astype(out.dtype)


def added(first, second):
    spec = pl.BlockSpec(memory_space=pltpu.VMEM)
    return pl.pallas_call(
        add_kernel,
        out_shape=jax.ShapeDtypeStruct(first.shape, jnp.bfloat16),
        in_specs=[spec, spec],
        out_specs=spec,
        compiler_params=memory(16),
        name="added",
    )(first, second)


def sum_over_panels(core, parts, received):
    both = ("obs", "pix")
    parts = [added(part, other) for part, other in zip(parts, received)]
    for order in ((4, 1), (1, 4)):
        perm = [(i, i ^ order[(i >> 1) & 1]) for i in range(8)]
        parts = [added(part, lax.ppermute(part, both, perm)) for part in parts]
    return collect(core, parts, [swap(part, "obs", 1) for part in parts])


def shards(spectra, enc_weight, pix_tile, pix_local, foot_weight, cotangent, adjoint, mixing):
    tile_count = lax.axis_size("pix")
    tile_rows = cotangent.shape[0]
    quarter = spectra.shape[0] // lax.axis_size("chan")
    tile = lax.axis_index("pix")
    chan = lax.axis_index("chan")
    first_row = chan * quarter

    near_first = swap(project(spectra, enc_weight, chan, (3,))[0], "chan", 1)
    places = (adjoint - (tile * tile_rows - HALO)) * 2
    places = (places[: NEIGH // 2] | (places[NEIGH // 2 :] << 16)).reshape(-1)

    above, below = edges(cotangent, "pix", HALO)
    capacity = 2 * quarter // tile_count
    pixels = (cotangent, above, below, places, mixing)
    rest = (spectra, enc_weight)
    paired = capacity >= quarter and tile_count == 2
    if paired:
        wanted, start, count = swap(pix_local, "pix", 1), first_row, quarter
    else:
        tile_ids = lax.dynamic_slice_in_dim(pix_tile[:, 0], first_row, quarter, 0)
        local_ids = lax.dynamic_slice_in_dim(pix_local, first_row, quarter, 0)
        slot_index, wanted = requests(tile_ids, local_ids, capacity)
        start, count = 0 * chan, wanted.shape[0]
    rows, shared, send = pixel_rows(*pixels, wanted, start, count, *rest, chan, (2, 1))
    near_first, rows = lax.optimization_barrier((near_first, rows))
    passed_on = (shared.astype(jnp.float32) + near_first.astype(jnp.float32)).astype(jnp.bfloat16)
    passed_on, send, rows, later = lax.optimization_barrier((passed_on, send, rows, chan))
    far = swap(passed_on, "chan", 2)
    near = swap(send, "chan", 1)
    (keep,) = project(*rest, later, (0,))
    if paired:
        answers = swap(rows, "pix", 1)
        (mine,) = pixel_rows(*pixels, pix_local, later * quarter, count, *rest, later, ())
    else:
        answers = lax.all_to_all(
            rows.reshape(tile_count, capacity, -1), "pix", split_axis=0, concat_axis=0, tiled=True
        )
        mine = answers = jnp.take(answers.reshape(tile_count * capacity, -1), slot_index, axis=0)
    grads = pre_gradient(tile, chan, keep, near, far, pix_tile, foot_weight, mine, answers)

    across = swap(grads, "chan", 3)
    beside = swap(grads, "chan", 1)
    last = swap(across, "chan", 1)
    early, held = early_product(spectra, chan, grads, beside, across)
    core = lax.axis_index("obs") & 1
    send, keep = late_product(core, held, early, last)
    if lax.axis_size("obs") == 4 and tile_count == 2:
        return sum_over_panels(core, keep, [swap(part, "obs", 1) for part in send])
    return lax.psum(collect(core, keep, send), ("obs", "pix"))


def solution(mesh):
    return jax.shard_map(
        shards,
        mesh=mesh,
        in_specs=(
            P(("obs", "pix"), "chan"),
            P("chan", None),
            P(("obs", "pix"), None),
            P(("obs", "pix")),
            P(("obs", "pix")),
            P("pix", None),
            P(None, "pix"),
            P(),
        ),
        out_specs=P("chan", None),
        check_vma=False,
    )
```

```python
import functools

import jax
import jax.numpy as jnp
from jax import lax
from jax.experimental import pallas as pl
from jax.experimental.pallas import tpu as pltpu
from jax.sharding import PartitionSpec as P

NEIGH = 8
HALO = 128
MIB = 1024 * 1024
LARGE = 52


def edges(value, axis, width):
    size, length = lax.axis_size(axis), value.shape[0]
    last = lax.slice_in_dim(value, length - width, length, axis=0)
    first = lax.slice_in_dim(value, 0, width, axis=0)
    if size == 2:
        index = lax.axis_index(axis)
        other = lax.ppermute(jnp.where(index == 0, last, first), axis, [(0, 1), (1, 0)])
        return other, other
    up = [(i, i + 1) for i in range(size - 1)]
    return lax.ppermute(last, axis, up), lax.ppermute(first, axis, [(j, i) for i, j in up])


def requests(tile_ids, local_ids, capacity):
    tile_count = lax.axis_size("pix")
    onehot = (tile_ids[:, None] == jnp.arange(tile_count, dtype=jnp.int32)[None, :]).astype(
        jnp.int32
    )
    place_rank = jnp.sum((jnp.cumsum(onehot, axis=0) - 1) * onehot, axis=1)
    slot_index = tile_ids * capacity + place_rank
    outgoing = jnp.full((tile_count * capacity,), 0, jnp.int32).at[slot_index].set(local_ids)
    outgoing = outgoing.reshape(tile_count, capacity)
    requested = lax.all_to_all(outgoing, "pix", split_axis=0, concat_axis=0, tiled=True)
    return slot_index, requested.reshape(-1)


def swap(value, axis, bit):
    size = 1
    for name in (axis,) if isinstance(axis, str) else axis:
        size *= lax.axis_size(name)
    return lax.ppermute(value, axis, [(i, i ^ bit) for i in range(size)])


def memory(mib):
    return pltpu.CompilerParams(vmem_limit_bytes=mib * MIB)


def quarter_copies(spectra, weight, held, near, sems, chan, bits):
    chunk = held.shape[0] // len(bits) // 2
    copies = [pltpu.make_async_copy(weight, near, sems.at[2 * len(bits)])]
    for turn in range(2 * len(bits)):
        first = ((chan ^ bits[turn // 2]) * 2 + turn % 2) * chunk
        copies.append(
            pltpu.make_async_copy(
                spectra.at[pl.ds(pl.multiple_of(first, chunk), chunk)],
                held.at[pl.ds(turn * chunk, chunk)],
                sems.at[turn],
            )
        )
    return copies


def project_rows(copies, held, near, outs):
    chunk = outs[0].shape[0] // 2
    copies[0].wait()
    for turn in range(2 * len(outs)):
        copies[turn + 1].wait()
        rows = held[turn * chunk : (turn + 1) * chunk, :]
        result = jnp.dot(rows, near[...], preferred_element_type=jnp.float32)
        first = turn % 2 * chunk
        outs[turn // 2][first : first + chunk, :] = result.astype(outs[0].dtype)


def project_kernel(bits, chan, spectra, weight, *refs):
    *outs, held, near, sems = refs
    copies = quarter_copies(spectra, weight, held, near, sems, chan[0], bits)
    for copy in copies:
        copy.start()
    project_rows(copies, held, near, outs)


def project(spectra, weight, chan, bits, grant):
    depth, width = weight.shape
    rows = spectra.shape[0] // 4
    hbm = pl.BlockSpec(memory_space=pltpu.HBM)
    return pl.pallas_call(
        functools.partial(project_kernel, bits),
        out_shape=(jax.ShapeDtypeStruct((rows, width), jnp.bfloat16),) * len(bits),
        in_specs=[pl.BlockSpec(memory_space=pltpu.SMEM), hbm, hbm],
        out_specs=(pl.BlockSpec(memory_space=pltpu.VMEM),) * len(bits),
        scratch_shapes=[
            pltpu.VMEM((len(bits) * rows, depth), jnp.bfloat16),
            pltpu.VMEM((depth, width), jnp.bfloat16),
            pltpu.SemaphoreType.DMA((2 * len(bits) + 1,)),
        ],
        compiler_params=memory(grant),
        cost_estimate=pl.CostEstimate(
            flops=2 * len(bits) * rows * depth * width,
            bytes_accessed=2 * len(bits) * rows * (depth + width) + 2 * depth * width,
            transcendentals=0,
        ),
        name="project",
    )(chan.reshape(1), spectra, weight)


def turned_product(left, right):
    return lax.dot_general(
        left, right, (((0,), (0,)), ((), ())), preferred_element_type=jnp.float32
    )


def early_kernel(chan, spectra, first, second, third, total, late, held, sems):
    rows = first.shape[0]
    copies = []
    for turn, bits in enumerate((0, 1, 3, 2)):
        start = pl.multiple_of((chan[0] ^ bits) * rows, rows)
        target = held.at[pl.ds(turn * rows, rows)] if turn < 3 else late
        copies.append(pltpu.make_async_copy(spectra.at[pl.ds(start, rows)], target, sems.at[turn]))
    for copy in copies:
        copy.start()
    copies[0].wait()
    product = turned_product(held[:rows, :], first[...])
    copies[1].wait()
    product += turned_product(held[rows : 2 * rows, :], second[...])
    copies[2].wait()
    total[...] = product + turned_product(held[2 * rows :, :], third[...])
    copies[3].wait()


def early_product(spectra, chan, first, second, third):
    depth = spectra.shape[1]
    rows, width = first.shape
    vmem = pl.BlockSpec(memory_space=pltpu.VMEM)
    return pl.pallas_call(
        early_kernel,
        out_shape=(
            jax.ShapeDtypeStruct((depth, width), jnp.float32),
            jax.ShapeDtypeStruct((rows, depth), jnp.bfloat16),
        ),
        in_specs=[
            pl.BlockSpec(memory_space=pltpu.SMEM),
            pl.BlockSpec(memory_space=pltpu.HBM),
            *[vmem] * 3,
        ],
        out_specs=(vmem, vmem),
        scratch_shapes=[
            pltpu.VMEM((3 * rows, depth), jnp.bfloat16),
            pltpu.SemaphoreType.DMA((4,)),
        ],
        compiler_params=memory(48),
        cost_estimate=pl.CostEstimate(
            flops=6 * rows * depth * width,
            bytes_accessed=8 * rows * depth + 4 * depth * width,
            transcendentals=0,
        ),
        name="early_product",
    )(chan.reshape(1), spectra, first, second, third)


def late_kernel(core, held, before, rows, *outs):
    *outs, total = outs
    total[...] = before[...] + turned_product(held[...], rows[...])
    size = outs[0].shape[0]
    for index, out in enumerate(outs):
        first = (core[0] ^ (1 - index // 2)) * 2 * size + index % 2 * size
        here = pl.ds(pl.multiple_of(first, size), size)
        out[...] = total[here, :].astype(out.dtype)


def late_product(core, held, before, rows):
    size, width = before.shape[0] // 4, before.shape[1]
    spec = pl.BlockSpec(memory_space=pltpu.VMEM)
    send = jax.ShapeDtypeStruct((size, width), jnp.bfloat16)
    keep = jax.ShapeDtypeStruct((size, width), jnp.float32)
    outs = pl.pallas_call(
        late_kernel,
        out_shape=(send, send, keep, keep),
        in_specs=[pl.BlockSpec(memory_space=pltpu.SMEM)] + [spec] * 3,
        out_specs=(spec,) * 4,
        scratch_shapes=[pltpu.VMEM(before.shape, jnp.float32)],
        compiler_params=memory(16),
        cost_estimate=pl.CostEstimate(
            flops=2 * held.shape[0] * held.shape[1] * width,
            bytes_accessed=2 * held.shape[0] * held.shape[1] + 16 * size * width,
            transcendentals=0,
        ),
        name="late_product",
    )(core.reshape(1), held, before, rows)
    return outs[:2], outs[2:]


def pixel_kernel(count, bits, where, places, wanted, cotangent, above, below, mixing, spectra,
                 weight, out, *refs):
    quarters, refs = refs[: len(bits)], refs[len(bits) :]
    table, scale, sums, held, near, names, block, factor, sems, more = refs
    start, chan = where[0], where[1]
    tile_rows, half = held.shape[0], table.shape[1]
    listed = names.shape[0]
    first_name = pl.multiple_of(start // listed * listed, listed)
    copies = [
        pltpu.make_async_copy(places, near, sems.at[4]),
        pltpu.make_async_copy(wanted.at[pl.ds(first_name, listed)], names, sems.at[5]),
    ]
    chunk = tile_rows // 4
    rows = [
        pltpu.make_async_copy(
            cotangent.at[pl.ds(n * chunk, chunk)], held.at[pl.ds(n * chunk, chunk)], sems.at[n]
        )
        for n in range(4)
    ]
    parts = quarter_copies(spectra, weight, block, factor, more, chan, bits) if bits else []
    for copy in copies + rows + parts:
        copy.start()

    def fill(first, values):
        values = values.astype(jnp.float32)
        for side in range(2):
            table[pl.ds(2 * first + side, values.shape[0], stride=2), :] = values[
                :, side * half : (side + 1) * half
            ]

    for side in range(2):
        scale[pl.ds(side, NEIGH, stride=2), :] = mixing[:, side * half : (side + 1) * half]
    scales = [scale[2 * k : 2 * k + 2, :] for k in range(NEIGH)]
    fill(0, above[...])
    fill(HALO + tile_rows, below[...])
    for n in range(4):
        rows[n].wait()
        for first in range(n * chunk, (n + 1) * chunk, 256):
            fill(HALO + first, held[first : first + 256, :])
    if bits:
        project_rows(parts, block, factor, quarters)
    for copy in copies:
        copy.wait()

    group = 32
    offset = start - first_name

    def body(turn, carry):
        base = turn * group
        totals = []
        for n in range(group):
            pixel = names[offset + base + n]
            terms = [table[pl.ds(2 * (pixel + HALO), 2), :]]
            for k in range(NEIGH // 2):
                pair = near[k * tile_rows + pixel]
                for place, scale in ((pair & 0xFFFF, k), (pair >> 16, k + NEIGH // 2)):
                    terms.append(table[pl.ds(place, 2), :] * scales[scale])
            while len(terms) > 1:
                pairs = [x + y for x, y in zip(terms[::2], terms[1::2])]
                terms = pairs + terms[len(terms) // 2 * 2 :]
            totals += terms
        for n, total in enumerate(totals):
            sums[pl.ds(2 * (base + n), 2), :] = total
        return carry

    lax.fori_loop(0, count // group, body, 0)
    for side in range(2):
        out[:, side * half : (side + 1) * half] = sums[pl.ds(side, count, stride=2), :].astype(
            out.dtype
        )


def pixel_rows(
    cotangent, above, below, places, mixing, wanted, start, count, spectra, weight, chan, bits
):
    tile_rows, width = cotangent.shape
    depth, rows = spectra.shape[1], spectra.shape[0] // 4
    listed = min(wanted.shape[0], 1024)
    anywhere = pl.BlockSpec(memory_space=pl.ANY)
    hbm = pl.BlockSpec(memory_space=pltpu.HBM)
    vmem = pl.BlockSpec(memory_space=pltpu.VMEM)
    return pl.pallas_call(
        functools.partial(pixel_kernel, count, bits),
        out_shape=(
            jax.ShapeDtypeStruct((count, width), jnp.bfloat16),
            *[jax.ShapeDtypeStruct((rows, width), jnp.bfloat16)] * len(bits),
        ),
        in_specs=[
            pl.BlockSpec(memory_space=pltpu.SMEM),
            anywhere,
            anywhere,
            hbm,
            *[vmem] * 3,
            hbm,
            hbm,
        ],
        out_specs=(vmem,) * (1 + len(bits)),
        scratch_shapes=[
            pltpu.VMEM((2 * (tile_rows + 2 * HALO), width // 2), jnp.float32),
            pltpu.VMEM((2 * NEIGH, width // 2), jnp.float32),
            pltpu.VMEM((2 * count, width // 2), jnp.float32),
            pltpu.VMEM(cotangent.shape, cotangent.dtype),
            pltpu.SMEM(places.shape, jnp.int32),
            pltpu.SMEM((listed,), jnp.int32),
            pltpu.VMEM((max(len(bits), 1) * rows, depth), jnp.bfloat16),
            pltpu.VMEM((depth, width), jnp.bfloat16),
            pltpu.SemaphoreType.DMA((6,)),
            pltpu.SemaphoreType.DMA((2 * len(bits) + 1,)),
        ],
        compiler_params=memory(LARGE),
        cost_estimate=pl.CostEstimate(
            flops=8 * NEIGH * count * 2048 * width,
            bytes_accessed=4 * tile_rows * width,
            transcendentals=0,
        ),
        name="pixel_rows",
    )(
        jnp.stack([start, chan]), places, wanted, cotangent, above, below, mixing, spectra, weight
    )


def gradient_kernel(where, keep, near, far, tiles, weights, mine, answers, out):
    tile, chan = where[0], where[1]
    rows = out.shape[0]
    size = tiles.shape[1]
    count = rows // size
    group = 8 // count
    wide = jnp.float32
    first = pl.multiple_of(chan // group * 8, 8)

    def columns(values):
        turned = values[pl.ds(first, 8), :].T
        places = [turned[:, n * count : (n + 1) * count] for n in range(group)]
        picked = places[0]
        for n in range(1, group):
            picked = jnp.where(chan % group == n, places[n], picked)
        return picked

    own = columns(tiles).astype(wide)
    factors = columns(weights)
    for n in range(count):
        here = slice(n * size, (n + 1) * size)
        pre = keep[here, :].astype(wide) + near[here, :].astype(wide) + far[here, :].astype(wide)
        sigma = jax.nn.sigmoid(pre)
        deriv = sigma * (1.0 + pre * (1.0 - sigma))
        fetched = jnp.where(
            own[:, n : n + 1] == tile.astype(wide),
            mine[here, :].astype(wide),
            answers[here, :].astype(wide),
        )
        out[here, :] = (factors[:, n : n + 1] * deriv * fetched).astype(out.dtype)


def pre_gradient(tile, chan, keep, near, far, tiles, weights, mine, answers):
    spec = pl.BlockSpec(memory_space=pltpu.VMEM)
    tiles, weights = tiles.reshape(-1, 128), weights.reshape(-1, 128)
    return pl.pallas_call(
        gradient_kernel,
        out_shape=jax.ShapeDtypeStruct(far.shape, jnp.bfloat16),
        in_specs=[pl.BlockSpec(memory_space=pltpu.SMEM)] + [spec] * 7,
        out_specs=spec,
        compiler_params=memory(16),
        name="pre_gradient",
    )(jnp.stack([tile, chan]), keep, near, far, tiles, weights, mine, answers)


def collect_kernel(where, *refs):
    *pieces, out = refs
    core, bits = where[0], (where[1], where[2])
    rows = pieces[0].shape[0]
    count = len(pieces) // 4
    for index, piece in enumerate(pieces):
        other, index = divmod(index, 2 * count)
        chunk, handed = divmod(index, 2)
        place = (core ^ other) * 2 * count + 2 * chunk + (bits[other] ^ handed)
        out[pl.ds(pl.multiple_of(place * rows, rows), rows), :] = piece[...].astype(jnp.float32)


def collect(where, own, received):
    spec = pl.BlockSpec(memory_space=pltpu.VMEM)
    pieces = [*own, *received]
    rows, width = sum(piece.shape[0] for piece in pieces), own[0].shape[1]
    return pl.pallas_call(
        collect_kernel,
        out_shape=jax.ShapeDtypeStruct((rows, width), jnp.float32),
        in_specs=[pl.BlockSpec(memory_space=pltpu.SMEM)] + [spec] * len(pieces),
        out_specs=spec,
        compiler_params=memory(16),
        name="collect",
    )(where, *pieces)


def add_kernel(first, second, out):
    out[...] = (first[...].astype(jnp.float32) + second[...].astype(jnp.float32)).astype(out.dtype)


def added(first, second):
    spec = pl.BlockSpec(memory_space=pltpu.VMEM)
    return pl.pallas_call(
        add_kernel,
        out_shape=jax.ShapeDtypeStruct(first.shape, jnp.bfloat16),
        in_specs=[spec, spec],
        out_specs=spec,
        compiler_params=memory(16),
        name="added",
    )(first, second)


def halve_kernel(where, first, second, send, keep):
    rows = keep.shape[0]
    for out, which in ((send, 1 - where[1]), (keep, where[1])):
        here = pl.ds(pl.multiple_of(which * rows, rows), rows)
        out[...] = (first[here, :] + second[here, :].astype(jnp.float32)).astype(out.dtype)


def halved(where, first, second):
    rows, width = first.shape[0] // 2, first.shape[1]
    spec = pl.BlockSpec(memory_space=pltpu.VMEM)
    return pl.pallas_call(
        halve_kernel,
        out_shape=(
            jax.ShapeDtypeStruct((rows, width), jnp.bfloat16),
            jax.ShapeDtypeStruct((rows, width), jnp.float32),
        ),
        in_specs=[pl.BlockSpec(memory_space=pltpu.SMEM), spec, spec],
        out_specs=(spec, spec),
        compiler_params=memory(16),
        name="halved",
    )(where, first, second)


def sum_over_panels(core, parts, received):
    both = ("obs", "pix")
    x, y = lax.axis_index("obs") >> 1, lax.axis_index("pix")
    where = jnp.stack([core, jnp.where(core == 0, x, y), jnp.where(core == 0, y, x)])

    def along(value, step):
        axis = ((4, 1), (1, 4))
        return lax.ppermute(value, both, [(i, i ^ axis[(i >> 1) & 1][step]) for i in range(8)])

    halves = [halved(where, part, other) for part, other in zip(parts, received)]
    sums = [added(keep, along(send, 0)) for send, keep in halves]
    sums = [added(value, along(value, 1)) for value in sums]
    pieces = []
    for value in sums:
        pieces += [value, along(value, 0)]
    return collect(where, pieces, [swap(piece, "obs", 1) for piece in pieces])


def shards(spectra, enc_weight, pix_tile, pix_local, foot_weight, cotangent, adjoint, mixing):
    tile_count = lax.axis_size("pix")
    tile_rows = cotangent.shape[0]
    quarter = spectra.shape[0] // lax.axis_size("chan")
    tile = lax.axis_index("pix")
    chan = lax.axis_index("chan")
    first_row = chan * quarter

    near_first = swap(project(spectra, enc_weight, chan, (3,), LARGE + 4)[0], "chan", 1)
    places = (adjoint - (tile * tile_rows - HALO)) * 2
    places = (places[: NEIGH // 2] | (places[NEIGH // 2 :] << 16)).reshape(-1)

    above, below = edges(cotangent, "pix", HALO)
    capacity = 2 * quarter // tile_count
    pixels = (cotangent, above, below, places, mixing)
    rest = (spectra, enc_weight)
    paired = capacity >= quarter and tile_count == 2
    if paired:
        wanted, start, count = swap(pix_local, "pix", 1), first_row, quarter
    else:
        tile_ids = lax.dynamic_slice_in_dim(pix_tile[:, 0], first_row, quarter, 0)
        local_ids = lax.dynamic_slice_in_dim(pix_local, first_row, quarter, 0)
        slot_index, wanted = requests(tile_ids, local_ids, capacity)
        start, count = 0 * chan, wanted.shape[0]
    rows, shared, send = pixel_rows(*pixels, wanted, start, count, *rest, chan, (2, 1))
    near_first, rows = lax.optimization_barrier((near_first, rows))
    passed_on = (shared.astype(jnp.float32) + near_first.astype(jnp.float32)).astype(jnp.bfloat16)
    passed_on, send, rows, later = lax.optimization_barrier((passed_on, send, rows, chan))
    far = swap(passed_on, "chan", 2)
    near = swap(send, "chan", 1)
    (keep,) = project(*rest, later, (0,), LARGE)
    if paired:
        answers = swap(rows, "pix", 1)
        (mine,) = pixel_rows(*pixels, pix_local, later * quarter, count, *rest, later, ())
    else:
        answers = lax.all_to_all(
            rows.reshape(tile_count, capacity, -1), "pix", split_axis=0, concat_axis=0, tiled=True
        )
        mine = answers = jnp.take(answers.reshape(tile_count * capacity, -1), slot_index, axis=0)
    grads = pre_gradient(tile, chan, keep, near, far, pix_tile, foot_weight, mine, answers)

    across = swap(grads, "chan", 3)
    beside = swap(grads, "chan", 1)
    last = swap(across, "chan", 1)
    early, held = early_product(spectra, chan, grads, beside, across)
    core = lax.axis_index("obs") & 1
    send, keep = late_product(core, held, early, last)
    if lax.axis_size("obs") == 4 and tile_count == 2:
        return sum_over_panels(core, keep, [swap(part, "obs", 1) for part in send])
    first, second = jnp.concatenate(keep), jnp.concatenate(send).astype(jnp.float32)
    first, second = jnp.where(core == 0, first, second), jnp.where(core == 0, second, first)
    return lax.psum(jnp.concatenate([first, second]), ("obs", "pix"))


def solution(mesh):
    return jax.shard_map(
        shards,
        mesh=mesh,
        in_specs=(
            P(("obs", "pix"), "chan"),
            P("chan", None),
            P(("obs", "pix"), None),
            P(("obs", "pix")),
            P(("obs", "pix")),
            P("pix", None),
            P(None, "pix"),
            P(),
        ),
        out_specs=P("chan", None),
        check_vma=False,
    )
```

```python
import functools

import jax
import jax.numpy as jnp
from jax import lax
from jax.experimental import pallas as pl
from jax.experimental.pallas import tpu as pltpu
from jax.sharding import PartitionSpec as P

NEIGH = 8
HALO = 128
MIB = 1024 * 1024
LARGE = 52


def edges(value, axis, width):
    size, length = lax.axis_size(axis), value.shape[0]
    last = lax.slice_in_dim(value, length - width, length, axis=0)
    first = lax.slice_in_dim(value, 0, width, axis=0)
    if size == 2:
        index = lax.axis_index(axis)
        other = lax.ppermute(jnp.where(index == 0, last, first), axis, [(0, 1), (1, 0)])
        return other, other
    up = [(i, i + 1) for i in range(size - 1)]
    return lax.ppermute(last, axis, up), lax.ppermute(first, axis, [(j, i) for i, j in up])


def requests(tile_ids, local_ids, capacity):
    tile_count = lax.axis_size("pix")
    onehot = (tile_ids[:, None] == jnp.arange(tile_count, dtype=jnp.int32)[None, :]).astype(
        jnp.int32
    )
    place_rank = jnp.sum((jnp.cumsum(onehot, axis=0) - 1) * onehot, axis=1)
    slot_index = tile_ids * capacity + place_rank
    outgoing = jnp.full((tile_count * capacity,), 0, jnp.int32).at[slot_index].set(local_ids)
    outgoing = outgoing.reshape(tile_count, capacity)
    requested = lax.all_to_all(outgoing, "pix", split_axis=0, concat_axis=0, tiled=True)
    return slot_index, requested.reshape(-1)


def swap(value, axis, bit):
    size = 1
    for name in (axis,) if isinstance(axis, str) else axis:
        size *= lax.axis_size(name)
    return lax.ppermute(value, axis, [(i, i ^ bit) for i in range(size)])


def memory(mib):
    return pltpu.CompilerParams(vmem_limit_bytes=mib * MIB)


def quarter_copies(spectra, weight, held, near, sems, chan, bits):
    chunk = held.shape[0] // len(bits) // 2
    copies = [pltpu.make_async_copy(weight, near, sems.at[2 * len(bits)])]
    for turn in range(2 * len(bits)):
        first = ((chan ^ bits[turn // 2]) * 2 + turn % 2) * chunk
        copies.append(
            pltpu.make_async_copy(
                spectra.at[pl.ds(pl.multiple_of(first, chunk), chunk)],
                held.at[pl.ds(turn * chunk, chunk)],
                sems.at[turn],
            )
        )
    return copies


def project_rows(copies, held, near, outs):
    chunk = outs[0].shape[0] // 2
    copies[0].wait()
    for turn in range(2 * len(outs)):
        copies[turn + 1].wait()
        rows = held[turn * chunk : (turn + 1) * chunk, :]
        result = jnp.dot(rows, near[...], preferred_element_type=jnp.float32)
        first = turn % 2 * chunk
        outs[turn // 2][first : first + chunk, :] = result.astype(outs[0].dtype)


def project_kernel(bits, chan, spectra, weight, *refs):
    *outs, held, near, sems = refs
    copies = quarter_copies(spectra, weight, held, near, sems, chan[0], bits)
    for copy in copies:
        copy.start()
    project_rows(copies, held, near, outs)


def project(spectra, weight, chan, bits, grant):
    depth, width = weight.shape
    rows = spectra.shape[0] // 4
    hbm = pl.BlockSpec(memory_space=pltpu.HBM)
    return pl.pallas_call(
        functools.partial(project_kernel, bits),
        out_shape=(jax.ShapeDtypeStruct((rows, width), jnp.bfloat16),) * len(bits),
        in_specs=[pl.BlockSpec(memory_space=pltpu.SMEM), hbm, hbm],
        out_specs=(pl.BlockSpec(memory_space=pltpu.VMEM),) * len(bits),
        scratch_shapes=[
            pltpu.VMEM((len(bits) * rows, depth), jnp.bfloat16),
            pltpu.VMEM((depth, width), jnp.bfloat16),
            pltpu.SemaphoreType.DMA((2 * len(bits) + 1,)),
        ],
        compiler_params=memory(grant),
        cost_estimate=pl.CostEstimate(
            flops=2 * len(bits) * rows * depth * width,
            bytes_accessed=2 * len(bits) * rows * (depth + width) + 2 * depth * width,
            transcendentals=0,
        ),
        name="project",
    )(chan.reshape(1), spectra, weight)


def turned_product(left, right):
    return lax.dot_general(
        left, right, (((0,), (0,)), ((), ())), preferred_element_type=jnp.float32
    )


def early_kernel(chan, spectra, first, second, third, total, late, held, sems):
    rows = first.shape[0]
    copies = []
    for turn, bits in enumerate((0, 1, 3, 2)):
        start = pl.multiple_of((chan[0] ^ bits) * rows, rows)
        target = held.at[pl.ds(turn * rows, rows)] if turn < 3 else late
        copies.append(pltpu.make_async_copy(spectra.at[pl.ds(start, rows)], target, sems.at[turn]))
    for copy in copies:
        copy.start()
    copies[0].wait()
    product = turned_product(held[:rows, :], first[...])
    copies[1].wait()
    product += turned_product(held[rows : 2 * rows, :], second[...])
    copies[2].wait()
    total[...] = product + turned_product(held[2 * rows :, :], third[...])
    copies[3].wait()


def early_product(spectra, chan, first, second, third):
    depth = spectra.shape[1]
    rows, width = first.shape
    vmem = pl.BlockSpec(memory_space=pltpu.VMEM)
    return pl.pallas_call(
        early_kernel,
        out_shape=(
            jax.ShapeDtypeStruct((depth, width), jnp.float32),
            jax.ShapeDtypeStruct((rows, depth), jnp.bfloat16),
        ),
        in_specs=[
            pl.BlockSpec(memory_space=pltpu.SMEM),
            pl.BlockSpec(memory_space=pltpu.HBM),
            *[vmem] * 3,
        ],
        out_specs=(vmem, vmem),
        scratch_shapes=[
            pltpu.VMEM((3 * rows, depth), jnp.bfloat16),
            pltpu.SemaphoreType.DMA((4,)),
        ],
        compiler_params=memory(48),
        cost_estimate=pl.CostEstimate(
            flops=6 * rows * depth * width,
            bytes_accessed=8 * rows * depth + 4 * depth * width,
            transcendentals=0,
        ),
        name="early_product",
    )(chan.reshape(1), spectra, first, second, third)


def late_kernel(core, held, before, rows, *outs):
    *outs, total = outs
    total[...] = before[...] + turned_product(held[...], rows[...])
    size = outs[0].shape[0]
    for index, out in enumerate(outs):
        first = (core[0] ^ (1 - index // 2)) * 2 * size + index % 2 * size
        here = pl.ds(pl.multiple_of(first, size), size)
        out[...] = total[here, :].astype(out.dtype)


def late_product(core, held, before, rows):
    size, width = before.shape[0] // 4, before.shape[1]
    spec = pl.BlockSpec(memory_space=pltpu.VMEM)
    send = jax.ShapeDtypeStruct((size, width), jnp.bfloat16)
    keep = jax.ShapeDtypeStruct((size, width), jnp.float32)
    outs = pl.pallas_call(
        late_kernel,
        out_shape=(send, send, keep, keep),
        in_specs=[pl.BlockSpec(memory_space=pltpu.SMEM)] + [spec] * 3,
        out_specs=(spec,) * 4,
        scratch_shapes=[pltpu.VMEM(before.shape, jnp.float32)],
        compiler_params=memory(16),
        cost_estimate=pl.CostEstimate(
            flops=2 * held.shape[0] * held.shape[1] * width,
            bytes_accessed=2 * held.shape[0] * held.shape[1] + 16 * size * width,
            transcendentals=0,
        ),
        name="late_product",
    )(core.reshape(1), held, before, rows)
    return outs[:2], outs[2:]


def pixel_kernel(count, bits, where, places, wanted, cotangent, above, below, mixing, spectra,
                 weight, out, *refs):
    quarters, refs = refs[: len(bits)], refs[len(bits) :]
    table, scale, sums, held, near, names, block, factor, sems, more = refs
    start, chan = where[0], where[1]
    tile_rows, half = held.shape[0], table.shape[1]
    listed = names.shape[0]
    first_name = pl.multiple_of(start // listed * listed, listed)
    copies = [
        pltpu.make_async_copy(places, near, sems.at[4]),
        pltpu.make_async_copy(wanted.at[pl.ds(first_name, listed)], names, sems.at[5]),
    ]
    chunk = tile_rows // 4
    rows = [
        pltpu.make_async_copy(
            cotangent.at[pl.ds(n * chunk, chunk)], held.at[pl.ds(n * chunk, chunk)], sems.at[n]
        )
        for n in range(4)
    ]
    parts = quarter_copies(spectra, weight, block, factor, more, chan, bits) if bits else []
    for copy in copies + rows + parts:
        copy.start()

    def fill(first, values):
        values = values.astype(jnp.float32)
        for side in range(2):
            table[pl.ds(2 * first + side, values.shape[0], stride=2), :] = values[
                :, side * half : (side + 1) * half
            ]

    for side in range(2):
        scale[pl.ds(side, NEIGH, stride=2), :] = mixing[:, side * half : (side + 1) * half]
    scales = [scale[2 * k : 2 * k + 2, :] for k in range(NEIGH)]
    fill(0, above[...])
    fill(HALO + tile_rows, below[...])
    for n in range(4):
        rows[n].wait()
        for first in range(n * chunk, (n + 1) * chunk, 256):
            fill(HALO + first, held[first : first + 256, :])
    if bits:
        project_rows(parts, block, factor, quarters)
    for copy in copies:
        copy.wait()

    group = 32
    offset = start - first_name

    def body(turn, carry):
        base = turn * group
        totals = []
        for n in range(group):
            pixel = names[offset + base + n]
            terms = [table[pl.ds(2 * (pixel + HALO), 2), :]]
            for k in range(NEIGH // 2):
                pair = near[k * tile_rows + pixel]
                for place, scale in ((pair & 0xFFFF, k), (pair >> 16, k + NEIGH // 2)):
                    terms.append(table[pl.ds(place, 2), :] * scales[scale])
            while len(terms) > 1:
                pairs = [x + y for x, y in zip(terms[::2], terms[1::2])]
                terms = pairs + terms[len(terms) // 2 * 2 :]
            totals += terms
        for n, total in enumerate(totals):
            sums[pl.ds(2 * (base + n), 2), :] = total
        return carry

    lax.fori_loop(0, count // group, body, 0)
    for side in range(2):
        out[:, side * half : (side + 1) * half] = sums[pl.ds(side, count, stride=2), :].astype(
            out.dtype
        )


def pixel_rows(
    cotangent, above, below, places, mixing, wanted, start, count, spectra, weight, chan, bits
):
    tile_rows, width = cotangent.shape
    depth, rows = spectra.shape[1], spectra.shape[0] // 4
    listed = min(wanted.shape[0], 1024)
    anywhere = pl.BlockSpec(memory_space=pl.ANY)
    hbm = pl.BlockSpec(memory_space=pltpu.HBM)
    vmem = pl.BlockSpec(memory_space=pltpu.VMEM)
    return pl.pallas_call(
        functools.partial(pixel_kernel, count, bits),
        out_shape=(
            jax.ShapeDtypeStruct((count, width), jnp.bfloat16),
            *[jax.ShapeDtypeStruct((rows, width), jnp.bfloat16)] * len(bits),
        ),
        in_specs=[
            pl.BlockSpec(memory_space=pltpu.SMEM),
            anywhere,
            anywhere,
            hbm,
            *[vmem] * 3,
            hbm,
            hbm,
        ],
        out_specs=(vmem,) * (1 + len(bits)),
        scratch_shapes=[
            pltpu.VMEM((2 * (tile_rows + 2 * HALO), width // 2), jnp.float32),
            pltpu.VMEM((2 * NEIGH, width // 2), jnp.float32),
            pltpu.VMEM((2 * count, width // 2), jnp.float32),
            pltpu.VMEM(cotangent.shape, cotangent.dtype),
            pltpu.SMEM(places.shape, jnp.int32),
            pltpu.SMEM((listed,), jnp.int32),
            pltpu.VMEM((max(len(bits), 1) * rows, depth), jnp.bfloat16),
            pltpu.VMEM((depth, width), jnp.bfloat16),
            pltpu.SemaphoreType.DMA((6,)),
            pltpu.SemaphoreType.DMA((2 * len(bits) + 1,)),
        ],
        compiler_params=memory(LARGE),
        cost_estimate=pl.CostEstimate(
            flops=8 * NEIGH * count * 2048 * width,
            bytes_accessed=4 * tile_rows * width,
            transcendentals=0,
        ),
        name="pixel_rows",
    )(
        jnp.stack([start, chan]), places, wanted, cotangent, above, below, mixing, spectra, weight
    )


def gradient_kernel(where, keep, near, far, tiles, weights, mine, answers, out):
    tile, chan = where[0], where[1]
    rows = out.shape[0]
    size = tiles.shape[1]
    count = rows // size
    group = 8 // count
    wide = jnp.float32
    first = pl.multiple_of(chan // group * 8, 8)

    def columns(values):
        turned = values[pl.ds(first, 8), :].T
        places = [turned[:, n * count : (n + 1) * count] for n in range(group)]
        picked = places[0]
        for n in range(1, group):
            picked = jnp.where(chan % group == n, places[n], picked)
        return picked

    own = columns(tiles).astype(wide)
    factors = columns(weights)
    for n in range(count):
        here = slice(n * size, (n + 1) * size)
        pre = keep[here, :].astype(wide) + near[here, :].astype(wide) + far[here, :].astype(wide)
        sigma = jax.nn.sigmoid(pre)
        deriv = sigma * (1.0 + pre * (1.0 - sigma))
        fetched = jnp.where(
            own[:, n : n + 1] == tile.astype(wide),
            mine[here, :].astype(wide),
            answers[here, :].astype(wide),
        )
        out[here, :] = (factors[:, n : n + 1] * deriv * fetched).astype(out.dtype)


def pre_gradient(tile, chan, keep, near, far, tiles, weights, mine, answers):
    spec = pl.BlockSpec(memory_space=pltpu.VMEM)
    tiles, weights = tiles.reshape(-1, 128), weights.reshape(-1, 128)
    return pl.pallas_call(
        gradient_kernel,
        out_shape=jax.ShapeDtypeStruct(far.shape, jnp.bfloat16),
        in_specs=[pl.BlockSpec(memory_space=pltpu.SMEM)] + [spec] * 7,
        out_specs=spec,
        compiler_params=memory(16),
        name="pre_gradient",
    )(jnp.stack([tile, chan]), keep, near, far, tiles, weights, mine, answers)


def collect_kernel(core, *refs):
    *pieces, out = refs
    half, rows = out.shape[0] // 2, pieces[0].shape[0]
    count = len(pieces) // 2
    for index, piece in enumerate(pieces):
        which = core[0] if index < count else 1 - core[0]
        first = which * half + (index % count) * rows
        out[pl.ds(pl.multiple_of(first, rows), rows), :] = piece[...].astype(jnp.float32)


def collect(core, own, received):
    spec = pl.BlockSpec(memory_space=pltpu.VMEM)
    pieces = [*own, *received]
    rows, width = sum(piece.shape[0] for piece in pieces), own[0].shape[1]
    return pl.pallas_call(
        collect_kernel,
        out_shape=jax.ShapeDtypeStruct((rows, width), jnp.float32),
        in_specs=[pl.BlockSpec(memory_space=pltpu.SMEM)] + [spec] * len(pieces),
        out_specs=spec,
        compiler_params=memory(16),
        name="collect",
    )(core.reshape(1), *pieces)


def add_kernel(first, second, out):
    out[...] = (first[...].astype(jnp.float32) + second[...].astype(jnp.float32)).astype(out.dtype)


def added(first, second):
    spec = pl.BlockSpec(memory_space=pltpu.VMEM)
    return pl.pallas_call(
        add_kernel,
        out_shape=jax.ShapeDtypeStruct(first.shape, jnp.bfloat16),
        in_specs=[spec, spec],
        out_specs=spec,
        compiler_params=memory(16),
        name="added",
    )(first, second)


def sum_over_panels(core, parts, received):
    both = ("obs", "pix")
    parts = [added(part, other) for part, other in zip(parts, received)]
    for order in ((4, 1), (1, 4)):
        perm = [(i, i ^ order[(i >> 1) & 1]) for i in range(8)]
        parts = [added(part, lax.ppermute(part, both, perm)) for part in parts]
    return collect(core, parts, [swap(part, "obs", 1) for part in parts])


def shards(spectra, enc_weight, pix_tile, pix_local, foot_weight, cotangent, adjoint, mixing):
    tile_count = lax.axis_size("pix")
    tile_rows = cotangent.shape[0]
    quarter = spectra.shape[0] // lax.axis_size("chan")
    tile = lax.axis_index("pix")
    chan = lax.axis_index("chan")
    first_row = chan * quarter

    near_first = swap(project(spectra, enc_weight, chan, (2,), LARGE + 4)[0], "chan", 1)
    places = (adjoint - (tile * tile_rows - HALO)) * 2
    places = (places[: NEIGH // 2] | (places[NEIGH // 2 :] << 16)).reshape(-1)

    above, below = edges(cotangent, "pix", HALO)
    capacity = 2 * quarter // tile_count
    pixels = (cotangent, above, below, places, mixing)
    rest = (spectra, enc_weight)
    paired = capacity >= quarter and tile_count == 2
    if paired:
        wanted, start, count = swap(pix_local, "pix", 1), first_row, quarter
    else:
        tile_ids = lax.dynamic_slice_in_dim(pix_tile[:, 0], first_row, quarter, 0)
        local_ids = lax.dynamic_slice_in_dim(pix_local, first_row, quarter, 0)
        slot_index, wanted = requests(tile_ids, local_ids, capacity)
        start, count = 0 * chan, wanted.shape[0]
    rows, shared, send = pixel_rows(*pixels, wanted, start, count, *rest, chan, (3, 1))
    near_first, rows = lax.optimization_barrier((near_first, rows))
    passed_on = (shared.astype(jnp.float32) + near_first.astype(jnp.float32)).astype(jnp.bfloat16)
    passed_on, send, rows, later = lax.optimization_barrier((passed_on, send, rows, chan))
    far = swap(passed_on, "chan", 3)
    near = swap(send, "chan", 1)
    (keep,) = project(*rest, later, (0,), LARGE)
    if paired:
        answers = swap(rows, "pix", 1)
        (mine,) = pixel_rows(*pixels, pix_local, later * quarter, count, *rest, later, ())
    else:
        answers = lax.all_to_all(
            rows.reshape(tile_count, capacity, -1), "pix", split_axis=0, concat_axis=0, tiled=True
        )
        mine = answers = jnp.take(answers.reshape(tile_count * capacity, -1), slot_index, axis=0)
    grads = pre_gradient(tile, chan, keep, near, far, pix_tile, foot_weight, mine, answers)

    across = swap(grads, "chan", 3)
    beside = swap(grads, "chan", 1)
    last = swap(across, "chan", 1)
    early, held = early_product(spectra, chan, grads, beside, across)
    core = lax.axis_index("obs") & 1
    send, keep = late_product(core, held, early, last)
    if lax.axis_size("obs") == 4 and tile_count == 2:
        return sum_over_panels(core, keep, [swap(part, "obs", 1) for part in send])
    return lax.psum(collect(core, keep, send), ("obs", "pix"))


def solution(mesh):
    return jax.shard_map(
        shards,
        mesh=mesh,
        in_specs=(
            P(("obs", "pix"), "chan"),
            P("chan", None),
            P(("obs", "pix"), None),
            P(("obs", "pix")),
            P(("obs", "pix")),
            P("pix", None),
            P(None, "pix"),
            P(),
        ),
        out_specs=P("chan", None),
        check_vma=False,
    )
```

```python
import functools

import jax
import jax.numpy as jnp
from jax import lax
from jax.experimental import pallas as pl
from jax.experimental.pallas import tpu as pltpu
from jax.sharding import PartitionSpec as P

NEIGH = 8
HALO = 128
MIB = 1024 * 1024
LARGE = 52


def edges(value, axis, width):
    size, length = lax.axis_size(axis), value.shape[0]
    last = lax.slice_in_dim(value, length - width, length, axis=0)
    first = lax.slice_in_dim(value, 0, width, axis=0)
    if size == 2:
        index = lax.axis_index(axis)
        other = lax.ppermute(jnp.where(index == 0, last, first), axis, [(0, 1), (1, 0)])
        return other, other
    up = [(i, i + 1) for i in range(size - 1)]
    return lax.ppermute(last, axis, up), lax.ppermute(first, axis, [(j, i) for i, j in up])


def requests(tile_ids, local_ids, capacity):
    tile_count = lax.axis_size("pix")
    onehot = (tile_ids[:, None] == jnp.arange(tile_count, dtype=jnp.int32)[None, :]).astype(
        jnp.int32
    )
    place_rank = jnp.sum((jnp.cumsum(onehot, axis=0) - 1) * onehot, axis=1)
    slot_index = tile_ids * capacity + place_rank
    outgoing = jnp.full((tile_count * capacity,), 0, jnp.int32).at[slot_index].set(local_ids)
    outgoing = outgoing.reshape(tile_count, capacity)
    requested = lax.all_to_all(outgoing, "pix", split_axis=0, concat_axis=0, tiled=True)
    return slot_index, requested.reshape(-1)


def swap(value, axis, bit):
    size = 1
    for name in (axis,) if isinstance(axis, str) else axis:
        size *= lax.axis_size(name)
    return lax.ppermute(value, axis, [(i, i ^ bit) for i in range(size)])


def memory(mib):
    return pltpu.CompilerParams(vmem_limit_bytes=mib * MIB)


def quarter_copies(spectra, held, sems, chan, bits):
    rows = spectra.shape[0] // 4
    return [
        pltpu.make_async_copy(
            spectra.at[pl.ds(pl.multiple_of((chan ^ bit) * rows, rows), rows)],
            held.at[pl.ds(turn * rows, rows)],
            sems.at[turn],
        )
        for turn, bit in enumerate(bits)
    ]


def project_rows(copies, held, weight, outs):
    rows = outs[0].shape[0] if outs else 0
    for turn, (copy, out) in enumerate(zip(copies, outs)):
        copy.wait()
        result = jnp.dot(
            held[turn * rows : (turn + 1) * rows, :],
            weight[...],
            preferred_element_type=jnp.float32,
        )
        out[...] = result.astype(out.dtype)


def project_kernel(bits, chan, spectra, weight, *refs):
    *outs, held, near, sems = refs
    copies = [pltpu.make_async_copy(weight, near, sems.at[len(bits)])]
    copies += quarter_copies(spectra, held, sems, chan[0], bits)
    for copy in copies:
        copy.start()
    copies[0].wait()
    project_rows(copies[1:], held, near, outs)


def project(spectra, weight, chan, bits, grant):
    depth, width = weight.shape
    rows = spectra.shape[0] // 4
    hbm = pl.BlockSpec(memory_space=pltpu.HBM)
    return pl.pallas_call(
        functools.partial(project_kernel, bits),
        out_shape=(jax.ShapeDtypeStruct((rows, width), jnp.bfloat16),) * len(bits),
        in_specs=[pl.BlockSpec(memory_space=pltpu.SMEM), hbm, hbm],
        out_specs=(pl.BlockSpec(memory_space=pltpu.VMEM),) * len(bits),
        scratch_shapes=[
            pltpu.VMEM((len(bits) * rows, depth), jnp.bfloat16),
            pltpu.VMEM((depth, width), jnp.bfloat16),
            pltpu.SemaphoreType.DMA((len(bits) + 1,)),
        ],
        compiler_params=memory(grant),
        cost_estimate=pl.CostEstimate(
            flops=2 * len(bits) * rows * depth * width,
            bytes_accessed=2 * len(bits) * rows * (depth + width) + 2 * depth * width,
            transcendentals=0,
        ),
        name="project",
    )(chan.reshape(1), spectra, weight)


def turned_product(left, right):
    return lax.dot_general(
        left, right, (((0,), (0,)), ((), ())), preferred_element_type=jnp.float32
    )


def early_kernel(chan, spectra, first, second, total, third, fourth, held, sems):
    rows = first.shape[0]
    targets = (held.at[pl.ds(0, rows)], held.at[pl.ds(rows, rows)], third, fourth)
    copies = []
    for turn, (bits, target) in enumerate(zip((0, 3, 1, 2), targets)):
        start = pl.multiple_of((chan[0] ^ bits) * rows, rows)
        copies.append(pltpu.make_async_copy(spectra.at[pl.ds(start, rows)], target, sems.at[turn]))
    for copy in copies:
        copy.start()
    copies[0].wait()
    product = turned_product(held[:rows, :], first[...])
    copies[1].wait()
    total[...] = product + turned_product(held[rows:, :], second[...])
    copies[2].wait()
    copies[3].wait()


def early_product(spectra, chan, first, second):
    depth = spectra.shape[1]
    rows, width = first.shape
    vmem = pl.BlockSpec(memory_space=pltpu.VMEM)
    return pl.pallas_call(
        early_kernel,
        out_shape=(
            jax.ShapeDtypeStruct((depth, width), jnp.float32),
            jax.ShapeDtypeStruct((rows, depth), jnp.bfloat16),
            jax.ShapeDtypeStruct((rows, depth), jnp.bfloat16),
        ),
        in_specs=[
            pl.BlockSpec(memory_space=pltpu.SMEM),
            pl.BlockSpec(memory_space=pltpu.HBM),
            vmem,
            vmem,
        ],
        out_specs=(vmem,) * 3,
        scratch_shapes=[
            pltpu.VMEM((2 * rows, depth), jnp.bfloat16),
            pltpu.SemaphoreType.DMA((4,)),
        ],
        compiler_params=memory(48),
        cost_estimate=pl.CostEstimate(
            flops=4 * rows * depth * width,
            bytes_accessed=8 * rows * depth + 4 * depth * width,
            transcendentals=0,
        ),
        name="early_product",
    )(chan.reshape(1), spectra, first, second)


def more_kernel(held, before, rows, total):
    total[...] = before[...] + turned_product(held[...], rows[...])


def more_product(held, before, rows):
    vmem = pl.BlockSpec(memory_space=pltpu.VMEM)
    return pl.pallas_call(
        more_kernel,
        out_shape=jax.ShapeDtypeStruct(before.shape, jnp.float32),
        in_specs=[vmem] * 3,
        out_specs=vmem,
        compiler_params=memory(16),
        cost_estimate=pl.CostEstimate(
            flops=2 * held.shape[0] * held.shape[1] * rows.shape[1],
            bytes_accessed=2 * held.shape[0] * held.shape[1] + 8 * before.size,
            transcendentals=0,
        ),
        name="more_product",
    )(held, before, rows)


def late_kernel(core, held, before, rows, *outs):
    *outs, total = outs
    total[...] = before[...] + turned_product(held[...], rows[...])
    size = outs[0].shape[0]
    for index, out in enumerate(outs):
        first = (core[0] ^ (1 - index // 2)) * 2 * size + index % 2 * size
        here = pl.ds(pl.multiple_of(first, size), size)
        out[...] = total[here, :].astype(out.dtype)


def late_product(core, held, before, rows):
    size, width = before.shape[0] // 4, before.shape[1]
    spec = pl.BlockSpec(memory_space=pltpu.VMEM)
    send = jax.ShapeDtypeStruct((size, width), jnp.bfloat16)
    keep = jax.ShapeDtypeStruct((size, width), jnp.float32)
    outs = pl.pallas_call(
        late_kernel,
        out_shape=(send, send, keep, keep),
        in_specs=[pl.BlockSpec(memory_space=pltpu.SMEM)] + [spec] * 3,
        out_specs=(spec,) * 4,
        scratch_shapes=[pltpu.VMEM(before.shape, jnp.float32)],
        compiler_params=memory(16),
        cost_estimate=pl.CostEstimate(
            flops=2 * held.shape[0] * held.shape[1] * width,
            bytes_accessed=2 * held.shape[0] * held.shape[1] + 16 * size * width,
            transcendentals=0,
        ),
        name="late_product",
    )(core.reshape(1), held, before, rows)
    return outs[:2], outs[2:]


def pixel_kernel(count, bits, where, places, wanted, cotangent, above, below, mixing, weight,
                 spectra, out, *refs):
    quarters, refs = refs[: len(bits)], refs[len(bits) :]
    table, scale, sums, near, names, held, sems = refs
    start, chan = where[0], where[1]
    tile_rows, half = cotangent.shape[0], table.shape[1]
    listed = names.shape[0]
    first_name = pl.multiple_of(start // listed * listed, listed)
    copies = [
        pltpu.make_async_copy(places, near, sems.at[len(bits)]),
        pltpu.make_async_copy(wanted.at[pl.ds(first_name, listed)], names, sems.at[len(bits) + 1]),
    ]
    parts = quarter_copies(spectra, held, sems, chan, bits)
    for copy in copies + parts:
        copy.start()

    def fill(first, values):
        values = values.astype(jnp.float32)
        for side in range(2):
            table[pl.ds(2 * first + side, values.shape[0], stride=2), :] = values[
                :, side * half : (side + 1) * half
            ]

    for side in range(2):
        scale[pl.ds(side, NEIGH, stride=2), :] = mixing[:, side * half : (side + 1) * half]
    scales = [scale[2 * k : 2 * k + 2, :] for k in range(NEIGH)]
    fill(0, above[...])
    fill(HALO + tile_rows, below[...])
    for first in range(0, tile_rows, 256):
        fill(HALO + first, cotangent[first : first + 256, :])
    project_rows(parts, held, weight, quarters)
    for copy in copies:
        copy.wait()

    group = 32
    offset = start - first_name

    def body(turn, carry):
        base = turn * group
        totals = []
        for n in range(group):
            pixel = names[offset + base + n]
            terms = [table[pl.ds(2 * (pixel + HALO), 2), :]]
            for k in range(NEIGH // 2):
                pair = near[k * tile_rows + pixel]
                for place, scale in ((pair & 0xFFFF, k), (pair >> 16, k + NEIGH // 2)):
                    terms.append(table[pl.ds(place, 2), :] * scales[scale])
            while len(terms) > 1:
                pairs = [x + y for x, y in zip(terms[::2], terms[1::2])]
                terms = pairs + terms[len(terms) // 2 * 2 :]
            totals += terms
        for n, total in enumerate(totals):
            sums[pl.ds(2 * (base + n), 2), :] = total
        return carry

    lax.fori_loop(0, count // group, body, 0)
    for side in range(2):
        out[:, side * half : (side + 1) * half] = sums[pl.ds(side, count, stride=2), :].astype(
            out.dtype
        )


def pixel_rows(
    cotangent, above, below, places, mixing, wanted, start, count, spectra, weight, chan, bits
):
    tile_rows, width = cotangent.shape
    depth, rows = spectra.shape[1], spectra.shape[0] // 4
    listed = min(wanted.shape[0], 1024)
    anywhere = pl.BlockSpec(memory_space=pl.ANY)
    vmem = pl.BlockSpec(memory_space=pltpu.VMEM)
    return pl.pallas_call(
        functools.partial(pixel_kernel, count, bits),
        out_shape=(
            jax.ShapeDtypeStruct((count, width), jnp.bfloat16),
            *[jax.ShapeDtypeStruct((rows, width), jnp.bfloat16)] * len(bits),
        ),
        in_specs=[
            pl.BlockSpec(memory_space=pltpu.SMEM),
            anywhere,
            anywhere,
            *[vmem] * 5,
            pl.BlockSpec(memory_space=pltpu.HBM),
        ],
        out_specs=(vmem,) * (1 + len(bits)),
        scratch_shapes=[
            pltpu.VMEM((2 * (tile_rows + 2 * HALO), width // 2), jnp.float32),
            pltpu.VMEM((2 * NEIGH, width // 2), jnp.float32),
            pltpu.VMEM((2 * count, width // 2), jnp.float32),
            pltpu.SMEM(places.shape, jnp.int32),
            pltpu.SMEM((listed,), jnp.int32),
            pltpu.VMEM((max(len(bits), 1) * rows, depth), jnp.bfloat16),
            pltpu.SemaphoreType.DMA((len(bits) + 2,)),
        ],
        compiler_params=memory(48),
        cost_estimate=pl.CostEstimate(
            flops=8 * NEIGH * count * 2048 * width,
            bytes_accessed=4 * tile_rows * width,
            transcendentals=0,
        ),
        name="pixel_rows",
    )(
        jnp.stack([start, chan]), places, wanted, cotangent, above, below, mixing, weight, spectra
    )


def gradient_kernel(where, keep, near, far, tiles, weights, mine, answers, out):
    tile, chan = where[0], where[1]
    rows = out.shape[0]
    size = tiles.shape[1]
    count = rows // size
    group = 8 // count
    wide = jnp.float32
    first = pl.multiple_of(chan // group * 8, 8)

    def columns(values):
        turned = values[pl.ds(first, 8), :].T
        places = [turned[:, n * count : (n + 1) * count] for n in range(group)]
        picked = places[0]
        for n in range(1, group):
            picked = jnp.where(chan % group == n, places[n], picked)
        return picked

    own = columns(tiles).astype(wide)
    factors = columns(weights)
    for n in range(count):
        here = slice(n * size, (n + 1) * size)
        pre = keep[here, :].astype(wide) + near[here, :].astype(wide) + far[here, :].astype(wide)
        sigma = jax.nn.sigmoid(pre)
        deriv = sigma * (1.0 + pre * (1.0 - sigma))
        fetched = jnp.where(
            own[:, n : n + 1] == tile.astype(wide),
            mine[here, :].astype(wide),
            answers[here, :].astype(wide),
        )
        out[here, :] = (factors[:, n : n + 1] * deriv * fetched).astype(out.dtype)


def pre_gradient(tile, chan, keep, near, far, tiles, weights, mine, answers):
    spec = pl.BlockSpec(memory_space=pltpu.VMEM)
    tiles, weights = tiles.reshape(-1, 128), weights.reshape(-1, 128)
    return pl.pallas_call(
        gradient_kernel,
        out_shape=jax.ShapeDtypeStruct(far.shape, jnp.bfloat16),
        in_specs=[pl.BlockSpec(memory_space=pltpu.SMEM)] + [spec] * 7,
        out_specs=spec,
        compiler_params=memory(16),
        name="pre_gradient",
    )(jnp.stack([tile, chan]), keep, near, far, tiles, weights, mine, answers)


def collect_kernel(core, *refs):
    *pieces, out = refs
    half, rows = out.shape[0] // 2, pieces[0].shape[0]
    count = len(pieces) // 2
    for index, piece in enumerate(pieces):
        which = core[0] if index < count else 1 - core[0]
        first = which * half + (index % count) * rows
        out[pl.ds(pl.multiple_of(first, rows), rows), :] = piece[...].astype(jnp.float32)


def collect(core, own, received):
    spec = pl.BlockSpec(memory_space=pltpu.VMEM)
    pieces = [*own, *received]
    rows, width = sum(piece.shape[0] for piece in pieces), own[0].shape[1]
    return pl.pallas_call(
        collect_kernel,
        out_shape=jax.ShapeDtypeStruct((rows, width), jnp.float32),
        in_specs=[pl.BlockSpec(memory_space=pltpu.SMEM)] + [spec] * len(pieces),
        out_specs=spec,
        compiler_params=memory(16),
        name="collect",
    )(core.reshape(1), *pieces)


def add_kernel(first, second, out):
    out[...] = (first[...].astype(jnp.float32) + second[...].astype(jnp.float32)).astype(out.dtype)


def added(first, second):
    spec = pl.BlockSpec(memory_space=pltpu.VMEM)
    return pl.pallas_call(
        add_kernel,
        out_shape=jax.ShapeDtypeStruct(first.shape, jnp.bfloat16),
        in_specs=[spec, spec],
        out_specs=spec,
        compiler_params=memory(16),
        name="added",
    )(first, second)


def sum_over_panels(core, parts, received):
    both = ("obs", "pix")
    parts = [added(part, other) for part, other in zip(parts, received)]
    for order in ((4, 1), (1, 4)):
        perm = [(i, i ^ order[(i >> 1) & 1]) for i in range(8)]
        parts = [added(part, lax.ppermute(part, both, perm)) for part in parts]
    return collect(core, parts, [swap(part, "obs", 1) for part in parts])


def shards(spectra, enc_weight, pix_tile, pix_local, foot_weight, cotangent, adjoint, mixing):
    tile_count = lax.axis_size("pix")
    tile_rows = cotangent.shape[0]
    quarter = spectra.shape[0] // lax.axis_size("chan")
    tile = lax.axis_index("pix")
    chan = lax.axis_index("chan")
    first_row = chan * quarter

    near_first = swap(project(spectra, enc_weight, chan, (2,), LARGE + 4)[0], "chan", 1)
    places = (adjoint - (tile * tile_rows - HALO)) * 2
    places = (places[: NEIGH // 2] | (places[NEIGH // 2 :] << 16)).reshape(-1)

    above, below = edges(cotangent, "pix", HALO)
    capacity = 2 * quarter // tile_count
    pixels = (cotangent, above, below, places, mixing)
    rest = (spectra, enc_weight)
    paired = capacity >= quarter and tile_count == 2
    if paired:
        wanted, start, count = swap(pix_local, "pix", 1), first_row, quarter
    else:
        tile_ids = lax.dynamic_slice_in_dim(pix_tile[:, 0], first_row, quarter, 0)
        local_ids = lax.dynamic_slice_in_dim(pix_local, first_row, quarter, 0)
        slot_index, wanted = requests(tile_ids, local_ids, capacity)
        start, count = 0 * chan, wanted.shape[0]
    rows, shared, send = pixel_rows(*pixels, wanted, start, count, *rest, chan, (3, 1))
    near_first, rows = lax.optimization_barrier((near_first, rows))
    passed_on = (shared.astype(jnp.float32) + near_first.astype(jnp.float32)).astype(jnp.bfloat16)
    passed_on, send, rows, later = lax.optimization_barrier((passed_on, send, rows, chan))
    far = swap(passed_on, "chan", 3)
    near = swap(send, "chan", 1)
    (keep,) = project(*rest, later, (0,), LARGE)
    if paired:
        answers = swap(rows, "pix", 1)
        (mine,) = pixel_rows(*pixels, pix_local, later * quarter, count, *rest, later, ())
    else:
        answers = lax.all_to_all(
            rows.reshape(tile_count, capacity, -1), "pix", split_axis=0, concat_axis=0, tiled=True
        )
        mine = answers = jnp.take(answers.reshape(tile_count * capacity, -1), slot_index, axis=0)
    grads = pre_gradient(tile, chan, keep, near, far, pix_tile, foot_weight, mine, answers)

    across = swap(grads, "chan", 3)
    beside = swap(grads, "chan", 1)
    last = swap(across, "chan", 1)
    early, held, held_last = early_product(spectra, chan, grads, across)
    early = more_product(held, early, beside)
    core = lax.axis_index("obs") & 1
    send, keep = late_product(core, held_last, early, last)
    if lax.axis_size("obs") == 4 and tile_count == 2:
        return sum_over_panels(core, keep, [swap(part, "obs", 1) for part in send])
    return lax.psum(collect(core, keep, send), ("obs", "pix"))


def solution(mesh):
    return jax.shard_map(
        shards,
        mesh=mesh,
        in_specs=(
            P(("obs", "pix"), "chan"),
            P("chan", None),
            P(("obs", "pix"), None),
            P(("obs", "pix")),
            P(("obs", "pix")),
            P("pix", None),
            P(None, "pix"),
            P(),
        ),
        out_specs=P("chan", None),
        check_vma=False,
    )
```

```python
import functools

import jax
import jax.numpy as jnp
from jax import lax
from jax.experimental import pallas as pl
from jax.experimental.pallas import tpu as pltpu
from jax.sharding import PartitionSpec as P

NEIGH = 8
HALO = 128
MIB = 1024 * 1024
LARGE = 52


def edges(value, axis, width):
    size, length = lax.axis_size(axis), value.shape[0]
    last = lax.slice_in_dim(value, length - width, length, axis=0)
    first = lax.slice_in_dim(value, 0, width, axis=0)
    if size == 2:
        index = lax.axis_index(axis)
        other = lax.ppermute(jnp.where(index == 0, last, first), axis, [(0, 1), (1, 0)])
        return other, other
    up = [(i, i + 1) for i in range(size - 1)]
    return lax.ppermute(last, axis, up), lax.ppermute(first, axis, [(j, i) for i, j in up])


def requests(tile_ids, local_ids, capacity):
    tile_count = lax.axis_size("pix")
    onehot = (tile_ids[:, None] == jnp.arange(tile_count, dtype=jnp.int32)[None, :]).astype(
        jnp.int32
    )
    place_rank = jnp.sum((jnp.cumsum(onehot, axis=0) - 1) * onehot, axis=1)
    slot_index = tile_ids * capacity + place_rank
    outgoing = jnp.full((tile_count * capacity,), 0, jnp.int32).at[slot_index].set(local_ids)
    outgoing = outgoing.reshape(tile_count, capacity)
    requested = lax.all_to_all(outgoing, "pix", split_axis=0, concat_axis=0, tiled=True)
    return slot_index, requested.reshape(-1)


def swap(value, axis, bit):
    size = 1
    for name in (axis,) if isinstance(axis, str) else axis:
        size *= lax.axis_size(name)
    return lax.ppermute(value, axis, [(i, i ^ bit) for i in range(size)])


def memory(mib):
    return pltpu.CompilerParams(vmem_limit_bytes=mib * MIB)


def quarter_copies(spectra, held, sems, chan, bits):
    rows = spectra.shape[0] // 4
    return [
        pltpu.make_async_copy(
            spectra.at[pl.ds(pl.multiple_of((chan ^ bit) * rows, rows), rows)],
            held.at[pl.ds(turn * rows, rows)],
            sems.at[turn],
        )
        for turn, bit in enumerate(bits)
    ]


def project_rows(copies, held, weight, outs):
    rows = outs[0].shape[0] if outs else 0
    for turn, (copy, out) in enumerate(zip(copies, outs)):
        copy.wait()
        result = jnp.dot(
            held[turn * rows : (turn + 1) * rows, :],
            weight[...],
            preferred_element_type=jnp.float32,
        )
        out[...] = result.astype(out.dtype)


def project_kernel(bits, chan, spectra, weight, *refs):
    *outs, held, near, sems = refs
    copies = [pltpu.make_async_copy(weight, near, sems.at[len(bits)])]
    copies += quarter_copies(spectra, held, sems, chan[0], bits)
    for copy in copies:
        copy.start()
    copies[0].wait()
    project_rows(copies[1:], held, near, outs)


def project(spectra, weight, chan, bits, grant):
    depth, width = weight.shape
    rows = spectra.shape[0] // 4
    hbm = pl.BlockSpec(memory_space=pltpu.HBM)
    return pl.pallas_call(
        functools.partial(project_kernel, bits),
        out_shape=(jax.ShapeDtypeStruct((rows, width), jnp.bfloat16),) * len(bits),
        in_specs=[pl.BlockSpec(memory_space=pltpu.SMEM), hbm, hbm],
        out_specs=(pl.BlockSpec(memory_space=pltpu.VMEM),) * len(bits),
        scratch_shapes=[
            pltpu.VMEM((len(bits) * rows, depth), jnp.bfloat16),
            pltpu.VMEM((depth, width), jnp.bfloat16),
            pltpu.SemaphoreType.DMA((len(bits) + 1,)),
        ],
        compiler_params=memory(grant),
        cost_estimate=pl.CostEstimate(
            flops=2 * len(bits) * rows * depth * width,
            bytes_accessed=2 * len(bits) * rows * (depth + width) + 2 * depth * width,
            transcendentals=0,
        ),
        name="project",
    )(chan.reshape(1), spectra, weight)


def turned_product(left, right):
    return lax.dot_general(
        left, right, (((0,), (0,)), ((), ())), preferred_element_type=jnp.float32
    )


def early_kernel(chan, spectra, first, second, total, third, fourth, held, sems):
    rows = first.shape[0]
    targets = (held.at[pl.ds(0, rows)], held.at[pl.ds(rows, rows)], third, fourth)
    copies = []
    for turn, (bits, target) in enumerate(zip((0, 3, 1, 2), targets)):
        start = pl.multiple_of((chan[0] ^ bits) * rows, rows)
        copies.append(pltpu.make_async_copy(spectra.at[pl.ds(start, rows)], target, sems.at[turn]))
    for copy in copies:
        copy.start()
    copies[0].wait()
    product = turned_product(held[:rows, :], first[...])
    copies[1].wait()
    total[...] = product + turned_product(held[rows:, :], second[...])
    copies[2].wait()
    copies[3].wait()


def early_product(spectra, chan, first, second):
    depth = spectra.shape[1]
    rows, width = first.shape
    vmem = pl.BlockSpec(memory_space=pltpu.VMEM)
    return pl.pallas_call(
        early_kernel,
        out_shape=(
            jax.ShapeDtypeStruct((depth, width), jnp.float32),
            jax.ShapeDtypeStruct((rows, depth), jnp.bfloat16),
            jax.ShapeDtypeStruct((rows, depth), jnp.bfloat16),
        ),
        in_specs=[
            pl.BlockSpec(memory_space=pltpu.SMEM),
            pl.BlockSpec(memory_space=pltpu.HBM),
            vmem,
            vmem,
        ],
        out_specs=(vmem,) * 3,
        scratch_shapes=[
            pltpu.VMEM((2 * rows, depth), jnp.bfloat16),
            pltpu.SemaphoreType.DMA((4,)),
        ],
        compiler_params=memory(48),
        cost_estimate=pl.CostEstimate(
            flops=4 * rows * depth * width,
            bytes_accessed=8 * rows * depth + 4 * depth * width,
            transcendentals=0,
        ),
        name="early_product",
    )(chan.reshape(1), spectra, first, second)


def more_kernel(held, before, rows, total):
    total[...] = before[...] + turned_product(held[...], rows[...])


def more_product(held, before, rows):
    vmem = pl.BlockSpec(memory_space=pltpu.VMEM)
    return pl.pallas_call(
        more_kernel,
        out_shape=jax.ShapeDtypeStruct(before.shape, jnp.float32),
        in_specs=[vmem] * 3,
        out_specs=vmem,
        compiler_params=memory(16),
        cost_estimate=pl.CostEstimate(
            flops=2 * held.shape[0] * held.shape[1] * rows.shape[1],
            bytes_accessed=2 * held.shape[0] * held.shape[1] + 8 * before.size,
            transcendentals=0,
        ),
        name="more_product",
    )(held, before, rows)


def late_kernel(core, held, before, rows, *outs):
    *outs, total = outs
    total[...] = before[...] + turned_product(held[...], rows[...])
    size = outs[0].shape[0]
    for index, out in enumerate(outs):
        first = (core[0] ^ (1 - index // 2)) * 2 * size + index % 2 * size
        here = pl.ds(pl.multiple_of(first, size), size)
        out[...] = total[here, :].astype(out.dtype)


def late_product(core, held, before, rows):
    size, width = before.shape[0] // 4, before.shape[1]
    spec = pl.BlockSpec(memory_space=pltpu.VMEM)
    send = jax.ShapeDtypeStruct((size, width), jnp.bfloat16)
    keep = jax.ShapeDtypeStruct((size, width), jnp.float32)
    outs = pl.pallas_call(
        late_kernel,
        out_shape=(send, send, keep, keep),
        in_specs=[pl.BlockSpec(memory_space=pltpu.SMEM)] + [spec] * 3,
        out_specs=(spec,) * 4,
        scratch_shapes=[pltpu.VMEM(before.shape, jnp.float32)],
        compiler_params=memory(16),
        cost_estimate=pl.CostEstimate(
            flops=2 * held.shape[0] * held.shape[1] * width,
            bytes_accessed=2 * held.shape[0] * held.shape[1] + 16 * size * width,
            transcendentals=0,
        ),
        name="late_product",
    )(core.reshape(1), held, before, rows)
    return outs[:2], outs[2:]


def pixel_kernel(count, bits, where, places, wanted, cotangent, above, below, mixing, weight,
                 spectra, out, *refs):
    quarters, refs = refs[: len(bits)], refs[len(bits) :]
    table, scale, sums, near, names, held, sems = refs
    start, chan = where[0], where[1]
    tile_rows, half = cotangent.shape[0], table.shape[1]
    listed = names.shape[0]
    first_name = pl.multiple_of(start // listed * listed, listed)
    copies = [
        pltpu.make_async_copy(places, near, sems.at[len(bits)]),
        pltpu.make_async_copy(wanted.at[pl.ds(first_name, listed)], names, sems.at[len(bits) + 1]),
    ]
    parts = quarter_copies(spectra, held, sems, chan, bits)
    for copy in copies + parts:
        copy.start()

    def fill(first, values):
        values = values.astype(jnp.float32)
        for side in range(2):
            table[pl.ds(2 * first + side, values.shape[0], stride=2), :] = values[
                :, side * half : (side + 1) * half
            ]

    for side in range(2):
        scale[pl.ds(side, NEIGH, stride=2), :] = mixing[:, side * half : (side + 1) * half]
    scales = [scale[2 * k : 2 * k + 2, :] for k in range(NEIGH)]
    fill(0, above[...])
    fill(HALO + tile_rows, below[...])
    for first in range(0, tile_rows, 256):
        fill(HALO + first, cotangent[first : first + 256, :])
    project_rows(parts, held, weight, quarters)
    for copy in copies:
        copy.wait()

    group = 32
    offset = start - first_name

    def body(turn, carry):
        base = turn * group
        totals = []
        for n in range(group):
            pixel = names[offset + base + n]
            terms = [table[pl.ds(2 * (pixel + HALO), 2), :]]
            for k in range(NEIGH // 2):
                pair = near[k * tile_rows + pixel]
                for place, scale in ((pair & 0xFFFF, k), (pair >> 16, k + NEIGH // 2)):
                    terms.append(table[pl.ds(place, 2), :] * scales[scale])
            while len(terms) > 1:
                pairs = [x + y for x, y in zip(terms[::2], terms[1::2])]
                terms = pairs + terms[len(terms) // 2 * 2 :]
            totals += terms
        for n, total in enumerate(totals):
            sums[pl.ds(2 * (base + n), 2), :] = total
        return carry

    lax.fori_loop(0, count // group, body, 0)
    for side in range(2):
        out[:, side * half : (side + 1) * half] = sums[pl.ds(side, count, stride=2), :].astype(
            out.dtype
        )


def pixel_rows(
    cotangent, above, below, places, mixing, wanted, start, count, spectra, weight, chan, bits
):
    tile_rows, width = cotangent.shape
    depth, rows = spectra.shape[1], spectra.shape[0] // 4
    listed = min(wanted.shape[0], 1024)
    anywhere = pl.BlockSpec(memory_space=pl.ANY)
    vmem = pl.BlockSpec(memory_space=pltpu.VMEM)
    return pl.pallas_call(
        functools.partial(pixel_kernel, count, bits),
        out_shape=(
            jax.ShapeDtypeStruct((count, width), jnp.bfloat16),
            *[jax.ShapeDtypeStruct((rows, width), jnp.bfloat16)] * len(bits),
        ),
        in_specs=[
            pl.BlockSpec(memory_space=pltpu.SMEM),
            anywhere,
            anywhere,
            *[vmem] * 5,
            pl.BlockSpec(memory_space=pltpu.HBM),
        ],
        out_specs=(vmem,) * (1 + len(bits)),
        scratch_shapes=[
            pltpu.VMEM((2 * (tile_rows + 2 * HALO), width // 2), jnp.float32),
            pltpu.VMEM((2 * NEIGH, width // 2), jnp.float32),
            pltpu.VMEM((2 * count, width // 2), jnp.float32),
            pltpu.SMEM(places.shape, jnp.int32),
            pltpu.SMEM((listed,), jnp.int32),
            pltpu.VMEM((max(len(bits), 1) * rows, depth), jnp.bfloat16),
            pltpu.SemaphoreType.DMA((len(bits) + 2,)),
        ],
        compiler_params=memory(47),
        cost_estimate=pl.CostEstimate(
            flops=8 * NEIGH * count * 2048 * width,
            bytes_accessed=4 * tile_rows * width,
            transcendentals=0,
        ),
        name="pixel_rows",
    )(
        jnp.stack([start, chan]), places, wanted, cotangent, above, below, mixing, weight, spectra
    )


def gradient_kernel(where, keep, near, far, tiles, weights, mine, answers, out):
    tile, chan = where[0], where[1]
    rows = out.shape[0]
    size = tiles.shape[1]
    count = rows // size
    group = 8 // count
    wide = jnp.float32
    first = pl.multiple_of(chan // group * 8, 8)

    def columns(values):
        turned = values[pl.ds(first, 8), :].T
        places = [turned[:, n * count : (n + 1) * count] for n in range(group)]
        picked = places[0]
        for n in range(1, group):
            picked = jnp.where(chan % group == n, places[n], picked)
        return picked

    own = columns(tiles).astype(wide)
    factors = columns(weights)
    for n in range(count):
        here = slice(n * size, (n + 1) * size)
        pre = keep[here, :].astype(wide) + near[here, :].astype(wide) + far[here, :].astype(wide)
        sigma = jax.nn.sigmoid(pre)
        deriv = sigma * (1.0 + pre * (1.0 - sigma))
        fetched = jnp.where(
            own[:, n : n + 1] == tile.astype(wide),
            mine[here, :].astype(wide),
            answers[here, :].astype(wide),
        )
        out[here, :] = (factors[:, n : n + 1] * deriv * fetched).astype(out.dtype)


def pre_gradient(tile, chan, keep, near, far, tiles, weights, mine, answers):
    spec = pl.BlockSpec(memory_space=pltpu.VMEM)
    tiles, weights = tiles.reshape(-1, 128), weights.reshape(-1, 128)
    return pl.pallas_call(
        gradient_kernel,
        out_shape=jax.ShapeDtypeStruct(far.shape, jnp.bfloat16),
        in_specs=[pl.BlockSpec(memory_space=pltpu.SMEM)] + [spec] * 7,
        out_specs=spec,
        compiler_params=memory(16),
        name="pre_gradient",
    )(jnp.stack([tile, chan]), keep, near, far, tiles, weights, mine, answers)


def collect_kernel(core, *refs):
    *pieces, out = refs
    half, rows = out.shape[0] // 2, pieces[0].shape[0]
    count = len(pieces) // 2
    for index, piece in enumerate(pieces):
        which = core[0] if index < count else 1 - core[0]
        first = which * half + (index % count) * rows
        out[pl.ds(pl.multiple_of(first, rows), rows), :] = piece[...].astype(jnp.float32)


def collect(core, own, received):
    spec = pl.BlockSpec(memory_space=pltpu.VMEM)
    pieces = [*own, *received]
    rows, width = sum(piece.shape[0] for piece in pieces), own[0].shape[1]
    return pl.pallas_call(
        collect_kernel,
        out_shape=jax.ShapeDtypeStruct((rows, width), jnp.float32),
        in_specs=[pl.BlockSpec(memory_space=pltpu.SMEM)] + [spec] * len(pieces),
        out_specs=spec,
        compiler_params=memory(16),
        name="collect",
    )(core.reshape(1), *pieces)


def add_kernel(first, second, out):
    out[...] = (first[...].astype(jnp.float32) + second[...].astype(jnp.float32)).astype(out.dtype)


def added(first, second):
    spec = pl.BlockSpec(memory_space=pltpu.VMEM)
    return pl.pallas_call(
        add_kernel,
        out_shape=jax.ShapeDtypeStruct(first.shape, jnp.bfloat16),
        in_specs=[spec, spec],
        out_specs=spec,
        compiler_params=memory(16),
        name="added",
    )(first, second)


def sum_over_panels(core, parts, received):
    both = ("obs", "pix")
    parts = [added(part, other) for part, other in zip(parts, received)]
    for order in ((4, 1), (1, 4)):
        perm = [(i, i ^ order[(i >> 1) & 1]) for i in range(8)]
        parts = [added(part, lax.ppermute(part, both, perm)) for part in parts]
    return collect(core, parts, [swap(part, "obs", 1) for part in parts])


def shards(spectra, enc_weight, pix_tile, pix_local, foot_weight, cotangent, adjoint, mixing):
    tile_count = lax.axis_size("pix")
    tile_rows = cotangent.shape[0]
    quarter = spectra.shape[0] // lax.axis_size("chan")
    tile = lax.axis_index("pix")
    chan = lax.axis_index("chan")
    first_row = chan * quarter

    near_first = swap(project(spectra, enc_weight, chan, (2,), LARGE + 2)[0], "chan", 1)
    places = (adjoint - (tile * tile_rows - HALO)) * 2
    places = (places[: NEIGH // 2] | (places[NEIGH // 2 :] << 16)).reshape(-1)

    above, below = edges(cotangent, "pix", HALO)
    capacity = 2 * quarter // tile_count
    pixels = (cotangent, above, below, places, mixing)
    rest = (spectra, enc_weight)
    paired = capacity >= quarter and tile_count == 2
    if paired:
        wanted, start, count = swap(pix_local, "pix", 1), first_row, quarter
    else:
        tile_ids = lax.dynamic_slice_in_dim(pix_tile[:, 0], first_row, quarter, 0)
        local_ids = lax.dynamic_slice_in_dim(pix_local, first_row, quarter, 0)
        slot_index, wanted = requests(tile_ids, local_ids, capacity)
        start, count = 0 * chan, wanted.shape[0]
    rows, shared, send = pixel_rows(*pixels, wanted, start, count, *rest, chan, (3, 1))
    near_first, rows = lax.optimization_barrier((near_first, rows))
    passed_on = (shared.astype(jnp.float32) + near_first.astype(jnp.float32)).astype(jnp.bfloat16)
    passed_on, send, rows, later = lax.optimization_barrier((passed_on, send, rows, chan))
    far = swap(passed_on, "chan", 3)
    near = swap(send, "chan", 1)
    (keep,) = project(*rest, later, (0,), LARGE)
    if paired:
        answers = swap(rows, "pix", 1)
        (mine,) = pixel_rows(*pixels, pix_local, later * quarter, count, *rest, later, ())
    else:
        answers = lax.all_to_all(
            rows.reshape(tile_count, capacity, -1), "pix", split_axis=0, concat_axis=0, tiled=True
        )
        mine = answers = jnp.take(answers.reshape(tile_count * capacity, -1), slot_index, axis=0)
    grads = pre_gradient(tile, chan, keep, near, far, pix_tile, foot_weight, mine, answers)

    across = swap(grads, "chan", 3)
    beside = swap(grads, "chan", 1)
    last = swap(across, "chan", 1)
    early, held, held_last = early_product(spectra, chan, grads, across)
    early = more_product(held, early, beside)
    core = lax.axis_index("obs") & 1
    send, keep = late_product(core, held_last, early, last)
    if lax.axis_size("obs") == 4 and tile_count == 2:
        return sum_over_panels(core, keep, [swap(part, "obs", 1) for part in send])
    return lax.psum(collect(core, keep, send), ("obs", "pix"))


def solution(mesh):
    return jax.shard_map(
        shards,
        mesh=mesh,
        in_specs=(
            P(("obs", "pix"), "chan"),
            P("chan", None),
            P(("obs", "pix"), None),
            P(("obs", "pix")),
            P(("obs", "pix")),
            P("pix", None),
            P(None, "pix"),
            P(),
        ),
        out_specs=P("chan", None),
        check_vma=False,
    )
```

```python
import functools

import jax
import jax.numpy as jnp
from jax import lax
from jax.experimental import pallas as pl
from jax.experimental.pallas import tpu as pltpu
from jax.sharding import PartitionSpec as P

NEIGH = 8
HALO = 128
MIB = 1024 * 1024
LARGE = 52


def edges(value, axis, width):
    size, length = lax.axis_size(axis), value.shape[0]
    last = lax.slice_in_dim(value, length - width, length, axis=0)
    first = lax.slice_in_dim(value, 0, width, axis=0)
    if size == 2:
        index = lax.axis_index(axis)
        other = lax.ppermute(jnp.where(index == 0, last, first), axis, [(0, 1), (1, 0)])
        return other, other
    up = [(i, i + 1) for i in range(size - 1)]
    return lax.ppermute(last, axis, up), lax.ppermute(first, axis, [(j, i) for i, j in up])


def requests(tile_ids, local_ids, capacity):
    tile_count = lax.axis_size("pix")
    onehot = (tile_ids[:, None] == jnp.arange(tile_count, dtype=jnp.int32)[None, :]).astype(
        jnp.int32
    )
    place_rank = jnp.sum((jnp.cumsum(onehot, axis=0) - 1) * onehot, axis=1)
    slot_index = tile_ids * capacity + place_rank
    outgoing = jnp.full((tile_count * capacity,), 0, jnp.int32).at[slot_index].set(local_ids)
    outgoing = outgoing.reshape(tile_count, capacity)
    requested = lax.all_to_all(outgoing, "pix", split_axis=0, concat_axis=0, tiled=True)
    return slot_index, requested.reshape(-1)


def swap(value, axis, bit):
    size = 1
    for name in (axis,) if isinstance(axis, str) else axis:
        size *= lax.axis_size(name)
    return lax.ppermute(value, axis, [(i, i ^ bit) for i in range(size)])


def memory(mib):
    return pltpu.CompilerParams(vmem_limit_bytes=mib * MIB)


def quarter_copies(spectra, held, sems, chan, bits):
    rows = spectra.shape[0] // 4
    return [
        pltpu.make_async_copy(
            spectra.at[pl.ds(pl.multiple_of((chan ^ bit) * rows, rows), rows)],
            held.at[pl.ds(turn * rows, rows)],
            sems.at[turn],
        )
        for turn, bit in enumerate(bits)
    ]


def project_rows(copies, held, weight, outs):
    rows = outs[0].shape[0] if outs else 0
    for turn, (copy, out) in enumerate(zip(copies, outs)):
        copy.wait()
        result = jnp.dot(
            held[turn * rows : (turn + 1) * rows, :],
            weight[...],
            preferred_element_type=jnp.float32,
        )
        out[...] = result.astype(out.dtype)


def project_kernel(bits, chan, spectra, weight, *refs):
    *outs, held, near, sems = refs
    copies = [pltpu.make_async_copy(weight, near, sems.at[len(bits)])]
    copies += quarter_copies(spectra, held, sems, chan[0], bits)
    for copy in copies:
        copy.start()
    copies[0].wait()
    project_rows(copies[1:], held, near, outs)


def project(spectra, weight, chan, bits, grant):
    depth, width = weight.shape
    rows = spectra.shape[0] // 4
    hbm = pl.BlockSpec(memory_space=pltpu.HBM)
    return pl.pallas_call(
        functools.partial(project_kernel, bits),
        out_shape=(jax.ShapeDtypeStruct((rows, width), jnp.bfloat16),) * len(bits),
        in_specs=[pl.BlockSpec(memory_space=pltpu.SMEM), hbm, hbm],
        out_specs=(pl.BlockSpec(memory_space=pltpu.VMEM),) * len(bits),
        scratch_shapes=[
            pltpu.VMEM((len(bits) * rows, depth), jnp.bfloat16),
            pltpu.VMEM((depth, width), jnp.bfloat16),
            pltpu.SemaphoreType.DMA((len(bits) + 1,)),
        ],
        compiler_params=memory(grant),
        cost_estimate=pl.CostEstimate(
            flops=2 * len(bits) * rows * depth * width,
            bytes_accessed=2 * len(bits) * rows * (depth + width) + 2 * depth * width,
            transcendentals=0,
        ),
        name="project",
    )(chan.reshape(1), spectra, weight)


def turned_product(left, right):
    return lax.dot_general(
        left, right, (((0,), (0,)), ((), ())), preferred_element_type=jnp.float32
    )


def early_kernel(chan, spectra, first, second, total, third, fourth, held, sems):
    rows = first.shape[0]
    targets = (held.at[pl.ds(0, rows)], held.at[pl.ds(rows, rows)], third, fourth)
    copies = []
    for turn, (bits, target) in enumerate(zip((0, 3, 1, 2), targets)):
        start = pl.multiple_of((chan[0] ^ bits) * rows, rows)
        copies.append(pltpu.make_async_copy(spectra.at[pl.ds(start, rows)], target, sems.at[turn]))
    for copy in copies:
        copy.start()
    copies[0].wait()
    product = turned_product(held[:rows, :], first[...])
    copies[1].wait()
    total[...] = product + turned_product(held[rows:, :], second[...])
    copies[2].wait()
    copies[3].wait()


def early_product(spectra, chan, first, second):
    depth = spectra.shape[1]
    rows, width = first.shape
    vmem = pl.BlockSpec(memory_space=pltpu.VMEM)
    return pl.pallas_call(
        early_kernel,
        out_shape=(
            jax.ShapeDtypeStruct((depth, width), jnp.float32),
            jax.ShapeDtypeStruct((rows, depth), jnp.bfloat16),
            jax.ShapeDtypeStruct((rows, depth), jnp.bfloat16),
        ),
        in_specs=[
            pl.BlockSpec(memory_space=pltpu.SMEM),
            pl.BlockSpec(memory_space=pltpu.HBM),
            vmem,
            vmem,
        ],
        out_specs=(vmem,) * 3,
        scratch_shapes=[
            pltpu.VMEM((2 * rows, depth), jnp.bfloat16),
            pltpu.SemaphoreType.DMA((4,)),
        ],
        compiler_params=memory(48),
        cost_estimate=pl.CostEstimate(
            flops=4 * rows * depth * width,
            bytes_accessed=8 * rows * depth + 4 * depth * width,
            transcendentals=0,
        ),
        name="early_product",
    )(chan.reshape(1), spectra, first, second)


def more_kernel(held, before, rows, total):
    total[...] = before[...] + turned_product(held[...], rows[...])


def more_product(held, before, rows):
    vmem = pl.BlockSpec(memory_space=pltpu.VMEM)
    return pl.pallas_call(
        more_kernel,
        out_shape=jax.ShapeDtypeStruct(before.shape, jnp.float32),
        in_specs=[vmem] * 3,
        out_specs=vmem,
        compiler_params=memory(16),
        cost_estimate=pl.CostEstimate(
            flops=2 * held.shape[0] * held.shape[1] * rows.shape[1],
            bytes_accessed=2 * held.shape[0] * held.shape[1] + 8 * before.size,
            transcendentals=0,
        ),
        name="more_product",
    )(held, before, rows)


def late_kernel(core, held, before, rows, *outs):
    *outs, total = outs
    total[...] = before[...] + turned_product(held[...], rows[...])
    size = outs[0].shape[0]
    for index, out in enumerate(outs):
        first = (core[0] ^ (1 - index // 2)) * 2 * size + index % 2 * size
        here = pl.ds(pl.multiple_of(first, size), size)
        out[...] = total[here, :].astype(out.dtype)


def late_product(core, held, before, rows):
    size, width = before.shape[0] // 4, before.shape[1]
    spec = pl.BlockSpec(memory_space=pltpu.VMEM)
    send = jax.ShapeDtypeStruct((size, width), jnp.bfloat16)
    keep = jax.ShapeDtypeStruct((size, width), jnp.float32)
    outs = pl.pallas_call(
        late_kernel,
        out_shape=(send, send, keep, keep),
        in_specs=[pl.BlockSpec(memory_space=pltpu.SMEM)] + [spec] * 3,
        out_specs=(spec,) * 4,
        scratch_shapes=[pltpu.VMEM(before.shape, jnp.float32)],
        compiler_params=memory(16),
        cost_estimate=pl.CostEstimate(
            flops=2 * held.shape[0] * held.shape[1] * width,
            bytes_accessed=2 * held.shape[0] * held.shape[1] + 16 * size * width,
            transcendentals=0,
        ),
        name="late_product",
    )(core.reshape(1), held, before, rows)
    return outs[:2], outs[2:]


def pixel_kernel(count, bits, where, places, wanted, cotangent, above, below, mixing, weight,
                 spectra, out, *refs):
    quarters, refs = refs[: len(bits)], refs[len(bits) :]
    table, scale, sums, near, names, held, tile, sems = refs
    start, chan = where[0], where[1]
    tile_rows, half = tile.shape[0], table.shape[1]
    listed = names.shape[0]
    first_name = pl.multiple_of(start // listed * listed, listed)
    copies = [
        pltpu.make_async_copy(places, near, sems.at[len(bits)]),
        pltpu.make_async_copy(wanted.at[pl.ds(first_name, listed)], names, sems.at[len(bits) + 1]),
    ]
    parts = quarter_copies(spectra, held, sems, chan, bits)
    chunk = tile_rows // 4
    rows = [
        pltpu.make_async_copy(
            cotangent.at[pl.ds(n * chunk, chunk)],
            tile.at[pl.ds(n * chunk, chunk)],
            sems.at[len(bits) + 2 + n],
        )
        for n in range(4)
    ]
    for copy in copies + rows + parts:
        copy.start()

    def fill(first, values):
        values = values.astype(jnp.float32)
        for side in range(2):
            table[pl.ds(2 * first + side, values.shape[0], stride=2), :] = values[
                :, side * half : (side + 1) * half
            ]

    for side in range(2):
        scale[pl.ds(side, NEIGH, stride=2), :] = mixing[:, side * half : (side + 1) * half]
    scales = [scale[2 * k : 2 * k + 2, :] for k in range(NEIGH)]
    fill(0, above[...])
    fill(HALO + tile_rows, below[...])
    for n in range(4):
        rows[n].wait()
        for first in range(n * chunk, (n + 1) * chunk, 256):
            fill(HALO + first, tile[first : first + 256, :])
    project_rows(parts, held, weight, quarters)
    for copy in copies:
        copy.wait()

    group = 32
    offset = start - first_name

    def body(turn, carry):
        base = turn * group
        totals = []
        for n in range(group):
            pixel = names[offset + base + n]
            terms = [table[pl.ds(2 * (pixel + HALO), 2), :]]
            for k in range(NEIGH // 2):
                pair = near[k * tile_rows + pixel]
                for place, scale in ((pair & 0xFFFF, k), (pair >> 16, k + NEIGH // 2)):
                    terms.append(table[pl.ds(place, 2), :] * scales[scale])
            while len(terms) > 1:
                pairs = [x + y for x, y in zip(terms[::2], terms[1::2])]
                terms = pairs + terms[len(terms) // 2 * 2 :]
            totals += terms
        for n, total in enumerate(totals):
            sums[pl.ds(2 * (base + n), 2), :] = total
        return carry

    lax.fori_loop(0, count // group, body, 0)
    for side in range(2):
        out[:, side * half : (side + 1) * half] = sums[pl.ds(side, count, stride=2), :].astype(
            out.dtype
        )


def pixel_rows(
    cotangent, above, below, places, mixing, wanted, start, count, spectra, weight, chan, bits
):
    tile_rows, width = cotangent.shape
    depth, rows = spectra.shape[1], spectra.shape[0] // 4
    listed = min(wanted.shape[0], 1024)
    anywhere = pl.BlockSpec(memory_space=pl.ANY)
    hbm = pl.BlockSpec(memory_space=pltpu.HBM)
    vmem = pl.BlockSpec(memory_space=pltpu.VMEM)
    return pl.pallas_call(
        functools.partial(pixel_kernel, count, bits),
        out_shape=(
            jax.ShapeDtypeStruct((count, width), jnp.bfloat16),
            *[jax.ShapeDtypeStruct((rows, width), jnp.bfloat16)] * len(bits),
        ),
        in_specs=[
            pl.BlockSpec(memory_space=pltpu.SMEM),
            anywhere,
            anywhere,
            hbm,
            *[vmem] * 4,
            hbm,
        ],
        out_specs=(vmem,) * (1 + len(bits)),
        scratch_shapes=[
            pltpu.VMEM((2 * (tile_rows + 2 * HALO), width // 2), jnp.float32),
            pltpu.VMEM((2 * NEIGH, width // 2), jnp.float32),
            pltpu.VMEM((2 * count, width // 2), jnp.float32),
            pltpu.SMEM(places.shape, jnp.int32),
            pltpu.SMEM((listed,), jnp.int32),
            pltpu.VMEM((max(len(bits), 1) * rows, depth), jnp.bfloat16),
            pltpu.VMEM(cotangent.shape, cotangent.dtype),
            pltpu.SemaphoreType.DMA((len(bits) + 6,)),
        ],
        compiler_params=memory(LARGE),
        cost_estimate=pl.CostEstimate(
            flops=8 * NEIGH * count * 2048 * width,
            bytes_accessed=4 * tile_rows * width,
            transcendentals=0,
        ),
        name="pixel_rows",
    )(
        jnp.stack([start, chan]), places, wanted, cotangent, above, below, mixing, weight, spectra
    )


def gradient_kernel(where, keep, near, far, tiles, weights, mine, answers, out):
    tile, chan = where[0], where[1]
    rows = out.shape[0]
    size = tiles.shape[1]
    count = rows // size
    group = 8 // count
    wide = jnp.float32
    first = pl.multiple_of(chan // group * 8, 8)

    def columns(values):
        turned = values[pl.ds(first, 8), :].T
        places = [turned[:, n * count : (n + 1) * count] for n in range(group)]
        picked = places[0]
        for n in range(1, group):
            picked = jnp.where(chan % group == n, places[n], picked)
        return picked

    own = columns(tiles).astype(wide)
    factors = columns(weights)
    for n in range(count):
        here = slice(n * size, (n + 1) * size)
        pre = keep[here, :].astype(wide) + near[here, :].astype(wide) + far[here, :].astype(wide)
        sigma = jax.nn.sigmoid(pre)
        deriv = sigma * (1.0 + pre * (1.0 - sigma))
        fetched = jnp.where(
            own[:, n : n + 1] == tile.astype(wide),
            mine[here, :].astype(wide),
            answers[here, :].astype(wide),
        )
        out[here, :] = (factors[:, n : n + 1] * deriv * fetched).astype(out.dtype)


def pre_gradient(tile, chan, keep, near, far, tiles, weights, mine, answers):
    spec = pl.BlockSpec(memory_space=pltpu.VMEM)
    tiles, weights = tiles.reshape(-1, 128), weights.reshape(-1, 128)
    return pl.pallas_call(
        gradient_kernel,
        out_shape=jax.ShapeDtypeStruct(far.shape, jnp.bfloat16),
        in_specs=[pl.BlockSpec(memory_space=pltpu.SMEM)] + [spec] * 7,
        out_specs=spec,
        compiler_params=memory(16),
        name="pre_gradient",
    )(jnp.stack([tile, chan]), keep, near, far, tiles, weights, mine, answers)


def collect_kernel(core, *refs):
    *pieces, out = refs
    half, rows = out.shape[0] // 2, pieces[0].shape[0]
    count = len(pieces) // 2
    for index, piece in enumerate(pieces):
        which = core[0] if index < count else 1 - core[0]
        first = which * half + (index % count) * rows
        out[pl.ds(pl.multiple_of(first, rows), rows), :] = piece[...].astype(jnp.float32)


def collect(core, own, received):
    spec = pl.BlockSpec(memory_space=pltpu.VMEM)
    pieces = [*own, *received]
    rows, width = sum(piece.shape[0] for piece in pieces), own[0].shape[1]
    return pl.pallas_call(
        collect_kernel,
        out_shape=jax.ShapeDtypeStruct((rows, width), jnp.float32),
        in_specs=[pl.BlockSpec(memory_space=pltpu.SMEM)] + [spec] * len(pieces),
        out_specs=spec,
        compiler_params=memory(16),
        name="collect",
    )(core.reshape(1), *pieces)


def add_kernel(first, second, out):
    out[...] = (first[...].astype(jnp.float32) + second[...].astype(jnp.float32)).astype(out.dtype)


def added(first, second):
    spec = pl.BlockSpec(memory_space=pltpu.VMEM)
    return pl.pallas_call(
        add_kernel,
        out_shape=jax.ShapeDtypeStruct(first.shape, jnp.bfloat16),
        in_specs=[spec, spec],
        out_specs=spec,
        compiler_params=memory(16),
        name="added",
    )(first, second)


def sum_over_panels(core, parts, received):
    both = ("obs", "pix")
    parts = [added(part, other) for part, other in zip(parts, received)]
    for order in ((4, 1), (1, 4)):
        perm = [(i, i ^ order[(i >> 1) & 1]) for i in range(8)]
        parts = [added(part, lax.ppermute(part, both, perm)) for part in parts]
    return collect(core, parts, [swap(part, "obs", 1) for part in parts])


def shards(spectra, enc_weight, pix_tile, pix_local, foot_weight, cotangent, adjoint, mixing):
    tile_count = lax.axis_size("pix")
    tile_rows = cotangent.shape[0]
    quarter = spectra.shape[0] // lax.axis_size("chan")
    tile = lax.axis_index("pix")
    chan = lax.axis_index("chan")
    first_row = chan * quarter

    near_first = swap(project(spectra, enc_weight, chan, (2,), LARGE + 4)[0], "chan", 1)
    places = (adjoint - (tile * tile_rows - HALO)) * 2
    places = (places[: NEIGH // 2] | (places[NEIGH // 2 :] << 16)).reshape(-1)

    above, below = edges(cotangent, "pix", HALO)
    capacity = 2 * quarter // tile_count
    pixels = (cotangent, above, below, places, mixing)
    rest = (spectra, enc_weight)
    paired = capacity >= quarter and tile_count == 2
    if paired:
        wanted, start, count = swap(pix_local, "pix", 1), first_row, quarter
    else:
        tile_ids = lax.dynamic_slice_in_dim(pix_tile[:, 0], first_row, quarter, 0)
        local_ids = lax.dynamic_slice_in_dim(pix_local, first_row, quarter, 0)
        slot_index, wanted = requests(tile_ids, local_ids, capacity)
        start, count = 0 * chan, wanted.shape[0]
    rows, shared, send = pixel_rows(*pixels, wanted, start, count, *rest, chan, (3, 1))
    near_first, rows = lax.optimization_barrier((near_first, rows))
    passed_on = (shared.astype(jnp.float32) + near_first.astype(jnp.float32)).astype(jnp.bfloat16)
    passed_on, send, rows, later = lax.optimization_barrier((passed_on, send, rows, chan))
    far = swap(passed_on, "chan", 3)
    near = swap(send, "chan", 1)
    (keep,) = project(*rest, later, (0,), LARGE)
    if paired:
        answers = swap(rows, "pix", 1)
        (mine,) = pixel_rows(*pixels, pix_local, later * quarter, count, *rest, later, ())
    else:
        answers = lax.all_to_all(
            rows.reshape(tile_count, capacity, -1), "pix", split_axis=0, concat_axis=0, tiled=True
        )
        mine = answers = jnp.take(answers.reshape(tile_count * capacity, -1), slot_index, axis=0)
    grads = pre_gradient(tile, chan, keep, near, far, pix_tile, foot_weight, mine, answers)

    across = swap(grads, "chan", 3)
    beside = swap(grads, "chan", 1)
    last = swap(across, "chan", 1)
    early, held, held_last = early_product(spectra, chan, grads, across)
    early = more_product(held, early, beside)
    core = lax.axis_index("obs") & 1
    send, keep = late_product(core, held_last, early, last)
    if lax.axis_size("obs") == 4 and tile_count == 2:
        return sum_over_panels(core, keep, [swap(part, "obs", 1) for part in send])
    return lax.psum(collect(core, keep, send), ("obs", "pix"))


def solution(mesh):
    return jax.shard_map(
        shards,
        mesh=mesh,
        in_specs=(
            P(("obs", "pix"), "chan"),
            P("chan", None),
            P(("obs", "pix"), None),
            P(("obs", "pix")),
            P(("obs", "pix")),
            P("pix", None),
            P(None, "pix"),
            P(),
        ),
        out_specs=P("chan", None),
        check_vma=False,
    )
```

```python
import functools

import jax
import jax.numpy as jnp
from jax import lax
from jax.experimental import pallas as pl
from jax.experimental.pallas import tpu as pltpu
from jax.sharding import PartitionSpec as P

NEIGH = 8
HALO = 128
MIB = 1024 * 1024
LARGE = 52


def edges(value, axis, width):
    size, length = lax.axis_size(axis), value.shape[0]
    last = lax.slice_in_dim(value, length - width, length, axis=0)
    first = lax.slice_in_dim(value, 0, width, axis=0)
    if size == 2:
        index = lax.axis_index(axis)
        other = lax.ppermute(jnp.where(index == 0, last, first), axis, [(0, 1), (1, 0)])
        return other, other
    up = [(i, i + 1) for i in range(size - 1)]
    return lax.ppermute(last, axis, up), lax.ppermute(first, axis, [(j, i) for i, j in up])


def requests(tile_ids, local_ids, capacity):
    tile_count = lax.axis_size("pix")
    onehot = (tile_ids[:, None] == jnp.arange(tile_count, dtype=jnp.int32)[None, :]).astype(
        jnp.int32
    )
    place_rank = jnp.sum((jnp.cumsum(onehot, axis=0) - 1) * onehot, axis=1)
    slot_index = tile_ids * capacity + place_rank
    outgoing = jnp.full((tile_count * capacity,), 0, jnp.int32).at[slot_index].set(local_ids)
    outgoing = outgoing.reshape(tile_count, capacity)
    requested = lax.all_to_all(outgoing, "pix", split_axis=0, concat_axis=0, tiled=True)
    return slot_index, requested.reshape(-1)


def swap(value, axis, bit):
    size = 1
    for name in (axis,) if isinstance(axis, str) else axis:
        size *= lax.axis_size(name)
    return lax.ppermute(value, axis, [(i, i ^ bit) for i in range(size)])


def memory(mib):
    return pltpu.CompilerParams(vmem_limit_bytes=mib * MIB)


def quarter_copies(spectra, held, sems, chan, bits):
    rows = spectra.shape[0] // 4
    return [
        pltpu.make_async_copy(
            spectra.at[pl.ds(pl.multiple_of((chan ^ bit) * rows, rows), rows)],
            held.at[pl.ds(turn * rows, rows)],
            sems.at[turn],
        )
        for turn, bit in enumerate(bits)
    ]


def project_rows(held, weight, turn, out):
    rows = out.shape[0]
    result = jnp.dot(
        held[turn * rows : (turn + 1) * rows, :], weight[...], preferred_element_type=jnp.float32
    )
    out[...] = result.astype(out.dtype)


def project_kernel(bits, chan, spectra, weight, *refs):
    *outs, held, near, sems = refs
    copies = [pltpu.make_async_copy(weight, near, sems.at[len(bits)])]
    copies += quarter_copies(spectra, held, sems, chan[0], bits)
    for copy in copies:
        copy.start()
    copies[0].wait()
    for turn, out in enumerate(outs):
        copies[turn + 1].wait()
        project_rows(held, near, turn, out)


def project(spectra, weight, chan, bits, grant):
    depth, width = weight.shape
    rows = spectra.shape[0] // 4
    hbm = pl.BlockSpec(memory_space=pltpu.HBM)
    return pl.pallas_call(
        functools.partial(project_kernel, bits),
        out_shape=(jax.ShapeDtypeStruct((rows, width), jnp.bfloat16),) * len(bits),
        in_specs=[pl.BlockSpec(memory_space=pltpu.SMEM), hbm, hbm],
        out_specs=(pl.BlockSpec(memory_space=pltpu.VMEM),) * len(bits),
        scratch_shapes=[
            pltpu.VMEM((len(bits) * rows, depth), jnp.bfloat16),
            pltpu.VMEM((depth, width), jnp.bfloat16),
            pltpu.SemaphoreType.DMA((len(bits) + 1,)),
        ],
        compiler_params=memory(grant),
        cost_estimate=pl.CostEstimate(
            flops=2 * len(bits) * rows * depth * width,
            bytes_accessed=2 * len(bits) * rows * (depth + width) + 2 * depth * width,
            transcendentals=0,
        ),
        name="project",
    )(chan.reshape(1), spectra, weight)


def turned_product(left, right):
    return lax.dot_general(
        left, right, (((0,), (0,)), ((), ())), preferred_element_type=jnp.float32
    )


def early_kernel(chan, spectra, first, second, total, third, fourth, held, sems):
    rows = first.shape[0]
    targets = (held.at[pl.ds(0, rows)], held.at[pl.ds(rows, rows)], third, fourth)
    copies = []
    for turn, (bits, target) in enumerate(zip((0, 3, 1, 2), targets)):
        start = pl.multiple_of((chan[0] ^ bits) * rows, rows)
        copies.append(pltpu.make_async_copy(spectra.at[pl.ds(start, rows)], target, sems.at[turn]))
    for copy in copies:
        copy.start()
    copies[0].wait()
    product = turned_product(held[:rows, :], first[...])
    copies[1].wait()
    total[...] = product + turned_product(held[rows:, :], second[...])
    copies[2].wait()
    copies[3].wait()


def early_product(spectra, chan, first, second):
    depth = spectra.shape[1]
    rows, width = first.shape
    vmem = pl.BlockSpec(memory_space=pltpu.VMEM)
    return pl.pallas_call(
        early_kernel,
        out_shape=(
            jax.ShapeDtypeStruct((depth, width), jnp.float32),
            jax.ShapeDtypeStruct((rows, depth), jnp.bfloat16),
            jax.ShapeDtypeStruct((rows, depth), jnp.bfloat16),
        ),
        in_specs=[
            pl.BlockSpec(memory_space=pltpu.SMEM),
            pl.BlockSpec(memory_space=pltpu.HBM),
            vmem,
            vmem,
        ],
        out_specs=(vmem,) * 3,
        scratch_shapes=[
            pltpu.VMEM((2 * rows, depth), jnp.bfloat16),
            pltpu.SemaphoreType.DMA((4,)),
        ],
        compiler_params=memory(48),
        cost_estimate=pl.CostEstimate(
            flops=4 * rows * depth * width,
            bytes_accessed=8 * rows * depth + 4 * depth * width,
            transcendentals=0,
        ),
        name="early_product",
    )(chan.reshape(1), spectra, first, second)


def more_kernel(held, before, rows, total):
    total[...] = before[...] + turned_product(held[...], rows[...])


def more_product(held, before, rows):
    vmem = pl.BlockSpec(memory_space=pltpu.VMEM)
    return pl.pallas_call(
        more_kernel,
        out_shape=jax.ShapeDtypeStruct(before.shape, jnp.float32),
        in_specs=[vmem] * 3,
        out_specs=vmem,
        compiler_params=memory(16),
        cost_estimate=pl.CostEstimate(
            flops=2 * held.shape[0] * held.shape[1] * rows.shape[1],
            bytes_accessed=2 * held.shape[0] * held.shape[1] + 8 * before.size,
            transcendentals=0,
        ),
        name="more_product",
    )(held, before, rows)


def late_kernel(core, held, before, rows, *outs):
    *outs, total = outs
    total[...] = before[...] + turned_product(held[...], rows[...])
    size = outs[0].shape[0]
    for index, out in enumerate(outs):
        first = (core[0] ^ (1 - index // 2)) * 2 * size + index % 2 * size
        here = pl.ds(pl.multiple_of(first, size), size)
        out[...] = total[here, :].astype(out.dtype)


def late_product(core, held, before, rows):
    size, width = before.shape[0] // 4, before.shape[1]
    spec = pl.BlockSpec(memory_space=pltpu.VMEM)
    send = jax.ShapeDtypeStruct((size, width), jnp.bfloat16)
    keep = jax.ShapeDtypeStruct((size, width), jnp.float32)
    outs = pl.pallas_call(
        late_kernel,
        out_shape=(send, send, keep, keep),
        in_specs=[pl.BlockSpec(memory_space=pltpu.SMEM)] + [spec] * 3,
        out_specs=(spec,) * 4,
        scratch_shapes=[pltpu.VMEM(before.shape, jnp.float32)],
        compiler_params=memory(16),
        cost_estimate=pl.CostEstimate(
            flops=2 * held.shape[0] * held.shape[1] * width,
            bytes_accessed=2 * held.shape[0] * held.shape[1] + 16 * size * width,
            transcendentals=0,
        ),
        name="late_product",
    )(core.reshape(1), held, before, rows)
    return outs[:2], outs[2:]


def pixel_kernel(count, bits, where, places, wanted, cotangent, above, below, mixing, weight,
                 spectra, out, *refs):
    quarters, refs = refs[: len(bits)], refs[len(bits) :]
    table, scale, sums, near, names, held, tile, sems = refs
    start, chan = where[0], where[1]
    tile_rows, half = tile.shape[0], table.shape[1]
    listed = names.shape[0]
    first_name = pl.multiple_of(start // listed * listed, listed)
    copies = [
        pltpu.make_async_copy(places, near, sems.at[len(bits)]),
        pltpu.make_async_copy(wanted.at[pl.ds(first_name, listed)], names, sems.at[len(bits) + 1]),
    ]
    parts = quarter_copies(spectra, held, sems, chan, bits)
    chunk = tile_rows // 4
    rows = [
        pltpu.make_async_copy(
            cotangent.at[pl.ds(n * chunk, chunk)],
            tile.at[pl.ds(n * chunk, chunk)],
            sems.at[len(bits) + 2 + n],
        )
        for n in range(4)
    ]
    order = copies + rows[:2] + parts[:1] + rows[2:] + parts[1:]
    for copy in order:
        copy.start()

    def fill(first, values):
        values = values.astype(jnp.float32)
        for side in range(2):
            table[pl.ds(2 * first + side, values.shape[0], stride=2), :] = values[
                :, side * half : (side + 1) * half
            ]

    for side in range(2):
        scale[pl.ds(side, NEIGH, stride=2), :] = mixing[:, side * half : (side + 1) * half]
    scales = [scale[2 * k : 2 * k + 2, :] for k in range(NEIGH)]
    fill(0, above[...])
    fill(HALO + tile_rows, below[...])
    for n in range(2):
        rows[2 * n].wait()
        rows[2 * n + 1].wait()
        if n < len(parts):
            parts[n].wait()
        for first in range(2 * n * chunk, 2 * (n + 1) * chunk, 256):
            fill(HALO + first, tile[first : first + 256, :])
        if n < len(parts):
            project_rows(held, weight, n, quarters[n])
    for copy in copies:
        copy.wait()

    group = 32
    offset = start - first_name

    def body(turn, carry):
        base = turn * group
        totals = []
        for n in range(group):
            pixel = names[offset + base + n]
            terms = [table[pl.ds(2 * (pixel + HALO), 2), :]]
            for k in range(NEIGH // 2):
                pair = near[k * tile_rows + pixel]
                for place, scale in ((pair & 0xFFFF, k), (pair >> 16, k + NEIGH // 2)):
                    terms.append(table[pl.ds(place, 2), :] * scales[scale])
            while len(terms) > 1:
                pairs = [x + y for x, y in zip(terms[::2], terms[1::2])]
                terms = pairs + terms[len(terms) // 2 * 2 :]
            totals += terms
        for n, total in enumerate(totals):
            sums[pl.ds(2 * (base + n), 2), :] = total
        return carry

    lax.fori_loop(0, count // group, body, 0)
    for side in range(2):
        out[:, side * half : (side + 1) * half] = sums[pl.ds(side, count, stride=2), :].astype(
            out.dtype
        )


def pixel_rows(
    cotangent, above, below, places, mixing, wanted, start, count, spectra, weight, chan, bits
):
    tile_rows, width = cotangent.shape
    depth, rows = spectra.shape[1], spectra.shape[0] // 4
    listed = min(wanted.shape[0], 1024)
    anywhere = pl.BlockSpec(memory_space=pl.ANY)
    hbm = pl.BlockSpec(memory_space=pltpu.HBM)
    vmem = pl.BlockSpec(memory_space=pltpu.VMEM)
    return pl.pallas_call(
        functools.partial(pixel_kernel, count, bits),
        out_shape=(
            jax.ShapeDtypeStruct((count, width), jnp.bfloat16),
            *[jax.ShapeDtypeStruct((rows, width), jnp.bfloat16)] * len(bits),
        ),
        in_specs=[
            pl.BlockSpec(memory_space=pltpu.SMEM),
            anywhere,
            anywhere,
            hbm,
            *[vmem] * 4,
            hbm,
        ],
        out_specs=(vmem,) * (1 + len(bits)),
        scratch_shapes=[
            pltpu.VMEM((2 * (tile_rows + 2 * HALO), width // 2), jnp.float32),
            pltpu.VMEM((2 * NEIGH, width // 2), jnp.float32),
            pltpu.VMEM((2 * count, width // 2), jnp.float32),
            pltpu.SMEM(places.shape, jnp.int32),
            pltpu.SMEM((listed,), jnp.int32),
            pltpu.VMEM((max(len(bits), 1) * rows, depth), jnp.bfloat16),
            pltpu.VMEM(cotangent.shape, cotangent.dtype),
            pltpu.SemaphoreType.DMA((len(bits) + 6,)),
        ],
        compiler_params=memory(LARGE),
        cost_estimate=pl.CostEstimate(
            flops=8 * NEIGH * count * 2048 * width,
            bytes_accessed=4 * tile_rows * width,
            transcendentals=0,
        ),
        name="pixel_rows",
    )(
        jnp.stack([start, chan]), places, wanted, cotangent, above, below, mixing, weight, spectra
    )


def gradient_kernel(where, keep, near, far, tiles, weights, mine, answers, out):
    tile, chan = where[0], where[1]
    rows = out.shape[0]
    size = tiles.shape[1]
    count = rows // size
    group = 8 // count
    wide = jnp.float32
    first = pl.multiple_of(chan // group * 8, 8)

    def columns(values):
        turned = values[pl.ds(first, 8), :].T
        places = [turned[:, n * count : (n + 1) * count] for n in range(group)]
        picked = places[0]
        for n in range(1, group):
            picked = jnp.where(chan % group == n, places[n], picked)
        return picked

    own = columns(tiles).astype(wide)
    factors = columns(weights)
    for n in range(count):
        here = slice(n * size, (n + 1) * size)
        pre = keep[here, :].astype(wide) + near[here, :].astype(wide) + far[here, :].astype(wide)
        sigma = jax.nn.sigmoid(pre)
        deriv = sigma * (1.0 + pre * (1.0 - sigma))
        fetched = jnp.where(
            own[:, n : n + 1] == tile.astype(wide),
            mine[here, :].astype(wide),
            answers[here, :].astype(wide),
        )
        out[here, :] = (factors[:, n : n + 1] * deriv * fetched).astype(out.dtype)


def pre_gradient(tile, chan, keep, near, far, tiles, weights, mine, answers):
    spec = pl.BlockSpec(memory_space=pltpu.VMEM)
    tiles, weights = tiles.reshape(-1, 128), weights.reshape(-1, 128)
    return pl.pallas_call(
        gradient_kernel,
        out_shape=jax.ShapeDtypeStruct(far.shape, jnp.bfloat16),
        in_specs=[pl.BlockSpec(memory_space=pltpu.SMEM)] + [spec] * 7,
        out_specs=spec,
        compiler_params=memory(16),
        name="pre_gradient",
    )(jnp.stack([tile, chan]), keep, near, far, tiles, weights, mine, answers)


def collect_kernel(core, *refs):
    *pieces, out = refs
    half, rows = out.shape[0] // 2, pieces[0].shape[0]
    count = len(pieces) // 2
    for index, piece in enumerate(pieces):
        which = core[0] if index < count else 1 - core[0]
        first = which * half + (index % count) * rows
        out[pl.ds(pl.multiple_of(first, rows), rows), :] = piece[...].astype(jnp.float32)


def collect(core, own, received):
    spec = pl.BlockSpec(memory_space=pltpu.VMEM)
    pieces = [*own, *received]
    rows, width = sum(piece.shape[0] for piece in pieces), own[0].shape[1]
    return pl.pallas_call(
        collect_kernel,
        out_shape=jax.ShapeDtypeStruct((rows, width), jnp.float32),
        in_specs=[pl.BlockSpec(memory_space=pltpu.SMEM)] + [spec] * len(pieces),
        out_specs=spec,
        compiler_params=memory(16),
        name="collect",
    )(core.reshape(1), *pieces)


def add_kernel(first, second, out):
    out[...] = (first[...].astype(jnp.float32) + second[...].astype(jnp.float32)).astype(out.dtype)


def added(first, second):
    spec = pl.BlockSpec(memory_space=pltpu.VMEM)
    return pl.pallas_call(
        add_kernel,
        out_shape=jax.ShapeDtypeStruct(first.shape, jnp.bfloat16),
        in_specs=[spec, spec],
        out_specs=spec,
        compiler_params=memory(16),
        name="added",
    )(first, second)


def hand_on_kernel(value, _, out):
    out[...] = value[...]


def handed_on(value, after):
    spec = pl.BlockSpec(memory_space=pltpu.VMEM)
    return pl.pallas_call(
        hand_on_kernel,
        out_shape=jax.ShapeDtypeStruct(value.shape, value.dtype),
        in_specs=[spec, spec],
        out_specs=spec,
        compiler_params=memory(16),
        name="handed_on",
    )(value, after)


def sum_over_panels(core, parts, received):
    both = ("obs", "pix")
    parts = [added(part, other) for part, other in zip(parts, received)]
    for order in ((4, 1), (1, 4)):
        perm = [(i, i ^ order[(i >> 1) & 1]) for i in range(8)]
        parts = [added(part, lax.ppermute(part, both, perm)) for part in parts]
    return collect(core, parts, [swap(part, "obs", 1) for part in parts])


def shards(spectra, enc_weight, pix_tile, pix_local, foot_weight, cotangent, adjoint, mixing):
    tile_count = lax.axis_size("pix")
    tile_rows = cotangent.shape[0]
    quarter = spectra.shape[0] // lax.axis_size("chan")
    tile = lax.axis_index("pix")
    chan = lax.axis_index("chan")
    first_row = chan * quarter

    near_first = swap(project(spectra, enc_weight, chan, (2,), LARGE + 4)[0], "chan", 1)
    places = (adjoint - (tile * tile_rows - HALO)) * 2
    places = (places[: NEIGH // 2] | (places[NEIGH // 2 :] << 16)).reshape(-1)

    above, below = edges(cotangent, "pix", HALO)
    capacity = 2 * quarter // tile_count
    pixels = (cotangent, above, below, places, mixing)
    rest = (spectra, enc_weight)
    paired = capacity >= quarter and tile_count == 2
    if paired:
        wanted, start, count = swap(pix_local, "pix", 1), first_row, quarter
    else:
        tile_ids = lax.dynamic_slice_in_dim(pix_tile[:, 0], first_row, quarter, 0)
        local_ids = lax.dynamic_slice_in_dim(pix_local, first_row, quarter, 0)
        slot_index, wanted = requests(tile_ids, local_ids, capacity)
        start, count = 0 * chan, wanted.shape[0]
    rows, shared, send = pixel_rows(*pixels, wanted, start, count, *rest, chan, (3, 1))
    near_first, rows = lax.optimization_barrier((near_first, rows))
    passed_on = (shared.astype(jnp.float32) + near_first.astype(jnp.float32)).astype(jnp.bfloat16)
    passed_on, send, rows, later = lax.optimization_barrier((passed_on, send, rows, chan))
    far = swap(passed_on, "chan", 3)
    near = swap(handed_on(send, passed_on), "chan", 1)
    (keep,) = project(*rest, later, (0,), LARGE)
    if paired:
        answers = swap(rows, "pix", 1)
        (mine,) = pixel_rows(*pixels, pix_local, later * quarter, count, *rest, later, ())
    else:
        answers = lax.all_to_all(
            rows.reshape(tile_count, capacity, -1), "pix", split_axis=0, concat_axis=0, tiled=True
        )
        mine = answers = jnp.take(answers.reshape(tile_count * capacity, -1), slot_index, axis=0)
    grads = pre_gradient(tile, chan, keep, near, far, pix_tile, foot_weight, mine, answers)

    across = swap(grads, "chan", 3)
    beside = swap(grads, "chan", 1)
    last = swap(across, "chan", 1)
    early, held, held_last = early_product(spectra, chan, grads, across)
    early = more_product(held, early, beside)
    core = lax.axis_index("obs") & 1
    send, keep = late_product(core, held_last, early, last)
    if lax.axis_size("obs") == 4 and tile_count == 2:
        return sum_over_panels(core, keep, [swap(part, "obs", 1) for part in send])
    return lax.psum(collect(core, keep, send), ("obs", "pix"))


def solution(mesh):
    return jax.shard_map(
        shards,
        mesh=mesh,
        in_specs=(
            P(("obs", "pix"), "chan"),
            P("chan", None),
            P(("obs", "pix"), None),
            P(("obs", "pix")),
            P(("obs", "pix")),
            P("pix", None),
            P(None, "pix"),
            P(),
        ),
        out_specs=P("chan", None),
        check_vma=False,
    )
```

```python
import functools

import jax
import jax.numpy as jnp
from jax import lax
from jax.experimental import pallas as pl
from jax.experimental.pallas import tpu as pltpu
from jax.sharding import PartitionSpec as P

NEIGH = 8
HALO = 128
MIB = 1024 * 1024
LARGE = 52


def edges(value, axis, width):
    size, length = lax.axis_size(axis), value.shape[0]
    last = lax.slice_in_dim(value, length - width, length, axis=0)
    first = lax.slice_in_dim(value, 0, width, axis=0)
    if size == 2:
        index = lax.axis_index(axis)
        other = lax.ppermute(jnp.where(index == 0, last, first), axis, [(0, 1), (1, 0)])
        return other, other
    up = [(i, i + 1) for i in range(size - 1)]
    return lax.ppermute(last, axis, up), lax.ppermute(first, axis, [(j, i) for i, j in up])


def requests(tile_ids, local_ids, capacity):
    tile_count = lax.axis_size("pix")
    onehot = (tile_ids[:, None] == jnp.arange(tile_count, dtype=jnp.int32)[None, :]).astype(
        jnp.int32
    )
    place_rank = jnp.sum((jnp.cumsum(onehot, axis=0) - 1) * onehot, axis=1)
    slot_index = tile_ids * capacity + place_rank
    outgoing = jnp.full((tile_count * capacity,), 0, jnp.int32).at[slot_index].set(local_ids)
    outgoing = outgoing.reshape(tile_count, capacity)
    requested = lax.all_to_all(outgoing, "pix", split_axis=0, concat_axis=0, tiled=True)
    return slot_index, requested.reshape(-1)


def swap(value, axis, bit):
    size = 1
    for name in (axis,) if isinstance(axis, str) else axis:
        size *= lax.axis_size(name)
    return lax.ppermute(value, axis, [(i, i ^ bit) for i in range(size)])


def memory(mib):
    return pltpu.CompilerParams(vmem_limit_bytes=mib * MIB)


def quarter_copies(spectra, held, sems, chan, bits):
    rows = spectra.shape[0] // 4
    return [
        pltpu.make_async_copy(
            spectra.at[pl.ds(pl.multiple_of((chan ^ bit) * rows, rows), rows)],
            held.at[pl.ds(turn * rows, rows)],
            sems.at[turn],
        )
        for turn, bit in enumerate(bits)
    ]


def project_rows(held, weight, turn, out):
    rows = out.shape[0]
    result = jnp.dot(
        held[turn * rows : (turn + 1) * rows, :], weight[...], preferred_element_type=jnp.float32
    )
    out[...] = result.astype(out.dtype)


def project_kernel(bits, chan, spectra, weight, *refs):
    *outs, held, near, sems = refs
    copies = [pltpu.make_async_copy(weight, near, sems.at[len(bits)])]
    copies += quarter_copies(spectra, held, sems, chan[0], bits)
    for copy in copies:
        copy.start()
    copies[0].wait()
    for turn, out in enumerate(outs):
        copies[turn + 1].wait()
        project_rows(held, near, turn, out)


def project(spectra, weight, chan, bits, grant):
    depth, width = weight.shape
    rows = spectra.shape[0] // 4
    hbm = pl.BlockSpec(memory_space=pltpu.HBM)
    return pl.pallas_call(
        functools.partial(project_kernel, bits),
        out_shape=(jax.ShapeDtypeStruct((rows, width), jnp.bfloat16),) * len(bits),
        in_specs=[pl.BlockSpec(memory_space=pltpu.SMEM), hbm, hbm],
        out_specs=(pl.BlockSpec(memory_space=pltpu.VMEM),) * len(bits),
        scratch_shapes=[
            pltpu.VMEM((len(bits) * rows, depth), jnp.bfloat16),
            pltpu.VMEM((depth, width), jnp.bfloat16),
            pltpu.SemaphoreType.DMA((len(bits) + 1,)),
        ],
        compiler_params=memory(grant),
        cost_estimate=pl.CostEstimate(
            flops=2 * len(bits) * rows * depth * width,
            bytes_accessed=2 * len(bits) * rows * (depth + width) + 2 * depth * width,
            transcendentals=0,
        ),
        name="project",
    )(chan.reshape(1), spectra, weight)


def turned_product(left, right):
    return lax.dot_general(
        left, right, (((0,), (0,)), ((), ())), preferred_element_type=jnp.float32
    )


def early_kernel(chan, spectra, first, second, total, third, fourth, held, sems):
    rows = first.shape[0]
    targets = (held.at[pl.ds(0, rows)], held.at[pl.ds(rows, rows)], third, fourth)
    copies = []
    for turn, (bits, target) in enumerate(zip((0, 3, 1, 2), targets)):
        start = pl.multiple_of((chan[0] ^ bits) * rows, rows)
        copies.append(pltpu.make_async_copy(spectra.at[pl.ds(start, rows)], target, sems.at[turn]))
    for copy in copies:
        copy.start()
    copies[0].wait()
    product = turned_product(held[:rows, :], first[...])
    copies[1].wait()
    total[...] = product + turned_product(held[rows:, :], second[...])
    copies[2].wait()
    copies[3].wait()


def early_product(spectra, chan, first, second):
    depth = spectra.shape[1]
    rows, width = first.shape
    vmem = pl.BlockSpec(memory_space=pltpu.VMEM)
    return pl.pallas_call(
        early_kernel,
        out_shape=(
            jax.ShapeDtypeStruct((depth, width), jnp.float32),
            jax.ShapeDtypeStruct((rows, depth), jnp.bfloat16),
            jax.ShapeDtypeStruct((rows, depth), jnp.bfloat16),
        ),
        in_specs=[
            pl.BlockSpec(memory_space=pltpu.SMEM),
            pl.BlockSpec(memory_space=pltpu.HBM),
            vmem,
            vmem,
        ],
        out_specs=(vmem,) * 3,
        scratch_shapes=[
            pltpu.VMEM((2 * rows, depth), jnp.bfloat16),
            pltpu.SemaphoreType.DMA((4,)),
        ],
        compiler_params=memory(48),
        cost_estimate=pl.CostEstimate(
            flops=4 * rows * depth * width,
            bytes_accessed=8 * rows * depth + 4 * depth * width,
            transcendentals=0,
        ),
        name="early_product",
    )(chan.reshape(1), spectra, first, second)


def more_kernel(held, before, rows, total):
    total[...] = before[...] + turned_product(held[...], rows[...])


def more_product(held, before, rows):
    vmem = pl.BlockSpec(memory_space=pltpu.VMEM)
    return pl.pallas_call(
        more_kernel,
        out_shape=jax.ShapeDtypeStruct(before.shape, jnp.float32),
        in_specs=[vmem] * 3,
        out_specs=vmem,
        compiler_params=memory(16),
        cost_estimate=pl.CostEstimate(
            flops=2 * held.shape[0] * held.shape[1] * rows.shape[1],
            bytes_accessed=2 * held.shape[0] * held.shape[1] + 8 * before.size,
            transcendentals=0,
        ),
        name="more_product",
    )(held, before, rows)


def chunks(half):
    first = half * 5 // 8 // 32 * 32
    return first, half - first


def late_kernel(core, held, before, rows, *outs):
    *outs, total = outs
    total[...] = before[...] + turned_product(held[...], rows[...])
    half = total.shape[0] // 2
    for index, out in enumerate(outs):
        size = out.shape[0]
        first = (core[0] ^ (1 - index // 2)) * half + index % 2 * (half - size)
        here = pl.ds(pl.multiple_of(first, 32), size)
        out[...] = total[here, :].astype(out.dtype)


def late_product(core, held, before, rows):
    depth, width = before.shape
    spec = pl.BlockSpec(memory_space=pltpu.VMEM)
    outs = pl.pallas_call(
        late_kernel,
        out_shape=tuple(
            jax.ShapeDtypeStruct((size, width), kind)
            for kind in (jnp.bfloat16, jnp.float32)
            for size in chunks(depth // 2)
        ),
        in_specs=[pl.BlockSpec(memory_space=pltpu.SMEM)] + [spec] * 3,
        out_specs=(spec,) * 4,
        scratch_shapes=[pltpu.VMEM(before.shape, jnp.float32)],
        compiler_params=memory(16),
        cost_estimate=pl.CostEstimate(
            flops=2 * held.shape[0] * held.shape[1] * width,
            bytes_accessed=2 * held.shape[0] * held.shape[1] + 8 * depth * width,
            transcendentals=0,
        ),
        name="late_product",
    )(core.reshape(1), held, before, rows)
    return outs[:2], outs[2:]


def pixel_kernel(count, bits, where, places, wanted, cotangent, above, below, mixing, weight,
                 spectra, out, *refs):
    quarters, refs = refs[: len(bits)], refs[len(bits) :]
    table, scale, sums, near, names, held, tile, sems = refs
    start, chan = where[0], where[1]
    tile_rows, half = tile.shape[0], table.shape[1]
    listed = names.shape[0]
    first_name = pl.multiple_of(start // listed * listed, listed)
    copies = [
        pltpu.make_async_copy(places, near, sems.at[len(bits)]),
        pltpu.make_async_copy(wanted.at[pl.ds(first_name, listed)], names, sems.at[len(bits) + 1]),
    ]
    parts = quarter_copies(spectra, held, sems, chan, bits)
    chunk = tile_rows // 4
    rows = [
        pltpu.make_async_copy(
            cotangent.at[pl.ds(n * chunk, chunk)],
            tile.at[pl.ds(n * chunk, chunk)],
            sems.at[len(bits) + 2 + n],
        )
        for n in range(4)
    ]
    order = copies + rows[:2] + parts[:1] + rows[2:] + parts[1:]
    for copy in order:
        copy.start()

    def fill(first, values):
        values = values.astype(jnp.float32)
        for side in range(2):
            table[pl.ds(2 * first + side, values.shape[0], stride=2), :] = values[
                :, side * half : (side + 1) * half
            ]

    for side in range(2):
        scale[pl.ds(side, NEIGH, stride=2), :] = mixing[:, side * half : (side + 1) * half]
    scales = [scale[2 * k : 2 * k + 2, :] for k in range(NEIGH)]
    fill(0, above[...])
    fill(HALO + tile_rows, below[...])
    for n in range(2):
        rows[2 * n].wait()
        rows[2 * n + 1].wait()
        if n < len(parts):
            parts[n].wait()
        for first in range(2 * n * chunk, 2 * (n + 1) * chunk, 256):
            fill(HALO + first, tile[first : first + 256, :])
        if n < len(parts):
            project_rows(held, weight, n, quarters[n])
    for copy in copies:
        copy.wait()

    group = 32
    offset = start - first_name

    def body(turn, carry):
        base = turn * group
        totals = []
        for n in range(group):
            pixel = names[offset + base + n]
            terms = [table[pl.ds(2 * (pixel + HALO), 2), :]]
            for k in range(NEIGH // 2):
                pair = near[k * tile_rows + pixel]
                for place, scale in ((pair & 0xFFFF, k), (pair >> 16, k + NEIGH // 2)):
                    terms.append(table[pl.ds(place, 2), :] * scales[scale])
            while len(terms) > 1:
                pairs = [x + y for x, y in zip(terms[::2], terms[1::2])]
                terms = pairs + terms[len(terms) // 2 * 2 :]
            totals += terms
        for n, total in enumerate(totals):
            sums[pl.ds(2 * (base + n), 2), :] = total
        return carry

    lax.fori_loop(0, count // group, body, 0)
    for side in range(2):
        out[:, side * half : (side + 1) * half] = sums[pl.ds(side, count, stride=2), :].astype(
            out.dtype
        )


def pixel_rows(
    cotangent, above, below, places, mixing, wanted, start, count, spectra, weight, chan, bits
):
    tile_rows, width = cotangent.shape
    depth, rows = spectra.shape[1], spectra.shape[0] // 4
    listed = min(wanted.shape[0], 1024)
    anywhere = pl.BlockSpec(memory_space=pl.ANY)
    hbm = pl.BlockSpec(memory_space=pltpu.HBM)
    vmem = pl.BlockSpec(memory_space=pltpu.VMEM)
    return pl.pallas_call(
        functools.partial(pixel_kernel, count, bits),
        out_shape=(
            jax.ShapeDtypeStruct((count, width), jnp.bfloat16),
            *[jax.ShapeDtypeStruct((rows, width), jnp.bfloat16)] * len(bits),
        ),
        in_specs=[
            pl.BlockSpec(memory_space=pltpu.SMEM),
            anywhere,
            anywhere,
            hbm,
            *[vmem] * 4,
            hbm,
        ],
        out_specs=(vmem,) * (1 + len(bits)),
        scratch_shapes=[
            pltpu.VMEM((2 * (tile_rows + 2 * HALO), width // 2), jnp.float32),
            pltpu.VMEM((2 * NEIGH, width // 2), jnp.float32),
            pltpu.VMEM((2 * count, width // 2), jnp.float32),
            pltpu.SMEM(places.shape, jnp.int32),
            pltpu.SMEM((listed,), jnp.int32),
            pltpu.VMEM((max(len(bits), 1) * rows, depth), jnp.bfloat16),
            pltpu.VMEM(cotangent.shape, cotangent.dtype),
            pltpu.SemaphoreType.DMA((len(bits) + 6,)),
        ],
        compiler_params=memory(LARGE),
        cost_estimate=pl.CostEstimate(
            flops=8 * NEIGH * count * 2048 * width,
            bytes_accessed=4 * tile_rows * width,
            transcendentals=0,
        ),
        name="pixel_rows",
    )(
        jnp.stack([start, chan]), places, wanted, cotangent, above, below, mixing, weight, spectra
    )


def gradient_kernel(where, keep, near, far, tiles, weights, mine, answers, out):
    tile, chan = where[0], where[1]
    rows = out.shape[0]
    size = tiles.shape[1]
    count = rows // size
    group = 8 // count
    wide = jnp.float32
    first = pl.multiple_of(chan // group * 8, 8)

    def columns(values):
        turned = values[pl.ds(first, 8), :].T
        places = [turned[:, n * count : (n + 1) * count] for n in range(group)]
        picked = places[0]
        for n in range(1, group):
            picked = jnp.where(chan % group == n, places[n], picked)
        return picked

    own = columns(tiles).astype(wide)
    factors = columns(weights)
    for n in range(count):
        here = slice(n * size, (n + 1) * size)
        pre = keep[here, :].astype(wide) + near[here, :].astype(wide) + far[here, :].astype(wide)
        sigma = jax.nn.sigmoid(pre)
        deriv = sigma * (1.0 + pre * (1.0 - sigma))
        fetched = jnp.where(
            own[:, n : n + 1] == tile.astype(wide),
            mine[here, :].astype(wide),
            answers[here, :].astype(wide),
        )
        out[here, :] = (factors[:, n : n + 1] * deriv * fetched).astype(out.dtype)


def pre_gradient(tile, chan, keep, near, far, tiles, weights, mine, answers):
    spec = pl.BlockSpec(memory_space=pltpu.VMEM)
    tiles, weights = tiles.reshape(-1, 128), weights.reshape(-1, 128)
    return pl.pallas_call(
        gradient_kernel,
        out_shape=jax.ShapeDtypeStruct(far.shape, jnp.bfloat16),
        in_specs=[pl.BlockSpec(memory_space=pltpu.SMEM)] + [spec] * 7,
        out_specs=spec,
        compiler_params=memory(16),
        name="pre_gradient",
    )(jnp.stack([tile, chan]), keep, near, far, tiles, weights, mine, answers)


def collect_kernel(core, *refs):
    *pieces, out = refs
    half = out.shape[0] // 2
    for index, piece in enumerate(pieces):
        which = core[0] if index < 2 else 1 - core[0]
        size = piece.shape[0]
        first = which * half + index % 2 * (half - size)
        out[pl.ds(pl.multiple_of(first, 32), size), :] = piece[...].astype(jnp.float32)


def collect(core, own, received):
    spec = pl.BlockSpec(memory_space=pltpu.VMEM)
    pieces = [*own, *received]
    rows, width = sum(piece.shape[0] for piece in pieces), own[0].shape[1]
    return pl.pallas_call(
        collect_kernel,
        out_shape=jax.ShapeDtypeStruct((rows, width), jnp.float32),
        in_specs=[pl.BlockSpec(memory_space=pltpu.SMEM)] + [spec] * len(pieces),
        out_specs=spec,
        compiler_params=memory(16),
        name="collect",
    )(core.reshape(1), *pieces)


def add_kernel(first, second, out):
    out[...] = (first[...].astype(jnp.float32) + second[...].astype(jnp.float32)).astype(out.dtype)


def added(first, second):
    spec = pl.BlockSpec(memory_space=pltpu.VMEM)
    return pl.pallas_call(
        add_kernel,
        out_shape=jax.ShapeDtypeStruct(first.shape, jnp.bfloat16),
        in_specs=[spec, spec],
        out_specs=spec,
        compiler_params=memory(16),
        name="added",
    )(first, second)


def sum_over_panels(core, parts, received):
    both = ("obs", "pix")
    parts = [added(part, other) for part, other in zip(parts, received)]
    for order in ((4, 1), (1, 4)):
        perm = [(i, i ^ order[(i >> 1) & 1]) for i in range(8)]
        parts = [added(part, lax.ppermute(part, both, perm)) for part in parts]
    return collect(core, parts, [swap(part, "obs", 1) for part in parts])


def shards(spectra, enc_weight, pix_tile, pix_local, foot_weight, cotangent, adjoint, mixing):
    tile_count = lax.axis_size("pix")
    tile_rows = cotangent.shape[0]
    quarter = spectra.shape[0] // lax.axis_size("chan")
    tile = lax.axis_index("pix")
    chan = lax.axis_index("chan")
    first_row = chan * quarter

    near_first = swap(project(spectra, enc_weight, chan, (2,), LARGE + 4)[0], "chan", 1)
    places = (adjoint - (tile * tile_rows - HALO)) * 2
    places = (places[: NEIGH // 2] | (places[NEIGH // 2 :] << 16)).reshape(-1)

    above, below = edges(cotangent, "pix", HALO)
    capacity = 2 * quarter // tile_count
    pixels = (cotangent, above, below, places, mixing)
    rest = (spectra, enc_weight)
    paired = capacity >= quarter and tile_count == 2
    if paired:
        wanted, start, count = swap(pix_local, "pix", 1), first_row, quarter
    else:
        tile_ids = lax.dynamic_slice_in_dim(pix_tile[:, 0], first_row, quarter, 0)
        local_ids = lax.dynamic_slice_in_dim(pix_local, first_row, quarter, 0)
        slot_index, wanted = requests(tile_ids, local_ids, capacity)
        start, count = 0 * chan, wanted.shape[0]
    rows, shared, send = pixel_rows(*pixels, wanted, start, count, *rest, chan, (3, 1))
    near_first, rows = lax.optimization_barrier((near_first, rows))
    passed_on = (shared.astype(jnp.float32) + near_first.astype(jnp.float32)).astype(jnp.bfloat16)
    passed_on, send, rows, later = lax.optimization_barrier((passed_on, send, rows, chan))
    far = swap(passed_on, "chan", 3)
    near = swap(send, "chan", 1)
    (keep,) = project(*rest, later, (0,), LARGE)
    if paired:
        answers = swap(rows, "pix", 1)
        (mine,) = pixel_rows(*pixels, pix_local, later * quarter, count, *rest, later, ())
    else:
        answers = lax.all_to_all(
            rows.reshape(tile_count, capacity, -1), "pix", split_axis=0, concat_axis=0, tiled=True
        )
        mine = answers = jnp.take(answers.reshape(tile_count * capacity, -1), slot_index, axis=0)
    grads = pre_gradient(tile, chan, keep, near, far, pix_tile, foot_weight, mine, answers)

    across = swap(grads, "chan", 3)
    beside = swap(grads, "chan", 1)
    last = swap(across, "chan", 1)
    early, held, held_last = early_product(spectra, chan, grads, across)
    early = more_product(held, early, beside)
    core = lax.axis_index("obs") & 1
    send, keep = late_product(core, held_last, early, last)
    if lax.axis_size("obs") == 4 and tile_count == 2:
        return sum_over_panels(core, keep, [swap(part, "obs", 1) for part in send])
    return lax.psum(collect(core, keep, send), ("obs", "pix"))


def solution(mesh):
    return jax.shard_map(
        shards,
        mesh=mesh,
        in_specs=(
            P(("obs", "pix"), "chan"),
            P("chan", None),
            P(("obs", "pix"), None),
            P(("obs", "pix")),
            P(("obs", "pix")),
            P("pix", None),
            P(None, "pix"),
            P(),
        ),
        out_specs=P("chan", None),
        check_vma=False,
    )
```

```python
import functools

import jax
import jax.numpy as jnp
from jax import lax
from jax.experimental import pallas as pl
from jax.experimental.pallas import tpu as pltpu
from jax.sharding import PartitionSpec as P

NEIGH = 8
HALO = 128
MIB = 1024 * 1024
LARGE = 52


def edges(value, axis, width):
    size, length = lax.axis_size(axis), value.shape[0]
    last = lax.slice_in_dim(value, length - width, length, axis=0)
    first = lax.slice_in_dim(value, 0, width, axis=0)
    if size == 2:
        index = lax.axis_index(axis)
        other = lax.ppermute(jnp.where(index == 0, last, first), axis, [(0, 1), (1, 0)])
        return other, other
    up = [(i, i + 1) for i in range(size - 1)]
    return lax.ppermute(last, axis, up), lax.ppermute(first, axis, [(j, i) for i, j in up])


def requests(tile_ids, local_ids, capacity):
    tile_count = lax.axis_size("pix")
    onehot = (tile_ids[:, None] == jnp.arange(tile_count, dtype=jnp.int32)[None, :]).astype(
        jnp.int32
    )
    place_rank = jnp.sum((jnp.cumsum(onehot, axis=0) - 1) * onehot, axis=1)
    slot_index = tile_ids * capacity + place_rank
    outgoing = jnp.full((tile_count * capacity,), 0, jnp.int32).at[slot_index].set(local_ids)
    outgoing = outgoing.reshape(tile_count, capacity)
    requested = lax.all_to_all(outgoing, "pix", split_axis=0, concat_axis=0, tiled=True)
    return slot_index, requested.reshape(-1)


def swap(value, axis, bit):
    size = 1
    for name in (axis,) if isinstance(axis, str) else axis:
        size *= lax.axis_size(name)
    return lax.ppermute(value, axis, [(i, i ^ bit) for i in range(size)])


def memory(mib):
    return pltpu.CompilerParams(vmem_limit_bytes=mib * MIB)


def quarter_copies(spectra, held, sems, chan, bits):
    rows = spectra.shape[0] // 4
    return [
        pltpu.make_async_copy(
            spectra.at[pl.ds(pl.multiple_of((chan ^ bit) * rows, rows), rows)],
            held.at[pl.ds(turn * rows, rows)],
            sems.at[turn],
        )
        for turn, bit in enumerate(bits)
    ]


def project_rows(held, weight, turn, out):
    rows = out.shape[0]
    result = jnp.dot(
        held[turn * rows : (turn + 1) * rows, :], weight[...], preferred_element_type=jnp.float32
    )
    out[...] = result.astype(out.dtype)


def project_kernel(bits, chan, spectra, weight, *refs):
    *outs, held, near, sems = refs
    copies = [pltpu.make_async_copy(weight, near, sems.at[len(bits)])]
    copies += quarter_copies(spectra, held, sems, chan[0], bits)
    for copy in copies:
        copy.start()
    copies[0].wait()
    for turn, out in enumerate(outs):
        copies[turn + 1].wait()
        project_rows(held, near, turn, out)


def project(spectra, weight, chan, bits, grant):
    depth, width = weight.shape
    rows = spectra.shape[0] // 4
    hbm = pl.BlockSpec(memory_space=pltpu.HBM)
    return pl.pallas_call(
        functools.partial(project_kernel, bits),
        out_shape=(jax.ShapeDtypeStruct((rows, width), jnp.bfloat16),) * len(bits),
        in_specs=[pl.BlockSpec(memory_space=pltpu.SMEM), hbm, hbm],
        out_specs=(pl.BlockSpec(memory_space=pltpu.VMEM),) * len(bits),
        scratch_shapes=[
            pltpu.VMEM((len(bits) * rows, depth), jnp.bfloat16),
            pltpu.VMEM((depth, width), jnp.bfloat16),
            pltpu.SemaphoreType.DMA((len(bits) + 1,)),
        ],
        compiler_params=memory(grant),
        cost_estimate=pl.CostEstimate(
            flops=2 * len(bits) * rows * depth * width,
            bytes_accessed=2 * len(bits) * rows * (depth + width) + 2 * depth * width,
            transcendentals=0,
        ),
        name="project",
    )(chan.reshape(1), spectra, weight)


def turned_product(left, right):
    return lax.dot_general(
        left, right, (((0,), (0,)), ((), ())), preferred_element_type=jnp.float32
    )


def early_kernel(chan, spectra, first, second, total, third, fourth, held, sems):
    rows = first.shape[0]
    targets = (held.at[pl.ds(0, rows)], held.at[pl.ds(rows, rows)], third, fourth)
    copies = []
    for turn, (bits, target) in enumerate(zip((0, 3, 1, 2), targets)):
        start = pl.multiple_of((chan[0] ^ bits) * rows, rows)
        copies.append(pltpu.make_async_copy(spectra.at[pl.ds(start, rows)], target, sems.at[turn]))
    for copy in copies:
        copy.start()
    copies[0].wait()
    product = turned_product(held[:rows, :], first[...])
    copies[1].wait()
    total[...] = product + turned_product(held[rows:, :], second[...])
    copies[2].wait()
    copies[3].wait()


def early_product(spectra, chan, first, second):
    depth = spectra.shape[1]
    rows, width = first.shape
    vmem = pl.BlockSpec(memory_space=pltpu.VMEM)
    return pl.pallas_call(
        early_kernel,
        out_shape=(
            jax.ShapeDtypeStruct((depth, width), jnp.float32),
            jax.ShapeDtypeStruct((rows, depth), jnp.bfloat16),
            jax.ShapeDtypeStruct((rows, depth), jnp.bfloat16),
        ),
        in_specs=[
            pl.BlockSpec(memory_space=pltpu.SMEM),
            pl.BlockSpec(memory_space=pltpu.HBM),
            vmem,
            vmem,
        ],
        out_specs=(vmem,) * 3,
        scratch_shapes=[
            pltpu.VMEM((2 * rows, depth), jnp.bfloat16),
            pltpu.SemaphoreType.DMA((4,)),
        ],
        compiler_params=memory(48),
        cost_estimate=pl.CostEstimate(
            flops=4 * rows * depth * width,
            bytes_accessed=8 * rows * depth + 4 * depth * width,
            transcendentals=0,
        ),
        name="early_product",
    )(chan.reshape(1), spectra, first, second)


def more_kernel(held, before, rows, total):
    total[...] = before[...] + turned_product(held[...], rows[...])


def more_product(held, before, rows):
    vmem = pl.BlockSpec(memory_space=pltpu.VMEM)
    return pl.pallas_call(
        more_kernel,
        out_shape=jax.ShapeDtypeStruct(before.shape, jnp.float32),
        in_specs=[vmem] * 3,
        out_specs=vmem,
        compiler_params=memory(16),
        cost_estimate=pl.CostEstimate(
            flops=2 * held.shape[0] * held.shape[1] * rows.shape[1],
            bytes_accessed=2 * held.shape[0] * held.shape[1] + 8 * before.size,
            transcendentals=0,
        ),
        name="more_product",
    )(held, before, rows)


def late_kernel(core, held, before, rows, *outs):
    *outs, total = outs
    total[...] = before[...] + turned_product(held[...], rows[...])
    size = outs[0].shape[0]
    for index, out in enumerate(outs):
        first = (core[0] ^ (1 - index // 2)) * 2 * size + index % 2 * size
        here = pl.ds(pl.multiple_of(first, size), size)
        out[...] = total[here, :].astype(out.dtype)


def late_product(core, held, before, rows):
    size, width = before.shape[0] // 4, before.shape[1]
    spec = pl.BlockSpec(memory_space=pltpu.VMEM)
    send = jax.ShapeDtypeStruct((size, width), jnp.bfloat16)
    keep = jax.ShapeDtypeStruct((size, width), jnp.float32)
    outs = pl.pallas_call(
        late_kernel,
        out_shape=(send, send, keep, keep),
        in_specs=[pl.BlockSpec(memory_space=pltpu.SMEM)] + [spec] * 3,
        out_specs=(spec,) * 4,
        scratch_shapes=[pltpu.VMEM(before.shape, jnp.float32)],
        compiler_params=memory(16),
        cost_estimate=pl.CostEstimate(
            flops=2 * held.shape[0] * held.shape[1] * width,
            bytes_accessed=2 * held.shape[0] * held.shape[1] + 16 * size * width,
            transcendentals=0,
        ),
        name="late_product",
    )(core.reshape(1), held, before, rows)
    return outs[:2], outs[2:]


def pixel_kernel(count, bits, where, places, wanted, cotangent, above, below, mixing, weight,
                 spectra, out, *refs):
    quarters, refs = refs[: len(bits)], refs[len(bits) :]
    table, scale, sums, near, names, held, tile, sems = refs
    start, chan = where[0], where[1]
    tile_rows, half = tile.shape[0], table.shape[1]
    listed = names.shape[0]
    first_name = pl.multiple_of(start // listed * listed, listed)
    copies = [
        pltpu.make_async_copy(places, near, sems.at[len(bits)]),
        pltpu.make_async_copy(wanted.at[pl.ds(first_name, listed)], names, sems.at[len(bits) + 1]),
    ]
    parts = quarter_copies(spectra, held, sems, chan, bits)
    chunk = tile_rows // 4
    rows = [
        pltpu.make_async_copy(
            cotangent.at[pl.ds(n * chunk, chunk)],
            tile.at[pl.ds(n * chunk, chunk)],
            sems.at[len(bits) + 2 + n],
        )
        for n in range(4)
    ]
    order = copies + rows[:2] + parts[:1] + rows[2:] + parts[1:]
    for copy in order:
        copy.start()

    def fill(first, values):
        values = values.astype(jnp.float32)
        for side in range(2):
            table[pl.ds(2 * first + side, values.shape[0], stride=2), :] = values[
                :, side * half : (side + 1) * half
            ]

    for side in range(2):
        scale[pl.ds(side, NEIGH, stride=2), :] = mixing[:, side * half : (side + 1) * half]
    scales = [scale[2 * k : 2 * k + 2, :] for k in range(NEIGH)]
    fill(0, above[...])
    fill(HALO + tile_rows, below[...])
    for n in range(2):
        rows[2 * n].wait()
        rows[2 * n + 1].wait()
        if n < len(parts):
            parts[n].wait()
        for first in range(2 * n * chunk, 2 * (n + 1) * chunk, 256):
            fill(HALO + first, tile[first : first + 256, :])
        if n < len(parts):
            project_rows(held, weight, n, quarters[n])
    for copy in copies:
        copy.wait()

    group = 32
    offset = start - first_name
    pixels = table.reshape(table.shape[0] // 2, 2, half)

    def body(turn, carry):
        base = turn * group
        totals = []
        for n in range(group):
            pixel = names[offset + base + n]
            terms = [pixels[pixel + HALO]]
            for k in range(NEIGH // 2):
                pair = near[k * tile_rows + pixel]
                for place, scale in ((pair & 0xFFFF, k), (pair >> 16, k + NEIGH // 2)):
                    terms.append(pixels[place] * scales[scale])
            while len(terms) > 1:
                pairs = [x + y for x, y in zip(terms[::2], terms[1::2])]
                terms = pairs + terms[len(terms) // 2 * 2 :]
            totals += terms
        for n, total in enumerate(totals):
            sums[pl.ds(2 * (base + n), 2), :] = total
        return carry

    lax.fori_loop(0, count // group, body, 0)
    for side in range(2):
        out[:, side * half : (side + 1) * half] = sums[pl.ds(side, count, stride=2), :].astype(
            out.dtype
        )


def pixel_rows(
    cotangent, above, below, places, mixing, wanted, start, count, spectra, weight, chan, bits
):
    tile_rows, width = cotangent.shape
    depth, rows = spectra.shape[1], spectra.shape[0] // 4
    listed = min(wanted.shape[0], 1024)
    anywhere = pl.BlockSpec(memory_space=pl.ANY)
    hbm = pl.BlockSpec(memory_space=pltpu.HBM)
    vmem = pl.BlockSpec(memory_space=pltpu.VMEM)
    return pl.pallas_call(
        functools.partial(pixel_kernel, count, bits),
        out_shape=(
            jax.ShapeDtypeStruct((count, width), jnp.bfloat16),
            *[jax.ShapeDtypeStruct((rows, width), jnp.bfloat16)] * len(bits),
        ),
        in_specs=[
            pl.BlockSpec(memory_space=pltpu.SMEM),
            anywhere,
            anywhere,
            hbm,
            *[vmem] * 4,
            hbm,
        ],
        out_specs=(vmem,) * (1 + len(bits)),
        scratch_shapes=[
            pltpu.VMEM((2 * (tile_rows + 2 * HALO), width // 2), jnp.float32),
            pltpu.VMEM((2 * NEIGH, width // 2), jnp.float32),
            pltpu.VMEM((2 * count, width // 2), jnp.float32),
            pltpu.SMEM(places.shape, jnp.int32),
            pltpu.SMEM((listed,), jnp.int32),
            pltpu.VMEM((max(len(bits), 1) * rows, depth), jnp.bfloat16),
            pltpu.VMEM(cotangent.shape, cotangent.dtype),
            pltpu.SemaphoreType.DMA((len(bits) + 6,)),
        ],
        compiler_params=memory(LARGE),
        cost_estimate=pl.CostEstimate(
            flops=8 * NEIGH * count * 2048 * width,
            bytes_accessed=4 * tile_rows * width,
            transcendentals=0,
        ),
        name="pixel_rows",
    )(
        jnp.stack([start, chan]), places, wanted, cotangent, above, below, mixing, weight, spectra
    )


def gradient_kernel(where, keep, near, far, tiles, weights, mine, answers, out):
    tile, chan = where[0], where[1]
    rows = out.shape[0]
    size = tiles.shape[1]
    count = rows // size
    group = 8 // count
    wide = jnp.float32
    first = pl.multiple_of(chan // group * 8, 8)

    def columns(values):
        turned = values[pl.ds(first, 8), :].T
        places = [turned[:, n * count : (n + 1) * count] for n in range(group)]
        picked = places[0]
        for n in range(1, group):
            picked = jnp.where(chan % group == n, places[n], picked)
        return picked

    own = columns(tiles).astype(wide)
    factors = columns(weights)
    for n in range(count):
        here = slice(n * size, (n + 1) * size)
        pre = keep[here, :].astype(wide) + near[here, :].astype(wide) + far[here, :].astype(wide)
        sigma = jax.nn.sigmoid(pre)
        deriv = sigma * (1.0 + pre * (1.0 - sigma))
        fetched = jnp.where(
            own[:, n : n + 1] == tile.astype(wide),
            mine[here, :].astype(wide),
            answers[here, :].astype(wide),
        )
        out[here, :] = (factors[:, n : n + 1] * deriv * fetched).astype(out.dtype)


def pre_gradient(tile, chan, keep, near, far, tiles, weights, mine, answers):
    spec = pl.BlockSpec(memory_space=pltpu.VMEM)
    tiles, weights = tiles.reshape(-1, 128), weights.reshape(-1, 128)
    return pl.pallas_call(
        gradient_kernel,
        out_shape=jax.ShapeDtypeStruct(far.shape, jnp.bfloat16),
        in_specs=[pl.BlockSpec(memory_space=pltpu.SMEM)] + [spec] * 7,
        out_specs=spec,
        compiler_params=memory(16),
        name="pre_gradient",
    )(jnp.stack([tile, chan]), keep, near, far, tiles, weights, mine, answers)


def collect_kernel(core, *refs):
    *pieces, out = refs
    half, rows = out.shape[0] // 2, pieces[0].shape[0]
    count = len(pieces) // 2
    for index, piece in enumerate(pieces):
        which = core[0] if index < count else 1 - core[0]
        first = which * half + (index % count) * rows
        out[pl.ds(pl.multiple_of(first, rows), rows), :] = piece[...].astype(jnp.float32)


def collect(core, own, received):
    spec = pl.BlockSpec(memory_space=pltpu.VMEM)
    pieces = [*own, *received]
    rows, width = sum(piece.shape[0] for piece in pieces), own[0].shape[1]
    return pl.pallas_call(
        collect_kernel,
        out_shape=jax.ShapeDtypeStruct((rows, width), jnp.float32),
        in_specs=[pl.BlockSpec(memory_space=pltpu.SMEM)] + [spec] * len(pieces),
        out_specs=spec,
        compiler_params=memory(16),
        name="collect",
    )(core.reshape(1), *pieces)


def add_kernel(first, second, out):
    out[...] = (first[...].astype(jnp.float32) + second[...].astype(jnp.float32)).astype(out.dtype)


def added(first, second):
    spec = pl.BlockSpec(memory_space=pltpu.VMEM)
    return pl.pallas_call(
        add_kernel,
        out_shape=jax.ShapeDtypeStruct(first.shape, jnp.bfloat16),
        in_specs=[spec, spec],
        out_specs=spec,
        compiler_params=memory(16),
        name="added",
    )(first, second)


def sum_over_panels(core, parts, received):
    both = ("obs", "pix")
    parts = [added(part, other) for part, other in zip(parts, received)]
    for order in ((4, 1), (1, 4)):
        perm = [(i, i ^ order[(i >> 1) & 1]) for i in range(8)]
        parts = [added(part, lax.ppermute(part, both, perm)) for part in parts]
    return collect(core, parts, [swap(part, "obs", 1) for part in parts])


def shards(spectra, enc_weight, pix_tile, pix_local, foot_weight, cotangent, adjoint, mixing):
    tile_count = lax.axis_size("pix")
    tile_rows = cotangent.shape[0]
    quarter = spectra.shape[0] // lax.axis_size("chan")
    tile = lax.axis_index("pix")
    chan = lax.axis_index("chan")
    first_row = chan * quarter

    near_first = swap(project(spectra, enc_weight, chan, (2,), LARGE + 4)[0], "chan", 1)
    places = adjoint - (tile * tile_rows - HALO)
    places = (places[: NEIGH // 2] | (places[NEIGH // 2 :] << 16)).reshape(-1)

    above, below = edges(cotangent, "pix", HALO)
    capacity = 2 * quarter // tile_count
    pixels = (cotangent, above, below, places, mixing)
    rest = (spectra, enc_weight)
    paired = capacity >= quarter and tile_count == 2
    if paired:
        wanted, start, count = swap(pix_local, "pix", 1), first_row, quarter
    else:
        tile_ids = lax.dynamic_slice_in_dim(pix_tile[:, 0], first_row, quarter, 0)
        local_ids = lax.dynamic_slice_in_dim(pix_local, first_row, quarter, 0)
        slot_index, wanted = requests(tile_ids, local_ids, capacity)
        start, count = 0 * chan, wanted.shape[0]
    rows, shared, send = pixel_rows(*pixels, wanted, start, count, *rest, chan, (3, 1))
    near_first, rows = lax.optimization_barrier((near_first, rows))
    passed_on = (shared.astype(jnp.float32) + near_first.astype(jnp.float32)).astype(jnp.bfloat16)
    passed_on, send, rows, later = lax.optimization_barrier((passed_on, send, rows, chan))
    far = swap(passed_on, "chan", 3)
    near = swap(send, "chan", 1)
    (keep,) = project(*rest, later, (0,), LARGE)
    if paired:
        answers = swap(rows, "pix", 1)
        (mine,) = pixel_rows(*pixels, pix_local, later * quarter, count, *rest, later, ())
    else:
        answers = lax.all_to_all(
            rows.reshape(tile_count, capacity, -1), "pix", split_axis=0, concat_axis=0, tiled=True
        )
        mine = answers = jnp.take(answers.reshape(tile_count * capacity, -1), slot_index, axis=0)
    grads = pre_gradient(tile, chan, keep, near, far, pix_tile, foot_weight, mine, answers)

    across = swap(grads, "chan", 3)
    beside = swap(grads, "chan", 1)
    last = swap(across, "chan", 1)
    early, held, held_last = early_product(spectra, chan, grads, across)
    early = more_product(held, early, beside)
    core = lax.axis_index("obs") & 1
    send, keep = late_product(core, held_last, early, last)
    if lax.axis_size("obs") == 4 and tile_count == 2:
        return sum_over_panels(core, keep, [swap(part, "obs", 1) for part in send])
    return lax.psum(collect(core, keep, send), ("obs", "pix"))


def solution(mesh):
    return jax.shard_map(
        shards,
        mesh=mesh,
        in_specs=(
            P(("obs", "pix"), "chan"),
            P("chan", None),
            P(("obs", "pix"), None),
            P(("obs", "pix")),
            P(("obs", "pix")),
            P("pix", None),
            P(None, "pix"),
            P(),
        ),
        out_specs=P("chan", None),
        check_vma=False,
    )
```

```python
import functools

import jax
import jax.numpy as jnp
from jax import lax
from jax.experimental import pallas as pl
from jax.experimental.pallas import tpu as pltpu
from jax.sharding import PartitionSpec as P

NEIGH = 8
HALO = 128
MIB = 1024 * 1024
LARGE = 52


def edges(value, axis, width):
    size, length = lax.axis_size(axis), value.shape[0]
    last = lax.slice_in_dim(value, length - width, length, axis=0)
    first = lax.slice_in_dim(value, 0, width, axis=0)
    if size == 2:
        index = lax.axis_index(axis)
        other = lax.ppermute(jnp.where(index == 0, last, first), axis, [(0, 1), (1, 0)])
        return other, other
    up = [(i, i + 1) for i in range(size - 1)]
    return lax.ppermute(last, axis, up), lax.ppermute(first, axis, [(j, i) for i, j in up])


def requests(tile_ids, local_ids, capacity):
    tile_count = lax.axis_size("pix")
    onehot = (tile_ids[:, None] == jnp.arange(tile_count, dtype=jnp.int32)[None, :]).astype(
        jnp.int32
    )
    place_rank = jnp.sum((jnp.cumsum(onehot, axis=0) - 1) * onehot, axis=1)
    slot_index = tile_ids * capacity + place_rank
    outgoing = jnp.full((tile_count * capacity,), 0, jnp.int32).at[slot_index].set(local_ids)
    outgoing = outgoing.reshape(tile_count, capacity)
    requested = lax.all_to_all(outgoing, "pix", split_axis=0, concat_axis=0, tiled=True)
    return slot_index, requested.reshape(-1)


def swap(value, axis, bit):
    size = 1
    for name in (axis,) if isinstance(axis, str) else axis:
        size *= lax.axis_size(name)
    return lax.ppermute(value, axis, [(i, i ^ bit) for i in range(size)])


def memory(mib):
    return pltpu.CompilerParams(vmem_limit_bytes=mib * MIB)


def quarter_copies(spectra, held, sems, chan, bits):
    rows = spectra.shape[0] // 4
    return [
        pltpu.make_async_copy(
            spectra.at[pl.ds(pl.multiple_of((chan ^ bit) * rows, rows), rows)],
            held.at[pl.ds(turn * rows, rows)],
            sems.at[turn],
        )
        for turn, bit in enumerate(bits)
    ]


def project_rows(held, weight, turn, out):
    rows = out.shape[0]
    result = jnp.dot(
        held[turn * rows : (turn + 1) * rows, :], weight[...], preferred_element_type=jnp.float32
    )
    out[...] = result.astype(out.dtype)


def project_kernel(bits, chan, spectra, weight, *refs):
    *outs, held, near, sems = refs
    copies = [pltpu.make_async_copy(weight, near, sems.at[len(bits)])]
    copies += quarter_copies(spectra, held, sems, chan[0], bits)
    for copy in copies:
        copy.start()
    copies[0].wait()
    for turn, out in enumerate(outs):
        copies[turn + 1].wait()
        project_rows(held, near, turn, out)


def project(spectra, weight, chan, bits, grant):
    depth, width = weight.shape
    rows = spectra.shape[0] // 4
    hbm = pl.BlockSpec(memory_space=pltpu.HBM)
    return pl.pallas_call(
        functools.partial(project_kernel, bits),
        out_shape=(jax.ShapeDtypeStruct((rows, width), jnp.bfloat16),) * len(bits),
        in_specs=[pl.BlockSpec(memory_space=pltpu.SMEM), hbm, hbm],
        out_specs=(pl.BlockSpec(memory_space=pltpu.VMEM),) * len(bits),
        scratch_shapes=[
            pltpu.VMEM((len(bits) * rows, depth), jnp.bfloat16),
            pltpu.VMEM((depth, width), jnp.bfloat16),
            pltpu.SemaphoreType.DMA((len(bits) + 1,)),
        ],
        compiler_params=memory(grant),
        cost_estimate=pl.CostEstimate(
            flops=2 * len(bits) * rows * depth * width,
            bytes_accessed=2 * len(bits) * rows * (depth + width) + 2 * depth * width,
            transcendentals=0,
        ),
        name="project",
    )(chan.reshape(1), spectra, weight)


def turned_product(left, right):
    return lax.dot_general(
        left, right, (((0,), (0,)), ((), ())), preferred_element_type=jnp.float32
    )


def early_kernel(chan, spectra, first, second, total, third, fourth, held, sems):
    rows = first.shape[0]
    targets = (held.at[pl.ds(0, rows)], held.at[pl.ds(rows, rows)], third, fourth)
    copies = []
    for turn, (bits, target) in enumerate(zip((0, 3, 1, 2), targets)):
        start = pl.multiple_of((chan[0] ^ bits) * rows, rows)
        copies.append(pltpu.make_async_copy(spectra.at[pl.ds(start, rows)], target, sems.at[turn]))
    for copy in copies:
        copy.start()
    copies[0].wait()
    product = turned_product(held[:rows, :], first[...])
    copies[1].wait()
    total[...] = product + turned_product(held[rows:, :], second[...])
    copies[2].wait()
    copies[3].wait()


def early_product(spectra, chan, first, second):
    depth = spectra.shape[1]
    rows, width = first.shape
    vmem = pl.BlockSpec(memory_space=pltpu.VMEM)
    return pl.pallas_call(
        early_kernel,
        out_shape=(
            jax.ShapeDtypeStruct((depth, width), jnp.float32),
            jax.ShapeDtypeStruct((rows, depth), jnp.bfloat16),
            jax.ShapeDtypeStruct((rows, depth), jnp.bfloat16),
        ),
        in_specs=[
            pl.BlockSpec(memory_space=pltpu.SMEM),
            pl.BlockSpec(memory_space=pltpu.HBM),
            vmem,
            vmem,
        ],
        out_specs=(vmem,) * 3,
        scratch_shapes=[
            pltpu.VMEM((2 * rows, depth), jnp.bfloat16),
            pltpu.SemaphoreType.DMA((4,)),
        ],
        compiler_params=memory(48),
        cost_estimate=pl.CostEstimate(
            flops=4 * rows * depth * width,
            bytes_accessed=8 * rows * depth + 4 * depth * width,
            transcendentals=0,
        ),
        name="early_product",
    )(chan.reshape(1), spectra, first, second)


def more_kernel(held, before, rows, total):
    total[...] = before[...] + turned_product(held[...], rows[...])


def more_product(held, before, rows):
    vmem = pl.BlockSpec(memory_space=pltpu.VMEM)
    return pl.pallas_call(
        more_kernel,
        out_shape=jax.ShapeDtypeStruct(before.shape, jnp.float32),
        in_specs=[vmem] * 3,
        out_specs=vmem,
        compiler_params=memory(16),
        cost_estimate=pl.CostEstimate(
            flops=2 * held.shape[0] * held.shape[1] * rows.shape[1],
            bytes_accessed=2 * held.shape[0] * held.shape[1] + 8 * before.size,
            transcendentals=0,
        ),
        name="more_product",
    )(held, before, rows)


def late_kernel(core, held, before, rows, *outs):
    *outs, total = outs
    total[...] = before[...] + turned_product(held[...], rows[...])
    size = outs[0].shape[0]
    for index, out in enumerate(outs):
        first = (core[0] ^ (1 - index // 2)) * 2 * size + index % 2 * size
        here = pl.ds(pl.multiple_of(first, size), size)
        out[...] = total[here, :].astype(out.dtype)


def late_product(core, held, before, rows):
    size, width = before.shape[0] // 4, before.shape[1]
    spec = pl.BlockSpec(memory_space=pltpu.VMEM)
    send = jax.ShapeDtypeStruct((size, width), jnp.bfloat16)
    keep = jax.ShapeDtypeStruct((size, width), jnp.float32)
    outs = pl.pallas_call(
        late_kernel,
        out_shape=(send, send, keep, keep),
        in_specs=[pl.BlockSpec(memory_space=pltpu.SMEM)] + [spec] * 3,
        out_specs=(spec,) * 4,
        scratch_shapes=[pltpu.VMEM(before.shape, jnp.float32)],
        compiler_params=memory(16),
        cost_estimate=pl.CostEstimate(
            flops=2 * held.shape[0] * held.shape[1] * width,
            bytes_accessed=2 * held.shape[0] * held.shape[1] + 16 * size * width,
            transcendentals=0,
        ),
        name="late_product",
    )(core.reshape(1), held, before, rows)
    return outs[:2], outs[2:]


def pixel_kernel(count, bits, where, places, wanted, cotangent, above, below, mixing, weight,
                 spectra, out, *refs):
    quarters, refs = refs[: len(bits)], refs[len(bits) :]
    table, scale, sums, near, names, held, tile, sems = refs
    start, chan = where[0], where[1]
    tile_rows, half = tile.shape[0], table.shape[1]
    listed = names.shape[0]
    first_name = pl.multiple_of(start // listed * listed, listed)
    copies = [
        pltpu.make_async_copy(places, near, sems.at[len(bits)]),
        pltpu.make_async_copy(wanted.at[pl.ds(first_name, listed)], names, sems.at[len(bits) + 1]),
    ]
    parts = quarter_copies(spectra, held, sems, chan, bits)
    chunk = tile_rows // 4
    rows = [
        pltpu.make_async_copy(
            cotangent.at[pl.ds(n * chunk, chunk)],
            tile.at[pl.ds(n * chunk, chunk)],
            sems.at[len(bits) + 2 + n],
        )
        for n in range(4)
    ]
    order = copies + rows[:2] + parts[:1] + rows[2:] + parts[1:]
    for copy in order:
        copy.start()

    def fill(first, values):
        values = values.astype(jnp.float32)
        for side in range(2):
            table[pl.ds(2 * first + side, values.shape[0], stride=2), :] = values[
                :, side * half : (side + 1) * half
            ]

    for side in range(2):
        scale[pl.ds(side, NEIGH, stride=2), :] = mixing[:, side * half : (side + 1) * half]
    scales = [scale[2 * k : 2 * k + 2, :] for k in range(NEIGH)]
    fill(0, above[...])
    fill(HALO + tile_rows, below[...])
    for n in range(2):
        rows[2 * n].wait()
        rows[2 * n + 1].wait()
        if n < len(parts):
            parts[n].wait()
        for first in range(2 * n * chunk, 2 * (n + 1) * chunk, 256):
            fill(HALO + first, tile[first : first + 256, :])
        if n < len(parts):
            project_rows(held, weight, n, quarters[n])
    for copy in copies:
        copy.wait()

    group = 32
    offset = start - first_name

    def body(turn, carry):
        base = turn * group
        totals = []
        for n in range(group):
            pixel = names[offset + base + n]
            terms = [table[pl.ds(2 * (pixel + HALO), 2), :]]
            for k in range(NEIGH // 2):
                pair = near[k * tile_rows + pixel]
                for place, scale in ((pair & 0xFFFF, k), (pair >> 16, k + NEIGH // 2)):
                    terms.append(table[pl.ds(place, 2), :] * scales[scale])
            while len(terms) > 1:
                pairs = [x + y for x, y in zip(terms[::2], terms[1::2])]
                terms = pairs + terms[len(terms) // 2 * 2 :]
            totals += terms
        for n, total in enumerate(totals):
            sums[pl.ds(2 * (base + n), 2), :] = total
        return carry

    lax.fori_loop(0, count // group, body, 0)
    for side in range(2):
        out[:, side * half : (side + 1) * half] = sums[pl.ds(side, count, stride=2), :].astype(
            out.dtype
        )


def pixel_rows(
    cotangent, above, below, places, mixing, wanted, start, count, spectra, weight, chan, bits
):
    tile_rows, width = cotangent.shape
    depth, rows = spectra.shape[1], spectra.shape[0] // 4
    listed = min(wanted.shape[0], 1024)
    anywhere = pl.BlockSpec(memory_space=pl.ANY)
    hbm = pl.BlockSpec(memory_space=pltpu.HBM)
    vmem = pl.BlockSpec(memory_space=pltpu.VMEM)
    return pl.pallas_call(
        functools.partial(pixel_kernel, count, bits),
        out_shape=(
            jax.ShapeDtypeStruct((count, width), jnp.bfloat16),
            *[jax.ShapeDtypeStruct((rows, width), jnp.bfloat16)] * len(bits),
        ),
        in_specs=[
            pl.BlockSpec(memory_space=pltpu.SMEM),
            anywhere,
            anywhere,
            hbm,
            *[vmem] * 4,
            hbm,
        ],
        out_specs=(vmem,) * (1 + len(bits)),
        scratch_shapes=[
            pltpu.VMEM((2 * (tile_rows + 2 * HALO), width // 2), jnp.float32),
            pltpu.VMEM((2 * NEIGH, width // 2), jnp.float32),
            pltpu.VMEM((2 * count, width // 2), jnp.float32),
            pltpu.SMEM(places.shape, jnp.int32),
            pltpu.SMEM((listed,), jnp.int32),
            pltpu.VMEM((max(len(bits), 1) * rows, depth), jnp.bfloat16),
            pltpu.VMEM(cotangent.shape, cotangent.dtype),
            pltpu.SemaphoreType.DMA((len(bits) + 6,)),
        ],
        compiler_params=memory(LARGE),
        cost_estimate=pl.CostEstimate(
            flops=8 * NEIGH * count * 2048 * width,
            bytes_accessed=4 * tile_rows * width,
            transcendentals=0,
        ),
        name="pixel_rows",
    )(
        jnp.stack([start, chan]), places, wanted, cotangent, above, below, mixing, weight, spectra
    )


def gradient_kernel(where, keep, near, far, tiles, weights, mine, answers, out):
    tile, chan = where[0], where[1]
    rows = out.shape[0]
    size = tiles.shape[1]
    count = rows // size
    group = 8 // count
    wide = jnp.float32
    first = pl.multiple_of(chan // group * 8, 8)

    def columns(values):
        turned = values[pl.ds(first, 8), :].T
        places = [turned[:, n * count : (n + 1) * count] for n in range(group)]
        picked = places[0]
        for n in range(1, group):
            picked = jnp.where(chan % group == n, places[n], picked)
        return picked

    own = columns(tiles).astype(wide)
    factors = columns(weights)
    for n in range(count):
        here = slice(n * size, (n + 1) * size)
        pre = keep[here, :].astype(wide) + near[here, :].astype(wide) + far[here, :].astype(wide)
        sigma = jax.nn.sigmoid(pre)
        deriv = sigma * (1.0 + pre * (1.0 - sigma))
        fetched = jnp.where(
            own[:, n : n + 1] == tile.astype(wide),
            mine[here, :].astype(wide),
            answers[here, :].astype(wide),
        )
        out[here, :] = (factors[:, n : n + 1] * deriv * fetched).astype(out.dtype)


def pre_gradient(tile, chan, keep, near, far, tiles, weights, mine, answers):
    spec = pl.BlockSpec(memory_space=pltpu.VMEM)
    tiles, weights = tiles.reshape(-1, 128), weights.reshape(-1, 128)
    return pl.pallas_call(
        gradient_kernel,
        out_shape=jax.ShapeDtypeStruct(far.shape, jnp.bfloat16),
        in_specs=[pl.BlockSpec(memory_space=pltpu.SMEM)] + [spec] * 7,
        out_specs=spec,
        compiler_params=memory(16),
        name="pre_gradient",
    )(jnp.stack([tile, chan]), keep, near, far, tiles, weights, mine, answers)


def collect_kernel(core, *refs):
    *pieces, out = refs
    half, rows = out.shape[0] // 2, pieces[0].shape[0]
    count = len(pieces) // 2
    for index, piece in enumerate(pieces):
        which = core[0] if index < count else 1 - core[0]
        first = which * half + (index % count) * rows
        out[pl.ds(pl.multiple_of(first, rows), rows), :] = piece[...].astype(jnp.float32)


def collect(core, own, received):
    spec = pl.BlockSpec(memory_space=pltpu.VMEM)
    pieces = [*own, *received]
    rows, width = sum(piece.shape[0] for piece in pieces), own[0].shape[1]
    return pl.pallas_call(
        collect_kernel,
        out_shape=jax.ShapeDtypeStruct((rows, width), jnp.float32),
        in_specs=[pl.BlockSpec(memory_space=pltpu.SMEM)] + [spec] * len(pieces),
        out_specs=spec,
        compiler_params=memory(16),
        name="collect",
    )(core.reshape(1), *pieces)


def add_kernel(first, second, out):
    out[...] = (first[...].astype(jnp.float32) + second[...].astype(jnp.float32)).astype(out.dtype)


def added(first, second):
    spec = pl.BlockSpec(memory_space=pltpu.VMEM)
    return pl.pallas_call(
        add_kernel,
        out_shape=jax.ShapeDtypeStruct(first.shape, jnp.bfloat16),
        in_specs=[spec, spec],
        out_specs=spec,
        compiler_params=memory(16),
        name="added",
    )(first, second)


def sum_over_panels(core, parts, received):
    both = ("obs", "pix")
    parts = [added(part, other) for part, other in zip(parts, received)]
    for order in ((4, 1), (1, 4)):
        perm = [(i, i ^ order[(i >> 1) & 1]) for i in range(8)]
        parts = [added(part, lax.ppermute(part, both, perm)) for part in parts]
    return collect(core, parts, [swap(part, "obs", 1) for part in parts])


def shards(spectra, enc_weight, pix_tile, pix_local, foot_weight, cotangent, adjoint, mixing):
    tile_count = lax.axis_size("pix")
    tile_rows = cotangent.shape[0]
    quarter = spectra.shape[0] // lax.axis_size("chan")
    tile = lax.axis_index("pix")
    chan = lax.axis_index("chan")
    first_row = chan * quarter

    near_first = swap(project(spectra, enc_weight, chan, (2,), LARGE + 4)[0], "chan", 1)
    places = (adjoint - (tile * tile_rows - HALO)) * 2
    places = (places[: NEIGH // 2] | (places[NEIGH // 2 :] << 16)).reshape(-1)

    above, below = edges(cotangent, "pix", HALO)
    capacity = 2 * quarter // tile_count
    pixels = (cotangent, above, below, places, mixing)
    rest = (spectra, enc_weight)
    paired = capacity >= quarter and tile_count == 2
    if paired:
        wanted, start, count = swap(pix_local, "pix", 1), first_row, quarter
    else:
        tile_ids = lax.dynamic_slice_in_dim(pix_tile[:, 0], first_row, quarter, 0)
        local_ids = lax.dynamic_slice_in_dim(pix_local, first_row, quarter, 0)
        slot_index, wanted = requests(tile_ids, local_ids, capacity)
        start, count = 0 * chan, wanted.shape[0]
    rows, shared, send = pixel_rows(*pixels, wanted, start, count, *rest, chan, (3, 1))
    near_first, rows = lax.optimization_barrier((near_first, rows))
    passed_on = (shared.astype(jnp.float32) + near_first.astype(jnp.float32)).astype(jnp.bfloat16)
    passed_on, send, rows, later = lax.optimization_barrier((passed_on, send, rows, chan))
    far = swap(passed_on, "chan", 3)
    near = swap(send, "chan", 1)
    if paired:
        answers = swap(rows, "pix", 1)
        mine, keep = pixel_rows(*pixels, pix_local, later * quarter, count, *rest, later, (0,))
    else:
        (keep,) = project(*rest, later, (0,), LARGE)
        answers = lax.all_to_all(
            rows.reshape(tile_count, capacity, -1), "pix", split_axis=0, concat_axis=0, tiled=True
        )
        mine = answers = jnp.take(answers.reshape(tile_count * capacity, -1), slot_index, axis=0)
    grads = pre_gradient(tile, chan, keep, near, far, pix_tile, foot_weight, mine, answers)

    across = swap(grads, "chan", 3)
    beside = swap(grads, "chan", 1)
    last = swap(across, "chan", 1)
    early, held, held_last = early_product(spectra, chan, grads, across)
    early = more_product(held, early, beside)
    core = lax.axis_index("obs") & 1
    send, keep = late_product(core, held_last, early, last)
    if lax.axis_size("obs") == 4 and tile_count == 2:
        return sum_over_panels(core, keep, [swap(part, "obs", 1) for part in send])
    return lax.psum(collect(core, keep, send), ("obs", "pix"))


def solution(mesh):
    return jax.shard_map(
        shards,
        mesh=mesh,
        in_specs=(
            P(("obs", "pix"), "chan"),
            P("chan", None),
            P(("obs", "pix"), None),
            P(("obs", "pix")),
            P(("obs", "pix")),
            P("pix", None),
            P(None, "pix"),
            P(),
        ),
        out_specs=P("chan", None),
        check_vma=False,
    )
```

```python
import functools

import jax
import jax.numpy as jnp
from jax import lax
from jax.experimental import pallas as pl
from jax.experimental.pallas import tpu as pltpu
from jax.sharding import PartitionSpec as P

NEIGH = 8
HALO = 128
MIB = 1024 * 1024
LARGE = 52


def edges(value, axis, width):
    size, length = lax.axis_size(axis), value.shape[0]
    last = lax.slice_in_dim(value, length - width, length, axis=0)
    first = lax.slice_in_dim(value, 0, width, axis=0)
    if size == 2:
        index = lax.axis_index(axis)
        other = lax.ppermute(jnp.where(index == 0, last, first), axis, [(0, 1), (1, 0)])
        return other, other
    up = [(i, i + 1) for i in range(size - 1)]
    return lax.ppermute(last, axis, up), lax.ppermute(first, axis, [(j, i) for i, j in up])


def requests(tile_ids, local_ids, capacity):
    tile_count = lax.axis_size("pix")
    onehot = (tile_ids[:, None] == jnp.arange(tile_count, dtype=jnp.int32)[None, :]).astype(
        jnp.int32
    )
    place_rank = jnp.sum((jnp.cumsum(onehot, axis=0) - 1) * onehot, axis=1)
    slot_index = tile_ids * capacity + place_rank
    outgoing = jnp.full((tile_count * capacity,), 0, jnp.int32).at[slot_index].set(local_ids)
    outgoing = outgoing.reshape(tile_count, capacity)
    requested = lax.all_to_all(outgoing, "pix", split_axis=0, concat_axis=0, tiled=True)
    return slot_index, requested.reshape(-1)


def swap(value, axis, bit):
    size = 1
    for name in (axis,) if isinstance(axis, str) else axis:
        size *= lax.axis_size(name)
    return lax.ppermute(value, axis, [(i, i ^ bit) for i in range(size)])


def memory(mib):
    return pltpu.CompilerParams(vmem_limit_bytes=mib * MIB)


def quarter_copies(spectra, held, sems, chan, bits):
    rows = spectra.shape[0] // 4
    return [
        pltpu.make_async_copy(
            spectra.at[pl.ds(pl.multiple_of((chan ^ bit) * rows, rows), rows)],
            held.at[pl.ds(turn * rows, rows)],
            sems.at[turn],
        )
        for turn, bit in enumerate(bits)
    ]


def project_rows(held, weight, turn, out):
    rows = out.shape[0]
    result = jnp.dot(
        held[turn * rows : (turn + 1) * rows, :], weight[...], preferred_element_type=jnp.float32
    )
    out[...] = result.astype(out.dtype)


def project_kernel(bits, chan, spectra, weight, *refs):
    *outs, held, near, sems = refs
    copies = [pltpu.make_async_copy(weight, near, sems.at[len(bits)])]
    copies += quarter_copies(spectra, held, sems, chan[0], bits)
    for copy in copies:
        copy.start()
    copies[0].wait()
    for turn, out in enumerate(outs):
        copies[turn + 1].wait()
        project_rows(held, near, turn, out)


def project(spectra, weight, chan, bits, grant):
    depth, width = weight.shape
    rows = spectra.shape[0] // 4
    hbm = pl.BlockSpec(memory_space=pltpu.HBM)
    return pl.pallas_call(
        functools.partial(project_kernel, bits),
        out_shape=(jax.ShapeDtypeStruct((rows, width), jnp.bfloat16),) * len(bits),
        in_specs=[pl.BlockSpec(memory_space=pltpu.SMEM), hbm, hbm],
        out_specs=(pl.BlockSpec(memory_space=pltpu.VMEM),) * len(bits),
        scratch_shapes=[
            pltpu.VMEM((len(bits) * rows, depth), jnp.bfloat16),
            pltpu.VMEM((depth, width), jnp.bfloat16),
            pltpu.SemaphoreType.DMA((len(bits) + 1,)),
        ],
        compiler_params=memory(grant),
        cost_estimate=pl.CostEstimate(
            flops=2 * len(bits) * rows * depth * width,
            bytes_accessed=2 * len(bits) * rows * (depth + width) + 2 * depth * width,
            transcendentals=0,
        ),
        name="project",
    )(chan.reshape(1), spectra, weight)


def turned_product(left, right):
    return lax.dot_general(
        left, right, (((0,), (0,)), ((), ())), preferred_element_type=jnp.float32
    )


def early_kernel(chan, spectra, first, second, total, third, fourth, held, sems):
    rows = first.shape[0]
    targets = (held.at[pl.ds(0, rows)], held.at[pl.ds(rows, rows)], third, fourth)
    copies = []
    for turn, (bits, target) in enumerate(zip((0, 3, 1, 2), targets)):
        start = pl.multiple_of((chan[0] ^ bits) * rows, rows)
        copies.append(pltpu.make_async_copy(spectra.at[pl.ds(start, rows)], target, sems.at[turn]))
    for copy in copies:
        copy.start()
    copies[0].wait()
    product = turned_product(held[:rows, :], first[...])
    copies[1].wait()
    total[...] = product + turned_product(held[rows:, :], second[...])
    copies[2].wait()
    copies[3].wait()


def early_product(spectra, chan, first, second):
    depth = spectra.shape[1]
    rows, width = first.shape
    vmem = pl.BlockSpec(memory_space=pltpu.VMEM)
    return pl.pallas_call(
        early_kernel,
        out_shape=(
            jax.ShapeDtypeStruct((depth, width), jnp.float32),
            jax.ShapeDtypeStruct((rows, depth), jnp.bfloat16),
            jax.ShapeDtypeStruct((rows, depth), jnp.bfloat16),
        ),
        in_specs=[
            pl.BlockSpec(memory_space=pltpu.SMEM),
            pl.BlockSpec(memory_space=pltpu.HBM),
            vmem,
            vmem,
        ],
        out_specs=(vmem,) * 3,
        scratch_shapes=[
            pltpu.VMEM((2 * rows, depth), jnp.bfloat16),
            pltpu.SemaphoreType.DMA((4,)),
        ],
        compiler_params=memory(48),
        cost_estimate=pl.CostEstimate(
            flops=4 * rows * depth * width,
            bytes_accessed=8 * rows * depth + 4 * depth * width,
            transcendentals=0,
        ),
        name="early_product",
    )(chan.reshape(1), spectra, first, second)


def more_kernel(held, before, rows, total):
    total[...] = before[...] + turned_product(held[...], rows[...])


def more_product(held, before, rows):
    vmem = pl.BlockSpec(memory_space=pltpu.VMEM)
    return pl.pallas_call(
        more_kernel,
        out_shape=jax.ShapeDtypeStruct(before.shape, jnp.float32),
        in_specs=[vmem] * 3,
        out_specs=vmem,
        compiler_params=memory(16),
        cost_estimate=pl.CostEstimate(
            flops=2 * held.shape[0] * held.shape[1] * rows.shape[1],
            bytes_accessed=2 * held.shape[0] * held.shape[1] + 8 * before.size,
            transcendentals=0,
        ),
        name="more_product",
    )(held, before, rows)


def late_kernel(core, held, before, rows, *outs):
    *outs, total = outs
    total[...] = before[...] + turned_product(held[...], rows[...])
    size = outs[0].shape[0]
    for index, out in enumerate(outs):
        first = (core[0] ^ (1 - index // 2)) * 2 * size + index % 2 * size
        here = pl.ds(pl.multiple_of(first, size), size)
        out[...] = total[here, :].astype(out.dtype)


def late_product(core, held, before, rows):
    size, width = before.shape[0] // 4, before.shape[1]
    spec = pl.BlockSpec(memory_space=pltpu.VMEM)
    send = jax.ShapeDtypeStruct((size, width), jnp.bfloat16)
    keep = jax.ShapeDtypeStruct((size, width), jnp.float32)
    outs = pl.pallas_call(
        late_kernel,
        out_shape=(send, send, keep, keep),
        in_specs=[pl.BlockSpec(memory_space=pltpu.SMEM)] + [spec] * 3,
        out_specs=(spec,) * 4,
        scratch_shapes=[pltpu.VMEM(before.shape, jnp.float32)],
        compiler_params=memory(16),
        cost_estimate=pl.CostEstimate(
            flops=2 * held.shape[0] * held.shape[1] * width,
            bytes_accessed=2 * held.shape[0] * held.shape[1] + 16 * size * width,
            transcendentals=0,
        ),
        name="late_product",
    )(core.reshape(1), held, before, rows)
    return outs[:2], outs[2:]


def pixel_kernel(count, bits, where, places, wanted, cotangent, above, below, mixing, weight,
                 spectra, out, *refs):
    quarters, refs = refs[: len(bits)], refs[len(bits) :]
    table, scale, sums, near, names, held, tile, sems = refs
    start, chan = where[0], where[1]
    tile_rows, half = tile.shape[0], table.shape[1]
    listed = names.shape[0]
    first_name = pl.multiple_of(start // listed * listed, listed)
    copies = [
        pltpu.make_async_copy(places, near, sems.at[len(bits)]),
        pltpu.make_async_copy(wanted.at[pl.ds(first_name, listed)], names, sems.at[len(bits) + 1]),
    ]
    parts = quarter_copies(spectra, held, sems, chan, bits)
    chunk = tile_rows // 4
    rows = [
        pltpu.make_async_copy(
            cotangent.at[pl.ds(n * chunk, chunk)],
            tile.at[pl.ds(n * chunk, chunk)],
            sems.at[len(bits) + 2 + n],
        )
        for n in range(4)
    ]
    order = copies + rows[:2] + parts[:1] + rows[2:] + parts[1:]
    for copy in order:
        copy.start()

    def fill(first, values):
        values = values.astype(jnp.float32)
        for side in range(2):
            table[pl.ds(2 * first + side, values.shape[0], stride=2), :] = values[
                :, side * half : (side + 1) * half
            ]

    for side in range(2):
        scale[pl.ds(side, NEIGH, stride=2), :] = mixing[:, side * half : (side + 1) * half]
    scales = [scale[2 * k : 2 * k + 2, :] for k in range(NEIGH)]
    fill(0, above[...])
    fill(HALO + tile_rows, below[...])
    for n in range(2):
        rows[2 * n].wait()
        rows[2 * n + 1].wait()
        if n < len(parts):
            parts[n].wait()
        for first in range(2 * n * chunk, 2 * (n + 1) * chunk, 256):
            fill(HALO + first, tile[first : first + 256, :])
        if n < len(parts):
            project_rows(held, weight, n, quarters[n])
    for copy in copies:
        copy.wait()

    group = 32
    offset = start - first_name

    def body(turn, carry):
        base = turn * group
        totals = []
        for n in range(group):
            pixel = names[offset + base + n]
            terms = [table[pl.ds(2 * (pixel + HALO), 2), :]]
            for k in range(NEIGH // 2):
                pair = near[k * tile_rows + pixel]
                for place, scale in ((pair & 0xFFFF, k), (pair >> 16, k + NEIGH // 2)):
                    terms.append(table[pl.ds(place, 2), :] * scales[scale])
            while len(terms) > 1:
                pairs = [x + y for x, y in zip(terms[::2], terms[1::2])]
                terms = pairs + terms[len(terms) // 2 * 2 :]
            totals += terms
        for n, total in enumerate(totals):
            sums[pl.ds(2 * (base + n), 2), :] = total
        return carry

    lax.fori_loop(0, count // group, body, 0)
    for side in range(2):
        out[:, side * half : (side + 1) * half] = sums[pl.ds(side, count, stride=2), :].astype(
            out.dtype
        )


def pixel_rows(
    cotangent, above, below, places, mixing, wanted, start, count, spectra, weight, chan, bits
):
    tile_rows, width = cotangent.shape
    depth, rows = spectra.shape[1], spectra.shape[0] // 4
    listed = min(wanted.shape[0], 1024)
    anywhere = pl.BlockSpec(memory_space=pl.ANY)
    hbm = pl.BlockSpec(memory_space=pltpu.HBM)
    vmem = pl.BlockSpec(memory_space=pltpu.VMEM)
    return pl.pallas_call(
        functools.partial(pixel_kernel, count, bits),
        out_shape=(
            jax.ShapeDtypeStruct((count, width), jnp.bfloat16),
            *[jax.ShapeDtypeStruct((rows, width), jnp.bfloat16)] * len(bits),
        ),
        in_specs=[
            pl.BlockSpec(memory_space=pltpu.SMEM),
            anywhere,
            anywhere,
            hbm,
            *[vmem] * 4,
            hbm,
        ],
        out_specs=(vmem,) * (1 + len(bits)),
        scratch_shapes=[
            pltpu.VMEM((2 * (tile_rows + 2 * HALO), width // 2), jnp.float32),
            pltpu.VMEM((2 * NEIGH, width // 2), jnp.float32),
            pltpu.VMEM((2 * count, width // 2), jnp.float32),
            pltpu.SMEM(places.shape, jnp.int32),
            pltpu.SMEM((listed,), jnp.int32),
            pltpu.VMEM((max(len(bits), 1) * rows, depth), jnp.bfloat16),
            pltpu.VMEM(cotangent.shape, cotangent.dtype),
            pltpu.SemaphoreType.DMA((len(bits) + 6,)),
        ],
        compiler_params=memory(LARGE),
        cost_estimate=pl.CostEstimate(
            flops=8 * NEIGH * count * 2048 * width,
            bytes_accessed=4 * tile_rows * width,
            transcendentals=0,
        ),
        name="pixel_rows",
    )(
        jnp.stack([start, chan]), places, wanted, cotangent, above, below, mixing, weight, spectra
    )


def gradient_kernel(where, first, second, third, fourth, tiles, weights, mine, answers, out):
    tile, chan = where[0], where[1]
    rows = out.shape[0]
    size = tiles.shape[1]
    count = rows // size
    group = 8 // count
    wide = jnp.float32
    start = pl.multiple_of(chan // group * 8, 8)

    def columns(values):
        turned = values[pl.ds(start, 8), :].T
        places = [turned[:, n * count : (n + 1) * count] for n in range(group)]
        picked = places[0]
        for n in range(1, group):
            picked = jnp.where(chan % group == n, places[n], picked)
        return picked

    own = columns(tiles).astype(wide)
    factors = columns(weights)
    for n in range(count):
        here = slice(n * size, (n + 1) * size)
        pre = first[here, :].astype(wide) + second[here, :].astype(wide)
        pre = pre + third[here, :].astype(wide) + fourth[here, :].astype(wide)
        sigma = jax.nn.sigmoid(pre)
        deriv = sigma * (1.0 + pre * (1.0 - sigma))
        fetched = jnp.where(
            own[:, n : n + 1] == tile.astype(wide),
            mine[here, :].astype(wide),
            answers[here, :].astype(wide),
        )
        out[here, :] = (factors[:, n : n + 1] * deriv * fetched).astype(out.dtype)


def pre_gradient(tile, chan, parts, tiles, weights, mine, answers):
    spec = pl.BlockSpec(memory_space=pltpu.VMEM)
    tiles, weights = tiles.reshape(-1, 128), weights.reshape(-1, 128)
    return pl.pallas_call(
        gradient_kernel,
        out_shape=jax.ShapeDtypeStruct(mine.shape, jnp.bfloat16),
        in_specs=[pl.BlockSpec(memory_space=pltpu.SMEM)] + [spec] * 8,
        out_specs=spec,
        compiler_params=memory(16),
        name="pre_gradient",
    )(jnp.stack([tile, chan]), *parts, tiles, weights, mine, answers)


def collect_kernel(core, *refs):
    *pieces, out = refs
    half, rows = out.shape[0] // 2, pieces[0].shape[0]
    count = len(pieces) // 2
    for index, piece in enumerate(pieces):
        which = core[0] if index < count else 1 - core[0]
        first = which * half + (index % count) * rows
        out[pl.ds(pl.multiple_of(first, rows), rows), :] = piece[...].astype(jnp.float32)


def collect(core, own, received):
    spec = pl.BlockSpec(memory_space=pltpu.VMEM)
    pieces = [*own, *received]
    rows, width = sum(piece.shape[0] for piece in pieces), own[0].shape[1]
    return pl.pallas_call(
        collect_kernel,
        out_shape=jax.ShapeDtypeStruct((rows, width), jnp.float32),
        in_specs=[pl.BlockSpec(memory_space=pltpu.SMEM)] + [spec] * len(pieces),
        out_specs=spec,
        compiler_params=memory(16),
        name="collect",
    )(core.reshape(1), *pieces)


def add_kernel(first, second, out):
    out[...] = (first[...].astype(jnp.float32) + second[...].astype(jnp.float32)).astype(out.dtype)


def added(first, second):
    spec = pl.BlockSpec(memory_space=pltpu.VMEM)
    return pl.pallas_call(
        add_kernel,
        out_shape=jax.ShapeDtypeStruct(first.shape, jnp.bfloat16),
        in_specs=[spec, spec],
        out_specs=spec,
        compiler_params=memory(16),
        name="added",
    )(first, second)


def sum_over_panels(core, parts, received):
    both = ("obs", "pix")
    parts = [added(part, other) for part, other in zip(parts, received)]
    for order in ((4, 1), (1, 4)):
        perm = [(i, i ^ order[(i >> 1) & 1]) for i in range(8)]
        parts = [added(part, lax.ppermute(part, both, perm)) for part in parts]
    return collect(core, parts, [swap(part, "obs", 1) for part in parts])


def shards(spectra, enc_weight, pix_tile, pix_local, foot_weight, cotangent, adjoint, mixing):
    tile_count = lax.axis_size("pix")
    tile_rows = cotangent.shape[0]
    quarter = spectra.shape[0] // lax.axis_size("chan")
    tile = lax.axis_index("pix")
    chan = lax.axis_index("chan")
    first_row = chan * quarter

    across, beyond = project(spectra, enc_weight, chan, (2, 3), LARGE + 4)
    parts = [swap(across, "chan", 2), swap(beyond, "chan", 3)]
    places = (adjoint - (tile * tile_rows - HALO)) * 2
    places = (places[: NEIGH // 2] | (places[NEIGH // 2 :] << 16)).reshape(-1)

    above, below = edges(cotangent, "pix", HALO)
    capacity = 2 * quarter // tile_count
    pixels = (cotangent, above, below, places, mixing)
    rest = (spectra, enc_weight)
    paired = capacity >= quarter and tile_count == 2
    if paired:
        wanted, start, count = swap(pix_local, "pix", 1), first_row, quarter
    else:
        tile_ids = lax.dynamic_slice_in_dim(pix_tile[:, 0], first_row, quarter, 0)
        local_ids = lax.dynamic_slice_in_dim(pix_local, first_row, quarter, 0)
        slot_index, wanted = requests(tile_ids, local_ids, capacity)
        start, count = 0 * chan, wanted.shape[0]
    rows, send = pixel_rows(*pixels, wanted, start, count, *rest, chan, (1,))
    rows, send, later = lax.optimization_barrier((rows, send, chan))
    parts.append(swap(send, "chan", 1))
    if paired:
        answers = swap(rows, "pix", 1)
        mine, keep = pixel_rows(*pixels, pix_local, later * quarter, count, *rest, later, (0,))
    else:
        (keep,) = project(*rest, later, (0,), LARGE)
        answers = lax.all_to_all(
            rows.reshape(tile_count, capacity, -1), "pix", split_axis=0, concat_axis=0, tiled=True
        )
        mine = answers = jnp.take(answers.reshape(tile_count * capacity, -1), slot_index, axis=0)
    parts.append(keep)
    grads = pre_gradient(tile, chan, parts, pix_tile, foot_weight, mine, answers)

    last = swap(grads, "chan", 2)
    across = swap(grads, "chan", 3)
    beside = swap(grads, "chan", 1)
    early, held, held_last = early_product(spectra, chan, grads, across)
    early = more_product(held, early, beside)
    core = lax.axis_index("obs") & 1
    send, keep = late_product(core, held_last, early, last)
    if lax.axis_size("obs") == 4 and tile_count == 2:
        return sum_over_panels(core, keep, [swap(part, "obs", 1) for part in send])
    return lax.psum(collect(core, keep, send), ("obs", "pix"))


def solution(mesh):
    return jax.shard_map(
        shards,
        mesh=mesh,
        in_specs=(
            P(("obs", "pix"), "chan"),
            P("chan", None),
            P(("obs", "pix"), None),
            P(("obs", "pix")),
            P(("obs", "pix")),
            P("pix", None),
            P(None, "pix"),
            P(),
        ),
        out_specs=P("chan", None),
        check_vma=False,
    )
```

```python
import functools

import jax
import jax.numpy as jnp
from jax import lax
from jax.experimental import pallas as pl
from jax.experimental.pallas import tpu as pltpu
from jax.sharding import PartitionSpec as P

NEIGH = 8
HALO = 128
MIB = 1024 * 1024
LARGE = 52


def edges(value, axis, width):
    size, length = lax.axis_size(axis), value.shape[0]
    last = lax.slice_in_dim(value, length - width, length, axis=0)
    first = lax.slice_in_dim(value, 0, width, axis=0)
    if size == 2:
        index = lax.axis_index(axis)
        other = lax.ppermute(jnp.where(index == 0, last, first), axis, [(0, 1), (1, 0)])
        return other, other
    up = [(i, i + 1) for i in range(size - 1)]
    return lax.ppermute(last, axis, up), lax.ppermute(first, axis, [(j, i) for i, j in up])


def requests(tile_ids, local_ids, capacity):
    tile_count = lax.axis_size("pix")
    onehot = (tile_ids[:, None] == jnp.arange(tile_count, dtype=jnp.int32)[None, :]).astype(
        jnp.int32
    )
    place_rank = jnp.sum((jnp.cumsum(onehot, axis=0) - 1) * onehot, axis=1)
    slot_index = tile_ids * capacity + place_rank
    outgoing = jnp.full((tile_count * capacity,), 0, jnp.int32).at[slot_index].set(local_ids)
    outgoing = outgoing.reshape(tile_count, capacity)
    requested = lax.all_to_all(outgoing, "pix", split_axis=0, concat_axis=0, tiled=True)
    return slot_index, requested.reshape(-1)


def swap(value, axis, bit):
    size = 1
    for name in (axis,) if isinstance(axis, str) else axis:
        size *= lax.axis_size(name)
    return lax.ppermute(value, axis, [(i, i ^ bit) for i in range(size)])


def memory(mib):
    return pltpu.CompilerParams(vmem_limit_bytes=mib * MIB)


def quarter_copies(spectra, held, sems, chan, bits):
    rows = spectra.shape[0] // 4
    return [
        pltpu.make_async_copy(
            spectra.at[pl.ds(pl.multiple_of((chan ^ bit) * rows, rows), rows)],
            held.at[pl.ds(turn * rows, rows)],
            sems.at[turn],
        )
        for turn, bit in enumerate(bits)
    ]


def project_rows(held, weight, turn, out):
    rows = out.shape[0]
    result = jnp.dot(
        held[turn * rows : (turn + 1) * rows, :], weight[...], preferred_element_type=jnp.float32
    )
    out[...] = result.astype(out.dtype)


def project_kernel(bits, chan, spectra, weight, *refs):
    *outs, held, near, sems = refs
    copies = [pltpu.make_async_copy(weight, near, sems.at[len(bits)])]
    copies += quarter_copies(spectra, held, sems, chan[0], bits)
    for copy in copies:
        copy.start()
    copies[0].wait()
    for turn, out in enumerate(outs):
        copies[turn + 1].wait()
        project_rows(held, near, turn, out)


def project(spectra, weight, chan, bits, grant):
    depth, width = weight.shape
    rows = spectra.shape[0] // 4
    hbm = pl.BlockSpec(memory_space=pltpu.HBM)
    return pl.pallas_call(
        functools.partial(project_kernel, bits),
        out_shape=(jax.ShapeDtypeStruct((rows, width), jnp.bfloat16),) * len(bits),
        in_specs=[pl.BlockSpec(memory_space=pltpu.SMEM), hbm, hbm],
        out_specs=(pl.BlockSpec(memory_space=pltpu.VMEM),) * len(bits),
        scratch_shapes=[
            pltpu.VMEM((len(bits) * rows, depth), jnp.bfloat16),
            pltpu.VMEM((depth, width), jnp.bfloat16),
            pltpu.SemaphoreType.DMA((len(bits) + 1,)),
        ],
        compiler_params=memory(grant),
        cost_estimate=pl.CostEstimate(
            flops=2 * len(bits) * rows * depth * width,
            bytes_accessed=2 * len(bits) * rows * (depth + width) + 2 * depth * width,
            transcendentals=0,
        ),
        name="project",
    )(chan.reshape(1), spectra, weight)


def turned_product(left, right):
    return lax.dot_general(
        left, right, (((0,), (0,)), ((), ())), preferred_element_type=jnp.float32
    )


def early_kernel(chan, spectra, first, second, total, third, fourth, held, sems):
    rows = first.shape[0]
    targets = (held.at[pl.ds(0, rows)], held.at[pl.ds(rows, rows)], third, fourth)
    copies = []
    for turn, (bits, target) in enumerate(zip((0, 3, 1, 2), targets)):
        start = pl.multiple_of((chan[0] ^ bits) * rows, rows)
        copies.append(pltpu.make_async_copy(spectra.at[pl.ds(start, rows)], target, sems.at[turn]))
    for copy in copies:
        copy.start()
    copies[0].wait()
    product = turned_product(held[:rows, :], first[...])
    copies[1].wait()
    total[...] = product + turned_product(held[rows:, :], second[...])
    copies[2].wait()
    copies[3].wait()


def early_product(spectra, chan, first, second):
    depth = spectra.shape[1]
    rows, width = first.shape
    vmem = pl.BlockSpec(memory_space=pltpu.VMEM)
    return pl.pallas_call(
        early_kernel,
        out_shape=(
            jax.ShapeDtypeStruct((depth, width), jnp.float32),
            jax.ShapeDtypeStruct((rows, depth), jnp.bfloat16),
            jax.ShapeDtypeStruct((rows, depth), jnp.bfloat16),
        ),
        in_specs=[
            pl.BlockSpec(memory_space=pltpu.SMEM),
            pl.BlockSpec(memory_space=pltpu.HBM),
            vmem,
            vmem,
        ],
        out_specs=(vmem,) * 3,
        scratch_shapes=[
            pltpu.VMEM((2 * rows, depth), jnp.bfloat16),
            pltpu.SemaphoreType.DMA((4,)),
        ],
        compiler_params=memory(48),
        cost_estimate=pl.CostEstimate(
            flops=4 * rows * depth * width,
            bytes_accessed=8 * rows * depth + 4 * depth * width,
            transcendentals=0,
        ),
        name="early_product",
    )(chan.reshape(1), spectra, first, second)


def more_kernel(held, before, rows, total):
    total[...] = before[...] + turned_product(held[...], rows[...])


def more_product(held, before, rows):
    vmem = pl.BlockSpec(memory_space=pltpu.VMEM)
    return pl.pallas_call(
        more_kernel,
        out_shape=jax.ShapeDtypeStruct(before.shape, jnp.float32),
        in_specs=[vmem] * 3,
        out_specs=vmem,
        compiler_params=memory(16),
        cost_estimate=pl.CostEstimate(
            flops=2 * held.shape[0] * held.shape[1] * rows.shape[1],
            bytes_accessed=2 * held.shape[0] * held.shape[1] + 8 * before.size,
            transcendentals=0,
        ),
        name="more_product",
    )(held, before, rows)


def late_kernel(core, held, before, rows, *outs):
    *outs, total = outs
    total[...] = before[...] + turned_product(held[...], rows[...])
    size = outs[0].shape[0]
    for index, out in enumerate(outs):
        first = (core[0] ^ (1 - index // 2)) * 2 * size + index % 2 * size
        here = pl.ds(pl.multiple_of(first, size), size)
        out[...] = total[here, :].astype(out.dtype)


def late_product(core, held, before, rows):
    size, width = before.shape[0] // 4, before.shape[1]
    spec = pl.BlockSpec(memory_space=pltpu.VMEM)
    send = jax.ShapeDtypeStruct((size, width), jnp.bfloat16)
    keep = jax.ShapeDtypeStruct((size, width), jnp.float32)
    outs = pl.pallas_call(
        late_kernel,
        out_shape=(send, send, keep, keep),
        in_specs=[pl.BlockSpec(memory_space=pltpu.SMEM)] + [spec] * 3,
        out_specs=(spec,) * 4,
        scratch_shapes=[pltpu.VMEM(before.shape, jnp.float32)],
        compiler_params=memory(16),
        cost_estimate=pl.CostEstimate(
            flops=2 * held.shape[0] * held.shape[1] * width,
            bytes_accessed=2 * held.shape[0] * held.shape[1] + 16 * size * width,
            transcendentals=0,
        ),
        name="late_product",
    )(core.reshape(1), held, before, rows)
    return outs[:2], outs[2:]


def pixel_kernel(count, bits, stride, where, places, wanted, cotangent, above, below, mixing, weight,
                 spectra, out, *refs):
    quarters, refs = refs[: len(bits)], refs[len(bits) :]
    table, scale, sums, near, names, held, tile, sems = refs
    chan = where[0]
    start = chan * stride
    tile_rows, half = tile.shape[0], table.shape[1]
    listed = names.shape[0]
    first_name = pl.multiple_of(start // listed * listed, listed)
    copies = [
        pltpu.make_async_copy(places, near, sems.at[len(bits)]),
        pltpu.make_async_copy(wanted.at[pl.ds(first_name, listed)], names, sems.at[len(bits) + 1]),
    ]
    parts = quarter_copies(spectra, held, sems, chan, bits)
    chunk = tile_rows // 4
    rows = [
        pltpu.make_async_copy(
            cotangent.at[pl.ds(n * chunk, chunk)],
            tile.at[pl.ds(n * chunk, chunk)],
            sems.at[len(bits) + 2 + n],
        )
        for n in range(4)
    ]
    order = copies + rows[:2] + parts[:1] + rows[2:] + parts[1:]
    for copy in order:
        copy.start()

    def fill(first, values):
        values = values.astype(jnp.float32)
        for side in range(2):
            table[pl.ds(2 * first + side, values.shape[0], stride=2), :] = values[
                :, side * half : (side + 1) * half
            ]

    for side in range(2):
        scale[pl.ds(side, NEIGH, stride=2), :] = mixing[:, side * half : (side + 1) * half]
    scales = [scale[2 * k : 2 * k + 2, :] for k in range(NEIGH)]
    fill(0, above[...])
    fill(HALO + tile_rows, below[...])
    for n in range(2):
        rows[2 * n].wait()
        rows[2 * n + 1].wait()
        if n < len(parts):
            parts[n].wait()
        for first in range(2 * n * chunk, 2 * (n + 1) * chunk, 256):
            fill(HALO + first, tile[first : first + 256, :])
        if n < len(parts):
            project_rows(held, weight, n, quarters[n])
    for copy in copies:
        copy.wait()

    group = 32
    offset = start - first_name

    def body(turn, carry):
        base = turn * group
        totals = []
        for n in range(group):
            pixel = names[offset + base + n]
            terms = [table[pl.ds(2 * (pixel + HALO), 2), :]]
            for k in range(NEIGH // 2):
                pair = near[k * tile_rows + pixel]
                for place, scale in ((pair & 0xFFFF, k), (pair >> 16, k + NEIGH // 2)):
                    terms.append(table[pl.ds(place, 2), :] * scales[scale])
            while len(terms) > 1:
                pairs = [x + y for x, y in zip(terms[::2], terms[1::2])]
                terms = pairs + terms[len(terms) // 2 * 2 :]
            totals += terms
        for n, total in enumerate(totals):
            sums[pl.ds(2 * (base + n), 2), :] = total
        return carry

    lax.fori_loop(0, count // group, body, 0)
    for side in range(2):
        out[:, side * half : (side + 1) * half] = sums[pl.ds(side, count, stride=2), :].astype(
            out.dtype
        )


def pixel_rows(
    cotangent, above, below, places, mixing, wanted, stride, count, spectra, weight, chan, bits
):
    tile_rows, width = cotangent.shape
    depth, rows = spectra.shape[1], spectra.shape[0] // 4
    listed = min(wanted.shape[0], 1024)
    anywhere = pl.BlockSpec(memory_space=pl.ANY)
    hbm = pl.BlockSpec(memory_space=pltpu.HBM)
    vmem = pl.BlockSpec(memory_space=pltpu.VMEM)
    return pl.pallas_call(
        functools.partial(pixel_kernel, count, bits, stride),
        out_shape=(
            jax.ShapeDtypeStruct((count, width), jnp.bfloat16),
            *[jax.ShapeDtypeStruct((rows, width), jnp.bfloat16)] * len(bits),
        ),
        in_specs=[
            pl.BlockSpec(memory_space=pltpu.SMEM),
            anywhere,
            anywhere,
            hbm,
            *[vmem] * 4,
            hbm,
        ],
        out_specs=(vmem,) * (1 + len(bits)),
        scratch_shapes=[
            pltpu.VMEM((2 * (tile_rows + 2 * HALO), width // 2), jnp.float32),
            pltpu.VMEM((2 * NEIGH, width // 2), jnp.float32),
            pltpu.VMEM((2 * count, width // 2), jnp.float32),
            pltpu.SMEM(places.shape, jnp.int32),
            pltpu.SMEM((listed,), jnp.int32),
            pltpu.VMEM((max(len(bits), 1) * rows, depth), jnp.bfloat16),
            pltpu.VMEM(cotangent.shape, cotangent.dtype),
            pltpu.SemaphoreType.DMA((len(bits) + 6,)),
        ],
        compiler_params=memory(LARGE),
        cost_estimate=pl.CostEstimate(
            flops=8 * NEIGH * count * 2048 * width,
            bytes_accessed=4 * tile_rows * width,
            transcendentals=0,
        ),
        name="pixel_rows",
    )(
        chan.reshape(1), places, wanted, cotangent, above, below, mixing, weight, spectra
    )


def gradient_kernel(tile_at, chan_at, keep, near, far, tiles, weights, mine, answers, out):
    tile, chan = tile_at[0], chan_at[0]
    rows = out.shape[0]
    size = tiles.shape[1]
    count = rows // size
    group = 8 // count
    wide = jnp.float32
    first = pl.multiple_of(chan // group * 8, 8)

    def columns(values):
        turned = values[pl.ds(first, 8), :].T
        places = [turned[:, n * count : (n + 1) * count] for n in range(group)]
        picked = places[0]
        for n in range(1, group):
            picked = jnp.where(chan % group == n, places[n], picked)
        return picked

    own = columns(tiles).astype(wide)
    factors = columns(weights)
    for n in range(count):
        here = slice(n * size, (n + 1) * size)
        pre = keep[here, :].astype(wide) + near[here, :].astype(wide) + far[here, :].astype(wide)
        sigma = jax.nn.sigmoid(pre)
        deriv = sigma * (1.0 + pre * (1.0 - sigma))
        fetched = jnp.where(
            own[:, n : n + 1] == tile.astype(wide),
            mine[here, :].astype(wide),
            answers[here, :].astype(wide),
        )
        out[here, :] = (factors[:, n : n + 1] * deriv * fetched).astype(out.dtype)


def pre_gradient(tile, chan, keep, near, far, tiles, weights, mine, answers):
    spec = pl.BlockSpec(memory_space=pltpu.VMEM)
    tiles, weights = tiles.reshape(-1, 128), weights.reshape(-1, 128)
    return pl.pallas_call(
        gradient_kernel,
        out_shape=jax.ShapeDtypeStruct(far.shape, jnp.bfloat16),
        in_specs=[pl.BlockSpec(memory_space=pltpu.SMEM)] * 2 + [spec] * 7,
        out_specs=spec,
        compiler_params=memory(16),
        name="pre_gradient",
    )(tile.reshape(1), chan.reshape(1), keep, near, far, tiles, weights, mine, answers)


def write_kernel(other, core, *refs):
    *pieces, out, first, second, sems = refs
    half, rows = out.shape[0] // 2, first.shape[0]
    copies = []
    for index, (piece, held) in enumerate(zip(pieces[-2:], (first, second))):
        held[...] = piece[...].astype(jnp.float32)
        place = (core[0] ^ other) * half + index * rows
        here = out.at[pl.ds(pl.multiple_of(place, rows), rows)]
        copies.append(pltpu.make_async_copy(held, here, sems.at[index]))
        copies[-1].start()
    for copy in copies:
        copy.wait()


def written(other, core, pieces, before=()):
    rows, width = pieces[0].shape
    spec = pl.BlockSpec(memory_space=pltpu.VMEM)
    hbm = pl.BlockSpec(memory_space=pltpu.HBM)
    return pl.pallas_call(
        functools.partial(write_kernel, other),
        out_shape=jax.ShapeDtypeStruct((4 * rows, width), jnp.float32),
        in_specs=[pl.BlockSpec(memory_space=pltpu.SMEM)] + [hbm] * len(before) + [spec] * 2,
        out_specs=hbm,
        input_output_aliases={1: 0} if before else {},
        scratch_shapes=[
            pltpu.VMEM((rows, width), jnp.float32),
            pltpu.VMEM((rows, width), jnp.float32),
            pltpu.SemaphoreType.DMA((2,)),
        ],
        compiler_params=memory(16),
        name="written",
    )(core.reshape(1), *before, *pieces)


def collect(core, own, received):
    return written(1, core, received, (written(0, core, own),))


def add_kernel(first, second, out):
    out[...] = (first[...].astype(jnp.float32) + second[...].astype(jnp.float32)).astype(out.dtype)


def added(first, second):
    spec = pl.BlockSpec(memory_space=pltpu.VMEM)
    return pl.pallas_call(
        add_kernel,
        out_shape=jax.ShapeDtypeStruct(first.shape, jnp.bfloat16),
        in_specs=[spec, spec],
        out_specs=spec,
        compiler_params=memory(16),
        name="added",
    )(first, second)


def sum_over_panels(core, parts, received):
    both = ("obs", "pix")
    parts = [added(part, other) for part, other in zip(parts, received)]
    for order in ((4, 1), (1, 4)):
        perm = [(i, i ^ order[(i >> 1) & 1]) for i in range(8)]
        parts = [added(part, lax.ppermute(part, both, perm)) for part in parts]
    return collect(core, parts, [swap(part, "obs", 1) for part in parts])


def shards(spectra, enc_weight, pix_tile, pix_local, foot_weight, cotangent, adjoint, mixing):
    tile_count = lax.axis_size("pix")
    tile_rows = cotangent.shape[0]
    quarter = spectra.shape[0] // lax.axis_size("chan")
    tile = lax.axis_index("pix")
    chan = lax.axis_index("chan")
    first_row = chan * quarter

    near_first = swap(project(spectra, enc_weight, chan, (2,), LARGE + 4)[0], "chan", 1)
    places = (adjoint - (tile * tile_rows - HALO)) * 2
    places = (places[: NEIGH // 2] | (places[NEIGH // 2 :] << 16)).reshape(-1)

    above, below = edges(cotangent, "pix", HALO)
    capacity = 2 * quarter // tile_count
    pixels = (cotangent, above, below, places, mixing)
    rest = (spectra, enc_weight)
    paired = capacity >= quarter and tile_count == 2
    if paired:
        wanted, stride, count = swap(pix_local, "pix", 1), quarter, quarter
    else:
        tile_ids = lax.dynamic_slice_in_dim(pix_tile[:, 0], first_row, quarter, 0)
        local_ids = lax.dynamic_slice_in_dim(pix_local, first_row, quarter, 0)
        slot_index, wanted = requests(tile_ids, local_ids, capacity)
        stride, count = 0, wanted.shape[0]
    rows, shared, send = pixel_rows(*pixels, wanted, stride, count, *rest, chan, (3, 1))
    near_first, rows = lax.optimization_barrier((near_first, rows))
    passed_on = (shared.astype(jnp.float32) + near_first.astype(jnp.float32)).astype(jnp.bfloat16)
    passed_on, send, rows, later = lax.optimization_barrier((passed_on, send, rows, chan))
    far = swap(passed_on, "chan", 3)
    near = swap(send, "chan", 1)
    if paired:
        answers = swap(rows, "pix", 1)
        mine, keep = pixel_rows(*pixels, pix_local, stride, count, *rest, later, (0,))
    else:
        (keep,) = project(*rest, later, (0,), LARGE)
        answers = lax.all_to_all(
            rows.reshape(tile_count, capacity, -1), "pix", split_axis=0, concat_axis=0, tiled=True
        )
        mine = answers = jnp.take(answers.reshape(tile_count * capacity, -1), slot_index, axis=0)
    grads = pre_gradient(tile, chan, keep, near, far, pix_tile, foot_weight, mine, answers)

    across = swap(grads, "chan", 3)
    beside = swap(grads, "chan", 1)
    last = swap(across, "chan", 1)
    early, held, held_last = early_product(spectra, chan, grads, across)
    early = more_product(held, early, beside)
    core = lax.axis_index("obs") & 1
    send, keep = late_product(core, held_last, early, last)
    if lax.axis_size("obs") == 4 and tile_count == 2:
        return sum_over_panels(core, keep, [swap(part, "obs", 1) for part in send])
    return lax.psum(collect(core, keep, send), ("obs", "pix"))


def solution(mesh):
    return jax.shard_map(
        shards,
        mesh=mesh,
        in_specs=(
            P(("obs", "pix"), "chan"),
            P("chan", None),
            P(("obs", "pix"), None),
            P(("obs", "pix")),
            P(("obs", "pix")),
            P("pix", None),
            P(None, "pix"),
            P(),
        ),
        out_specs=P("chan", None),
        check_vma=False,
    )
```

```python
import functools

import jax
import jax.numpy as jnp
from jax import lax
from jax.experimental import pallas as pl
from jax.experimental.pallas import tpu as pltpu
from jax.sharding import PartitionSpec as P

NEIGH = 8
HALO = 128
MIB = 1024 * 1024
LARGE = 52


def edge_kernel(tile, value, out, sem):
    first = (1 - tile[0]) * (value.shape[0] - out.shape[0])
    rows = value.at[pl.ds(pl.multiple_of(first, out.shape[0]), out.shape[0])]
    copy = pltpu.make_async_copy(rows, out, sem)
    copy.start()
    copy.wait()


def edge(tile, value, width):
    return pl.pallas_call(
        edge_kernel,
        out_shape=jax.ShapeDtypeStruct((width, value.shape[1]), value.dtype),
        in_specs=[
            pl.BlockSpec(memory_space=pltpu.SMEM),
            pl.BlockSpec(memory_space=pltpu.HBM),
        ],
        out_specs=pl.BlockSpec(memory_space=pltpu.VMEM),
        scratch_shapes=[pltpu.SemaphoreType.DMA],
        compiler_params=memory(LARGE),
        name="edge",
    )(tile.reshape(1), value)


def edges(value, axis, width):
    size, length = lax.axis_size(axis), value.shape[0]
    if size == 2:
        other = swap(edge(lax.axis_index(axis), value, width), axis, 1)
        return other, other
    last = lax.slice_in_dim(value, length - width, length, axis=0)
    first = lax.slice_in_dim(value, 0, width, axis=0)
    up = [(i, i + 1) for i in range(size - 1)]
    return lax.ppermute(last, axis, up), lax.ppermute(first, axis, [(j, i) for i, j in up])


def requests(tile_ids, local_ids, capacity):
    tile_count = lax.axis_size("pix")
    onehot = (tile_ids[:, None] == jnp.arange(tile_count, dtype=jnp.int32)[None, :]).astype(
        jnp.int32
    )
    place_rank = jnp.sum((jnp.cumsum(onehot, axis=0) - 1) * onehot, axis=1)
    slot_index = tile_ids * capacity + place_rank
    outgoing = jnp.full((tile_count * capacity,), 0, jnp.int32).at[slot_index].set(local_ids)
    outgoing = outgoing.reshape(tile_count, capacity)
    requested = lax.all_to_all(outgoing, "pix", split_axis=0, concat_axis=0, tiled=True)
    return slot_index, requested.reshape(-1)


def swap(value, axis, bit):
    size = 1
    for name in (axis,) if isinstance(axis, str) else axis:
        size *= lax.axis_size(name)
    return lax.ppermute(value, axis, [(i, i ^ bit) for i in range(size)])


def memory(mib):
    return pltpu.CompilerParams(vmem_limit_bytes=mib * MIB)


def quarter_copies(spectra, held, sems, chan, bits):
    rows = spectra.shape[0] // 4
    return [
        pltpu.make_async_copy(
            spectra.at[pl.ds(pl.multiple_of((chan ^ bit) * rows, rows), rows)],
            held.at[pl.ds(turn * rows, rows)],
            sems.at[turn],
        )
        for turn, bit in enumerate(bits)
    ]


def project_rows(held, weight, turn, out):
    rows = out.shape[0]
    result = jnp.dot(
        held[turn * rows : (turn + 1) * rows, :], weight[...], preferred_element_type=jnp.float32
    )
    out[...] = result.astype(out.dtype)


def project_kernel(bits, chan, spectra, weight, *refs):
    *outs, held, near, sems = refs
    copies = [pltpu.make_async_copy(weight, near, sems.at[len(bits)])]
    copies += quarter_copies(spectra, held, sems, chan[0], bits)
    for copy in copies:
        copy.start()
    copies[0].wait()
    for turn, out in enumerate(outs):
        copies[turn + 1].wait()
        project_rows(held, near, turn, out)


def project(spectra, weight, chan, bits, grant):
    depth, width = weight.shape
    rows = spectra.shape[0] // 4
    hbm = pl.BlockSpec(memory_space=pltpu.HBM)
    return pl.pallas_call(
        functools.partial(project_kernel, bits),
        out_shape=(jax.ShapeDtypeStruct((rows, width), jnp.bfloat16),) * len(bits),
        in_specs=[pl.BlockSpec(memory_space=pltpu.SMEM), hbm, hbm],
        out_specs=(pl.BlockSpec(memory_space=pltpu.VMEM),) * len(bits),
        scratch_shapes=[
            pltpu.VMEM((len(bits) * rows, depth), jnp.bfloat16),
            pltpu.VMEM((depth, width), jnp.bfloat16),
            pltpu.SemaphoreType.DMA((len(bits) + 1,)),
        ],
        compiler_params=memory(grant),
        cost_estimate=pl.CostEstimate(
            flops=2 * len(bits) * rows * depth * width,
            bytes_accessed=2 * len(bits) * rows * (depth + width) + 2 * depth * width,
            transcendentals=0,
        ),
        name="project",
    )(chan.reshape(1), spectra, weight)


def turned_product(left, right):
    return lax.dot_general(
        left, right, (((0,), (0,)), ((), ())), preferred_element_type=jnp.float32
    )


def early_kernel(chan, spectra, first, second, total, third, fourth, held, sems):
    rows = first.shape[0]
    targets = (held.at[pl.ds(0, rows)], held.at[pl.ds(rows, rows)], third, fourth)
    copies = []
    for turn, (bits, target) in enumerate(zip((0, 3, 1, 2), targets)):
        start = pl.multiple_of((chan[0] ^ bits) * rows, rows)
        copies.append(pltpu.make_async_copy(spectra.at[pl.ds(start, rows)], target, sems.at[turn]))
    for copy in copies:
        copy.start()
    copies[0].wait()
    product = turned_product(held[:rows, :], first[...])
    copies[1].wait()
    total[...] = product + turned_product(held[rows:, :], second[...])
    copies[2].wait()
    copies[3].wait()


def early_product(spectra, chan, first, second):
    depth = spectra.shape[1]
    rows, width = first.shape
    vmem = pl.BlockSpec(memory_space=pltpu.VMEM)
    return pl.pallas_call(
        early_kernel,
        out_shape=(
            jax.ShapeDtypeStruct((depth, width), jnp.float32),
            jax.ShapeDtypeStruct((rows, depth), jnp.bfloat16),
            jax.ShapeDtypeStruct((rows, depth), jnp.bfloat16),
        ),
        in_specs=[
            pl.BlockSpec(memory_space=pltpu.SMEM),
            pl.BlockSpec(memory_space=pltpu.HBM),
            vmem,
            vmem,
        ],
        out_specs=(vmem,) * 3,
        scratch_shapes=[
            pltpu.VMEM((2 * rows, depth), jnp.bfloat16),
            pltpu.SemaphoreType.DMA((4,)),
        ],
        compiler_params=memory(48),
        cost_estimate=pl.CostEstimate(
            flops=4 * rows * depth * width,
            bytes_accessed=8 * rows * depth + 4 * depth * width,
            transcendentals=0,
        ),
        name="early_product",
    )(chan.reshape(1), spectra, first, second)


def more_kernel(held, before, rows, total):
    total[...] = before[...] + turned_product(held[...], rows[...])


def more_product(held, before, rows):
    vmem = pl.BlockSpec(memory_space=pltpu.VMEM)
    return pl.pallas_call(
        more_kernel,
        out_shape=jax.ShapeDtypeStruct(before.shape, jnp.float32),
        in_specs=[vmem] * 3,
        out_specs=vmem,
        compiler_params=memory(16),
        cost_estimate=pl.CostEstimate(
            flops=2 * held.shape[0] * held.shape[1] * rows.shape[1],
            bytes_accessed=2 * held.shape[0] * held.shape[1] + 8 * before.size,
            transcendentals=0,
        ),
        name="more_product",
    )(held, before, rows)


def late_kernel(core, held, before, rows, *outs):
    *outs, total = outs
    total[...] = before[...] + turned_product(held[...], rows[...])
    size = outs[0].shape[0]
    for index, out in enumerate(outs):
        first = (core[0] ^ (1 - index // 2)) * 2 * size + index % 2 * size
        here = pl.ds(pl.multiple_of(first, size), size)
        out[...] = total[here, :].astype(out.dtype)


def late_product(core, held, before, rows):
    size, width = before.shape[0] // 4, before.shape[1]
    spec = pl.BlockSpec(memory_space=pltpu.VMEM)
    send = jax.ShapeDtypeStruct((size, width), jnp.bfloat16)
    keep = jax.ShapeDtypeStruct((size, width), jnp.float32)
    outs = pl.pallas_call(
        late_kernel,
        out_shape=(send, send, keep, keep),
        in_specs=[pl.BlockSpec(memory_space=pltpu.SMEM)] + [spec] * 3,
        out_specs=(spec,) * 4,
        scratch_shapes=[pltpu.VMEM(before.shape, jnp.float32)],
        compiler_params=memory(16),
        cost_estimate=pl.CostEstimate(
            flops=2 * held.shape[0] * held.shape[1] * width,
            bytes_accessed=2 * held.shape[0] * held.shape[1] + 16 * size * width,
            transcendentals=0,
        ),
        name="late_product",
    )(core.reshape(1), held, before, rows)
    return outs[:2], outs[2:]


def pixel_kernel(count, bits, stride, where, places, wanted, cotangent, above, below, mixing, weight,
                 spectra, out, *refs):
    quarters, refs = refs[: len(bits)], refs[len(bits) :]
    table, scale, sums, near, names, held, tile, sems = refs
    chan = where[0]
    start = chan * stride
    tile_rows, half = tile.shape[0], table.shape[1]
    listed = names.shape[0]
    first_name = pl.multiple_of(start // listed * listed, listed)
    copies = [
        pltpu.make_async_copy(places, near, sems.at[len(bits)]),
        pltpu.make_async_copy(wanted.at[pl.ds(first_name, listed)], names, sems.at[len(bits) + 1]),
    ]
    parts = quarter_copies(spectra, held, sems, chan, bits)
    chunk = tile_rows // 4
    rows = [
        pltpu.make_async_copy(
            cotangent.at[pl.ds(n * chunk, chunk)],
            tile.at[pl.ds(n * chunk, chunk)],
            sems.at[len(bits) + 2 + n],
        )
        for n in range(4)
    ]
    order = copies + rows[:2] + parts[:1] + rows[2:] + parts[1:]
    for copy in order:
        copy.start()

    def fill(first, values):
        values = values.astype(jnp.float32)
        for side in range(2):
            table[pl.ds(2 * first + side, values.shape[0], stride=2), :] = values[
                :, side * half : (side + 1) * half
            ]

    for side in range(2):
        scale[pl.ds(side, NEIGH, stride=2), :] = mixing[:, side * half : (side + 1) * half]
    scales = [scale[2 * k : 2 * k + 2, :] for k in range(NEIGH)]
    fill(0, above[...])
    fill(HALO + tile_rows, below[...])
    for n in range(2):
        rows[2 * n].wait()
        rows[2 * n + 1].wait()
        if n < len(parts):
            parts[n].wait()
        for first in range(2 * n * chunk, 2 * (n + 1) * chunk, 256):
            fill(HALO + first, tile[first : first + 256, :])
        if n < len(parts):
            project_rows(held, weight, n, quarters[n])
    for copy in copies:
        copy.wait()

    group = 32
    offset = start - first_name

    def body(turn, carry):
        base = turn * group
        totals = []
        for n in range(group):
            pixel = names[offset + base + n]
            terms = [table[pl.ds(2 * (pixel + HALO), 2), :]]
            for k in range(NEIGH // 2):
                pair = near[k * tile_rows + pixel]
                for place, scale in ((pair & 0xFFFF, k), (pair >> 16, k + NEIGH // 2)):
                    terms.append(table[pl.ds(place, 2), :] * scales[scale])
            while len(terms) > 1:
                pairs = [x + y for x, y in zip(terms[::2], terms[1::2])]
                terms = pairs + terms[len(terms) // 2 * 2 :]
            totals += terms
        for n, total in enumerate(totals):
            sums[pl.ds(2 * (base + n), 2), :] = total
        return carry

    lax.fori_loop(0, count // group, body, 0)
    for side in range(2):
        out[:, side * half : (side + 1) * half] = sums[pl.ds(side, count, stride=2), :].astype(
            out.dtype
        )


def pixel_rows(
    cotangent, above, below, places, mixing, wanted, stride, count, spectra, weight, chan, bits
):
    tile_rows, width = cotangent.shape
    depth, rows = spectra.shape[1], spectra.shape[0] // 4
    listed = min(wanted.shape[0], 1024)
    anywhere = pl.BlockSpec(memory_space=pl.ANY)
    hbm = pl.BlockSpec(memory_space=pltpu.HBM)
    vmem = pl.BlockSpec(memory_space=pltpu.VMEM)
    return pl.pallas_call(
        functools.partial(pixel_kernel, count, bits, stride),
        out_shape=(
            jax.ShapeDtypeStruct((count, width), jnp.bfloat16),
            *[jax.ShapeDtypeStruct((rows, width), jnp.bfloat16)] * len(bits),
        ),
        in_specs=[
            pl.BlockSpec(memory_space=pltpu.SMEM),
            anywhere,
            anywhere,
            hbm,
            *[vmem] * 4,
            hbm,
        ],
        out_specs=(vmem,) * (1 + len(bits)),
        scratch_shapes=[
            pltpu.VMEM((2 * (tile_rows + 2 * HALO), width // 2), jnp.float32),
            pltpu.VMEM((2 * NEIGH, width // 2), jnp.float32),
            pltpu.VMEM((2 * count, width // 2), jnp.float32),
            pltpu.SMEM(places.shape, jnp.int32),
            pltpu.SMEM((listed,), jnp.int32),
            pltpu.VMEM((max(len(bits), 1) * rows, depth), jnp.bfloat16),
            pltpu.VMEM(cotangent.shape, cotangent.dtype),
            pltpu.SemaphoreType.DMA((len(bits) + 6,)),
        ],
        compiler_params=memory(LARGE),
        cost_estimate=pl.CostEstimate(
            flops=8 * NEIGH * count * 2048 * width,
            bytes_accessed=4 * tile_rows * width,
            transcendentals=0,
        ),
        name="pixel_rows",
    )(
        chan.reshape(1), places, wanted, cotangent, above, below, mixing, weight, spectra
    )


def gradient_kernel(tile_at, chan_at, keep, near, far, tiles, weights, mine, answers, out):
    tile, chan = tile_at[0], chan_at[0]
    rows = out.shape[0]
    size = tiles.shape[1]
    count = rows // size
    group = 8 // count
    wide = jnp.float32
    first = pl.multiple_of(chan // group * 8, 8)

    def columns(values):
        turned = values[pl.ds(first, 8), :].T
        places = [turned[:, n * count : (n + 1) * count] for n in range(group)]
        picked = places[0]
        for n in range(1, group):
            picked = jnp.where(chan % group == n, places[n], picked)
        return picked

    own = columns(tiles).astype(wide)
    factors = columns(weights)
    for n in range(count):
        here = slice(n * size, (n + 1) * size)
        pre = keep[here, :].astype(wide) + near[here, :].astype(wide) + far[here, :].astype(wide)
        sigma = jax.nn.sigmoid(pre)
        deriv = sigma * (1.0 + pre * (1.0 - sigma))
        fetched = jnp.where(
            own[:, n : n + 1] == tile.astype(wide),
            mine[here, :].astype(wide),
            answers[here, :].astype(wide),
        )
        out[here, :] = (factors[:, n : n + 1] * deriv * fetched).astype(out.dtype)


def pre_gradient(tile, chan, keep, near, far, tiles, weights, mine, answers):
    spec = pl.BlockSpec(memory_space=pltpu.VMEM)
    tiles, weights = tiles.reshape(-1, 128), weights.reshape(-1, 128)
    return pl.pallas_call(
        gradient_kernel,
        out_shape=jax.ShapeDtypeStruct(far.shape, jnp.bfloat16),
        in_specs=[pl.BlockSpec(memory_space=pltpu.SMEM)] * 2 + [spec] * 7,
        out_specs=spec,
        compiler_params=memory(16),
        name="pre_gradient",
    )(tile.reshape(1), chan.reshape(1), keep, near, far, tiles, weights, mine, answers)


def write_kernel(other, index, core, *refs):
    piece, out, held, sem = refs[-4:]
    rows = held.shape[0]
    held[...] = piece[...].astype(jnp.float32)
    first = ((core[0] ^ other) * 2 + index) * rows
    copy = pltpu.make_async_copy(held, out.at[pl.ds(pl.multiple_of(first, rows), rows)], sem)
    copy.start()
    copy.wait()


def written(other, index, core, piece, before=()):
    rows, width = piece.shape
    hbm = pl.BlockSpec(memory_space=pltpu.HBM)
    return pl.pallas_call(
        functools.partial(write_kernel, other, index),
        out_shape=jax.ShapeDtypeStruct((4 * rows, width), jnp.float32),
        in_specs=[
            pl.BlockSpec(memory_space=pltpu.SMEM),
            *[hbm] * len(before),
            pl.BlockSpec(memory_space=pltpu.VMEM),
        ],
        out_specs=hbm,
        input_output_aliases={1: 0} if before else {},
        scratch_shapes=[pltpu.VMEM((rows, width), jnp.float32), pltpu.SemaphoreType.DMA],
        compiler_params=memory(16),
        name="written",
    )(core.reshape(1), *before, piece)


def collect(core, own, received):
    result = ()
    for index in range(2):
        for other, pieces in enumerate((own, received)):
            result = (written(other, index, core, pieces[index], result),)
    return result[0]


def add_kernel(first, second, out):
    out[...] = (first[...].astype(jnp.float32) + second[...].astype(jnp.float32)).astype(out.dtype)


def added(first, second):
    spec = pl.BlockSpec(memory_space=pltpu.VMEM)
    return pl.pallas_call(
        add_kernel,
        out_shape=jax.ShapeDtypeStruct(first.shape, jnp.bfloat16),
        in_specs=[spec, spec],
        out_specs=spec,
        compiler_params=memory(16),
        name="added",
    )(first, second)


def sum_over_panels(core, parts, received):
    both = ("obs", "pix")
    parts = [added(part, other) for part, other in zip(parts, received)]
    for order in ((4, 1), (1, 4)):
        perm = [(i, i ^ order[(i >> 1) & 1]) for i in range(8)]
        parts = [added(part, lax.ppermute(part, both, perm)) for part in parts]
    return collect(core, parts, [swap(part, "obs", 1) for part in parts])


def shards(spectra, enc_weight, pix_tile, pix_local, foot_weight, cotangent, adjoint, mixing):
    tile_count = lax.axis_size("pix")
    tile_rows = cotangent.shape[0]
    quarter = spectra.shape[0] // lax.axis_size("chan")
    tile = lax.axis_index("pix")
    chan = lax.axis_index("chan")
    first_row = chan * quarter

    near_first = swap(project(spectra, enc_weight, chan, (2,), LARGE + 4)[0], "chan", 1)
    places = (adjoint - (tile * tile_rows - HALO)) * 2
    places = (places[: NEIGH // 2] | (places[NEIGH // 2 :] << 16)).reshape(-1)

    above, below = edges(cotangent, "pix", HALO)
    capacity = 2 * quarter // tile_count
    pixels = (cotangent, above, below, places, mixing)
    rest = (spectra, enc_weight)
    paired = capacity >= quarter and tile_count == 2
    if paired:
        wanted, stride, count = swap(pix_local, "pix", 1), quarter, quarter
    else:
        tile_ids = lax.dynamic_slice_in_dim(pix_tile[:, 0], first_row, quarter, 0)
        local_ids = lax.dynamic_slice_in_dim(pix_local, first_row, quarter, 0)
        slot_index, wanted = requests(tile_ids, local_ids, capacity)
        stride, count = 0, wanted.shape[0]
    rows, shared, send = pixel_rows(*pixels, wanted, stride, count, *rest, chan, (3, 1))
    near_first, rows = lax.optimization_barrier((near_first, rows))
    passed_on = (shared.astype(jnp.float32) + near_first.astype(jnp.float32)).astype(jnp.bfloat16)
    passed_on, send, rows, later = lax.optimization_barrier((passed_on, send, rows, chan))
    far = swap(passed_on, "chan", 3)
    near = swap(send, "chan", 1)
    if paired:
        answers = swap(rows, "pix", 1)
        mine, keep = pixel_rows(*pixels, pix_local, stride, count, *rest, later, (0,))
    else:
        (keep,) = project(*rest, later, (0,), LARGE)
        answers = lax.all_to_all(
            rows.reshape(tile_count, capacity, -1), "pix", split_axis=0, concat_axis=0, tiled=True
        )
        mine = answers = jnp.take(answers.reshape(tile_count * capacity, -1), slot_index, axis=0)
    grads = pre_gradient(tile, chan, keep, near, far, pix_tile, foot_weight, mine, answers)

    across = swap(grads, "chan", 3)
    beside = swap(grads, "chan", 1)
    last = swap(across, "chan", 1)
    early, held, held_last = early_product(spectra, chan, grads, across)
    early = more_product(held, early, beside)
    core = lax.axis_index("obs") & 1
    send, keep = late_product(core, held_last, early, last)
    if lax.axis_size("obs") == 4 and tile_count == 2:
        return sum_over_panels(core, keep, [swap(part, "obs", 1) for part in send])
    return lax.psum(collect(core, keep, send), ("obs", "pix"))


def solution(mesh):
    return jax.shard_map(
        shards,
        mesh=mesh,
        in_specs=(
            P(("obs", "pix"), "chan"),
            P("chan", None),
            P(("obs", "pix"), None),
            P(("obs", "pix")),
            P(("obs", "pix")),
            P("pix", None),
            P(None, "pix"),
            P(),
        ),
        out_specs=P("chan", None),
        check_vma=False,
    )
```

```python
import functools

import jax
import jax.numpy as jnp
from jax import lax
from jax.experimental import pallas as pl
from jax.experimental.pallas import tpu as pltpu
from jax.sharding import PartitionSpec as P

NEIGH = 8
HALO = 128
MIB = 1024 * 1024
LARGE = 52


def edges(value, axis, width):
    size, length = lax.axis_size(axis), value.shape[0]
    last = lax.slice_in_dim(value, length - width, length, axis=0)
    first = lax.slice_in_dim(value, 0, width, axis=0)
    if size == 2:
        index = lax.axis_index(axis)
        other = lax.ppermute(jnp.where(index == 0, last, first), axis, [(0, 1), (1, 0)])
        return other, other
    up = [(i, i + 1) for i in range(size - 1)]
    return lax.ppermute(last, axis, up), lax.ppermute(first, axis, [(j, i) for i, j in up])


def requests(tile_ids, local_ids, capacity):
    tile_count = lax.axis_size("pix")
    onehot = (tile_ids[:, None] == jnp.arange(tile_count, dtype=jnp.int32)[None, :]).astype(
        jnp.int32
    )
    place_rank = jnp.sum((jnp.cumsum(onehot, axis=0) - 1) * onehot, axis=1)
    slot_index = tile_ids * capacity + place_rank
    outgoing = jnp.full((tile_count * capacity,), 0, jnp.int32).at[slot_index].set(local_ids)
    outgoing = outgoing.reshape(tile_count, capacity)
    requested = lax.all_to_all(outgoing, "pix", split_axis=0, concat_axis=0, tiled=True)
    return slot_index, requested.reshape(-1)


def swap(value, axis, bit):
    size = 1
    for name in (axis,) if isinstance(axis, str) else axis:
        size *= lax.axis_size(name)
    return lax.ppermute(value, axis, [(i, i ^ bit) for i in range(size)])


def memory(mib):
    return pltpu.CompilerParams(vmem_limit_bytes=mib * MIB)


def quarter_copies(spectra, held, sems, chan, bits):
    rows = spectra.shape[0] // 4
    return [
        pltpu.make_async_copy(
            spectra.at[pl.ds(pl.multiple_of((chan ^ bit) * rows, rows), rows)],
            held.at[pl.ds(turn * rows, rows)],
            sems.at[turn],
        )
        for turn, bit in enumerate(bits)
    ]


def project_rows(held, weight, turn, out):
    rows = out.shape[0]
    result = jnp.dot(
        held[turn * rows : (turn + 1) * rows, :], weight[...], preferred_element_type=jnp.float32
    )
    out[...] = result.astype(out.dtype)


def project_kernel(bits, chan, spectra, weight, *refs):
    *outs, held, near, sems = refs
    copies = [pltpu.make_async_copy(weight, near, sems.at[len(bits)])]
    copies += quarter_copies(spectra, held, sems, chan[0], bits)
    for copy in copies:
        copy.start()
    copies[0].wait()
    for turn, out in enumerate(outs):
        copies[turn + 1].wait()
        project_rows(held, near, turn, out)


def project(spectra, weight, chan, bits, grant):
    depth, width = weight.shape
    rows = spectra.shape[0] // 4
    hbm = pl.BlockSpec(memory_space=pltpu.HBM)
    return pl.pallas_call(
        functools.partial(project_kernel, bits),
        out_shape=(jax.ShapeDtypeStruct((rows, width), jnp.bfloat16),) * len(bits),
        in_specs=[pl.BlockSpec(memory_space=pltpu.SMEM), hbm, hbm],
        out_specs=(pl.BlockSpec(memory_space=pltpu.VMEM),) * len(bits),
        scratch_shapes=[
            pltpu.VMEM((len(bits) * rows, depth), jnp.bfloat16),
            pltpu.VMEM((depth, width), jnp.bfloat16),
            pltpu.SemaphoreType.DMA((len(bits) + 1,)),
        ],
        compiler_params=memory(grant),
        cost_estimate=pl.CostEstimate(
            flops=2 * len(bits) * rows * depth * width,
            bytes_accessed=2 * len(bits) * rows * (depth + width) + 2 * depth * width,
            transcendentals=0,
        ),
        name="project",
    )(chan.reshape(1), spectra, weight)


def turned_product(left, right):
    return lax.dot_general(
        left, right, (((0,), (0,)), ((), ())), preferred_element_type=jnp.float32
    )


def early_kernel(chan, spectra, first, second, total, third, fourth, held, sems):
    rows = first.shape[0]
    targets = (held.at[pl.ds(0, rows)], held.at[pl.ds(rows, rows)], third, fourth)
    copies = []
    for turn, (bits, target) in enumerate(zip((0, 3, 1, 2), targets)):
        start = pl.multiple_of((chan[0] ^ bits) * rows, rows)
        copies.append(pltpu.make_async_copy(spectra.at[pl.ds(start, rows)], target, sems.at[turn]))
    for copy in copies:
        copy.start()
    copies[0].wait()
    product = turned_product(held[:rows, :], first[...])
    copies[1].wait()
    total[...] = product + turned_product(held[rows:, :], second[...])
    copies[2].wait()
    copies[3].wait()


def early_product(spectra, chan, first, second):
    depth = spectra.shape[1]
    rows, width = first.shape
    vmem = pl.BlockSpec(memory_space=pltpu.VMEM)
    return pl.pallas_call(
        early_kernel,
        out_shape=(
            jax.ShapeDtypeStruct((depth, width), jnp.float32),
            jax.ShapeDtypeStruct((rows, depth), jnp.bfloat16),
            jax.ShapeDtypeStruct((rows, depth), jnp.bfloat16),
        ),
        in_specs=[
            pl.BlockSpec(memory_space=pltpu.SMEM),
            pl.BlockSpec(memory_space=pltpu.HBM),
            vmem,
            vmem,
        ],
        out_specs=(vmem,) * 3,
        scratch_shapes=[
            pltpu.VMEM((2 * rows, depth), jnp.bfloat16),
            pltpu.SemaphoreType.DMA((4,)),
        ],
        compiler_params=memory(48),
        cost_estimate=pl.CostEstimate(
            flops=4 * rows * depth * width,
            bytes_accessed=8 * rows * depth + 4 * depth * width,
            transcendentals=0,
        ),
        name="early_product",
    )(chan.reshape(1), spectra, first, second)


def more_kernel(held, before, rows, total):
    total[...] = before[...] + turned_product(held[...], rows[...])


def more_product(held, before, rows):
    vmem = pl.BlockSpec(memory_space=pltpu.VMEM)
    return pl.pallas_call(
        more_kernel,
        out_shape=jax.ShapeDtypeStruct(before.shape, jnp.float32),
        in_specs=[vmem] * 3,
        out_specs=vmem,
        compiler_params=memory(16),
        cost_estimate=pl.CostEstimate(
            flops=2 * held.shape[0] * held.shape[1] * rows.shape[1],
            bytes_accessed=2 * held.shape[0] * held.shape[1] + 8 * before.size,
            transcendentals=0,
        ),
        name="more_product",
    )(held, before, rows)


def late_kernel(core, held, before, rows, *outs):
    *outs, total = outs
    total[...] = before[...] + turned_product(held[...], rows[...])
    size = outs[0].shape[0]
    for index, out in enumerate(outs):
        first = (core[0] ^ (1 - index // 2)) * 2 * size + index % 2 * size
        here = pl.ds(pl.multiple_of(first, size), size)
        out[...] = total[here, :].astype(out.dtype)


def late_product(core, held, before, rows):
    size, width = before.shape[0] // 4, before.shape[1]
    spec = pl.BlockSpec(memory_space=pltpu.VMEM)
    send = jax.ShapeDtypeStruct((size, width), jnp.bfloat16)
    keep = jax.ShapeDtypeStruct((size, width), jnp.float32)
    outs = pl.pallas_call(
        late_kernel,
        out_shape=(send, send, keep, keep),
        in_specs=[pl.BlockSpec(memory_space=pltpu.SMEM)] + [spec] * 3,
        out_specs=(spec,) * 4,
        scratch_shapes=[pltpu.VMEM(before.shape, jnp.float32)],
        compiler_params=memory(16),
        cost_estimate=pl.CostEstimate(
            flops=2 * held.shape[0] * held.shape[1] * width,
            bytes_accessed=2 * held.shape[0] * held.shape[1] + 16 * size * width,
            transcendentals=0,
        ),
        name="late_product",
    )(core.reshape(1), held, before, rows)
    return outs[:2], outs[2:]


def pixel_kernel(count, bits, stride, skip, where, places, wanted, cotangent, above, below, mixing, weight,
                 spectra, out, *refs):
    quarters, refs = refs[: len(bits)], refs[len(bits) :]
    table, scale, sums, near, names, held, tile, sems = refs
    chan = where[0]
    start = chan * stride + skip
    tile_rows, half = tile.shape[0], table.shape[1]
    listed = names.shape[0]
    first_name = pl.multiple_of(start // listed * listed, listed)
    copies = [
        pltpu.make_async_copy(places, near, sems.at[len(bits)]),
        pltpu.make_async_copy(wanted.at[pl.ds(first_name, listed)], names, sems.at[len(bits) + 1]),
    ]
    parts = quarter_copies(spectra, held, sems, chan, bits)
    chunk = tile_rows // 4
    rows = [
        pltpu.make_async_copy(
            cotangent.at[pl.ds(n * chunk, chunk)],
            tile.at[pl.ds(n * chunk, chunk)],
            sems.at[len(bits) + 2 + n],
        )
        for n in range(4)
    ]
    order = copies + rows[:2] + parts[:1] + rows[2:] + parts[1:]
    for copy in order:
        copy.start()

    def fill(first, values):
        values = values.astype(jnp.float32)
        for side in range(2):
            table[pl.ds(2 * first + side, values.shape[0], stride=2), :] = values[
                :, side * half : (side + 1) * half
            ]

    for side in range(2):
        scale[pl.ds(side, NEIGH, stride=2), :] = mixing[:, side * half : (side + 1) * half]
    scales = [scale[2 * k : 2 * k + 2, :] for k in range(NEIGH)]
    fill(0, above[...])
    fill(HALO + tile_rows, below[...])
    for n in range(2):
        rows[2 * n].wait()
        rows[2 * n + 1].wait()
        if n < len(parts):
            parts[n].wait()
        for first in range(2 * n * chunk, 2 * (n + 1) * chunk, 256):
            fill(HALO + first, tile[first : first + 256, :])
        if n < len(parts):
            project_rows(held, weight, n, quarters[n])
    for copy in copies:
        copy.wait()

    group = 32
    offset = start - first_name

    def body(turn, carry):
        base = turn * group
        totals = []
        for n in range(group):
            pixel = names[offset + base + n]
            terms = [table[pl.ds(2 * (pixel + HALO), 2), :]]
            for k in range(NEIGH // 2):
                pair = near[k * tile_rows + pixel]
                for place, scale in ((pair & 0xFFFF, k), (pair >> 16, k + NEIGH // 2)):
                    terms.append(table[pl.ds(place, 2), :] * scales[scale])
            while len(terms) > 1:
                pairs = [x + y for x, y in zip(terms[::2], terms[1::2])]
                terms = pairs + terms[len(terms) // 2 * 2 :]
            totals += terms
        for n, total in enumerate(totals):
            sums[pl.ds(2 * (base + n), 2), :] = total
        return carry

    lax.fori_loop(0, count // group, body, 0)
    for side in range(2):
        out[:, side * half : (side + 1) * half] = sums[pl.ds(side, count, stride=2), :].astype(
            out.dtype
        )


def pixel_rows(
    cotangent, above, below, places, mixing, wanted, stride, count, spectra, weight, chan, bits, skip=0
):
    tile_rows, width = cotangent.shape
    depth, rows = spectra.shape[1], spectra.shape[0] // 4
    listed = min(wanted.shape[0], 1024)
    anywhere = pl.BlockSpec(memory_space=pl.ANY)
    hbm = pl.BlockSpec(memory_space=pltpu.HBM)
    vmem = pl.BlockSpec(memory_space=pltpu.VMEM)
    return pl.pallas_call(
        functools.partial(pixel_kernel, count, bits, stride, skip),
        out_shape=(
            jax.ShapeDtypeStruct((count, width), jnp.bfloat16),
            *[jax.ShapeDtypeStruct((rows, width), jnp.bfloat16)] * len(bits),
        ),
        in_specs=[
            pl.BlockSpec(memory_space=pltpu.SMEM),
            anywhere,
            anywhere,
            hbm,
            *[vmem] * 4,
            hbm,
        ],
        out_specs=(vmem,) * (1 + len(bits)),
        scratch_shapes=[
            pltpu.VMEM((2 * (tile_rows + 2 * HALO), width // 2), jnp.float32),
            pltpu.VMEM((2 * NEIGH, width // 2), jnp.float32),
            pltpu.VMEM((2 * count, width // 2), jnp.float32),
            pltpu.SMEM(places.shape, jnp.int32),
            pltpu.SMEM((listed,), jnp.int32),
            pltpu.VMEM((max(len(bits), 1) * rows, depth), jnp.bfloat16),
            pltpu.VMEM(cotangent.shape, cotangent.dtype),
            pltpu.SemaphoreType.DMA((len(bits) + 6,)),
        ],
        compiler_params=memory(LARGE),
        cost_estimate=pl.CostEstimate(
            flops=8 * NEIGH * count * 2048 * width,
            bytes_accessed=4 * tile_rows * width,
            transcendentals=0,
        ),
        name="pixel_rows",
    )(
        chan.reshape(1), places, wanted, cotangent, above, below, mixing, weight, spectra
    )


def gradient_kernel(tile_at, chan_at, keep, near, far, tiles, weights, mine, answers, out):
    tile, chan = tile_at[0], chan_at[0]
    rows = out.shape[0]
    size = tiles.shape[1]
    count = rows // size
    group = 8 // count
    wide = jnp.float32
    first = pl.multiple_of(chan // group * 8, 8)

    def columns(values):
        turned = values[pl.ds(first, 8), :].T
        places = [turned[:, n * count : (n + 1) * count] for n in range(group)]
        picked = places[0]
        for n in range(1, group):
            picked = jnp.where(chan % group == n, places[n], picked)
        return picked

    own = columns(tiles).astype(wide)
    factors = columns(weights)
    for n in range(count):
        here = slice(n * size, (n + 1) * size)
        pre = keep[here, :].astype(wide) + near[here, :].astype(wide) + far[here, :].astype(wide)
        sigma = jax.nn.sigmoid(pre)
        deriv = sigma * (1.0 + pre * (1.0 - sigma))
        fetched = jnp.where(
            own[:, n : n + 1] == tile.astype(wide),
            mine[here, :].astype(wide),
            answers[here, :].astype(wide),
        )
        out[here, :] = (factors[:, n : n + 1] * deriv * fetched).astype(out.dtype)


def pre_gradient(tile, chan, keep, near, far, tiles, weights, mine, answers):
    spec = pl.BlockSpec(memory_space=pltpu.VMEM)
    tiles, weights = tiles.reshape(-1, 128), weights.reshape(-1, 128)
    return pl.pallas_call(
        gradient_kernel,
        out_shape=jax.ShapeDtypeStruct(far.shape, jnp.bfloat16),
        in_specs=[pl.BlockSpec(memory_space=pltpu.SMEM)] * 2 + [spec] * 7,
        out_specs=spec,
        compiler_params=memory(16),
        name="pre_gradient",
    )(tile.reshape(1), chan.reshape(1), keep, near, far, tiles, weights, mine, answers)


def write_kernel(other, core, *refs):
    *pieces, out, first, second, sems = refs
    half, rows = out.shape[0] // 2, first.shape[0]
    copies = []
    for index, (piece, held) in enumerate(zip(pieces[-2:], (first, second))):
        held[...] = piece[...].astype(jnp.float32)
        place = (core[0] ^ other) * half + index * rows
        here = out.at[pl.ds(pl.multiple_of(place, rows), rows)]
        copies.append(pltpu.make_async_copy(held, here, sems.at[index]))
        copies[-1].start()
    for copy in copies:
        copy.wait()


def written(other, core, pieces, before=()):
    rows, width = pieces[0].shape
    spec = pl.BlockSpec(memory_space=pltpu.VMEM)
    hbm = pl.BlockSpec(memory_space=pltpu.HBM)
    return pl.pallas_call(
        functools.partial(write_kernel, other),
        out_shape=jax.ShapeDtypeStruct((4 * rows, width), jnp.float32),
        in_specs=[pl.BlockSpec(memory_space=pltpu.SMEM)] + [hbm] * len(before) + [spec] * 2,
        out_specs=hbm,
        input_output_aliases={1: 0} if before else {},
        scratch_shapes=[
            pltpu.VMEM((rows, width), jnp.float32),
            pltpu.VMEM((rows, width), jnp.float32),
            pltpu.SemaphoreType.DMA((2,)),
        ],
        compiler_params=memory(16),
        name="written",
    )(core.reshape(1), *before, *pieces)


def collect(core, own, received):
    return written(1, core, received, (written(0, core, own),))


def add_kernel(first, second, out):
    out[...] = (first[...].astype(jnp.float32) + second[...].astype(jnp.float32)).astype(out.dtype)


def added(first, second):
    spec = pl.BlockSpec(memory_space=pltpu.VMEM)
    return pl.pallas_call(
        add_kernel,
        out_shape=jax.ShapeDtypeStruct(first.shape, jnp.bfloat16),
        in_specs=[spec, spec],
        out_specs=spec,
        compiler_params=memory(16),
        name="added",
    )(first, second)


def sum_over_panels(core, parts, received):
    both = ("obs", "pix")
    parts = [added(part, other) for part, other in zip(parts, received)]
    for order in ((4, 1), (1, 4)):
        perm = [(i, i ^ order[(i >> 1) & 1]) for i in range(8)]
        parts = [added(part, lax.ppermute(part, both, perm)) for part in parts]
    return collect(core, parts, [swap(part, "obs", 1) for part in parts])


def shards(spectra, enc_weight, pix_tile, pix_local, foot_weight, cotangent, adjoint, mixing):
    tile_count = lax.axis_size("pix")
    tile_rows = cotangent.shape[0]
    quarter = spectra.shape[0] // lax.axis_size("chan")
    tile = lax.axis_index("pix")
    chan = lax.axis_index("chan")
    first_row = chan * quarter

    near_first = swap(project(spectra, enc_weight, chan, (2,), LARGE + 4)[0], "chan", 1)
    places = (adjoint - (tile * tile_rows - HALO)) * 2
    places = (places[: NEIGH // 2] | (places[NEIGH // 2 :] << 16)).reshape(-1)

    above, below = edges(cotangent, "pix", HALO)
    capacity = 2 * quarter // tile_count
    pixels = (cotangent, above, below, places, mixing)
    rest = (spectra, enc_weight)
    paired = capacity >= quarter and tile_count == 2
    if paired:
        wanted, stride, count = swap(pix_local, "pix", 1), quarter, quarter
    else:
        tile_ids = lax.dynamic_slice_in_dim(pix_tile[:, 0], first_row, quarter, 0)
        local_ids = lax.dynamic_slice_in_dim(pix_local, first_row, quarter, 0)
        slot_index, wanted = requests(tile_ids, local_ids, capacity)
        stride, count = 0, wanted.shape[0]
    part = count // 2
    rows, shared, send = pixel_rows(*pixels, wanted, stride, part, *rest, chan, (3, 1))
    near_first, rows = lax.optimization_barrier((near_first, rows))
    passed_on = (shared.astype(jnp.float32) + near_first.astype(jnp.float32)).astype(jnp.bfloat16)
    passed_on, send, rows, later = lax.optimization_barrier((passed_on, send, rows, chan))
    far = swap(passed_on, "chan", 3)
    near = swap(send, "chan", 1)
    (more,) = pixel_rows(*pixels, wanted, stride, count - part, *rest, later, (), part)
    rows = jnp.concatenate([rows, more])
    rows, later = lax.optimization_barrier((rows, later))
    if paired:
        answers = swap(rows, "pix", 1)
        mine, keep = pixel_rows(*pixels, pix_local, stride, count, *rest, later, (0,))
    else:
        (keep,) = project(*rest, later, (0,), LARGE)
        answers = lax.all_to_all(
            rows.reshape(tile_count, capacity, -1), "pix", split_axis=0, concat_axis=0, tiled=True
        )
        mine = answers = jnp.take(answers.reshape(tile_count * capacity, -1), slot_index, axis=0)
    grads = pre_gradient(tile, chan, keep, near, far, pix_tile, foot_weight, mine, answers)

    across = swap(grads, "chan", 3)
    beside = swap(grads, "chan", 1)
    last = swap(across, "chan", 1)
    early, held, held_last = early_product(spectra, chan, grads, across)
    early = more_product(held, early, beside)
    core = lax.axis_index("obs") & 1
    send, keep = late_product(core, held_last, early, last)
    if lax.axis_size("obs") == 4 and tile_count == 2:
        return sum_over_panels(core, keep, [swap(part, "obs", 1) for part in send])
    return lax.psum(collect(core, keep, send), ("obs", "pix"))


def solution(mesh):
    return jax.shard_map(
        shards,
        mesh=mesh,
        in_specs=(
            P(("obs", "pix"), "chan"),
            P("chan", None),
            P(("obs", "pix"), None),
            P(("obs", "pix")),
            P(("obs", "pix")),
            P("pix", None),
            P(None, "pix"),
            P(),
        ),
        out_specs=P("chan", None),
        check_vma=False,
    )
```

```python
import functools

import jax
import jax.numpy as jnp
from jax import lax
from jax.experimental import pallas as pl
from jax.experimental.pallas import tpu as pltpu
from jax.sharding import PartitionSpec as P

NEIGH = 8
HALO = 128
MIB = 1024 * 1024
LARGE = 52
CHUNKS = 3


def edges(value, axis, width):
    size, length = lax.axis_size(axis), value.shape[0]
    last = lax.slice_in_dim(value, length - width, length, axis=0)
    first = lax.slice_in_dim(value, 0, width, axis=0)
    if size == 2:
        index = lax.axis_index(axis)
        other = lax.ppermute(jnp.where(index == 0, last, first), axis, [(0, 1), (1, 0)])
        return other, other
    up = [(i, i + 1) for i in range(size - 1)]
    return lax.ppermute(last, axis, up), lax.ppermute(first, axis, [(j, i) for i, j in up])


def requests(tile_ids, local_ids, capacity):
    tile_count = lax.axis_size("pix")
    onehot = (tile_ids[:, None] == jnp.arange(tile_count, dtype=jnp.int32)[None, :]).astype(
        jnp.int32
    )
    place_rank = jnp.sum((jnp.cumsum(onehot, axis=0) - 1) * onehot, axis=1)
    slot_index = tile_ids * capacity + place_rank
    outgoing = jnp.full((tile_count * capacity,), 0, jnp.int32).at[slot_index].set(local_ids)
    outgoing = outgoing.reshape(tile_count, capacity)
    requested = lax.all_to_all(outgoing, "pix", split_axis=0, concat_axis=0, tiled=True)
    return slot_index, requested.reshape(-1)


def swap(value, axis, bit):
    size = 1
    for name in (axis,) if isinstance(axis, str) else axis:
        size *= lax.axis_size(name)
    return lax.ppermute(value, axis, [(i, i ^ bit) for i in range(size)])


def memory(mib):
    return pltpu.CompilerParams(vmem_limit_bytes=mib * MIB)


def quarter_copies(spectra, held, sems, chan, bits):
    rows = spectra.shape[0] // 4
    return [
        pltpu.make_async_copy(
            spectra.at[pl.ds(pl.multiple_of((chan ^ bit) * rows, rows), rows)],
            held.at[pl.ds(turn * rows, rows)],
            sems.at[turn],
        )
        for turn, bit in enumerate(bits)
    ]


def project_rows(held, weight, turn, out):
    rows = out.shape[0]
    result = jnp.dot(
        held[turn * rows : (turn + 1) * rows, :], weight[...], preferred_element_type=jnp.float32
    )
    out[...] = result.astype(out.dtype)


def project_kernel(bits, chan, spectra, weight, *refs):
    *outs, held, near, sems = refs
    copies = [pltpu.make_async_copy(weight, near, sems.at[len(bits)])]
    copies += quarter_copies(spectra, held, sems, chan[0], bits)
    for copy in copies:
        copy.start()
    copies[0].wait()
    for turn, out in enumerate(outs):
        copies[turn + 1].wait()
        project_rows(held, near, turn, out)


def project(spectra, weight, chan, bits, grant):
    depth, width = weight.shape
    rows = spectra.shape[0] // 4
    hbm = pl.BlockSpec(memory_space=pltpu.HBM)
    return pl.pallas_call(
        functools.partial(project_kernel, bits),
        out_shape=(jax.ShapeDtypeStruct((rows, width), jnp.bfloat16),) * len(bits),
        in_specs=[pl.BlockSpec(memory_space=pltpu.SMEM), hbm, hbm],
        out_specs=(pl.BlockSpec(memory_space=pltpu.VMEM),) * len(bits),
        scratch_shapes=[
            pltpu.VMEM((len(bits) * rows, depth), jnp.bfloat16),
            pltpu.VMEM((depth, width), jnp.bfloat16),
            pltpu.SemaphoreType.DMA((len(bits) + 1,)),
        ],
        compiler_params=memory(grant),
        cost_estimate=pl.CostEstimate(
            flops=2 * len(bits) * rows * depth * width,
            bytes_accessed=2 * len(bits) * rows * (depth + width) + 2 * depth * width,
            transcendentals=0,
        ),
        name="project",
    )(chan.reshape(1), spectra, weight)


def turned_product(left, right):
    return lax.dot_general(
        left, right, (((0,), (0,)), ((), ())), preferred_element_type=jnp.float32
    )


def early_kernel(chan, spectra, first, second, total, third, fourth, held, sems):
    rows = first.shape[0]
    targets = (held.at[pl.ds(0, rows)], held.at[pl.ds(rows, rows)], third, fourth)
    copies = []
    for turn, (bits, target) in enumerate(zip((0, 3, 1, 2), targets)):
        start = pl.multiple_of((chan[0] ^ bits) * rows, rows)
        copies.append(pltpu.make_async_copy(spectra.at[pl.ds(start, rows)], target, sems.at[turn]))
    for copy in copies:
        copy.start()
    copies[0].wait()
    product = turned_product(held[:rows, :], first[...])
    copies[1].wait()
    total[...] = product + turned_product(held[rows:, :], second[...])
    copies[2].wait()
    copies[3].wait()


def early_product(spectra, chan, first, second):
    depth = spectra.shape[1]
    rows, width = first.shape
    vmem = pl.BlockSpec(memory_space=pltpu.VMEM)
    return pl.pallas_call(
        early_kernel,
        out_shape=(
            jax.ShapeDtypeStruct((depth, width), jnp.float32),
            jax.ShapeDtypeStruct((rows, depth), jnp.bfloat16),
            jax.ShapeDtypeStruct((rows, depth), jnp.bfloat16),
        ),
        in_specs=[
            pl.BlockSpec(memory_space=pltpu.SMEM),
            pl.BlockSpec(memory_space=pltpu.HBM),
            vmem,
            vmem,
        ],
        out_specs=(vmem,) * 3,
        scratch_shapes=[
            pltpu.VMEM((2 * rows, depth), jnp.bfloat16),
            pltpu.SemaphoreType.DMA((4,)),
        ],
        compiler_params=memory(48),
        cost_estimate=pl.CostEstimate(
            flops=4 * rows * depth * width,
            bytes_accessed=8 * rows * depth + 4 * depth * width,
            transcendentals=0,
        ),
        name="early_product",
    )(chan.reshape(1), spectra, first, second)


def more_kernel(held, before, rows, total):
    total[...] = before[...] + turned_product(held[...], rows[...])


def more_product(held, before, rows):
    vmem = pl.BlockSpec(memory_space=pltpu.VMEM)
    return pl.pallas_call(
        more_kernel,
        out_shape=jax.ShapeDtypeStruct(before.shape, jnp.float32),
        in_specs=[vmem] * 3,
        out_specs=vmem,
        compiler_params=memory(16),
        cost_estimate=pl.CostEstimate(
            flops=2 * held.shape[0] * held.shape[1] * rows.shape[1],
            bytes_accessed=2 * held.shape[0] * held.shape[1] + 8 * before.size,
            transcendentals=0,
        ),
        name="more_product",
    )(held, before, rows)


def late_kernel(core, held, before, rows, *outs):
    *outs, total = outs
    total[...] = before[...] + turned_product(held[...], rows[...])
    size = outs[0].shape[0]
    for index, out in enumerate(outs):
        first = (core[0] ^ (1 - index // CHUNKS)) * CHUNKS * size + index % CHUNKS * size
        here = pl.ds(pl.multiple_of(first, size), size)
        out[...] = total[here, :].astype(out.dtype)


def late_product(core, held, before, rows):
    size, width = before.shape[0] // (2 * CHUNKS), before.shape[1]
    spec = pl.BlockSpec(memory_space=pltpu.VMEM)
    send = jax.ShapeDtypeStruct((size, width), jnp.bfloat16)
    keep = jax.ShapeDtypeStruct((size, width), jnp.float32)
    outs = pl.pallas_call(
        late_kernel,
        out_shape=(send,) * CHUNKS + (keep,) * CHUNKS,
        in_specs=[pl.BlockSpec(memory_space=pltpu.SMEM)] + [spec] * 3,
        out_specs=(spec,) * (2 * CHUNKS),
        scratch_shapes=[pltpu.VMEM(before.shape, jnp.float32)],
        compiler_params=memory(16),
        cost_estimate=pl.CostEstimate(
            flops=2 * held.shape[0] * held.shape[1] * width,
            bytes_accessed=2 * held.shape[0] * held.shape[1] + 16 * size * width,
            transcendentals=0,
        ),
        name="late_product",
    )(core.reshape(1), held, before, rows)
    return outs[:CHUNKS], outs[CHUNKS:]


def pixel_kernel(count, bits, stride, where, places, wanted, cotangent, above, below, mixing, weight,
                 spectra, out, *refs):
    quarters, refs = refs[: len(bits)], refs[len(bits) :]
    table, scale, sums, near, names, held, tile, sems = refs
    chan = where[0]
    start = chan * stride
    tile_rows, half = tile.shape[0], table.shape[1]
    listed = names.shape[0]
    first_name = pl.multiple_of(start // listed * listed, listed)
    copies = [
        pltpu.make_async_copy(places, near, sems.at[len(bits)]),
        pltpu.make_async_copy(wanted.at[pl.ds(first_name, listed)], names, sems.at[len(bits) + 1]),
    ]
    parts = quarter_copies(spectra, held, sems, chan, bits)
    chunk = tile_rows // 4
    rows = [
        pltpu.make_async_copy(
            cotangent.at[pl.ds(n * chunk, chunk)],
            tile.at[pl.ds(n * chunk, chunk)],
            sems.at[len(bits) + 2 + n],
        )
        for n in range(4)
    ]
    order = copies + rows[:2] + parts[:1] + rows[2:] + parts[1:]
    for copy in order:
        copy.start()

    def fill(first, values):
        values = values.astype(jnp.float32)
        for side in range(2):
            table[pl.ds(2 * first + side, values.shape[0], stride=2), :] = values[
                :, side * half : (side + 1) * half
            ]

    for side in range(2):
        scale[pl.ds(side, NEIGH, stride=2), :] = mixing[:, side * half : (side + 1) * half]
    scales = [scale[2 * k : 2 * k + 2, :] for k in range(NEIGH)]
    fill(0, above[...])
    fill(HALO + tile_rows, below[...])
    for n in range(2):
        rows[2 * n].wait()
        rows[2 * n + 1].wait()
        if n < len(parts):
            parts[n].wait()
        for first in range(2 * n * chunk, 2 * (n + 1) * chunk, 256):
            fill(HALO + first, tile[first : first + 256, :])
        if n < len(parts):
            project_rows(held, weight, n, quarters[n])
    for copy in copies:
        copy.wait()

    group = 32
    offset = start - first_name

    def body(turn, carry):
        base = turn * group
        totals = []
        for n in range(group):
            pixel = names[offset + base + n]
            terms = [table[pl.ds(2 * (pixel + HALO), 2), :]]
            for k in range(NEIGH // 2):
                pair = near[k * tile_rows + pixel]
                for place, scale in ((pair & 0xFFFF, k), (pair >> 16, k + NEIGH // 2)):
                    terms.append(table[pl.ds(place, 2), :] * scales[scale])
            while len(terms) > 1:
                pairs = [x + y for x, y in zip(terms[::2], terms[1::2])]
                terms = pairs + terms[len(terms) // 2 * 2 :]
            totals += terms
        for n, total in enumerate(totals):
            sums[pl.ds(2 * (base + n), 2), :] = total
        return carry

    lax.fori_loop(0, count // group, body, 0)
    for side in range(2):
        out[:, side * half : (side + 1) * half] = sums[pl.ds(side, count, stride=2), :].astype(
            out.dtype
        )


def pixel_rows(
    cotangent, above, below, places, mixing, wanted, stride, count, spectra, weight, chan, bits
):
    tile_rows, width = cotangent.shape
    depth, rows = spectra.shape[1], spectra.shape[0] // 4
    listed = min(wanted.shape[0], 1024)
    anywhere = pl.BlockSpec(memory_space=pl.ANY)
    hbm = pl.BlockSpec(memory_space=pltpu.HBM)
    vmem = pl.BlockSpec(memory_space=pltpu.VMEM)
    return pl.pallas_call(
        functools.partial(pixel_kernel, count, bits, stride),
        out_shape=(
            jax.ShapeDtypeStruct((count, width), jnp.bfloat16),
            *[jax.ShapeDtypeStruct((rows, width), jnp.bfloat16)] * len(bits),
        ),
        in_specs=[
            pl.BlockSpec(memory_space=pltpu.SMEM),
            anywhere,
            anywhere,
            hbm,
            *[vmem] * 4,
            hbm,
        ],
        out_specs=(vmem,) * (1 + len(bits)),
        scratch_shapes=[
            pltpu.VMEM((2 * (tile_rows + 2 * HALO), width // 2), jnp.float32),
            pltpu.VMEM((2 * NEIGH, width // 2), jnp.float32),
            pltpu.VMEM((2 * count, width // 2), jnp.float32),
            pltpu.SMEM(places.shape, jnp.int32),
            pltpu.SMEM((listed,), jnp.int32),
            pltpu.VMEM((max(len(bits), 1) * rows, depth), jnp.bfloat16),
            pltpu.VMEM(cotangent.shape, cotangent.dtype),
            pltpu.SemaphoreType.DMA((len(bits) + 6,)),
        ],
        compiler_params=memory(LARGE),
        cost_estimate=pl.CostEstimate(
            flops=8 * NEIGH * count * 2048 * width,
            bytes_accessed=4 * tile_rows * width,
            transcendentals=0,
        ),
        name="pixel_rows",
    )(
        chan.reshape(1), places, wanted, cotangent, above, below, mixing, weight, spectra
    )


def gradient_kernel(tile_at, chan_at, keep, near, far, tiles, weights, mine, answers, out):
    tile, chan = tile_at[0], chan_at[0]
    rows = out.shape[0]
    size = tiles.shape[1]
    count = rows // size
    group = 8 // count
    wide = jnp.float32
    first = pl.multiple_of(chan // group * 8, 8)

    def columns(values):
        turned = values[pl.ds(first, 8), :].T
        places = [turned[:, n * count : (n + 1) * count] for n in range(group)]
        picked = places[0]
        for n in range(1, group):
            picked = jnp.where(chan % group == n, places[n], picked)
        return picked

    own = columns(tiles).astype(wide)
    factors = columns(weights)
    for n in range(count):
        here = slice(n * size, (n + 1) * size)
        pre = keep[here, :].astype(wide) + near[here, :].astype(wide) + far[here, :].astype(wide)
        sigma = jax.nn.sigmoid(pre)
        deriv = sigma * (1.0 + pre * (1.0 - sigma))
        fetched = jnp.where(
            own[:, n : n + 1] == tile.astype(wide),
            mine[here, :].astype(wide),
            answers[here, :].astype(wide),
        )
        out[here, :] = (factors[:, n : n + 1] * deriv * fetched).astype(out.dtype)


def pre_gradient(tile, chan, keep, near, far, tiles, weights, mine, answers):
    spec = pl.BlockSpec(memory_space=pltpu.VMEM)
    tiles, weights = tiles.reshape(-1, 128), weights.reshape(-1, 128)
    return pl.pallas_call(
        gradient_kernel,
        out_shape=jax.ShapeDtypeStruct(far.shape, jnp.bfloat16),
        in_specs=[pl.BlockSpec(memory_space=pltpu.SMEM)] * 2 + [spec] * 7,
        out_specs=spec,
        compiler_params=memory(16),
        name="pre_gradient",
    )(tile.reshape(1), chan.reshape(1), keep, near, far, tiles, weights, mine, answers)


def write_kernel(other, core, *refs):
    out, holds, sems = refs[-CHUNKS - 2], refs[-CHUNKS - 1 : -1], refs[-1]
    pieces = refs[-2 * CHUNKS - 2 : -CHUNKS - 2]
    half, rows = out.shape[0] // 2, holds[0].shape[0]
    copies = []
    for index, (piece, held) in enumerate(zip(pieces, holds)):
        held[...] = piece[...].astype(jnp.float32)
        place = (core[0] ^ other) * half + index * rows
        here = out.at[pl.ds(pl.multiple_of(place, rows), rows)]
        copies.append(pltpu.make_async_copy(held, here, sems.at[index]))
        copies[-1].start()
    for copy in copies:
        copy.wait()


def written(other, core, pieces, before=()):
    rows, width = pieces[0].shape
    spec = pl.BlockSpec(memory_space=pltpu.VMEM)
    hbm = pl.BlockSpec(memory_space=pltpu.HBM)
    return pl.pallas_call(
        functools.partial(write_kernel, other),
        out_shape=jax.ShapeDtypeStruct((2 * CHUNKS * rows, width), jnp.float32),
        in_specs=[pl.BlockSpec(memory_space=pltpu.SMEM)] + [hbm] * len(before) + [spec] * CHUNKS,
        out_specs=hbm,
        input_output_aliases={1: 0} if before else {},
        scratch_shapes=[
            *[pltpu.VMEM((rows, width), jnp.float32)] * CHUNKS,
            pltpu.SemaphoreType.DMA((CHUNKS,)),
        ],
        compiler_params=memory(16),
        name="written",
    )(core.reshape(1), *before, *pieces)


def collect(core, own, received):
    return written(1, core, received, (written(0, core, own),))


def add_kernel(first, second, out):
    out[...] = (first[...].astype(jnp.float32) + second[...].astype(jnp.float32)).astype(out.dtype)


def added(first, second):
    spec = pl.BlockSpec(memory_space=pltpu.VMEM)
    return pl.pallas_call(
        add_kernel,
        out_shape=jax.ShapeDtypeStruct(first.shape, jnp.bfloat16),
        in_specs=[spec, spec],
        out_specs=spec,
        compiler_params=memory(16),
        name="added",
    )(first, second)


def sum_over_panels(core, parts, received):
    both = ("obs", "pix")
    parts = [added(part, other) for part, other in zip(parts, received)]
    for order in ((4, 1), (1, 4)):
        perm = [(i, i ^ order[(i >> 1) & 1]) for i in range(8)]
        parts = [added(part, lax.ppermute(part, both, perm)) for part in parts]
    return collect(core, parts, [swap(part, "obs", 1) for part in parts])


def shards(spectra, enc_weight, pix_tile, pix_local, foot_weight, cotangent, adjoint, mixing):
    tile_count = lax.axis_size("pix")
    tile_rows = cotangent.shape[0]
    quarter = spectra.shape[0] // lax.axis_size("chan")
    tile = lax.axis_index("pix")
    chan = lax.axis_index("chan")
    first_row = chan * quarter

    near_first = swap(project(spectra, enc_weight, chan, (2,), LARGE + 4)[0], "chan", 1)
    places = (adjoint - (tile * tile_rows - HALO)) * 2
    places = (places[: NEIGH // 2] | (places[NEIGH // 2 :] << 16)).reshape(-1)

    above, below = edges(cotangent, "pix", HALO)
    capacity = 2 * quarter // tile_count
    pixels = (cotangent, above, below, places, mixing)
    rest = (spectra, enc_weight)
    paired = capacity >= quarter and tile_count == 2
    if paired:
        wanted, stride, count = swap(pix_local, "pix", 1), quarter, quarter
    else:
        tile_ids = lax.dynamic_slice_in_dim(pix_tile[:, 0], first_row, quarter, 0)
        local_ids = lax.dynamic_slice_in_dim(pix_local, first_row, quarter, 0)
        slot_index, wanted = requests(tile_ids, local_ids, capacity)
        stride, count = 0, wanted.shape[0]
    rows, shared, send = pixel_rows(*pixels, wanted, stride, count, *rest, chan, (3, 1))
    near_first, rows = lax.optimization_barrier((near_first, rows))
    passed_on = (shared.astype(jnp.float32) + near_first.astype(jnp.float32)).astype(jnp.bfloat16)
    passed_on, send, rows, later = lax.optimization_barrier((passed_on, send, rows, chan))
    far = swap(passed_on, "chan", 3)
    near = swap(send, "chan", 1)
    if paired:
        answers = swap(rows, "pix", 1)
        mine, keep = pixel_rows(*pixels, pix_local, stride, count, *rest, later, (0,))
    else:
        (keep,) = project(*rest, later, (0,), LARGE)
        answers = lax.all_to_all(
            rows.reshape(tile_count, capacity, -1), "pix", split_axis=0, concat_axis=0, tiled=True
        )
        mine = answers = jnp.take(answers.reshape(tile_count * capacity, -1), slot_index, axis=0)
    grads = pre_gradient(tile, chan, keep, near, far, pix_tile, foot_weight, mine, answers)

    across = swap(grads, "chan", 3)
    beside = swap(grads, "chan", 1)
    last = swap(across, "chan", 1)
    early, held, held_last = early_product(spectra, chan, grads, across)
    early = more_product(held, early, beside)
    core = lax.axis_index("obs") & 1
    send, keep = late_product(core, held_last, early, last)
    if lax.axis_size("obs") == 4 and tile_count == 2:
        return sum_over_panels(core, keep, [swap(part, "obs", 1) for part in send])
    return lax.psum(collect(core, keep, send), ("obs", "pix"))


def solution(mesh):
    return jax.shard_map(
        shards,
        mesh=mesh,
        in_specs=(
            P(("obs", "pix"), "chan"),
            P("chan", None),
            P(("obs", "pix"), None),
            P(("obs", "pix")),
            P(("obs", "pix")),
            P("pix", None),
            P(None, "pix"),
            P(),
        ),
        out_specs=P("chan", None),
        check_vma=False,
    )
```

```python
import functools

import jax
import jax.numpy as jnp
from jax import lax
from jax.experimental import pallas as pl
from jax.experimental.pallas import tpu as pltpu
from jax.sharding import PartitionSpec as P

NEIGH = 8
HALO = 128
MIB = 1024 * 1024
LARGE = 52


def edges(value, axis, width):
    size, length = lax.axis_size(axis), value.shape[0]
    last = lax.slice_in_dim(value, length - width, length, axis=0)
    first = lax.slice_in_dim(value, 0, width, axis=0)
    if size == 2:
        index = lax.axis_index(axis)
        other = lax.ppermute(jnp.where(index == 0, last, first), axis, [(0, 1), (1, 0)])
        return other, other
    up = [(i, i + 1) for i in range(size - 1)]
    return lax.ppermute(last, axis, up), lax.ppermute(first, axis, [(j, i) for i, j in up])


def requests(tile_ids, local_ids, capacity):
    tile_count = lax.axis_size("pix")
    onehot = (tile_ids[:, None] == jnp.arange(tile_count, dtype=jnp.int32)[None, :]).astype(
        jnp.int32
    )
    place_rank = jnp.sum((jnp.cumsum(onehot, axis=0) - 1) * onehot, axis=1)
    slot_index = tile_ids * capacity + place_rank
    outgoing = jnp.full((tile_count * capacity,), 0, jnp.int32).at[slot_index].set(local_ids)
    outgoing = outgoing.reshape(tile_count, capacity)
    requested = lax.all_to_all(outgoing, "pix", split_axis=0, concat_axis=0, tiled=True)
    return slot_index, requested.reshape(-1)


def swap(value, axis, bit):
    size = 1
    for name in (axis,) if isinstance(axis, str) else axis:
        size *= lax.axis_size(name)
    return lax.ppermute(value, axis, [(i, i ^ bit) for i in range(size)])


def memory(mib):
    return pltpu.CompilerParams(vmem_limit_bytes=mib * MIB)


def quarter_copies(spectra, held, sems, chan, bits):
    rows = spectra.shape[0] // 4
    return [
        pltpu.make_async_copy(
            spectra.at[pl.ds(pl.multiple_of((chan ^ bit) * rows, rows), rows)],
            held.at[pl.ds(turn * rows, rows)],
            sems.at[turn],
        )
        for turn, bit in enumerate(bits)
    ]


def project_rows(held, weight, turn, out):
    rows = out.shape[0]
    result = jnp.dot(
        held[turn * rows : (turn + 1) * rows, :], weight[...], preferred_element_type=jnp.float32
    )
    out[...] = result.astype(out.dtype)


def project_kernel(bits, chan, spectra, weight, *refs):
    *outs, held, near, sems = refs
    copies = [pltpu.make_async_copy(weight, near, sems.at[len(bits)])]
    copies += quarter_copies(spectra, held, sems, chan[0], bits)
    for copy in copies:
        copy.start()
    copies[0].wait()
    for turn, out in enumerate(outs):
        copies[turn + 1].wait()
        project_rows(held, near, turn, out)


def project(spectra, weight, chan, bits, grant):
    depth, width = weight.shape
    rows = spectra.shape[0] // 4
    hbm = pl.BlockSpec(memory_space=pltpu.HBM)
    return pl.pallas_call(
        functools.partial(project_kernel, bits),
        out_shape=(jax.ShapeDtypeStruct((rows, width), jnp.bfloat16),) * len(bits),
        in_specs=[pl.BlockSpec(memory_space=pltpu.SMEM), hbm, hbm],
        out_specs=(pl.BlockSpec(memory_space=pltpu.VMEM),) * len(bits),
        scratch_shapes=[
            pltpu.VMEM((len(bits) * rows, depth), jnp.bfloat16),
            pltpu.VMEM((depth, width), jnp.bfloat16),
            pltpu.SemaphoreType.DMA((len(bits) + 1,)),
        ],
        compiler_params=memory(grant),
        cost_estimate=pl.CostEstimate(
            flops=2 * len(bits) * rows * depth * width,
            bytes_accessed=2 * len(bits) * rows * (depth + width) + 2 * depth * width,
            transcendentals=0,
        ),
        name="project",
    )(chan.reshape(1), spectra, weight)


def turned_product(left, right):
    return lax.dot_general(
        left, right, (((0,), (0,)), ((), ())), preferred_element_type=jnp.float32
    )


def early_kernel(chan, spectra, first, second, total, third, fourth, held, sems):
    rows = first.shape[0]
    targets = (held.at[pl.ds(0, rows)], held.at[pl.ds(rows, rows)], third, fourth)
    copies = []
    for turn, (bits, target) in enumerate(zip((0, 3, 1, 2), targets)):
        start = pl.multiple_of((chan[0] ^ bits) * rows, rows)
        copies.append(pltpu.make_async_copy(spectra.at[pl.ds(start, rows)], target, sems.at[turn]))
    for copy in copies:
        copy.start()
    copies[0].wait()
    product = turned_product(held[:rows, :], first[...])
    copies[1].wait()
    total[...] = product + turned_product(held[rows:, :], second[...])
    copies[2].wait()
    copies[3].wait()


def early_product(spectra, chan, first, second):
    depth = spectra.shape[1]
    rows, width = first.shape
    vmem = pl.BlockSpec(memory_space=pltpu.VMEM)
    return pl.pallas_call(
        early_kernel,
        out_shape=(
            jax.ShapeDtypeStruct((depth, width), jnp.float32),
            jax.ShapeDtypeStruct((rows, depth), jnp.bfloat16),
            jax.ShapeDtypeStruct((rows, depth), jnp.bfloat16),
        ),
        in_specs=[
            pl.BlockSpec(memory_space=pltpu.SMEM),
            pl.BlockSpec(memory_space=pltpu.HBM),
            vmem,
            vmem,
        ],
        out_specs=(vmem,) * 3,
        scratch_shapes=[
            pltpu.VMEM((2 * rows, depth), jnp.bfloat16),
            pltpu.SemaphoreType.DMA((4,)),
        ],
        compiler_params=memory(48),
        cost_estimate=pl.CostEstimate(
            flops=4 * rows * depth * width,
            bytes_accessed=8 * rows * depth + 4 * depth * width,
            transcendentals=0,
        ),
        name="early_product",
    )(chan.reshape(1), spectra, first, second)


def more_kernel(held, before, rows, total):
    total[...] = before[...] + turned_product(held[...], rows[...])


def more_product(held, before, rows):
    vmem = pl.BlockSpec(memory_space=pltpu.VMEM)
    return pl.pallas_call(
        more_kernel,
        out_shape=jax.ShapeDtypeStruct(before.shape, jnp.float32),
        in_specs=[vmem] * 3,
        out_specs=vmem,
        compiler_params=memory(16),
        cost_estimate=pl.CostEstimate(
            flops=2 * held.shape[0] * held.shape[1] * rows.shape[1],
            bytes_accessed=2 * held.shape[0] * held.shape[1] + 8 * before.size,
            transcendentals=0,
        ),
        name="more_product",
    )(held, before, rows)


def late_kernel(core, held, before, rows, *outs):
    *outs, total = outs
    total[...] = before[...] + turned_product(held[...], rows[...])
    size = outs[0].shape[0]
    for index, out in enumerate(outs):
        first = (core[0] ^ (1 - index // 2)) * 2 * size + index % 2 * size
        here = pl.ds(pl.multiple_of(first, size), size)
        out[...] = total[here, :].astype(out.dtype)


def late_product(core, held, before, rows):
    size, width = before.shape[0] // 4, before.shape[1]
    spec = pl.BlockSpec(memory_space=pltpu.VMEM)
    send = jax.ShapeDtypeStruct((size, width), jnp.bfloat16)
    keep = jax.ShapeDtypeStruct((size, width), jnp.float32)
    outs = pl.pallas_call(
        late_kernel,
        out_shape=(send, send, keep, keep),
        in_specs=[pl.BlockSpec(memory_space=pltpu.SMEM)] + [spec] * 3,
        out_specs=(spec,) * 4,
        scratch_shapes=[pltpu.VMEM(before.shape, jnp.float32)],
        compiler_params=memory(16),
        cost_estimate=pl.CostEstimate(
            flops=2 * held.shape[0] * held.shape[1] * width,
            bytes_accessed=2 * held.shape[0] * held.shape[1] + 16 * size * width,
            transcendentals=0,
        ),
        name="late_product",
    )(core.reshape(1), held, before, rows)
    return outs[:2], outs[2:]


def pixel_kernel(count, bits, stride, where, places, wanted, cotangent, above, below, mixing, weight,
                 spectra, out, *refs):
    quarters, refs = refs[: len(bits)], refs[len(bits) :]
    table, scale, sums, near, names, held, tile, sems = refs
    chan = where[0]
    start = chan * stride
    tile_rows, half = tile.shape[0], table.shape[1]
    listed = names.shape[0]
    first_name = pl.multiple_of(start // listed * listed, listed)
    copies = [
        pltpu.make_async_copy(places, near, sems.at[len(bits)]),
        pltpu.make_async_copy(wanted.at[pl.ds(first_name, listed)], names, sems.at[len(bits) + 1]),
    ]
    parts = quarter_copies(spectra, held, sems, chan, bits)
    chunk = tile_rows // 4
    rows = [
        pltpu.make_async_copy(
            cotangent.at[pl.ds(n * chunk, chunk)],
            tile.at[pl.ds(n * chunk, chunk)],
            sems.at[len(bits) + 2 + n],
        )
        for n in range(4)
    ]
    order = copies + rows[:2] + parts[:1] + rows[2:] + parts[1:]
    for copy in order:
        copy.start()

    def fill(first, values):
        values = values.astype(jnp.float32)
        for side in range(2):
            table[pl.ds(2 * first + side, values.shape[0], stride=2), :] = values[
                :, side * half : (side + 1) * half
            ]

    for side in range(2):
        scale[pl.ds(side, NEIGH, stride=2), :] = mixing[:, side * half : (side + 1) * half]
    scales = [scale[2 * k : 2 * k + 2, :] for k in range(NEIGH)]
    fill(0, above[...])
    fill(HALO + tile_rows, below[...])
    for n in range(2):
        rows[2 * n].wait()
        rows[2 * n + 1].wait()
        if n < len(parts):
            parts[n].wait()
        for first in range(2 * n * chunk, 2 * (n + 1) * chunk, 256):
            fill(HALO + first, tile[first : first + 256, :])
        if n < len(parts):
            project_rows(held, weight, n, quarters[n])
    for copy in copies:
        copy.wait()

    group = 32
    offset = start - first_name

    def body(turn, carry):
        base = turn * group
        totals = []
        for n in range(group):
            pixel = names[offset + base + n]
            terms = [table[pl.ds(2 * (pixel + HALO), 2), :]]
            for k in range(NEIGH // 2):
                pair = near[k * tile_rows + pixel]
                for place, scale in ((pair & 0xFFFF, k), (pair >> 16, k + NEIGH // 2)):
                    terms.append(table[pl.ds(place, 2), :] * scales[scale])
            while len(terms) > 1:
                pairs = [x + y for x, y in zip(terms[::2], terms[1::2])]
                terms = pairs + terms[len(terms) // 2 * 2 :]
            totals += terms
        for n, total in enumerate(totals):
            sums[pl.ds(2 * (base + n), 2), :] = total
        return carry

    lax.fori_loop(0, count // group, body, 0)
    for side in range(2):
        out[:, side * half : (side + 1) * half] = sums[pl.ds(side, count, stride=2), :].astype(
            out.dtype
        )


def pixel_rows(
    cotangent, above, below, places, mixing, wanted, stride, count, spectra, weight, chan, bits
):
    tile_rows, width = cotangent.shape
    depth, rows = spectra.shape[1], spectra.shape[0] // 4
    listed = min(wanted.shape[0], 1024)
    anywhere = pl.BlockSpec(memory_space=pl.ANY)
    hbm = pl.BlockSpec(memory_space=pltpu.HBM)
    vmem = pl.BlockSpec(memory_space=pltpu.VMEM)
    return pl.pallas_call(
        functools.partial(pixel_kernel, count, bits, stride),
        out_shape=(
            jax.ShapeDtypeStruct((count, width), jnp.bfloat16),
            *[jax.ShapeDtypeStruct((rows, width), jnp.bfloat16)] * len(bits),
        ),
        in_specs=[
            pl.BlockSpec(memory_space=pltpu.SMEM),
            anywhere,
            anywhere,
            hbm,
            *[vmem] * 4,
            hbm,
        ],
        out_specs=(vmem,) * (1 + len(bits)),
        scratch_shapes=[
            pltpu.VMEM((2 * (tile_rows + 2 * HALO), width // 2), jnp.float32),
            pltpu.VMEM((2 * NEIGH, width // 2), jnp.float32),
            pltpu.VMEM((2 * count, width // 2), jnp.float32),
            pltpu.SMEM(places.shape, jnp.int32),
            pltpu.SMEM((listed,), jnp.int32),
            pltpu.VMEM((max(len(bits), 1) * rows, depth), jnp.bfloat16),
            pltpu.VMEM(cotangent.shape, cotangent.dtype),
            pltpu.SemaphoreType.DMA((len(bits) + 6,)),
        ],
        compiler_params=memory(LARGE),
        cost_estimate=pl.CostEstimate(
            flops=8 * NEIGH * count * 2048 * width,
            bytes_accessed=4 * tile_rows * width,
            transcendentals=0,
        ),
        name="pixel_rows",
    )(
        chan.reshape(1), places, wanted, cotangent, above, below, mixing, weight, spectra
    )


def gradient_kernel(tile_at, chan_at, keep, near, far, tiles, weights, mine, answers, out):
    tile, chan = tile_at[0], chan_at[0]
    rows = out.shape[0]
    size = tiles.shape[1]
    count = rows // size
    group = 8 // count
    wide = jnp.float32
    first = pl.multiple_of(chan // group * 8, 8)

    def columns(values):
        turned = values[pl.ds(first, 8), :].T
        places = [turned[:, n * count : (n + 1) * count] for n in range(group)]
        picked = places[0]
        for n in range(1, group):
            picked = jnp.where(chan % group == n, places[n], picked)
        return picked

    own = columns(tiles).astype(wide)
    factors = columns(weights)
    for n in range(count):
        here = slice(n * size, (n + 1) * size)
        pre = keep[here, :].astype(wide) + near[here, :].astype(wide) + far[here, :].astype(wide)
        sigma = jax.nn.sigmoid(pre)
        deriv = sigma * (1.0 + pre * (1.0 - sigma))
        fetched = jnp.where(
            own[:, n : n + 1] == tile.astype(wide),
            mine[here, :].astype(wide),
            answers[here, :].astype(wide),
        )
        out[here, :] = (factors[:, n : n + 1] * deriv * fetched).astype(out.dtype)


def pre_gradient(tile, chan, keep, near, far, tiles, weights, mine, answers):
    spec = pl.BlockSpec(memory_space=pltpu.VMEM)
    tiles, weights = tiles.reshape(-1, 128), weights.reshape(-1, 128)
    return pl.pallas_call(
        gradient_kernel,
        out_shape=jax.ShapeDtypeStruct(far.shape, jnp.bfloat16),
        in_specs=[pl.BlockSpec(memory_space=pltpu.SMEM)] * 2 + [spec] * 7,
        out_specs=spec,
        compiler_params=memory(16),
        name="pre_gradient",
    )(tile.reshape(1), chan.reshape(1), keep, near, far, tiles, weights, mine, answers)


def write_kernel(other, core, *refs):
    *pieces, out, first, second, sems = refs
    half, rows = out.shape[0] // 2, first.shape[0]
    copies = []
    for index, (piece, held) in enumerate(zip(pieces[-2:], (first, second))):
        held[...] = piece[...].astype(jnp.float32)
        place = (core[0] ^ other) * half + index * rows
        here = out.at[pl.ds(pl.multiple_of(place, rows), rows)]
        copies.append(pltpu.make_async_copy(held, here, sems.at[index]))
        copies[-1].start()
    for copy in copies:
        copy.wait()


def written(other, core, pieces, before=()):
    rows, width = pieces[0].shape
    spec = pl.BlockSpec(memory_space=pltpu.VMEM)
    hbm = pl.BlockSpec(memory_space=pltpu.HBM)
    return pl.pallas_call(
        functools.partial(write_kernel, other),
        out_shape=jax.ShapeDtypeStruct((4 * rows, width), jnp.float32),
        in_specs=[pl.BlockSpec(memory_space=pltpu.SMEM)] + [hbm] * len(before) + [spec] * 2,
        out_specs=hbm,
        input_output_aliases={1: 0} if before else {},
        scratch_shapes=[
            pltpu.VMEM((rows, width), jnp.float32),
            pltpu.VMEM((rows, width), jnp.float32),
            pltpu.SemaphoreType.DMA((2,)),
        ],
        compiler_params=memory(16),
        name="written",
    )(core.reshape(1), *before, *pieces)


def collect(core, own, received):
    return written(1, core, received, (written(0, core, own),))


def add_kernel(first, second, out):
    out[...] = (first[...].astype(jnp.float32) + second[...].astype(jnp.float32)).astype(out.dtype)


def added(first, second):
    spec = pl.BlockSpec(memory_space=pltpu.VMEM)
    return pl.pallas_call(
        add_kernel,
        out_shape=jax.ShapeDtypeStruct(first.shape, jnp.bfloat16),
        in_specs=[spec, spec],
        out_specs=spec,
        compiler_params=memory(16),
        name="added",
    )(first, second)


def hand_on_kernel(value, out):
    out[...] = value[...]


def handed_on(value):
    spec = pl.BlockSpec(memory_space=pltpu.VMEM)
    return pl.pallas_call(
        hand_on_kernel,
        out_shape=jax.ShapeDtypeStruct(value.shape, value.dtype),
        in_specs=[spec],
        out_specs=spec,
        compiler_params=memory(16),
        name="handed_on",
    )(value)


def sum_over_panels(core, parts, received):
    both = ("obs", "pix")
    parts = [added(part, other) for part, other in zip(parts, received)]
    for order in ((4, 1), (1, 4)):
        perm = [(i, i ^ order[(i >> 1) & 1]) for i in range(8)]
        parts = [added(part, lax.ppermute(part, both, perm)) for part in parts]
    return collect(core, parts, [swap(part, "obs", 1) for part in parts])


def shards(spectra, enc_weight, pix_tile, pix_local, foot_weight, cotangent, adjoint, mixing):
    tile_count = lax.axis_size("pix")
    tile_rows = cotangent.shape[0]
    quarter = spectra.shape[0] // lax.axis_size("chan")
    tile = lax.axis_index("pix")
    chan = lax.axis_index("chan")
    first_row = chan * quarter

    near_first = swap(project(spectra, enc_weight, chan, (2,), LARGE + 4)[0], "chan", 1)
    places = (adjoint - (tile * tile_rows - HALO)) * 2
    places = (places[: NEIGH // 2] | (places[NEIGH // 2 :] << 16)).reshape(-1)

    above, below = edges(cotangent, "pix", HALO)
    capacity = 2 * quarter // tile_count
    pixels = (cotangent, above, below, places, mixing)
    rest = (spectra, enc_weight)
    paired = capacity >= quarter and tile_count == 2
    if paired:
        wanted, stride, count = swap(pix_local, "pix", 1), quarter, quarter
    else:
        tile_ids = lax.dynamic_slice_in_dim(pix_tile[:, 0], first_row, quarter, 0)
        local_ids = lax.dynamic_slice_in_dim(pix_local, first_row, quarter, 0)
        slot_index, wanted = requests(tile_ids, local_ids, capacity)
        stride, count = 0, wanted.shape[0]
    rows, shared, send = pixel_rows(*pixels, wanted, stride, count, *rest, chan, (3, 1))
    near_first, rows = lax.optimization_barrier((near_first, rows))
    passed_on = (shared.astype(jnp.float32) + near_first.astype(jnp.float32)).astype(jnp.bfloat16)
    passed_on, send, rows, later = lax.optimization_barrier((passed_on, send, rows, chan))
    far = swap(passed_on, "chan", 3)
    near = swap(send, "chan", 1)
    if paired:
        answers = swap(rows, "pix", 1)
        mine, keep = pixel_rows(*pixels, pix_local, stride, count, *rest, later, (0,))
    else:
        (keep,) = project(*rest, later, (0,), LARGE)
        answers = lax.all_to_all(
            rows.reshape(tile_count, capacity, -1), "pix", split_axis=0, concat_axis=0, tiled=True
        )
        mine = answers = jnp.take(answers.reshape(tile_count * capacity, -1), slot_index, axis=0)
    grads = pre_gradient(tile, chan, keep, near, far, pix_tile, foot_weight, mine, answers)

    across = swap(handed_on(grads), "chan", 3)
    beside = swap(grads, "chan", 1)
    last = swap(across, "chan", 1)
    early, held, held_last = early_product(spectra, chan, grads, across)
    early = more_product(held, early, beside)
    core = lax.axis_index("obs") & 1
    send, keep = late_product(core, held_last, early, last)
    if lax.axis_size("obs") == 4 and tile_count == 2:
        return sum_over_panels(core, keep, [swap(part, "obs", 1) for part in send])
    return lax.psum(collect(core, keep, send), ("obs", "pix"))


def solution(mesh):
    return jax.shard_map(
        shards,
        mesh=mesh,
        in_specs=(
            P(("obs", "pix"), "chan"),
            P("chan", None),
            P(("obs", "pix"), None),
            P(("obs", "pix")),
            P(("obs", "pix")),
            P("pix", None),
            P(None, "pix"),
            P(),
        ),
        out_specs=P("chan", None),
        check_vma=False,
    )
```

```python
import functools

import jax
import jax.numpy as jnp
from jax import lax
from jax.experimental import pallas as pl
from jax.experimental.pallas import tpu as pltpu
from jax.sharding import PartitionSpec as P

NEIGH = 8
HALO = 128
MIB = 1024 * 1024
LARGE = 52
CHUNKS = 4


def edges(value, axis, width):
    size, length = lax.axis_size(axis), value.shape[0]
    last = lax.slice_in_dim(value, length - width, length, axis=0)
    first = lax.slice_in_dim(value, 0, width, axis=0)
    if size == 2:
        index = lax.axis_index(axis)
        other = lax.ppermute(jnp.where(index == 0, last, first), axis, [(0, 1), (1, 0)])
        return other, other
    up = [(i, i + 1) for i in range(size - 1)]
    return lax.ppermute(last, axis, up), lax.ppermute(first, axis, [(j, i) for i, j in up])


def requests(tile_ids, local_ids, capacity):
    tile_count = lax.axis_size("pix")
    onehot = (tile_ids[:, None] == jnp.arange(tile_count, dtype=jnp.int32)[None, :]).astype(
        jnp.int32
    )
    place_rank = jnp.sum((jnp.cumsum(onehot, axis=0) - 1) * onehot, axis=1)
    slot_index = tile_ids * capacity + place_rank
    outgoing = jnp.full((tile_count * capacity,), 0, jnp.int32).at[slot_index].set(local_ids)
    outgoing = outgoing.reshape(tile_count, capacity)
    requested = lax.all_to_all(outgoing, "pix", split_axis=0, concat_axis=0, tiled=True)
    return slot_index, requested.reshape(-1)


def swap(value, axis, bit):
    size = 1
    for name in (axis,) if isinstance(axis, str) else axis:
        size *= lax.axis_size(name)
    return lax.ppermute(value, axis, [(i, i ^ bit) for i in range(size)])


def memory(mib):
    return pltpu.CompilerParams(vmem_limit_bytes=mib * MIB)


def quarter_copies(spectra, held, sems, chan, bits):
    rows = spectra.shape[0] // 4
    return [
        pltpu.make_async_copy(
            spectra.at[pl.ds(pl.multiple_of((chan ^ bit) * rows, rows), rows)],
            held.at[pl.ds(turn * rows, rows)],
            sems.at[turn],
        )
        for turn, bit in enumerate(bits)
    ]


def project_rows(held, weight, turn, out):
    rows = out.shape[0]
    result = jnp.dot(
        held[turn * rows : (turn + 1) * rows, :], weight[...], preferred_element_type=jnp.float32
    )
    out[...] = result.astype(out.dtype)


def project_kernel(bits, chan, spectra, weight, *refs):
    *outs, held, near, sems = refs
    copies = [pltpu.make_async_copy(weight, near, sems.at[len(bits)])]
    copies += quarter_copies(spectra, held, sems, chan[0], bits)
    for copy in copies:
        copy.start()
    copies[0].wait()
    for turn, out in enumerate(outs):
        copies[turn + 1].wait()
        project_rows(held, near, turn, out)


def project(spectra, weight, chan, bits, grant):
    depth, width = weight.shape
    rows = spectra.shape[0] // 4
    hbm = pl.BlockSpec(memory_space=pltpu.HBM)
    return pl.pallas_call(
        functools.partial(project_kernel, bits),
        out_shape=(jax.ShapeDtypeStruct((rows, width), jnp.bfloat16),) * len(bits),
        in_specs=[pl.BlockSpec(memory_space=pltpu.SMEM), hbm, hbm],
        out_specs=(pl.BlockSpec(memory_space=pltpu.VMEM),) * len(bits),
        scratch_shapes=[
            pltpu.VMEM((len(bits) * rows, depth), jnp.bfloat16),
            pltpu.VMEM((depth, width), jnp.bfloat16),
            pltpu.SemaphoreType.DMA((len(bits) + 1,)),
        ],
        compiler_params=memory(grant),
        cost_estimate=pl.CostEstimate(
            flops=2 * len(bits) * rows * depth * width,
            bytes_accessed=2 * len(bits) * rows * (depth + width) + 2 * depth * width,
            transcendentals=0,
        ),
        name="project",
    )(chan.reshape(1), spectra, weight)


def turned_product(left, right):
    return lax.dot_general(
        left, right, (((0,), (0,)), ((), ())), preferred_element_type=jnp.float32
    )


def early_kernel(chan, spectra, first, second, total, third, fourth, held, sems):
    rows = first.shape[0]
    targets = (held.at[pl.ds(0, rows)], held.at[pl.ds(rows, rows)], third, fourth)
    copies = []
    for turn, (bits, target) in enumerate(zip((0, 3, 1, 2), targets)):
        start = pl.multiple_of((chan[0] ^ bits) * rows, rows)
        copies.append(pltpu.make_async_copy(spectra.at[pl.ds(start, rows)], target, sems.at[turn]))
    for copy in copies:
        copy.start()
    copies[0].wait()
    product = turned_product(held[:rows, :], first[...])
    copies[1].wait()
    total[...] = product + turned_product(held[rows:, :], second[...])
    copies[2].wait()
    copies[3].wait()


def early_product(spectra, chan, first, second):
    depth = spectra.shape[1]
    rows, width = first.shape
    vmem = pl.BlockSpec(memory_space=pltpu.VMEM)
    return pl.pallas_call(
        early_kernel,
        out_shape=(
            jax.ShapeDtypeStruct((depth, width), jnp.float32),
            jax.ShapeDtypeStruct((rows, depth), jnp.bfloat16),
            jax.ShapeDtypeStruct((rows, depth), jnp.bfloat16),
        ),
        in_specs=[
            pl.BlockSpec(memory_space=pltpu.SMEM),
            pl.BlockSpec(memory_space=pltpu.HBM),
            vmem,
            vmem,
        ],
        out_specs=(vmem,) * 3,
        scratch_shapes=[
            pltpu.VMEM((2 * rows, depth), jnp.bfloat16),
            pltpu.SemaphoreType.DMA((4,)),
        ],
        compiler_params=memory(48),
        cost_estimate=pl.CostEstimate(
            flops=4 * rows * depth * width,
            bytes_accessed=8 * rows * depth + 4 * depth * width,
            transcendentals=0,
        ),
        name="early_product",
    )(chan.reshape(1), spectra, first, second)


def more_kernel(held, before, rows, total):
    total[...] = before[...] + turned_product(held[...], rows[...])


def more_product(held, before, rows):
    vmem = pl.BlockSpec(memory_space=pltpu.VMEM)
    return pl.pallas_call(
        more_kernel,
        out_shape=jax.ShapeDtypeStruct(before.shape, jnp.float32),
        in_specs=[vmem] * 3,
        out_specs=vmem,
        compiler_params=memory(16),
        cost_estimate=pl.CostEstimate(
            flops=2 * held.shape[0] * held.shape[1] * rows.shape[1],
            bytes_accessed=2 * held.shape[0] * held.shape[1] + 8 * before.size,
            transcendentals=0,
        ),
        name="more_product",
    )(held, before, rows)


def late_kernel(core, held, before, rows, *outs):
    *outs, total = outs
    total[...] = before[...] + turned_product(held[...], rows[...])
    size = outs[0].shape[0]
    for index, out in enumerate(outs):
        first = (core[0] ^ (1 - index // CHUNKS)) * CHUNKS * size + index % CHUNKS * size
        here = pl.ds(pl.multiple_of(first, size), size)
        out[...] = total[here, :].astype(out.dtype)


def late_product(core, held, before, rows):
    size, width = before.shape[0] // (2 * CHUNKS), before.shape[1]
    spec = pl.BlockSpec(memory_space=pltpu.VMEM)
    send = jax.ShapeDtypeStruct((size, width), jnp.bfloat16)
    keep = jax.ShapeDtypeStruct((size, width), jnp.float32)
    outs = pl.pallas_call(
        late_kernel,
        out_shape=(send,) * CHUNKS + (keep,) * CHUNKS,
        in_specs=[pl.BlockSpec(memory_space=pltpu.SMEM)] + [spec] * 3,
        out_specs=(spec,) * (2 * CHUNKS),
        scratch_shapes=[pltpu.VMEM(before.shape, jnp.float32)],
        compiler_params=memory(16),
        cost_estimate=pl.CostEstimate(
            flops=2 * held.shape[0] * held.shape[1] * width,
            bytes_accessed=2 * held.shape[0] * held.shape[1] + 16 * size * width,
            transcendentals=0,
        ),
        name="late_product",
    )(core.reshape(1), held, before, rows)
    return outs[:CHUNKS], outs[CHUNKS:]


def pixel_kernel(count, bits, stride, where, places, wanted, cotangent, above, below, mixing, weight,
                 spectra, out, *refs):
    quarters, refs = refs[: len(bits)], refs[len(bits) :]
    table, scale, sums, near, names, held, tile, sems = refs
    chan = where[0]
    start = chan * stride
    tile_rows, half = tile.shape[0], table.shape[1]
    listed = names.shape[0]
    first_name = pl.multiple_of(start // listed * listed, listed)
    copies = [
        pltpu.make_async_copy(places, near, sems.at[len(bits)]),
        pltpu.make_async_copy(wanted.at[pl.ds(first_name, listed)], names, sems.at[len(bits) + 1]),
    ]
    parts = quarter_copies(spectra, held, sems, chan, bits)
    chunk = tile_rows // 4
    rows = [
        pltpu.make_async_copy(
            cotangent.at[pl.ds(n * chunk, chunk)],
            tile.at[pl.ds(n * chunk, chunk)],
            sems.at[len(bits) + 2 + n],
        )
        for n in range(4)
    ]
    order = copies + rows[:2] + parts[:1] + rows[2:] + parts[1:]
    for copy in order:
        copy.start()

    def fill(first, values):
        values = values.astype(jnp.float32)
        for side in range(2):
            table[pl.ds(2 * first + side, values.shape[0], stride=2), :] = values[
                :, side * half : (side + 1) * half
            ]

    for side in range(2):
        scale[pl.ds(side, NEIGH, stride=2), :] = mixing[:, side * half : (side + 1) * half]
    scales = [scale[2 * k : 2 * k + 2, :] for k in range(NEIGH)]
    fill(0, above[...])
    fill(HALO + tile_rows, below[...])
    for n in range(2):
        rows[2 * n].wait()
        rows[2 * n + 1].wait()
        if n < len(parts):
            parts[n].wait()
        for first in range(2 * n * chunk, 2 * (n + 1) * chunk, 256):
            fill(HALO + first, tile[first : first + 256, :])
        if n < len(parts):
            project_rows(held, weight, n, quarters[n])
    for copy in copies:
        copy.wait()

    group = 32
    offset = start - first_name

    def body(turn, carry):
        base = turn * group
        totals = []
        for n in range(group):
            pixel = names[offset + base + n]
            terms = [table[pl.ds(2 * (pixel + HALO), 2), :]]
            for k in range(NEIGH // 2):
                pair = near[k * tile_rows + pixel]
                for place, scale in ((pair & 0xFFFF, k), (pair >> 16, k + NEIGH // 2)):
                    terms.append(table[pl.ds(place, 2), :] * scales[scale])
            while len(terms) > 1:
                pairs = [x + y for x, y in zip(terms[::2], terms[1::2])]
                terms = pairs + terms[len(terms) // 2 * 2 :]
            totals += terms
        for n, total in enumerate(totals):
            sums[pl.ds(2 * (base + n), 2), :] = total
        return carry

    lax.fori_loop(0, count // group, body, 0)
    for side in range(2):
        out[:, side * half : (side + 1) * half] = sums[pl.ds(side, count, stride=2), :].astype(
            out.dtype
        )


def pixel_rows(
    cotangent, above, below, places, mixing, wanted, stride, count, spectra, weight, chan, bits
):
    tile_rows, width = cotangent.shape
    depth, rows = spectra.shape[1], spectra.shape[0] // 4
    listed = min(wanted.shape[0], 1024)
    anywhere = pl.BlockSpec(memory_space=pl.ANY)
    hbm = pl.BlockSpec(memory_space=pltpu.HBM)
    vmem = pl.BlockSpec(memory_space=pltpu.VMEM)
    return pl.pallas_call(
        functools.partial(pixel_kernel, count, bits, stride),
        out_shape=(
            jax.ShapeDtypeStruct((count, width), jnp.bfloat16),
            *[jax.ShapeDtypeStruct((rows, width), jnp.bfloat16)] * len(bits),
        ),
        in_specs=[
            pl.BlockSpec(memory_space=pltpu.SMEM),
            anywhere,
            anywhere,
            hbm,
            *[vmem] * 4,
            hbm,
        ],
        out_specs=(vmem,) * (1 + len(bits)),
        scratch_shapes=[
            pltpu.VMEM((2 * (tile_rows + 2 * HALO), width // 2), jnp.float32),
            pltpu.VMEM((2 * NEIGH, width // 2), jnp.float32),
            pltpu.VMEM((2 * count, width // 2), jnp.float32),
            pltpu.SMEM(places.shape, jnp.int32),
            pltpu.SMEM((listed,), jnp.int32),
            pltpu.VMEM((max(len(bits), 1) * rows, depth), jnp.bfloat16),
            pltpu.VMEM(cotangent.shape, cotangent.dtype),
            pltpu.SemaphoreType.DMA((len(bits) + 6,)),
        ],
        compiler_params=memory(LARGE),
        cost_estimate=pl.CostEstimate(
            flops=8 * NEIGH * count * 2048 * width,
            bytes_accessed=4 * tile_rows * width,
            transcendentals=0,
        ),
        name="pixel_rows",
    )(
        chan.reshape(1), places, wanted, cotangent, above, below, mixing, weight, spectra
    )


def gradient_kernel(tile_at, chan_at, keep, near, far, tiles, weights, mine, answers, out):
    tile, chan = tile_at[0], chan_at[0]
    rows = out.shape[0]
    size = tiles.shape[1]
    count = rows // size
    group = 8 // count
    wide = jnp.float32
    first = pl.multiple_of(chan // group * 8, 8)

    def columns(values):
        turned = values[pl.ds(first, 8), :].T
        places = [turned[:, n * count : (n + 1) * count] for n in range(group)]
        picked = places[0]
        for n in range(1, group):
            picked = jnp.where(chan % group == n, places[n], picked)
        return picked

    own = columns(tiles).astype(wide)
    factors = columns(weights)
    for n in range(count):
        here = slice(n * size, (n + 1) * size)
        pre = keep[here, :].astype(wide) + near[here, :].astype(wide) + far[here, :].astype(wide)
        sigma = jax.nn.sigmoid(pre)
        deriv = sigma * (1.0 + pre * (1.0 - sigma))
        fetched = jnp.where(
            own[:, n : n + 1] == tile.astype(wide),
            mine[here, :].astype(wide),
            answers[here, :].astype(wide),
        )
        out[here, :] = (factors[:, n : n + 1] * deriv * fetched).astype(out.dtype)


def pre_gradient(tile, chan, keep, near, far, tiles, weights, mine, answers):
    spec = pl.BlockSpec(memory_space=pltpu.VMEM)
    tiles, weights = tiles.reshape(-1, 128), weights.reshape(-1, 128)
    return pl.pallas_call(
        gradient_kernel,
        out_shape=jax.ShapeDtypeStruct(far.shape, jnp.bfloat16),
        in_specs=[pl.BlockSpec(memory_space=pltpu.SMEM)] * 2 + [spec] * 7,
        out_specs=spec,
        compiler_params=memory(16),
        name="pre_gradient",
    )(tile.reshape(1), chan.reshape(1), keep, near, far, tiles, weights, mine, answers)


def write_kernel(other, core, *refs):
    out, holds, sems = refs[-CHUNKS - 2], refs[-CHUNKS - 1 : -1], refs[-1]
    pieces = refs[-2 * CHUNKS - 2 : -CHUNKS - 2]
    half, rows = out.shape[0] // 2, holds[0].shape[0]
    copies = []
    for index, (piece, held) in enumerate(zip(pieces, holds)):
        held[...] = piece[...].astype(jnp.float32)
        place = (core[0] ^ other) * half + index * rows
        here = out.at[pl.ds(pl.multiple_of(place, rows), rows)]
        copies.append(pltpu.make_async_copy(held, here, sems.at[index]))
        copies[-1].start()
    for copy in copies:
        copy.wait()


def written(other, core, pieces, before=()):
    rows, width = pieces[0].shape
    spec = pl.BlockSpec(memory_space=pltpu.VMEM)
    hbm = pl.BlockSpec(memory_space=pltpu.HBM)
    return pl.pallas_call(
        functools.partial(write_kernel, other),
        out_shape=jax.ShapeDtypeStruct((2 * CHUNKS * rows, width), jnp.float32),
        in_specs=[pl.BlockSpec(memory_space=pltpu.SMEM)] + [hbm] * len(before) + [spec] * CHUNKS,
        out_specs=hbm,
        input_output_aliases={1: 0} if before else {},
        scratch_shapes=[
            *[pltpu.VMEM((rows, width), jnp.float32)] * CHUNKS,
            pltpu.SemaphoreType.DMA((CHUNKS,)),
        ],
        compiler_params=memory(16),
        name="written",
    )(core.reshape(1), *before, *pieces)


def collect(core, own, received):
    return written(1, core, received, (written(0, core, own),))


def add_kernel(first, second, out):
    out[...] = (first[...].astype(jnp.float32) + second[...].astype(jnp.float32)).astype(out.dtype)


def added(first, second):
    spec = pl.BlockSpec(memory_space=pltpu.VMEM)
    return pl.pallas_call(
        add_kernel,
        out_shape=jax.ShapeDtypeStruct(first.shape, jnp.bfloat16),
        in_specs=[spec, spec],
        out_specs=spec,
        compiler_params=memory(16),
        name="added",
    )(first, second)


def sum_over_panels(core, parts, received):
    both = ("obs", "pix")
    parts = [added(part, other) for part, other in zip(parts, received)]
    for order in ((4, 1), (1, 4)):
        perm = [(i, i ^ order[(i >> 1) & 1]) for i in range(8)]
        parts = [added(part, lax.ppermute(part, both, perm)) for part in parts]
    return collect(core, parts, [swap(part, "obs", 1) for part in parts])


def shards(spectra, enc_weight, pix_tile, pix_local, foot_weight, cotangent, adjoint, mixing):
    tile_count = lax.axis_size("pix")
    tile_rows = cotangent.shape[0]
    quarter = spectra.shape[0] // lax.axis_size("chan")
    tile = lax.axis_index("pix")
    chan = lax.axis_index("chan")
    first_row = chan * quarter

    near_first = swap(project(spectra, enc_weight, chan, (2,), LARGE + 4)[0], "chan", 1)
    places = (adjoint - (tile * tile_rows - HALO)) * 2
    places = (places[: NEIGH // 2] | (places[NEIGH // 2 :] << 16)).reshape(-1)

    above, below = edges(cotangent, "pix", HALO)
    capacity = 2 * quarter // tile_count
    pixels = (cotangent, above, below, places, mixing)
    rest = (spectra, enc_weight)
    paired = capacity >= quarter and tile_count == 2
    if paired:
        wanted, stride, count = swap(pix_local, "pix", 1), quarter, quarter
    else:
        tile_ids = lax.dynamic_slice_in_dim(pix_tile[:, 0], first_row, quarter, 0)
        local_ids = lax.dynamic_slice_in_dim(pix_local, first_row, quarter, 0)
        slot_index, wanted = requests(tile_ids, local_ids, capacity)
        stride, count = 0, wanted.shape[0]
    rows, shared, send = pixel_rows(*pixels, wanted, stride, count, *rest, chan, (3, 1))
    near_first, rows = lax.optimization_barrier((near_first, rows))
    passed_on = (shared.astype(jnp.float32) + near_first.astype(jnp.float32)).astype(jnp.bfloat16)
    passed_on, send, rows, later = lax.optimization_barrier((passed_on, send, rows, chan))
    far = swap(passed_on, "chan", 3)
    near = swap(send, "chan", 1)
    if paired:
        answers = swap(rows, "pix", 1)
        mine, keep = pixel_rows(*pixels, pix_local, stride, count, *rest, later, (0,))
    else:
        (keep,) = project(*rest, later, (0,), LARGE)
        answers = lax.all_to_all(
            rows.reshape(tile_count, capacity, -1), "pix", split_axis=0, concat_axis=0, tiled=True
        )
        mine = answers = jnp.take(answers.reshape(tile_count * capacity, -1), slot_index, axis=0)
    grads = pre_gradient(tile, chan, keep, near, far, pix_tile, foot_weight, mine, answers)

    across = swap(grads, "chan", 3)
    beside = swap(grads, "chan", 1)
    last = swap(across, "chan", 1)
    early, held, held_last = early_product(spectra, chan, grads, across)
    early = more_product(held, early, beside)
    core = lax.axis_index("obs") & 1
    send, keep = late_product(core, held_last, early, last)
    if lax.axis_size("obs") == 4 and tile_count == 2:
        return sum_over_panels(core, keep, [swap(part, "obs", 1) for part in send])
    return lax.psum(collect(core, keep, send), ("obs", "pix"))


def solution(mesh):
    return jax.shard_map(
        shards,
        mesh=mesh,
        in_specs=(
            P(("obs", "pix"), "chan"),
            P("chan", None),
            P(("obs", "pix"), None),
            P(("obs", "pix")),
            P(("obs", "pix")),
            P("pix", None),
            P(None, "pix"),
            P(),
        ),
        out_specs=P("chan", None),
        check_vma=False,
    )
```
